32 devices in a mesh: wide: 16 (over z, y, core), narrow: 2 (over x).
Axes of the slice: x: 2, y: 2, z: 4, core: 2. Of those that a mesh axis runs over, the one named last changes fastest.
Arguments:
- tokens: bfloat16 [32768, 768], P(('wide', 'narrow')), may hold values from -6 to 6
- lengths: int32 [32], P(('wide', 'narrow')), may hold values from 512 to 1024, as said below
- raw_taps: float32 [1024, 768], P('narrow'), may hold values from -0.375 to 0.375
- ln1_gain: float32 [768], replicated, may hold values from 0.1 to 1.9
- ln1_shift: float32 [768], replicated, may hold values from -3 to 3
- w_in: bfloat16 [768, 1536], replicated, may hold values from -0.21875 to 0.21875
- w_out: bfloat16 [768, 768], replicated, may hold values from -0.21875 to 0.21875
- ln2_gain: float32 [768], replicated, may hold values from 0.1 to 1.9
- ln2_shift: float32 [768], replicated, may hold values from -3 to 3
- w_up: bfloat16 [768, 3072], replicated, may hold values from -0.21875 to 0.21875
- w_down: bfloat16 [3072, 768], replicated, may hold values from -0.109375 to 0.109375
- cotangent: bfloat16 [32768, 768], P(('wide', 'narrow')), may hold values from -6 to 6
Outputs:
- block_out: bfloat16 [32768, 768], P(('wide', 'narrow'))
- input_grad: float32 [32768, 768], P(('wide', 'narrow'))
- raw_grad: float32 [1024, 768], P('narrow')
- ln1_gain_grad: float32 [768], P(('wide', 'narrow'))
- ln1_shift_grad: float32 [768], P(('wide', 'narrow'))
- w_in_grad: float32 [768, 1536], P(('wide', 'narrow'))
- w_out_grad: float32 [768, 768], P(('wide', 'narrow'))
- ln2_gain_grad: float32 [768], P(('wide', 'narrow'))
- ln2_shift_grad: float32 [768], P(('wide', 'narrow'))
- w_up_grad: float32 [768, 3072], P(('wide', 'narrow'))
- w_down_grad: float32 [3072, 768], P(('wide', 'narrow'))
The draws below stay inside these ranges and needn't reach their ends.
Inputs may be any that keep to these rules, and one draw needn't show every extreme that they name: `lengths`: each entry is 1024 (the row holds one sequence) or 1024//2 (the row holds two sequences of 512 tokens); exactly half of the rows hold one sequence.
All inputs are finite; a program needn't handle non-finite values.
Results may differ from the reference program's by a relative error of at most 0.017.
Values may be sent and summed in bfloat16 or wider, within the bound.
A program may use at most 384 MiB of HBM per device.

```python
import jax
import jax.numpy as jnp
from jax import lax

D = 768
FF = 3072
SEQ = 1024
TAPS = 1024
ROWS = 32
TOKENS = 32768


def draw_lengths(key, part):
    key = jax.random.fold_in(key, 7)
    ordering = jax.random.permutation(key, ROWS)
    return SEQ // 2 * (1 + (ordering < ROWS // 2).astype(jnp.int32))


def steps_of(key, shape, split, smallest, largest):
    def one(axis_at, parts):
        heights = jax.random.uniform(jax.random.fold_in(jax.random.fold_in(key, 6), axis_at), (parts,), jnp.float32, smallest / len(split), largest / len(split))
        return jnp.repeat(jnp.exp(heights), shape[axis_at] // parts).reshape((-1,) + (1,) * (len(shape) - axis_at - 1))

    factor_of = one(*split[0])
    for cut in split[1:]:
        factor_of = factor_of * one(*cut)
    return factor_of


def centred(own_key, extent, width, most, split=(), kind=jnp.bfloat16):
    entries = jax.random.normal(own_key, extent, jnp.float32) * width
    if len(split) > 0:
        entries = steps_of(own_key, extent, split, -0.22, 0.18) * entries
    return jnp.clip(entries, min=-most, max=most).astype(kind)


def setup_inputs(seed: int = 0) -> dict:
    seeds = jax.random.split(jax.random.key(seed), 13)
    return {
        "tokens": centred(seeds[0], (TOKENS, D), 1.0, 6.0, ((0, 32),)),
        "lengths": draw_lengths(jax.random.fold_in(seeds[12], 71), 0),
        "raw_taps": centred(seeds[2], (TAPS, D), (2.0 / SEQ ** 0.5), 0.375, ((0, 2),), jnp.float32),
        "ln1_gain": jnp.clip(1.0 + 0.18 * jax.random.normal(seeds[3], (D,), jnp.float32), 0.1, 1.9),
        "ln1_shift": centred(seeds[4], (D,), 0.5, 3.0, (), jnp.float32),
        "w_in": centred(seeds[5], (D, 2 * D), D ** -0.5, 0.21875),
        "w_out": centred(seeds[6], (D, D), D ** -0.5, 0.21875),
        "ln2_gain": jnp.clip(1.0 + 0.18 * jax.random.normal(seeds[7], (D,), jnp.float32), 0.1, 1.9),
        "ln2_shift": centred(seeds[8], (D,), 0.5, 3.0, (), jnp.float32),
        "w_up": centred(seeds[9], (D, FF), D ** -0.5, 0.21875),
        "w_down": centred(seeds[10], (FF, D), FF ** -0.5, 0.109375),
        "cotangent": centred(seeds[11], (TOKENS, D), 1.0, 6.0, ((0, 32),)),
    }


shrink_level = 0.003
eps_norm = 1e-05
highest = lax.Precision.HIGHEST

@jax.custom_vjp
def low(v):
    return lax.optimization_barrier(v.astype(jnp.bfloat16)).astype(jnp.float32)

@jax.custom_vjp
def low_back(v):
    return v

def low_keep(v):
    return (low(v), None)

def low_pass(kept, grad):
    return (grad,)

def back_keep(v):
    return (v, None)

def back_low(kept, grad):
    return (low(grad),)
low.defvjp(low_keep, low_pass)
low_back.defvjp(back_keep, back_low)

def layer_norm(values, gain_vec, shift_vec):
    centered = values - lax.optimization_barrier(jnp.mean(values, axis=-1, keepdims=True))
    variance = lax.optimization_barrier(jnp.mean(centered * centered, axis=-1, keepdims=True))
    return centered * lax.rsqrt(variance + eps_norm) * gain_vec + shift_vec

def prepare(raw_values):
    squashed = raw_values - jnp.clip(raw_values, -shrink_level, shrink_level)
    padded = jnp.pad(squashed, ((1, 1), (0, 0)))
    return (padded[:-2] + padded[1:-1] + padded[2:]) / 3.0

def long_conv(signal, kernel):
    length_n = signal.shape[0]
    signal_spec = jnp.fft.rfft(signal, n=2 * length_n, axis=0)
    kernel_spec = jnp.fft.rfft(kernel[:length_n], n=2 * length_n, axis=0)
    return jnp.fft.irfft(signal_spec * kernel_spec, n=2 * length_n, axis=0)[:length_n]

def forward(inputs, first_len, raw_values, ln1_gain, ln1_shift, w_in, w_out, ln2_gain, ln2_shift, w_up, w_down):
    length_n, feat_width = inputs.shape
    kernel = low(prepare(raw_values))
    normed = low(layer_norm(inputs, ln1_gain, ln1_shift))
    projected = low_back(jnp.dot(normed, w_in, precision=highest))
    signal = low(projected[:, :feat_width])
    gate_vals = projected[:, feat_width:]
    positions = jnp.arange(length_n, dtype=jnp.int32)[:, None]
    second_part = (positions >= first_len).astype(inputs.dtype)
    mixed = (1.0 - second_part) * long_conv(signal, kernel) + second_part * long_conv(signal * second_part, kernel)
    mixed = low_back(mixed)
    branch = low(mixed * gate_vals)
    residual = inputs + low_back(jnp.dot(branch, w_out, precision=highest))
    normed2 = low(layer_norm(residual, ln2_gain, ln2_shift))
    hidden = low_back(jnp.dot(normed2, w_up, precision=highest))
    active = low(jax.nn.gelu(hidden))
    return residual + low_back(jnp.dot(active, w_down, precision=highest))

def reference(tokens, lengths, raw_taps, ln1_gain, ln1_shift, w_in, w_out, ln2_gain, ln2_shift, w_up, w_down, cotangent):
    feat_width = tokens.shape[1]
    row_inputs = tokens.astype(jnp.float32).reshape(ROWS, SEQ, feat_width)
    row_cots = cotangent.astype(jnp.float32).reshape(ROWS, SEQ, feat_width)
    weights_list = (raw_taps, ln1_gain, ln1_shift, w_in.astype(jnp.float32), w_out.astype(jnp.float32), ln2_gain, ln2_shift, w_up.astype(jnp.float32), w_down.astype(jnp.float32))
    grad_zeros = jax.tree.map(lambda leaf: jnp.zeros(leaf.shape, jnp.float32), weights_list)

    def scan_step(grad_totals, row_items):
        row_input, first_len, row_cot = row_items

        def row_forward(inputs, *weights):
            return forward(inputs, first_len, *weights)
        row_out, pullback = jax.vjp(row_forward, row_input, *weights_list)
        grads = pullback(row_cot)
        grad_totals = jax.tree.map(jnp.add, grad_totals, tuple(grads[1:]))
        return (grad_totals, (row_out.astype(jnp.bfloat16), grads[0]))
    totals, (row_outs, row_grads) = lax.scan(scan_step, grad_zeros, (row_inputs, lengths, row_cots))
    return (row_outs.reshape(TOKENS, feat_width), row_grads.reshape(TOKENS, feat_width), totals[0], totals[1], totals[2], totals[3], totals[4], totals[5], totals[6], totals[7], totals[8])
```

```python
import jax
import jax.numpy as jnp
import numpy as np
from jax import lax
from jax.sharding import PartitionSpec as P

shrink_level = 0.003
eps_norm = 1e-05


def wave_table(half):
    period = 4 * half
    phase = (np.outer(2 * np.arange(half) + 1, np.arange(half)) % period) * (2 * np.pi / period)
    return np.concatenate([np.cos(phase), -np.sin(phase)], axis=0)


def to_waves(table, block):
    return jnp.einsum("kn,nc->kc", table, block, preferred_element_type=jnp.float32)


def from_waves(table, waves):
    return jnp.einsum(
        "kn,kc->nc", table, waves.astype(jnp.bfloat16), preferred_element_type=jnp.float32
    )


def norm_parts(values):
    centered = values - jnp.mean(values, axis=-1, keepdims=True)
    inverse = lax.rsqrt(jnp.mean(centered * centered, axis=-1, keepdims=True) + eps_norm)
    return (centered * inverse, inverse)


def norm_back(upstream, unit_vals, inverse, gain_vec):
    scaled = upstream * gain_vec
    return inverse * (
        scaled
        - jnp.mean(scaled, axis=-1, keepdims=True)
        - unit_vals * jnp.mean(scaled * unit_vals, axis=-1, keepdims=True)
    )


def split(waves):
    half = waves.shape[0] // 2
    return waves[:half], waves[half:]


def times(left, right):
    lr, li = split(left)
    rr, ri = split(right)
    return jnp.concatenate([lr * rr - li * ri, lr * ri + li * rr], axis=0)


def conj_times(left, right):
    lr, li = split(left)
    rr, ri = split(right)
    return jnp.concatenate([lr * rr + li * ri, lr * ri - li * rr], axis=0)


def turned(waves, sign):
    wr, wi = split(waves)
    index = lax.broadcasted_iota(jnp.int32, (wr.shape[0], 1), 0)
    parity = sign * (1.0 - 2.0 * (index % 2).astype(jnp.float32))
    return jnp.concatenate([-parity * wi, parity * wr], axis=0)


def pool(values):
    padded = jnp.pad(values, ((1, 1), (0, 0)))
    return (padded[:-2] + padded[1:-1] + padded[2:]) / 3.0


def local(
    tokens,
    lengths,
    raw_taps,
    ln1_gain,
    ln1_shift,
    w_in,
    w_out,
    ln2_gain,
    ln2_shift,
    w_up,
    w_down,
    cotangent,
):
    tok_count, feat_width = tokens.shape
    row_count = lengths.shape[0]
    row_len = tok_count // row_count
    half = row_len // 2
    table = jnp.asarray(wave_table(half), jnp.bfloat16)
    scale = 1.0 / half
    long_rows = (lengths > half).astype(jnp.float32)

    squashed = raw_taps - jnp.clip(raw_taps, -shrink_level, shrink_level)
    gathered = lax.all_gather(squashed.astype(jnp.bfloat16), "narrow", axis=0, tiled=True)
    kernel = pool(gathered.astype(jnp.float32)).astype(jnp.bfloat16)
    kernel_low = to_waves(table, kernel[:half])
    kernel_cross = to_waves(table, kernel[half : 2 * half]) + turned(kernel_low, 1.0)

    inputs = tokens.astype(jnp.float32)
    unit_one, inverse_one = norm_parts(inputs)
    normed = (unit_one * ln1_gain + ln1_shift).astype(jnp.bfloat16)
    projected = jnp.dot(normed, w_in, preferred_element_type=jnp.float32)
    signal = projected[:, :feat_width].astype(jnp.bfloat16)
    gate_vals = projected[:, feat_width:]
    signal_waves = []
    mixed = []
    for row in range(row_count):
        first = to_waves(table, signal[row * row_len : row * row_len + half])
        second = to_waves(table, signal[row * row_len + half : (row + 1) * row_len])
        signal_waves.append((first, second))
        mixed.append(from_waves(table, times(first, kernel_low) * scale))
        mixed.append(
            from_waves(
                table,
                (times(second, kernel_low) + long_rows[row] * times(first, kernel_cross)) * scale,
            )
        )
    mixed = jnp.concatenate(mixed, axis=0)
    branch = (mixed * gate_vals).astype(jnp.bfloat16)
    residual = inputs + jnp.dot(branch, w_out, preferred_element_type=jnp.float32)
    unit_two, inverse_two = norm_parts(residual)
    normed2 = (unit_two * ln2_gain + ln2_shift).astype(jnp.bfloat16)
    hidden = jnp.dot(normed2, w_up, preferred_element_type=jnp.float32)
    active = jax.nn.gelu(hidden).astype(jnp.bfloat16)
    block_out = (residual + jnp.dot(active, w_down, preferred_element_type=jnp.float32)).astype(
        jnp.bfloat16
    )
    w_down_grad = jnp.einsum("tf,td->fd", active, cotangent, preferred_element_type=jnp.float32)
    d_active = jnp.einsum("td,fd->tf", cotangent, w_down, preferred_element_type=jnp.float32)
    gelu_pull = jax.vjp(jax.nn.gelu, hidden)[1]
    d_hidden = gelu_pull(d_active)[0].astype(jnp.bfloat16)
    w_up_grad = jnp.einsum("td,tf->df", normed2, d_hidden, preferred_element_type=jnp.float32)
    d_normed2 = jnp.einsum("tf,df->td", d_hidden, w_up, preferred_element_type=jnp.float32)
    ln2_gain_grad = jnp.sum(d_normed2 * unit_two, axis=0)
    ln2_shift_grad = jnp.sum(d_normed2, axis=0)
    d_residual = cotangent.astype(jnp.float32) + norm_back(
        d_normed2, unit_two, inverse_two, ln2_gain
    )
    d_outproj = d_residual.astype(jnp.bfloat16)
    w_out_grad = jnp.einsum("td,te->de", branch, d_outproj, preferred_element_type=jnp.float32)
    d_branch = jnp.einsum("te,de->td", d_outproj, w_out, preferred_element_type=jnp.float32)
    d_mixed = (d_branch * gate_vals).astype(jnp.bfloat16)
    d_gate = d_branch * mixed
    d_signal = []
    low_grad = 0.0
    cross_grad = 0.0
    for row in range(row_count):
        first, second = signal_waves[row]
        d_first = to_waves(table, d_mixed[row * row_len : row * row_len + half]) * scale
        d_second = to_waves(table, d_mixed[row * row_len + half : (row + 1) * row_len]) * scale
        d_cross = d_second * long_rows[row]
        d_signal.append(
            from_waves(table, conj_times(kernel_low, d_first) + conj_times(kernel_cross, d_cross))
        )
        d_signal.append(from_waves(table, conj_times(kernel_low, d_second)))
        low_grad = low_grad + conj_times(first, d_first) + conj_times(second, d_second)
        cross_grad = cross_grad + conj_times(first, d_cross)
    low_grad = low_grad + turned(cross_grad, -1.0)
    d_kernel = jnp.concatenate([from_waves(table, low_grad), from_waves(table, cross_grad)], axis=0)
    d_signal = jnp.concatenate(d_signal, axis=0)
    d_projected = jnp.concatenate([d_signal, d_gate], axis=1).astype(jnp.bfloat16)
    w_in_grad = jnp.einsum("td,te->de", normed, d_projected, preferred_element_type=jnp.float32)
    d_normed = jnp.einsum("te,de->td", d_projected, w_in, preferred_element_type=jnp.float32)
    ln1_gain_grad = jnp.sum(d_normed * unit_one, axis=0)
    ln1_shift_grad = jnp.sum(d_normed, axis=0)
    input_grad = d_residual + norm_back(d_normed, unit_one, inverse_one, ln1_gain)

    shares = lax.psum_scatter(
        pool(d_kernel).astype(jnp.bfloat16), "narrow", scatter_dimension=0, tiled=True
    )
    summed = lax.psum(shares, "wide").astype(jnp.float32)
    raw_grad = summed * (jnp.abs(raw_taps) > shrink_level).astype(jnp.float32)

    def scatter(values):
        return lax.psum_scatter(
            values.astype(jnp.bfloat16), ("wide", "narrow"), scatter_dimension=0, tiled=True
        ).astype(jnp.float32)

    def scatter_wide(values):
        return lax.psum_scatter(values, ("wide", "narrow"), scatter_dimension=0, tiled=True)

    return (
        block_out,
        input_grad,
        raw_grad,
        scatter_wide(ln1_gain_grad),
        scatter_wide(ln1_shift_grad),
        scatter(w_in_grad),
        scatter(w_out_grad),
        scatter_wide(ln2_gain_grad),
        scatter_wide(ln2_shift_grad),
        scatter(w_up_grad),
        scatter(w_down_grad),
    )


def solution(mesh):
    spread = P(("wide", "narrow"))
    rows = P(("wide", "narrow"), None)
    placed = (rows, spread, P("narrow", None)) + (P(),) * 8 + (rows,)
    return jax.shard_map(
        local,
        mesh=mesh,
        in_specs=placed,
        out_specs=(rows, rows, P("narrow", None), spread, spread, rows, rows, spread, spread, rows, rows),
        check_vma=False,
    )
```

```python
import functools

import jax
import jax.numpy as jnp
import numpy as np
from jax import lax
from jax.experimental import pallas as pl
from jax.experimental.pallas import tpu as pltpu
from jax.sharding import PartitionSpec as P

shrink_level = 0.003
eps_norm = 1e-05


def wave_table(half):
    period = 4 * half
    phase = (np.outer(2 * np.arange(half) + 1, np.arange(half)) % period) * (2 * np.pi / period)
    return np.concatenate([np.cos(phase), -np.sin(phase)], axis=0)


def to_waves(table, block):
    return jnp.einsum("kn,nc->kc", table, block, preferred_element_type=jnp.float32)


def from_waves(table, waves):
    return jnp.einsum(
        "kn,kc->nc", table, waves.astype(jnp.bfloat16), preferred_element_type=jnp.float32
    )


def norm_parts(values):
    centered = values - jnp.mean(values, axis=-1, keepdims=True)
    inverse = lax.rsqrt(jnp.mean(centered * centered, axis=-1, keepdims=True) + eps_norm)
    return (centered * inverse, inverse)


def norm_back(upstream, unit_vals, inverse, gain_vec):
    scaled = upstream * gain_vec
    return inverse * (
        scaled
        - jnp.mean(scaled, axis=-1, keepdims=True)
        - unit_vals * jnp.mean(scaled * unit_vals, axis=-1, keepdims=True)
    )


def split(waves):
    half = waves.shape[0] // 2
    return waves[:half], waves[half:]


def times(left, right):
    lr, li = split(left)
    rr, ri = split(right)
    return jnp.concatenate([lr * rr - li * ri, lr * ri + li * rr], axis=0)


def conj_times(left, right):
    lr, li = split(left)
    rr, ri = split(right)
    return jnp.concatenate([lr * rr + li * ri, lr * ri - li * rr], axis=0)


def turned(waves, sign):
    wr, wi = split(waves)
    index = lax.broadcasted_iota(jnp.int32, (wr.shape[0], 1), 0)
    parity = sign * (1.0 - 2.0 * (index % 2).astype(jnp.float32))
    return jnp.concatenate([-parity * wi, parity * wr], axis=0)


def pool(values):
    padded = jnp.pad(values, ((1, 1), (0, 0)))
    return (padded[:-2] + padded[1:-1] + padded[2:]) / 3.0


def local(
    tokens,
    lengths,
    raw_taps,
    ln1_gain,
    ln1_shift,
    w_in,
    w_out,
    ln2_gain,
    ln2_shift,
    w_up,
    w_down,
    cotangent,
):
    tok_count, feat_width = tokens.shape
    row_count = lengths.shape[0]
    row_len = tok_count // row_count
    half = row_len // 2
    table = jnp.asarray(wave_table(half), jnp.bfloat16)
    scale = 1.0 / half
    long_rows = (lengths > half).astype(jnp.float32)

    squashed = raw_taps - jnp.clip(raw_taps, -shrink_level, shrink_level)
    gathered = lax.all_gather(squashed.astype(jnp.bfloat16), "narrow", axis=0, tiled=True)
    kernel = pool(gathered.astype(jnp.float32)).astype(jnp.bfloat16)
    kernel_low = to_waves(table, kernel[:half])
    kernel_cross = to_waves(table, kernel[half : 2 * half]) + turned(kernel_low, 1.0)

    inputs = tokens.astype(jnp.float32)
    unit_one, inverse_one = norm_parts(inputs)
    normed = (unit_one * ln1_gain + ln1_shift).astype(jnp.bfloat16)
    projected = jnp.dot(normed, w_in, preferred_element_type=jnp.float32)
    signal = projected[:, :feat_width].astype(jnp.bfloat16)
    gate_vals = projected[:, feat_width:]
    signal_waves = []
    mixed = []
    for row in range(row_count):
        first = to_waves(table, signal[row * row_len : row * row_len + half])
        second = to_waves(table, signal[row * row_len + half : (row + 1) * row_len])
        signal_waves.append((first, second))
        mixed.append(from_waves(table, times(first, kernel_low) * scale))
        mixed.append(
            from_waves(
                table,
                (times(second, kernel_low) + long_rows[row] * times(first, kernel_cross)) * scale,
            )
        )
    mixed = jnp.concatenate(mixed, axis=0)
    branch = (mixed * gate_vals).astype(jnp.bfloat16)
    residual = inputs + jnp.dot(branch, w_out, preferred_element_type=jnp.float32)
    unit_two, inverse_two = norm_parts(residual)
    normed2 = (unit_two * ln2_gain + ln2_shift).astype(jnp.bfloat16)
    hidden = jnp.dot(normed2, w_up, preferred_element_type=jnp.float32)
    active = jax.nn.gelu(hidden).astype(jnp.bfloat16)
    block_out = (residual + jnp.dot(active, w_down, preferred_element_type=jnp.float32)).astype(
        jnp.bfloat16
    )
    w_down_grad = jnp.einsum("tf,td->fd", active, cotangent, preferred_element_type=jnp.float32)
    d_active = jnp.einsum("td,fd->tf", cotangent, w_down, preferred_element_type=jnp.float32)
    gelu_pull = jax.vjp(jax.nn.gelu, hidden)[1]
    d_hidden = gelu_pull(d_active)[0].astype(jnp.bfloat16)
    w_up_grad = jnp.einsum("td,tf->df", normed2, d_hidden, preferred_element_type=jnp.float32)
    d_normed2 = jnp.einsum("tf,df->td", d_hidden, w_up, preferred_element_type=jnp.float32)
    ln2_gain_grad = jnp.sum(d_normed2 * unit_two, axis=0)
    ln2_shift_grad = jnp.sum(d_normed2, axis=0)
    d_residual = cotangent.astype(jnp.float32) + norm_back(
        d_normed2, unit_two, inverse_two, ln2_gain
    )
    d_outproj = d_residual.astype(jnp.bfloat16)
    w_out_grad = jnp.einsum("td,te->de", branch, d_outproj, preferred_element_type=jnp.float32)
    d_branch = jnp.einsum("te,de->td", d_outproj, w_out, preferred_element_type=jnp.float32)
    d_mixed = (d_branch * gate_vals).astype(jnp.bfloat16)
    d_gate = d_branch * mixed
    d_signal = []
    low_grad = 0.0
    cross_grad = 0.0
    for row in range(row_count):
        first, second = signal_waves[row]
        d_first = to_waves(table, d_mixed[row * row_len : row * row_len + half]) * scale
        d_second = to_waves(table, d_mixed[row * row_len + half : (row + 1) * row_len]) * scale
        d_cross = d_second * long_rows[row]
        d_signal.append(
            from_waves(table, conj_times(kernel_low, d_first) + conj_times(kernel_cross, d_cross))
        )
        d_signal.append(from_waves(table, conj_times(kernel_low, d_second)))
        low_grad = low_grad + conj_times(first, d_first) + conj_times(second, d_second)
        cross_grad = cross_grad + conj_times(first, d_cross)
    low_grad = low_grad + turned(cross_grad, -1.0)
    d_kernel = jnp.concatenate([from_waves(table, low_grad), from_waves(table, cross_grad)], axis=0)
    d_signal = jnp.concatenate(d_signal, axis=0)
    d_projected = jnp.concatenate([d_signal, d_gate], axis=1).astype(jnp.bfloat16)
    w_in_grad = jnp.einsum("td,te->de", normed, d_projected, preferred_element_type=jnp.float32)
    d_normed = jnp.einsum("te,de->td", d_projected, w_in, preferred_element_type=jnp.float32)
    ln1_gain_grad = jnp.sum(d_normed * unit_one, axis=0)
    ln1_shift_grad = jnp.sum(d_normed, axis=0)
    input_grad = d_residual + norm_back(d_normed, unit_one, inverse_one, ln1_gain)

    shares = lax.psum_scatter(
        pool(d_kernel).astype(jnp.bfloat16), "narrow", scatter_dimension=0, tiled=True
    )
    summed = lax.psum(shares, "wide").astype(jnp.float32)
    raw_grad = summed * (jnp.abs(raw_taps) > shrink_level).astype(jnp.float32)

    def scatter(values):
        return lax.psum_scatter(
            values.astype(jnp.bfloat16), ("wide", "narrow"), scatter_dimension=0, tiled=True
        ).astype(jnp.float32)

    def scatter_wide(values):
        return lax.psum_scatter(values, ("wide", "narrow"), scatter_dimension=0, tiled=True)

    return (
        block_out,
        input_grad,
        raw_grad,
        scatter_wide(ln1_gain_grad),
        scatter_wide(ln1_shift_grad),
        scatter(w_in_grad),
        scatter(w_out_grad),
        scatter_wide(ln2_gain_grad),
        scatter_wide(ln2_shift_grad),
        scatter(w_up_grad),
        scatter(w_down_grad),
    )


MESH = pl.DeviceIdType.MESH
PART = 9
STORES = 30
VMEM_BYTES = 60 * 2**20
FLIGHTS = 3


def dot_nn(left, right):
    return lax.dot_general(left, right, (((1,), (0,)), ((), ())), preferred_element_type=jnp.float32)


def dot_nt(left, right):
    return lax.dot_general(left, right, (((1,), (1,)), ((), ())), preferred_element_type=jnp.float32)


def dot_tn(left, right):
    return lax.dot_general(left, right, (((0,), (0,)), ((), ())), preferred_element_type=jnp.float32)


def gelu_both(hidden):
    inner = 0.7978845608028654
    cubic = inner * 0.044715
    square = hidden * hidden
    bent = jnp.tanh(hidden * (inner + cubic * square))
    share = 0.5 + 0.5 * bent
    slope = share + (0.5 * hidden) * (1.0 - bent * bent) * (inner + (3.0 * cubic) * square)
    return hidden * share, slope


def column_sums(values):
    rows, width = values.shape
    return jnp.sum(values.reshape(rows // 8, 8, width), axis=0)


class Place:
    def __init__(self, planes):
        wide = lax.axis_index("wide")
        self.narrow = lax.axis_index("narrow")
        self.wide = wide
        self.core = wide % 2
        self.y = (wide // 2) % 2
        self.z = wide // 4
        self.x = self.narrow
        self.planes = planes
        self.sibling = (wide + 1 - 2 * self.core, self.narrow)
        self.next_x = (wide, 1 - self.narrow)
        self.next_y = (wide + 2 - 4 * self.y, self.narrow)

    def plane(self, step):
        other = (self.z + step) % self.planes
        return (self.wide + 4 * (other - self.z), self.narrow), other


class Chunk:
    def __init__(self, place, held, inbox, sems, x_first, target=None):
        self.place = place
        self.views = (held, inbox, sems)
        self.target = target
        self.first, self.second = (place.x, place.y) if x_first else (place.y, place.x)
        self.to_first, self.to_second = (
            (place.next_x, place.next_y) if x_first else (place.next_y, place.next_x)
        )
        self.x_first = x_first

    @property
    def held(self):
        ref, at = self.views[0]
        return ref.at[at]

    @property
    def inbox(self):
        return [ref if at is None else ref.at[at] for ref, at in self.views[1]]

    @property
    def sems(self):
        return [ref.at[at] for ref, at in self.views[2]]

    def slot(self, y, core, x):
        first, second = (x, y) if self.x_first else (y, x)
        return ((core * 2 + first) * 2 + second) * self.place.planes

    def copy(self, stage):
        planes, core = self.place.planes, self.place.core
        first, second = self.first, self.second
        start, count, device = (
            (4 * planes * (1 - core), 4 * planes, self.place.sibling),
            (4 * planes * core + 2 * planes * (1 - first), 2 * planes, self.to_first),
            (4 * planes * core + 2 * planes * first + planes * (1 - second), planes, self.to_second),
        )[stage]
        return pltpu.make_async_remote_copy(
            src_ref=self.held.at[pl.ds(start, count)],
            dst_ref=self.inbox[stage],
            send_sem=self.sems[0].at[stage],
            recv_sem=self.sems[1].at[stage],
            device_id=device,
            device_id_type=MESH,
        )

    def add(self, start, landing, count):
        def body(index, carry):
            at = start + index
            self.held[at] = (
                self.held[at].astype(jnp.float32) + landing[index].astype(jnp.float32)
            ).astype(self.held.dtype)
            return carry

        lax.fori_loop(0, count, body, 0)

    def start(self):
        self.copy(0).start()

    def over_core(self):
        planes = self.place.planes
        self.copy(0).wait()
        self.add(4 * planes * self.place.core, self.inbox[0], 4 * planes)
        self.copy(1).start()

    def over_first(self):
        planes = self.place.planes
        self.copy(1).wait()
        self.add(4 * planes * self.place.core + 2 * planes * self.first, self.inbox[1], 2 * planes)
        self.copy(2).start()

    def base(self):
        planes, place = self.place.planes, self.place
        return 4 * planes * place.core + 2 * planes * self.first + planes * self.second

    def plane_copy(self, step):
        device, other = self.place.plane(step)
        if self.target is None:
            return pltpu.make_async_remote_copy(
                src_ref=self.held.at[self.base() + other],
                dst_ref=self.inbox[3].at[step - 1],
                send_sem=self.sems[0].at[2 + step],
                recv_sem=self.sems[1].at[2 + step],
                device_id=device,
                device_id_type=MESH,
            )
        return pltpu.make_async_remote_copy(
            src_ref=self.held.at[pl.ds(self.base(), self.place.planes)],
            dst_ref=self.inbox[3].at[step - 1],
            send_sem=self.sems[0].at[2 + step],
            recv_sem=self.sems[1].at[2 + step],
            device_id=device,
            device_id_type=MESH,
        )

    def each_plane(self, act):
        for step in range(1, self.place.planes):
            if self.target is None:
                act(self.plane_copy(step))
            else:

                @pl.when((self.place.z + step) % self.place.planes == self.target)
                def _():
                    act(self.plane_copy(step))

    def over_second(self):
        self.copy(2).wait()
        planes = self.place.planes
        self.add(self.base(), self.inbox[2], planes)
        if self.target is None:
            self.inbox[3][planes - 1] = self.held[self.base() + self.place.z]
        else:

            @pl.when(self.place.z == self.target)
            def _():
                for index in range(planes):
                    self.inbox[3][planes - 1, index] = self.held[self.base() + index]

        self.each_plane(lambda copy: copy.start())

    def sent(self):
        self.each_plane(lambda copy: copy.wait_send())

    def arrived(self):
        for step in range(1, self.place.planes):
            self.plane_copy(step).wait_recv()

    def total(self, index):
        terms = [
            self.inbox[3][step] if self.target is None else self.inbox[3][step, index]
            for step in range(self.place.planes)
        ]
        return sum(term.astype(jnp.float32) for term in terms)


def store_rows(chunk, values, first_row):
    width = values.shape[1]
    for k in range(values.shape[0] // 24):
        shard = first_row // 24 + k
        z, y, core, x = shard // 8, shard // 4 % 2, shard // 2 % 2, shard % 2
        at = chunk.slot(y, core, x) + z
        block = values[24 * k : 24 * k + 24]
        rest = block[16:24]
        chunk.held[at, :, 0:width] = block[0:16].astype(jnp.bfloat16)
        chunk.held[at, :, width : width + width // 2] = jnp.concatenate(
            [rest[:, : width // 2], rest[:, width // 2 :]], axis=0
        ).astype(jnp.bfloat16)


def load_rows(block, width):
    rest = block[:, width:]
    return jnp.concatenate(
        [block[:, :width], jnp.concatenate([rest[0:8], rest[8:16]], axis=1)], axis=0
    )


def tile_runs(sub, width):
    tiles = width // 128
    runs, tile = [], 0
    while tile < tiles:
        line = sub * tiles + tile
        count = min(tiles - tile, PART - line % PART)
        runs.append((tile, line // PART, line % PART, count))
        tile += count
    return runs


def store_shards(chunk, values, first_row):
    width = values.shape[1]
    for k in range(values.shape[0] // 16):
        row = first_row + 16 * k
        shard, sub = row // 96, row % 96 // 16
        base = chunk.slot(shard // 4, shard // 2 % 2, shard % 2)
        for tile, block, at, count in tile_runs(sub, width):
            chunk.held[base + block, :, 128 * at : 128 * (at + count)] = values[
                16 * k : 16 * k + 16, 128 * tile : 128 * (tile + count)
            ].astype(jnp.bfloat16)


class Taps:
    def __init__(self, place, held, inbox, result, sems, rows):
        self.place, self.held, self.inbox, self.result, self.sems = place, held, inbox, result, sems
        self.rows = rows

    def part(self, x, core, y, plane, count):
        planes = self.place.planes
        return pl.ds((((x * 2 + core) * 2 + y) * planes + plane) * self.rows, count * self.rows)

    def add(self, target, landing):
        self.held[target, :] = (
            self.held[target, :].astype(jnp.float32) + landing[...].astype(jnp.float32)
        ).astype(self.held.dtype)

    def copy(self, kind, step=0):
        place, planes = self.place, self.place.planes
        x, core, y, z = place.x, place.core, place.y, place.z
        if kind == "core":
            source, landing = self.part(step, 1 - core, 0, 0, 2 * planes), self.inbox[0].at[step]
            stage, device = step, place.sibling
        elif kind == "x":
            source, landing = self.part(1 - x, core, 0, 0, 2 * planes), self.inbox[1]
            stage, device = 2, place.next_x
        elif kind == "y":
            source, landing = self.part(x, core, 1 - y, 0, planes), self.inbox[2]
            stage, device = 3, place.next_y
        elif kind == "plane":
            device, other = place.plane(step)
            source, landing = self.part(x, core, y, other, 1), self.inbox[3].at[step - 1]
            stage = 3 + step
        else:
            if kind == "back plane":
                mine, stage, device = (0, core, y, z, 1), 2 + planes + step, place.plane(step)[0]
            elif kind == "back y":
                mine, stage, device = (0, core, y, 0, planes), 2 + 2 * planes, place.next_y
            else:
                mine, stage, device = (0, core, 0, 0, 2 * planes), 3 + 2 * planes, place.sibling
            landing = self.result.at[self.part(*mine), :]
        return pltpu.make_async_remote_copy(
            src_ref=landing if kind.startswith("back") else self.held.at[source, :],
            dst_ref=landing,
            send_sem=self.sems[0].at[stage],
            recv_sem=self.sems[1].at[stage],
            device_id=device,
            device_id_type=MESH,
        )

    def start(self):
        for x in range(2):
            self.copy("core", x).start()

    def over_core(self):
        for x in range(2):
            self.copy("core", x).wait()
            self.add(self.part(x, self.place.core, 0, 0, 2 * self.place.planes), self.inbox[0].at[x])
        self.copy("x").start()

    def over_x(self):
        place = self.place
        self.copy("x").wait()
        self.add(self.part(place.x, place.core, 0, 0, 2 * place.planes), self.inbox[1])
        self.copy("y").start()

    def over_y(self):
        place = self.place
        self.copy("y").wait()
        self.add(self.part(place.x, place.core, place.y, 0, place.planes), self.inbox[2])
        for step in range(1, place.planes):
            self.copy("plane", step).start()

    def over_planes(self):
        place = self.place
        total = self.held[self.part(place.x, place.core, place.y, place.z, 1), :].astype(jnp.float32)
        for step in range(1, place.planes):
            self.copy("plane", step).wait()
            total = total + self.inbox[3][step - 1].astype(jnp.float32)
        self.result[self.part(0, place.core, place.y, place.z, 1), :] = total.astype(self.result.dtype)
        for step in range(1, place.planes):
            self.copy("back plane", step).start()

    def back_y(self):
        for step in range(1, self.place.planes):
            self.copy("back plane", step).wait()
        self.copy("back y").start()

    def back_core(self):
        self.copy("back y").wait()
        self.copy("back core").start()

    def finish(self):
        self.copy("back core").wait()


class Sums:
    def __init__(self, place, levels, inbox, sems):
        self.place, self.levels, self.inbox, self.sems = place, levels, inbox, sems

    def copy(self, level, step=0):
        place = self.place
        device = (place.sibling, place.next_x, place.next_y)[level] if level < 3 else place.plane(step)[0]
        landing = level + max(step - 1, 0)
        return pltpu.make_async_remote_copy(
            src_ref=self.levels.at[level],
            dst_ref=self.inbox.at[landing],
            send_sem=self.sems[0].at[landing],
            recv_sem=self.sems[1].at[landing],
            device_id=device,
            device_id_type=MESH,
        )

    def start(self):
        self.copy(0).start()

    def over(self, level):
        self.copy(level).wait()
        self.levels[level + 1] = self.levels[level] + self.inbox[level]
        if level < 2:
            self.copy(level + 1).start()
        else:
            for step in range(1, self.place.planes):
                self.copy(3, step).start()

    def finish(self):
        total = self.levels[3]
        for step in range(1, self.place.planes):
            self.copy(3, step).wait()
            total = total + self.inbox[2 + step]
        return total


def block_kernel(
    planes,
    tokens, cotangent, residual, normed2, normed2_t, branch_t, normed_t, gate_vals, mixed,
    signal_waves, kernel_waves, w_in, w_out, w_up, w_down, table, table_t,
    gains, long_row,
    block_out, input_grad, taps_out, sums_out, w_in_grad, w_out_grad, w_up_grad, w_down_grad,
    held, inbox0, inbox1, inbox2, inbox_u, inbox_n, taps_held, taps0, taps1, taps2, taps3, taps_sum,
    levels, sums_inbox, cot, active, running, branch_v, normed_v, w_in_v, w_out_v,
    table_v, table_tv, d_out, d_gate, d_mix, d_signal,
    send_sems, recv_sems, taps_send, taps_recv, sums_send, sums_recv, load_sems,
):
    tok_count, feat = cot.shape
    half = tok_count // 2
    tile = active.shape[2]
    step_rows = 256
    row_steps = tok_count // step_rows
    place = Place(planes)

    loads = {}

    class Load:
        def __init__(self, source, target):
            self.ends, self.at = (source, target), len(loads)

        def copy(self):
            source, target = (end() if callable(end) else end for end in self.ends)
            return pltpu.make_async_copy(source, target, load_sems.at[self.at])

        def wait(self):
            self.copy().wait()

    def load(name, source, target):
        loads[name] = Load(source, target)
        loads[name].copy().start()

    barrier = pltpu.get_barrier_semaphore()
    partners = [place.sibling, place.next_x, place.next_y] + [
        place.plane(step)[0] for step in range(1, planes)
    ]
    for partner in partners:
        pl.semaphore_signal(barrier, inc=1, device_id=partner, device_id_type=MESH)
    pl.semaphore_wait(barrier, len(partners))

    def chunk(index, step, kind, target=None):
        at = step % FLIGHTS * 2 + kind
        ring = step % 2 * 2 + kind
        if target is None:
            far = (inbox_u, index // 2 if index < 2 * planes else index - planes)
        else:
            far = (inbox_n, None)
        return Chunk(
            place,
            (held, at),
            ((inbox0, ring), (inbox1, ring), (inbox2, ring), far),
            ((send_sems, index), (recv_sems, index)),
            kind == 0,
            target,
        )

    ups = [chunk(2 * t, t, 0) for t in range(planes)]
    downs = [chunk(2 * t + 1, t, 1, t) for t in range(planes)]

    def rows_of(index):
        return pl.ds(pl.multiple_of(index * step_rows, step_rows), step_rows)

    def forward_back(gate_v, mixed_v):
        def feed_forward(normed_2, normed_2t, d_hidden, up_tiles, down_tiles):
            def load_tile(t):
                cols = pl.ds(t * tile, tile)
                load(("up", t), lambda: w_up.at[:, cols], lambda: up_tiles.at[t % 2])
                load(("down", t), lambda: w_down.at[cols, :], lambda: down_tiles.at[t % 2])

            load("normed2", normed2, normed_2)
            load_tile(0)
            load("cot", cotangent, cot)
            load("normed2_t", normed2_t, normed_2t)
            for name, source, target in (
                ("gate", gate_vals, gate_v),
                ("mixed", mixed, mixed_v),
                ("w_out", w_out, w_out_v),
                ("branch", branch_t, branch_v),
                ("normed", normed_t, normed_v),
                ("w_in", w_in, w_in_v),
                ("table", table, table_v),
                ("table_t", table_t, table_tv),
            ):
                load(name, source, target)
            loads["normed2"].wait()
            loads["cot"].wait()

            for t in range(planes):
                up_tile, down_tile = up_tiles.at[t % 2], down_tiles.at[t % 2]
                loads["up", t].wait()
                loads["down", t].wait()
                if t + 1 < planes:
                    load_tile(t + 1)

                def rows_step(index, carry):
                    rows = rows_of(index)
                    hidden = dot_nn(normed_2[rows, :], up_tile[...])
                    d_active = dot_nt(cot[rows, :], down_tile[...])
                    value, slope = gelu_both(hidden)
                    active[t, rows, :] = value.astype(jnp.bfloat16)
                    d_value = (d_active * slope).astype(jnp.bfloat16)
                    d_hidden[rows, :] = d_value
                    back = dot_nt(d_value, up_tile[...])
                    if t == 0:
                        running[rows, :] = back
                    else:
                        running[rows, :] += back
                    return carry

                lax.fori_loop(0, row_steps // 2, rows_step, 0)
                if t >= 1:
                    ups[t - 1].over_core()
                    downs[t - 1].over_core()
                if t >= 2:
                    ups[t - 2].over_second()
                    downs[t - 2].over_second()
                lax.fori_loop(row_steps // 2, row_steps, rows_step, 0)
                if t >= FLIGHTS:
                    ups[t - FLIGHTS].sent()
                    downs[t - FLIGHTS].sent()
                for part in range(2):
                    cols = tile // 2
                    store_shards(
                        downs[t], dot_tn(active[t, :, part * cols : (part + 1) * cols], cot[...]), part * cols
                    )
                downs[t].start()
                if t >= 1:
                    ups[t - 1].over_first()
                    downs[t - 1].over_first()
                if t == 0:
                    loads["normed2_t"].wait()
                for part in range(2):
                    rows = feat // 2
                    store_rows(
                        ups[t], dot_nn(normed_2t[part * rows : (part + 1) * rows, :], d_hidden[...]), part * rows
                    )
                ups[t].start()

        pl.run_scoped(
            feed_forward,
            pltpu.VMEM((tok_count, feat), jnp.bfloat16),
            pltpu.VMEM((feat, tok_count), jnp.bfloat16),
            pltpu.VMEM((tok_count, tile), jnp.bfloat16),
            pltpu.VMEM((2, feat, tile), jnp.bfloat16),
            pltpu.VMEM((2, tile, feat), jnp.bfloat16),
        )

        def norm_two_back(left_v):
            load("left", residual.at[0 : tok_count // 2, :], left_v.at[0 : tok_count // 2, :])
            load("left end", residual.at[tok_count // 2 :, :], left_v.at[tok_count // 2 :, :])
            for name in ("gate", "mixed", "w_out", "left"):
                loads[name].wait()

            def back_step(index, carry):
                gain_sum, shift_sum = carry
                rows = rows_of(index)
                left = left_v[rows, :]
                centered = left - jnp.mean(left, axis=-1, keepdims=True)
                inverse = lax.rsqrt(jnp.mean(centered * centered, axis=-1, keepdims=True) + eps_norm)
                unit = centered * inverse
                grad = running[rows, :]
                scaled = grad * gains[2:3, :]
                d_left = cot[rows, :].astype(jnp.float32) + inverse * (
                    scaled
                    - jnp.mean(scaled, axis=-1, keepdims=True)
                    - unit * jnp.mean(scaled * unit, axis=-1, keepdims=True)
                )
                running[rows, :] = d_left
                d_low = d_left.astype(jnp.bfloat16)
                d_out[rows, :] = d_low
                d_branch = dot_nt(d_low, w_out_v[...])
                d_mix[rows, :] = (
                    d_branch * gate_v[rows, :].astype(jnp.float32) * (1.0 / half)
                ).astype(jnp.bfloat16)
                d_gate[rows, :] = (d_branch * mixed_v[rows, :].astype(jnp.float32)).astype(jnp.bfloat16)
                return gain_sum + column_sums(grad * unit), shift_sum + column_sums(grad)

            zero = jnp.zeros((8, feat), jnp.float32)
            carry = lax.fori_loop(0, row_steps // 2, back_step, (zero, zero))
            ups[planes - 1].over_core()
            downs[planes - 1].over_core()
            ups[planes - 2].over_second()
            downs[planes - 2].over_second()
            loads["left end"].wait()
            gain_sum, shift_sum = lax.fori_loop(row_steps // 2, row_steps, back_step, carry)
            levels[0] = jnp.zeros(levels.shape[1:], jnp.float32)
            levels[0, 0:1, :] = jnp.sum(gain_sum, axis=0, keepdims=True)
            levels[0, 1:2, :] = jnp.sum(shift_sum, axis=0, keepdims=True)

        pl.run_scoped(norm_two_back, pltpu.VMEM((tok_count, feat), jnp.float32))

    pl.run_scoped(
        forward_back,
        pltpu.VMEM((tok_count, feat), jnp.bfloat16),
        pltpu.VMEM((tok_count, feat), jnp.bfloat16),
    )

    out_chunk = chunk(2 * planes, planes, 0)
    gate_chunk = chunk(2 * planes + 1, planes, 1)
    signal_chunk = chunk(2 * planes + 2, planes + 1, 0)
    taps = Taps(
        place, taps_held, (taps0, taps1, taps2, taps3), taps_sum, (taps_send, taps_recv),
        tok_count // (8 * planes),
    )
    sums = Sums(place, levels, sums_inbox, (sums_send, sums_recv))

    def weight_rows(target, left_t, right):
        for part in range(2):
            rows = feat // 2
            store_rows(target, dot_nn(left_t[part * rows : (part + 1) * rows, :], right[...]), part * rows)
        target.start()

    def mixer_back(waves, kernels, d_kernel, d_taps, d_waves):
        load("waves", signal_waves, waves)
        load("kernels", kernel_waves, kernels)
        loads["branch"].wait()
        ups[planes - 3].sent()
        downs[planes - 3].sent()
        weight_rows(out_chunk, branch_v, d_out)
        ups[planes - 1].over_first()
        downs[planes - 1].over_first()
        for name in ("waves", "kernels", "table", "table_t"):
            loads[name].wait()
        wave_rows, wave_cols = 256, 256

        def wave_step(down, cols):
            real = pl.ds(pl.multiple_of(down * wave_rows, wave_rows), wave_rows)
            imag = pl.ds(pl.multiple_of(half + down * wave_rows, wave_rows), wave_rows)
            first_r = dot_nn(table_v[real, :], d_mix[0:half, cols])
            first_i = dot_nn(table_v[imag, :], d_mix[0:half, cols])
            second_r = dot_nn(table_v[real, :], d_mix[half:, cols])
            second_i = dot_nn(table_v[imag, :], d_mix[half:, cols])

            def wide(ref, which, rows):
                return ref[which, rows, cols].astype(jnp.float32)

            def keep(ref, which, rows, values):
                at = cols if ref.shape[2] == feat else slice(None)
                ref[which, rows, at] = values.astype(jnp.bfloat16)

            low_r, low_i = wide(kernels, 0, real), wide(kernels, 0, imag)
            cross_r, cross_i = wide(kernels, 1, real), wide(kernels, 1, imag)
            keep(d_waves, 0, real, low_r * first_r + low_i * first_i + cross_r * second_r + cross_i * second_i)
            keep(d_waves, 0, imag, low_r * first_i - low_i * first_r + cross_r * second_i - cross_i * second_r)
            keep(d_waves, 1, real, low_r * second_r + low_i * second_i)
            keep(d_waves, 1, imag, low_r * second_i - low_i * second_r)
            head_r, head_i = wide(waves, 0, real), wide(waves, 0, imag)
            tail_r, tail_i = wide(waves, 1, real), wide(waves, 1, imag)
            long = long_row[0:1, cols]
            far_r = (head_r * second_r + head_i * second_i) * long
            far_i = (head_r * second_i - head_i * second_r) * long
            odd = lax.broadcasted_iota(jnp.int32, (wave_rows, 1), 0) % 2
            parity = (1 - 2 * odd).astype(jnp.float32)
            keep(d_kernel, 1, real, far_r)
            keep(d_kernel, 1, imag, far_i)
            keep(
                d_kernel,
                0,
                real,
                head_r * first_r + head_i * first_i + tail_r * second_r + tail_i * second_i + parity * far_i,
            )
            keep(
                d_kernel,
                0,
                imag,
                head_r * first_i - head_i * first_r + tail_r * second_i - tail_i * second_r - parity * far_r,
            )

        pad = 8
        d_taps[0:pad, :] = jnp.zeros((pad, wave_cols), jnp.float32)
        d_taps[pad + tok_count :, :] = jnp.zeros((pad, wave_cols), jnp.float32)
        pool_rows = 128

        def column_step(across, carry):
            cols = pl.ds(pl.multiple_of(across * wave_cols, wave_cols), wave_cols)
            for down in range(half // wave_rows):
                wave_step(down, cols)
            for which in range(2):
                d_taps[pad + which * half : pad + (which + 1) * half, :] = dot_nn(table_tv[...], d_kernel[which])
            for index in range(tok_count // pool_rows):
                at = pad + index * pool_rows
                taps_held[at - pad : at - pad + pool_rows, cols] = (
                    (
                        d_taps[at - 1 : at - 1 + pool_rows, :]
                        + d_taps[at : at + pool_rows, :]
                        + d_taps[at + 1 : at + 1 + pool_rows, :]
                    )
                    / 3.0
                ).astype(jnp.bfloat16)
            return carry

        lax.fori_loop(0, feat // wave_cols, column_step, 0)
        taps.start()
        ups[planes - 1].over_second()
        downs[planes - 1].over_second()
        out_chunk.over_core()
        for which in range(2):

            def signal_step(index, carry):
                at = pl.multiple_of(index * step_rows, step_rows)
                d_signal[pl.ds(which * half + at, step_rows), :] = dot_nn(
                    table_tv[pl.ds(at, step_rows), :], d_waves[which]
                ).astype(jnp.bfloat16)
                return carry

            lax.fori_loop(0, half // step_rows, signal_step, 0)

    pl.run_scoped(
        mixer_back,
        pltpu.VMEM((2, tok_count, feat), jnp.bfloat16),
        pltpu.VMEM((2, tok_count, feat), jnp.bfloat16),
        pltpu.VMEM((2, tok_count, 256), jnp.bfloat16),
        pltpu.VMEM((tok_count + 16, 256), jnp.float32),
        pltpu.VMEM((2, tok_count, feat), jnp.bfloat16),
    )

    taps.over_core()
    loads["normed"].wait()
    ups[planes - 2].sent()
    weight_rows(signal_chunk, normed_v, d_signal)
    out_chunk.over_first()
    taps.over_x()
    weight_rows(gate_chunk, normed_v, d_gate)
    out_chunk.over_second()
    signal_chunk.over_core()
    taps.over_y()

    def finish(down_v, left_v, tokens_v, grad_stage, out_stage):
        def load_again(t):
            rows = pl.ds(t * tile, tile)
            load(("again", t), lambda: w_down.at[rows, :], lambda: down_v.at[t])

        load("tokens", tokens, tokens_v)
        for t in range(planes):
            load_again(t)
        load("left again", residual, left_v)
        loads["tokens"].wait()
        loads["w_in"].wait()
        gate_chunk.over_core()

        def grad_copy(index, slot):
            return pltpu.make_async_copy(
                grad_stage.at[slot], input_grad.at[rows_of(index), :], load_sems.at[STORES + slot]
            )

        def input_step(index, carry):
            gain_sum, shift_sum = carry
            rows = rows_of(index)
            slot = index % 2
            d_normed = dot_nt(d_signal[rows, :], w_in_v[:, 0:feat]) + dot_nt(
                d_gate[rows, :], w_in_v[:, feat:]
            )
            values = tokens_v[rows, :].astype(jnp.float32)
            centered = values - jnp.mean(values, axis=-1, keepdims=True)
            inverse = lax.rsqrt(jnp.mean(centered * centered, axis=-1, keepdims=True) + eps_norm)
            unit = centered * inverse
            scaled = d_normed * gains[0:1, :]

            @pl.when(index >= 2)
            def _():
                grad_copy(index - 2, slot).wait()

            grad_stage[slot] = running[rows, :] + inverse * (
                scaled
                - jnp.mean(scaled, axis=-1, keepdims=True)
                - unit * jnp.mean(scaled * unit, axis=-1, keepdims=True)
            )
            grad_copy(index, slot).start()
            return gain_sum + column_sums(d_normed * unit), shift_sum + column_sums(d_normed)

        zero = jnp.zeros((8, feat), jnp.float32)
        carry = lax.fori_loop(0, row_steps // 2, input_step, (zero, zero))
        signal_chunk.over_first()
        taps.over_planes()
        gain_sum, shift_sum = lax.fori_loop(row_steps // 2, row_steps, input_step, carry)
        levels[0, 2:3, :] = jnp.sum(gain_sum, axis=0, keepdims=True)
        levels[0, 3:4, :] = jnp.sum(shift_sum, axis=0, keepdims=True)
        sums.start()
        gate_chunk.over_first()
        signal_chunk.over_second()
        taps.back_y()
        for t in range(planes):
            loads["again", t].wait()
        loads["left again"].wait()

        def out_copy(index, slot):
            return pltpu.make_async_copy(
                out_stage.at[slot], block_out.at[rows_of(index), :], load_sems.at[STORES + 2 + slot]
            )

        def out_step(index, carry):
            rows = rows_of(index)
            slot = index % 2
            total = left_v[rows, :]
            for t in range(planes):
                total = total + dot_nn(active[t, rows, :], down_v[t])

            @pl.when(index >= 2)
            def _():
                out_copy(index - 2, slot).wait()

            out_stage[slot] = total.astype(jnp.bfloat16)
            out_copy(index, slot).start()
            return carry

        lax.fori_loop(0, 1, out_step, 0)
        sums.over(0)
        gate_chunk.over_second()
        lax.fori_loop(1, 2, out_step, 0)
        sums.over(1)
        taps.back_core()
        lax.fori_loop(2, 3, out_step, 0)
        sums.over(2)
        lax.fori_loop(3, row_steps, out_step, 0)
        for index in (row_steps - 2, row_steps - 1):
            grad_copy(index, index % 2).wait()
            out_copy(index, index % 2).wait()

    pl.run_scoped(
        finish,
        pltpu.VMEM((planes, tile, feat), jnp.bfloat16),
        pltpu.VMEM((tok_count, feat), jnp.float32),
        pltpu.VMEM((tok_count, feat), jnp.bfloat16),
        pltpu.VMEM((2, step_rows, feat), jnp.float32),
        pltpu.VMEM((2, step_rows, feat), jnp.bfloat16),
    )

    def own_rows(target):
        target.arrived()
        return load_rows(target.total(0), feat)

    for t in range(planes):
        w_up_grad[:, t * tile : (t + 1) * tile] = own_rows(ups[t])
    w_out_grad[...] = own_rows(out_chunk)
    w_in_grad[:, 0:feat] = own_rows(signal_chunk)
    w_in_grad[:, feat:] = own_rows(gate_chunk)
    for t in range(planes):

        @pl.when(place.z == t)
        def _():
            downs[t].arrived()
            for index in range(planes):
                block = downs[t].total(index)
                for sub in range(6):
                    for first, line, at, count in tile_runs(sub, feat):
                        if line == index:
                            w_down_grad[16 * sub : 16 * sub + 16, 128 * first : 128 * (first + count)] = block[
                                :, 128 * at : 128 * (at + count)
                            ]

    sums_out[...] = sums.finish()
    taps.finish()
    taps_store = pltpu.make_async_copy(taps_sum, taps_out, load_sems.at[STORES + 4])
    taps_store.start()
    for one in (downs[planes - 2], ups[planes - 1], downs[planes - 1], out_chunk, gate_chunk, signal_chunk):
        one.sent()
    taps_store.wait()


def linked_block(
    planes,
    tokens,
    lengths,
    raw_taps,
    ln1_gain,
    ln1_shift,
    w_in,
    w_out,
    ln2_gain,
    ln2_shift,
    w_up,
    w_down,
    cotangent,
):
    tok_count, feat = tokens.shape
    half = tok_count // 2
    tile = w_up.shape[1] // planes
    table = jnp.asarray(wave_table(half), jnp.bfloat16)
    table_t = jnp.asarray(wave_table(half).T, jnp.bfloat16)
    scale = 1.0 / half
    long_row = (lengths > half).astype(jnp.float32)

    squashed = raw_taps - jnp.clip(raw_taps, -shrink_level, shrink_level)
    gathered = lax.all_gather(squashed.astype(jnp.bfloat16), "narrow", axis=0, tiled=True)
    kernel = pool(gathered.astype(jnp.float32)).astype(jnp.bfloat16)
    kernel_low = to_waves(table, kernel[:half])
    kernel_cross = long_row[0] * (to_waves(table, kernel[half:]) + turned(kernel_low, 1.0))

    inputs = tokens.astype(jnp.float32)
    unit_one, _ = norm_parts(inputs)
    normed = (unit_one * ln1_gain + ln1_shift).astype(jnp.bfloat16)
    projected = jnp.dot(normed, w_in, preferred_element_type=jnp.float32)
    signal = projected[:, :feat].astype(jnp.bfloat16)
    gate_vals = projected[:, feat:]
    first = to_waves(table, signal[:half])
    second = to_waves(table, signal[half:])
    mixed = jnp.concatenate(
        [
            from_waves(table, times(first, kernel_low) * scale),
            from_waves(table, (times(second, kernel_low) + times(first, kernel_cross)) * scale),
        ],
        axis=0,
    )
    branch = (mixed * gate_vals).astype(jnp.bfloat16)
    residual = inputs + jnp.dot(branch, w_out, preferred_element_type=jnp.float32)
    unit_two, _ = norm_parts(residual)
    normed2 = (unit_two * ln2_gain + ln2_shift).astype(jnp.bfloat16)
    gains = jnp.stack([ln1_gain, ln1_shift, ln2_gain, ln2_shift] + [ln1_gain] * 4)

    shares = 8 * planes
    rows = feat // shares
    block = (16, 128 * PART)
    chunks = 2 * planes + 3
    bf16, f32 = jnp.bfloat16, jnp.float32
    whole = pl.BlockSpec(memory_space=pl.ANY)
    near = pl.BlockSpec(memory_space=pltpu.VMEM)
    results = pl.pallas_call(
        functools.partial(block_kernel, planes),
        out_shape=(
            jax.ShapeDtypeStruct((tok_count, feat), bf16),
            jax.ShapeDtypeStruct((tok_count, feat), f32),
            jax.ShapeDtypeStruct((half, feat), bf16),
            jax.ShapeDtypeStruct((8, feat), f32),
            jax.ShapeDtypeStruct((rows, 2 * feat), f32),
            jax.ShapeDtypeStruct((rows, feat), f32),
            jax.ShapeDtypeStruct((rows, planes * tile), f32),
            jax.ShapeDtypeStruct((tile // 8, feat), f32),
        ),
        in_specs=[whole] * 17 + [near] * 2,
        out_specs=(whole,) * 3 + (near,) * 5,
        scratch_shapes=[
            pltpu.VMEM((2 * FLIGHTS, shares) + block, bf16),
            pltpu.VMEM((4, 4 * planes) + block, bf16),
            pltpu.VMEM((4, 2 * planes) + block, bf16),
            pltpu.VMEM((4, planes) + block, bf16),
            pltpu.VMEM((planes + 3, planes) + block, bf16),
            pltpu.VMEM((planes, planes) + block, bf16),
            pltpu.VMEM((tok_count, feat), bf16),
            pltpu.VMEM((2, tok_count // 4, feat), bf16),
            pltpu.VMEM((tok_count // 4, feat), bf16),
            pltpu.VMEM((tok_count // 8, feat), bf16),
            pltpu.VMEM((planes - 1, tok_count // shares, feat), bf16),
            pltpu.VMEM((half, feat), bf16),
            pltpu.VMEM((4, 8, feat), f32),
            pltpu.VMEM((planes + 2, 8, feat), f32),
            pltpu.VMEM((tok_count, feat), bf16),
            pltpu.VMEM((planes, tok_count, tile), bf16),
            pltpu.VMEM((tok_count, feat), f32),
            pltpu.VMEM((feat, tok_count), bf16),
            pltpu.VMEM((feat, tok_count), bf16),
            pltpu.VMEM((feat, 2 * feat), bf16),
            pltpu.VMEM((feat, feat), bf16),
            pltpu.VMEM((tok_count, half), bf16),
            pltpu.VMEM((half, tok_count), bf16),
            pltpu.VMEM((tok_count, feat), bf16),
            pltpu.VMEM((tok_count, feat), bf16),
            pltpu.VMEM((tok_count, feat), bf16),
            pltpu.VMEM((tok_count, feat), bf16),
            pltpu.SemaphoreType.DMA((chunks, planes + 2)),
            pltpu.SemaphoreType.DMA((chunks, planes + 2)),
            pltpu.SemaphoreType.DMA((2 * planes + 4,)),
            pltpu.SemaphoreType.DMA((2 * planes + 4,)),
            pltpu.SemaphoreType.DMA((planes + 2,)),
            pltpu.SemaphoreType.DMA((planes + 2,)),
            pltpu.SemaphoreType.DMA((STORES + 5,)),
        ],
        compiler_params=pltpu.CompilerParams(
            collective_id=1, has_side_effects=True, vmem_limit_bytes=VMEM_BYTES
        ),
        cost_estimate=pl.CostEstimate(
            flops=2 * tok_count * feat * (5 * w_up.shape[1] + 9 * feat),
            bytes_accessed=40 * tok_count * feat,
            transcendentals=tok_count * w_up.shape[1],
        ),
    )(
        tokens,
        cotangent,
        residual,
        normed2,
        normed2.T,
        branch.T,
        normed.T,
        gate_vals.astype(bf16),
        mixed.astype(bf16),
        jnp.stack([first, second]).astype(bf16),
        jnp.stack([kernel_low, kernel_cross]).astype(bf16),
        w_in,
        w_out,
        w_up,
        w_down,
        table,
        table_t,
        gains,
        jnp.broadcast_to(long_row[:, None], (1, feat)),
    )
    block_out, input_grad, taps_sum, sums, w_in_grad, w_out_grad, w_up_grad, w_down_grad = results
    raw_grad = taps_sum.astype(f32) * (jnp.abs(raw_taps) > shrink_level).astype(f32)
    share = lax.axis_index("wide") * 2 + lax.axis_index("narrow")
    mine = lax.dynamic_slice(sums, (0, share * rows), (8, rows))
    return (
        block_out,
        input_grad,
        raw_grad,
        mine[2],
        mine[3],
        w_in_grad,
        w_out_grad,
        mine[0],
        mine[1],
        w_up_grad,
        w_down_grad,
    )


def solution(mesh):
    spread = P(("wide", "narrow"))
    rows = P(("wide", "narrow"), None)
    placed = (rows, spread, P("narrow", None)) + (P(),) * 8 + (rows,)
    wide, narrow = mesh.shape["wide"], mesh.shape["narrow"]

    def block(tokens, lengths, raw_taps, *others):
        fits = (
            narrow == 2
            and wide % 4 == 0
            and wide >= 12
            and lengths.shape[0] == 1
            and raw_taps.shape[0] * 2 == tokens.shape[0]
            and tokens.shape[1] == 24 * wide * narrow
            and others[-2].shape[0] == 96 * wide * narrow
            and tokens.shape[0] % 512 == 0
        )
        if fits:
            return linked_block(wide // 4, tokens, lengths, raw_taps, *others)
        return local(tokens, lengths, raw_taps, *others)

    return jax.shard_map(
        block,
        mesh=mesh,
        in_specs=placed,
        out_specs=(rows, rows, P("narrow", None), spread, spread, rows, rows, spread, spread, rows, rows),
        check_vma=False,
    )
```

```python
import functools

import jax
import jax.numpy as jnp
import numpy as np
from jax import lax
from jax.experimental import pallas as pl
from jax.experimental.pallas import tpu as pltpu
from jax.sharding import PartitionSpec as P

shrink_level = 0.003
eps_norm = 1e-05


def wave_table(half):
    period = 4 * half
    phase = (np.outer(2 * np.arange(half) + 1, np.arange(half)) % period) * (2 * np.pi / period)
    return np.concatenate([np.cos(phase), -np.sin(phase)], axis=0)


def to_waves(table, block):
    return jnp.einsum("kn,nc->kc", table, block, preferred_element_type=jnp.float32)


def from_waves(table, waves):
    return jnp.einsum(
        "kn,kc->nc", table, waves.astype(jnp.bfloat16), preferred_element_type=jnp.float32
    )


def norm_parts(values):
    centered = values - jnp.mean(values, axis=-1, keepdims=True)
    inverse = lax.rsqrt(jnp.mean(centered * centered, axis=-1, keepdims=True) + eps_norm)
    return (centered * inverse, inverse)


def norm_back(upstream, unit_vals, inverse, gain_vec):
    scaled = upstream * gain_vec
    return inverse * (
        scaled
        - jnp.mean(scaled, axis=-1, keepdims=True)
        - unit_vals * jnp.mean(scaled * unit_vals, axis=-1, keepdims=True)
    )


def split(waves):
    half = waves.shape[0] // 2
    return waves[:half], waves[half:]


def times(left, right):
    lr, li = split(left)
    rr, ri = split(right)
    return jnp.concatenate([lr * rr - li * ri, lr * ri + li * rr], axis=0)


def conj_times(left, right):
    lr, li = split(left)
    rr, ri = split(right)
    return jnp.concatenate([lr * rr + li * ri, lr * ri - li * rr], axis=0)


def turned(waves, sign):
    wr, wi = split(waves)
    index = lax.broadcasted_iota(jnp.int32, (wr.shape[0], 1), 0)
    parity = sign * (1.0 - 2.0 * (index % 2).astype(jnp.float32))
    return jnp.concatenate([-parity * wi, parity * wr], axis=0)


def pool(values):
    padded = jnp.pad(values, ((1, 1), (0, 0)))
    return (padded[:-2] + padded[1:-1] + padded[2:]) / 3.0


def local(
    tokens,
    lengths,
    raw_taps,
    ln1_gain,
    ln1_shift,
    w_in,
    w_out,
    ln2_gain,
    ln2_shift,
    w_up,
    w_down,
    cotangent,
):
    tok_count, feat_width = tokens.shape
    row_count = lengths.shape[0]
    row_len = tok_count // row_count
    half = row_len // 2
    table = jnp.asarray(wave_table(half), jnp.bfloat16)
    scale = 1.0 / half
    long_rows = (lengths > half).astype(jnp.float32)

    squashed = raw_taps - jnp.clip(raw_taps, -shrink_level, shrink_level)
    gathered = lax.all_gather(squashed.astype(jnp.bfloat16), "narrow", axis=0, tiled=True)
    kernel = pool(gathered.astype(jnp.float32)).astype(jnp.bfloat16)
    kernel_low = to_waves(table, kernel[:half])
    kernel_cross = to_waves(table, kernel[half : 2 * half]) + turned(kernel_low, 1.0)

    inputs = tokens.astype(jnp.float32)
    unit_one, inverse_one = norm_parts(inputs)
    normed = (unit_one * ln1_gain + ln1_shift).astype(jnp.bfloat16)
    projected = jnp.dot(normed, w_in, preferred_element_type=jnp.float32)
    signal = projected[:, :feat_width].astype(jnp.bfloat16)
    gate_vals = projected[:, feat_width:]
    signal_waves = []
    mixed = []
    for row in range(row_count):
        first = to_waves(table, signal[row * row_len : row * row_len + half])
        second = to_waves(table, signal[row * row_len + half : (row + 1) * row_len])
        signal_waves.append((first, second))
        mixed.append(from_waves(table, times(first, kernel_low) * scale))
        mixed.append(
            from_waves(
                table,
                (times(second, kernel_low) + long_rows[row] * times(first, kernel_cross)) * scale,
            )
        )
    mixed = jnp.concatenate(mixed, axis=0)
    branch = (mixed * gate_vals).astype(jnp.bfloat16)
    residual = inputs + jnp.dot(branch, w_out, preferred_element_type=jnp.float32)
    unit_two, inverse_two = norm_parts(residual)
    normed2 = (unit_two * ln2_gain + ln2_shift).astype(jnp.bfloat16)
    hidden = jnp.dot(normed2, w_up, preferred_element_type=jnp.float32)
    active = jax.nn.gelu(hidden).astype(jnp.bfloat16)
    block_out = (residual + jnp.dot(active, w_down, preferred_element_type=jnp.float32)).astype(
        jnp.bfloat16
    )
    w_down_grad = jnp.einsum("tf,td->fd", active, cotangent, preferred_element_type=jnp.float32)
    d_active = jnp.einsum("td,fd->tf", cotangent, w_down, preferred_element_type=jnp.float32)
    gelu_pull = jax.vjp(jax.nn.gelu, hidden)[1]
    d_hidden = gelu_pull(d_active)[0].astype(jnp.bfloat16)
    w_up_grad = jnp.einsum("td,tf->df", normed2, d_hidden, preferred_element_type=jnp.float32)
    d_normed2 = jnp.einsum("tf,df->td", d_hidden, w_up, preferred_element_type=jnp.float32)
    ln2_gain_grad = jnp.sum(d_normed2 * unit_two, axis=0)
    ln2_shift_grad = jnp.sum(d_normed2, axis=0)
    d_residual = cotangent.astype(jnp.float32) + norm_back(
        d_normed2, unit_two, inverse_two, ln2_gain
    )
    d_outproj = d_residual.astype(jnp.bfloat16)
    w_out_grad = jnp.einsum("td,te->de", branch, d_outproj, preferred_element_type=jnp.float32)
    d_branch = jnp.einsum("te,de->td", d_outproj, w_out, preferred_element_type=jnp.float32)
    d_mixed = (d_branch * gate_vals).astype(jnp.bfloat16)
    d_gate = d_branch * mixed
    d_signal = []
    low_grad = 0.0
    cross_grad = 0.0
    for row in range(row_count):
        first, second = signal_waves[row]
        d_first = to_waves(table, d_mixed[row * row_len : row * row_len + half]) * scale
        d_second = to_waves(table, d_mixed[row * row_len + half : (row + 1) * row_len]) * scale
        d_cross = d_second * long_rows[row]
        d_signal.append(
            from_waves(table, conj_times(kernel_low, d_first) + conj_times(kernel_cross, d_cross))
        )
        d_signal.append(from_waves(table, conj_times(kernel_low, d_second)))
        low_grad = low_grad + conj_times(first, d_first) + conj_times(second, d_second)
        cross_grad = cross_grad + conj_times(first, d_cross)
    low_grad = low_grad + turned(cross_grad, -1.0)
    d_kernel = jnp.concatenate([from_waves(table, low_grad), from_waves(table, cross_grad)], axis=0)
    d_signal = jnp.concatenate(d_signal, axis=0)
    d_projected = jnp.concatenate([d_signal, d_gate], axis=1).astype(jnp.bfloat16)
    w_in_grad = jnp.einsum("td,te->de", normed, d_projected, preferred_element_type=jnp.float32)
    d_normed = jnp.einsum("te,de->td", d_projected, w_in, preferred_element_type=jnp.float32)
    ln1_gain_grad = jnp.sum(d_normed * unit_one, axis=0)
    ln1_shift_grad = jnp.sum(d_normed, axis=0)
    input_grad = d_residual + norm_back(d_normed, unit_one, inverse_one, ln1_gain)

    shares = lax.psum_scatter(
        pool(d_kernel).astype(jnp.bfloat16), "narrow", scatter_dimension=0, tiled=True
    )
    summed = lax.psum(shares, "wide").astype(jnp.float32)
    raw_grad = summed * (jnp.abs(raw_taps) > shrink_level).astype(jnp.float32)

    def scatter(values):
        return lax.psum_scatter(
            values.astype(jnp.bfloat16), ("wide", "narrow"), scatter_dimension=0, tiled=True
        ).astype(jnp.float32)

    def scatter_wide(values):
        return lax.psum_scatter(values, ("wide", "narrow"), scatter_dimension=0, tiled=True)

    return (
        block_out,
        input_grad,
        raw_grad,
        scatter_wide(ln1_gain_grad),
        scatter_wide(ln1_shift_grad),
        scatter(w_in_grad),
        scatter(w_out_grad),
        scatter_wide(ln2_gain_grad),
        scatter_wide(ln2_shift_grad),
        scatter(w_up_grad),
        scatter(w_down_grad),
    )


MESH = pl.DeviceIdType.MESH
PART = 9
STORES = 30
VMEM_BYTES = 60 * 2**20
FLIGHTS = 3


def dot_nn(left, right):
    return lax.dot_general(left, right, (((1,), (0,)), ((), ())), preferred_element_type=jnp.float32)


def dot_nt(left, right):
    return lax.dot_general(left, right, (((1,), (1,)), ((), ())), preferred_element_type=jnp.float32)


def dot_tn(left, right):
    return lax.dot_general(left, right, (((0,), (0,)), ((), ())), preferred_element_type=jnp.float32)


def gelu_both(hidden):
    inner = 0.7978845608028654
    cubic = inner * 0.044715
    square = hidden * hidden
    bent = jnp.tanh(hidden * (inner + cubic * square))
    share = 0.5 + 0.5 * bent
    slope = share + (0.5 * hidden) * (1.0 - bent * bent) * (inner + (3.0 * cubic) * square)
    return hidden * share, slope


def column_sums(values):
    rows, width = values.shape
    return jnp.sum(values.reshape(rows // 8, 8, width), axis=0)


class Place:
    def __init__(self, planes):
        wide = lax.axis_index("wide")
        self.narrow = lax.axis_index("narrow")
        self.wide = wide
        self.core = wide % 2
        self.y = (wide // 2) % 2
        self.z = wide // 4
        self.x = self.narrow
        self.planes = planes
        self.sibling = (wide + 1 - 2 * self.core, self.narrow)
        self.next_x = (wide, 1 - self.narrow)
        self.next_y = (wide + 2 - 4 * self.y, self.narrow)

    def plane(self, step):
        other = (self.z + step) % self.planes
        return (self.wide + 4 * (other - self.z), self.narrow), other


class Chunk:
    def __init__(self, place, held, inbox, sems, x_first, target=None):
        self.place = place
        self.views = (held, inbox, sems)
        self.target = target
        self.first, self.second = (place.x, place.y) if x_first else (place.y, place.x)
        self.to_first, self.to_second = (
            (place.next_x, place.next_y) if x_first else (place.next_y, place.next_x)
        )
        self.x_first = x_first

    @property
    def held(self):
        ref, at = self.views[0]
        return ref.at[at]

    @property
    def inbox(self):
        return [ref if at is None else ref.at[at] for ref, at in self.views[1]]

    @property
    def sems(self):
        return [ref.at[at] for ref, at in self.views[2]]

    def slot(self, y, core, x):
        first, second = (x, y) if self.x_first else (y, x)
        return ((core * 2 + first) * 2 + second) * self.place.planes

    def copy(self, stage):
        planes, core = self.place.planes, self.place.core
        first, second = self.first, self.second
        start, count, device = (
            (4 * planes * (1 - core), 4 * planes, self.place.sibling),
            (4 * planes * core + 2 * planes * (1 - first), 2 * planes, self.to_first),
            (4 * planes * core + 2 * planes * first + planes * (1 - second), planes, self.to_second),
        )[stage]
        return pltpu.make_async_remote_copy(
            src_ref=self.held.at[pl.ds(start, count)],
            dst_ref=self.inbox[stage],
            send_sem=self.sems[0].at[stage],
            recv_sem=self.sems[1].at[stage],
            device_id=device,
            device_id_type=MESH,
        )

    def add(self, start, landing, count):
        def body(index, carry):
            at = start + index
            self.held[at] = (
                self.held[at].astype(jnp.float32) + landing[index].astype(jnp.float32)
            ).astype(self.held.dtype)
            return carry

        lax.fori_loop(0, count, body, 0)

    def start(self):
        self.copy(0).start()

    def over_core(self):
        planes = self.place.planes
        self.copy(0).wait()
        self.add(4 * planes * self.place.core, self.inbox[0], 4 * planes)
        self.copy(1).start()

    def over_first(self):
        planes = self.place.planes
        self.copy(1).wait()
        self.add(4 * planes * self.place.core + 2 * planes * self.first, self.inbox[1], 2 * planes)
        self.copy(2).start()

    def base(self):
        planes, place = self.place.planes, self.place
        return 4 * planes * place.core + 2 * planes * self.first + planes * self.second

    def plane_copy(self, step):
        device, other = self.place.plane(step)
        if self.target is None:
            return pltpu.make_async_remote_copy(
                src_ref=self.held.at[self.base() + other],
                dst_ref=self.inbox[3].at[step - 1],
                send_sem=self.sems[0].at[2 + step],
                recv_sem=self.sems[1].at[2 + step],
                device_id=device,
                device_id_type=MESH,
            )
        return pltpu.make_async_remote_copy(
            src_ref=self.held.at[pl.ds(self.base(), self.place.planes)],
            dst_ref=self.inbox[3].at[step - 1],
            send_sem=self.sems[0].at[2 + step],
            recv_sem=self.sems[1].at[2 + step],
            device_id=device,
            device_id_type=MESH,
        )

    def each_plane(self, act):
        for step in range(1, self.place.planes):
            if self.target is None:
                act(self.plane_copy(step))
            else:

                @pl.when((self.place.z + step) % self.place.planes == self.target)
                def _():
                    act(self.plane_copy(step))

    def over_second(self):
        self.copy(2).wait()
        planes = self.place.planes
        self.add(self.base(), self.inbox[2], planes)
        if self.target is None:
            self.inbox[3][planes - 1] = self.held[self.base() + self.place.z]
        else:

            @pl.when(self.place.z == self.target)
            def _():
                for index in range(planes):
                    self.inbox[3][planes - 1, index] = self.held[self.base() + index]

        self.each_plane(lambda copy: copy.start())

    def sent(self):
        self.each_plane(lambda copy: copy.wait_send())

    def arrived(self):
        for step in range(1, self.place.planes):
            self.plane_copy(step).wait_recv()

    def total(self, index):
        terms = [
            self.inbox[3][step] if self.target is None else self.inbox[3][step, index]
            for step in range(self.place.planes)
        ]
        return sum(term.astype(jnp.float32) for term in terms)


def store_rows(chunk, values, first_row):
    width = values.shape[1]
    for k in range(values.shape[0] // 24):
        shard = first_row // 24 + k
        z, y, core, x = shard // 8, shard // 4 % 2, shard // 2 % 2, shard % 2
        at = chunk.slot(y, core, x) + z
        block = values[24 * k : 24 * k + 24]
        rest = block[16:24]
        chunk.held[at, :, 0:width] = block[0:16].astype(jnp.bfloat16)
        chunk.held[at, :, width : width + width // 2] = jnp.concatenate(
            [rest[:, : width // 2], rest[:, width // 2 :]], axis=0
        ).astype(jnp.bfloat16)


def load_rows(block, width):
    rest = block[:, width:]
    return jnp.concatenate(
        [block[:, :width], jnp.concatenate([rest[0:8], rest[8:16]], axis=1)], axis=0
    )


def tile_runs(sub, width):
    tiles = width // 128
    runs, tile = [], 0
    while tile < tiles:
        line = sub * tiles + tile
        count = min(tiles - tile, PART - line % PART)
        runs.append((tile, line // PART, line % PART, count))
        tile += count
    return runs


def store_shards(chunk, values, first_row):
    width = values.shape[1]
    for k in range(values.shape[0] // 16):
        row = first_row + 16 * k
        shard, sub = row // 96, row % 96 // 16
        base = chunk.slot(shard // 4, shard // 2 % 2, shard % 2)
        for tile, block, at, count in tile_runs(sub, width):
            chunk.held[base + block, :, 128 * at : 128 * (at + count)] = values[
                16 * k : 16 * k + 16, 128 * tile : 128 * (tile + count)
            ].astype(jnp.bfloat16)


class Taps:
    def __init__(self, place, held, inbox, result, sems, rows):
        self.place, self.held, self.inbox, self.result, self.sems = place, held, inbox, result, sems
        self.rows = rows

    def part(self, x, core, y, plane, count):
        planes = self.place.planes
        return pl.ds((((x * 2 + core) * 2 + y) * planes + plane) * self.rows, count * self.rows)

    def add(self, target, landing):
        self.held[target, :] = (
            self.held[target, :].astype(jnp.float32) + landing[...].astype(jnp.float32)
        ).astype(self.held.dtype)

    def copy(self, kind, step=0):
        place, planes = self.place, self.place.planes
        x, core, y, z = place.x, place.core, place.y, place.z
        if kind == "core":
            source, landing = self.part(step, 1 - core, 0, 0, 2 * planes), self.inbox[0].at[step]
            stage, device = step, place.sibling
        elif kind == "x":
            source, landing = self.part(1 - x, core, 0, 0, 2 * planes), self.inbox[1]
            stage, device = 2, place.next_x
        elif kind == "y":
            source, landing = self.part(x, core, 1 - y, 0, planes), self.inbox[2]
            stage, device = 3, place.next_y
        elif kind == "plane":
            device, other = place.plane(step)
            source, landing = self.part(x, core, y, other, 1), self.inbox[3].at[step - 1]
            stage = 3 + step
        else:
            if kind == "back plane":
                mine, stage, device = (0, core, y, z, 1), 2 + planes + step, place.plane(step)[0]
            elif kind == "back y":
                mine, stage, device = (0, core, y, 0, planes), 2 + 2 * planes, place.next_y
            else:
                mine, stage, device = (0, core, 0, 0, 2 * planes), 3 + 2 * planes, place.sibling
            landing = self.result.at[self.part(*mine), :]
        return pltpu.make_async_remote_copy(
            src_ref=landing if kind.startswith("back") else self.held.at[source, :],
            dst_ref=landing,
            send_sem=self.sems[0].at[stage],
            recv_sem=self.sems[1].at[stage],
            device_id=device,
            device_id_type=MESH,
        )

    def start(self):
        for x in range(2):
            self.copy("core", x).start()

    def over_core(self):
        for x in range(2):
            self.copy("core", x).wait()
            self.add(self.part(x, self.place.core, 0, 0, 2 * self.place.planes), self.inbox[0].at[x])
        self.copy("x").start()

    def over_x(self):
        place = self.place
        self.copy("x").wait()
        self.add(self.part(place.x, place.core, 0, 0, 2 * place.planes), self.inbox[1])
        self.copy("y").start()

    def over_y(self):
        place = self.place
        self.copy("y").wait()
        self.add(self.part(place.x, place.core, place.y, 0, place.planes), self.inbox[2])
        for step in range(1, place.planes):
            self.copy("plane", step).start()

    def over_planes(self):
        place = self.place
        total = self.held[self.part(place.x, place.core, place.y, place.z, 1), :].astype(jnp.float32)
        for step in range(1, place.planes):
            self.copy("plane", step).wait()
            total = total + self.inbox[3][step - 1].astype(jnp.float32)
        self.result[self.part(0, place.core, place.y, place.z, 1), :] = total.astype(self.result.dtype)
        for step in range(1, place.planes):
            self.copy("back plane", step).start()

    def back_y(self):
        for step in range(1, self.place.planes):
            self.copy("back plane", step).wait()
        self.copy("back y").start()

    def back_core(self):
        self.copy("back y").wait()
        self.copy("back core").start()

    def finish(self):
        self.copy("back core").wait()


class Sums:
    def __init__(self, place, levels, inbox, sems):
        self.place, self.levels, self.inbox, self.sems = place, levels, inbox, sems

    def copy(self, level, step=0):
        place = self.place
        device = (place.sibling, place.next_x, place.next_y)[level] if level < 3 else place.plane(step)[0]
        landing = level + max(step - 1, 0)
        return pltpu.make_async_remote_copy(
            src_ref=self.levels.at[level],
            dst_ref=self.inbox.at[landing],
            send_sem=self.sems[0].at[landing],
            recv_sem=self.sems[1].at[landing],
            device_id=device,
            device_id_type=MESH,
        )

    def start(self):
        self.copy(0).start()

    def over(self, level):
        self.copy(level).wait()
        self.levels[level + 1] = self.levels[level] + self.inbox[level]
        if level < 2:
            self.copy(level + 1).start()
        else:
            for step in range(1, self.place.planes):
                self.copy(3, step).start()

    def finish(self):
        total = self.levels[3]
        for step in range(1, self.place.planes):
            self.copy(3, step).wait()
            total = total + self.inbox[2 + step]
        return total


def block_kernel(
    planes,
    lengths,
    tokens, cotangent, raw_taps, w_in, w_out, w_up, w_down, table, table_t,
    ln1_gain, ln1_shift, ln2_gain, ln2_shift,
    block_out, input_grad, taps_out, residual, sums_out, w_in_grad, w_out_grad, w_up_grad, w_down_grad,
    held, inbox0, inbox1, inbox2, inbox_u, inbox_n, taps_held, taps0, taps1, taps2, taps3, taps_sum,
    levels, sums_inbox, cot, active, running, branch_v, normed_v, w_out_v,
    gate_v, mixed_v, waves, kernels,
    send_sems, recv_sems, taps_send, taps_recv, sums_send, sums_recv, share_send, share_recv, load_sems,
):
    tok_count, feat = cot.shape
    half = tok_count // 2
    tile = active.shape[2]
    step_rows = 256
    row_steps = tok_count // step_rows
    place = Place(planes)

    loads = {}

    class Load:
        def __init__(self, source, target):
            self.ends, self.at = (source, target), len(loads)

        def copy(self):
            source, target = (end() if callable(end) else end for end in self.ends)
            return pltpu.make_async_copy(source, target, load_sems.at[self.at])

        def wait(self):
            self.copy().wait()

    def load(name, source, target):
        loads[name] = Load(source, target)
        loads[name].copy().start()

    barrier = pltpu.get_barrier_semaphore()
    partners = [place.sibling, place.next_x, place.next_y] + [
        place.plane(step)[0] for step in range(1, planes)
    ]
    for partner in partners:
        pl.semaphore_signal(barrier, inc=1, device_id=partner, device_id_type=MESH)
    long = jnp.where(lengths[0] > half, 1.0, 0.0).astype(jnp.float32)

    def chunk(index, step, kind, target=None):
        at = step % FLIGHTS * 2 + kind
        ring = step % 2 * 2 + kind
        if target is None:
            far = (inbox_u, index // 2 if index < 2 * planes else index - planes)
        else:
            far = (inbox_n, None)
        return Chunk(
            place,
            (held, at),
            ((inbox0, ring), (inbox1, ring), (inbox2, ring), far),
            ((send_sems, index), (recv_sems, index)),
            kind == 0,
            target,
        )

    ups = [chunk(2 * t, t, 0) for t in range(planes)]
    downs = [chunk(2 * t + 1, t, 1, t) for t in range(planes)]

    def rows_of(index):
        return pl.ds(pl.multiple_of(index * step_rows, step_rows), step_rows)

    def norm_of(values):
        centered = values - jnp.mean(values, axis=-1, keepdims=True)
        inverse = lax.rsqrt(jnp.mean(centered * centered, axis=-1, keepdims=True) + eps_norm)
        return centered * inverse, inverse

    def stash_copy(index):
        rows = rows_of(index)
        return pltpu.make_async_copy(running.at[rows, :], residual.at[rows, :], load_sems.at[STORES + 5])

    def share_copy(which):
        block = half // 2
        block_x = place.x if which == 0 else 1 - place.x
        rows = pl.ds(pl.multiple_of(block_x * half + place.core * block, block), block)
        return pltpu.make_async_remote_copy(
            src_ref=taps_held.at[rows, :],
            dst_ref=taps_held.at[rows, :],
            send_sem=share_send.at[which],
            recv_sem=share_recv.at[which],
            device_id=place.next_x if which == 0 else place.sibling,
            device_id_type=MESH,
        )

    def forward_back(normed_2, normed_2t, up_tiles, down_tiles):
        def load_tile(t):
            cols = pl.ds(t * tile, tile)
            load(("up", t), lambda: w_up.at[:, cols], lambda: up_tiles.at[t % 2])
            load(("down", t), lambda: w_down.at[cols, :], lambda: down_tiles.at[t % 2])

        def mix(tokens_v, kernel, w_in_v, table_v, table_tv):
            load("taps", raw_taps, running.at[0:half, :])
            load("tokens", tokens, tokens_v)
            load("w_in", w_in, w_in_v)
            load("table", table, table_v)
            load("table_t", table_t, table_tv)
            load("w_out", w_out, w_out_v)
            load_tile(0)
            load("cot", cotangent, cot)

            loads["taps"].wait()

            def squash_step(index, carry):
                rows = pl.ds(pl.multiple_of(index * 128, 128), 128)
                raw = running[rows, :]
                taps_held[pl.ds(pl.multiple_of(place.x * half + index * 128, 128), 128), :] = (
                    raw - jnp.clip(raw, -shrink_level, shrink_level)
                ).astype(jnp.bfloat16)
                return carry

            lax.fori_loop(0, half // 128, squash_step, 0)
            pl.semaphore_wait(barrier, len(partners))
            share_copy(0).start()
            loads["tokens"].wait()
            loads["w_in"].wait()

            def project_step(index, carry):
                rows = rows_of(index)
                unit, _ = norm_of(tokens_v[rows, :].astype(jnp.float32))
                low = (unit * ln1_gain[...][None, :] + ln1_shift[...][None, :]).astype(jnp.bfloat16)
                normed_v[:, rows] = low.T
                active[1, rows, :] = dot_nn(low, w_in_v[:, 0:feat]).astype(jnp.bfloat16)
                gate_v[rows, :] = dot_nn(low, w_in_v[:, feat:]).astype(jnp.bfloat16)
                return carry

            lax.fori_loop(0, row_steps, project_step, 0)
            share_copy(0).wait()
            share_copy(1).start()
            loads["table"].wait()

            def signal_wave_step(index, carry):
                rows = rows_of(index)
                for which in range(2):
                    waves[which, rows, :] = dot_nn(
                        table_v[rows, :], active[1, which * half : (which + 1) * half, :]
                    ).astype(jnp.bfloat16)
                return carry

            lax.fori_loop(0, row_steps, signal_wave_step, 0)
            share_copy(1).wait()
            pool_rows = 128
            for index in range(tok_count // pool_rows):
                at = index * pool_rows
                first, last = max(at - 16, 0), min(at + pool_rows + 16, tok_count)
                around = taps_held[first:last, :].astype(jnp.float32)
                if at == 0:
                    around = jnp.concatenate([jnp.zeros((16, feat), jnp.float32), around], axis=0)
                if last == tok_count:
                    around = jnp.concatenate([around, jnp.zeros((16, feat), jnp.float32)], axis=0)
                kernel[at : at + pool_rows, :] = (
                    (around[15 : 15 + pool_rows] + around[16 : 16 + pool_rows] + around[17 : 17 + pool_rows])
                    / 3.0
                ).astype(jnp.bfloat16)

            def spread_step(index, carry):
                down, across = index // (feat // 256), index % (feat // 256)
                real = pl.ds(pl.multiple_of(down * 256, 256), 256)
                imag = pl.ds(pl.multiple_of(half + down * 256, 256), 256)
                cols = pl.ds(pl.multiple_of(across * 256, 256), 256)
                low_r = dot_nn(table_v[real, :], kernel[0:half, cols])
                low_i = dot_nn(table_v[imag, :], kernel[0:half, cols])
                high_r = dot_nn(table_v[real, :], kernel[half:, cols])
                high_i = dot_nn(table_v[imag, :], kernel[half:, cols])
                odd = lax.broadcasted_iota(jnp.int32, (256, 1), 0) % 2
                parity = (1 - 2 * odd).astype(jnp.float32)
                cross_r = long * (high_r - parity * low_i)
                cross_i = long * (high_i + parity * low_r)
                kernels[0, real, cols] = low_r.astype(jnp.bfloat16)
                kernels[0, imag, cols] = low_i.astype(jnp.bfloat16)
                kernels[1, real, cols] = cross_r.astype(jnp.bfloat16)
                kernels[1, imag, cols] = cross_i.astype(jnp.bfloat16)
                head_r = waves[0, real, cols].astype(jnp.float32)
                head_i = waves[0, imag, cols].astype(jnp.float32)
                tail_r = waves[1, real, cols].astype(jnp.float32)
                tail_i = waves[1, imag, cols].astype(jnp.float32)
                scale = 1.0 / half
                active[2, real, cols] = ((low_r * head_r - low_i * head_i) * scale).astype(jnp.bfloat16)
                active[2, imag, cols] = ((low_r * head_i + low_i * head_r) * scale).astype(jnp.bfloat16)
                active[3, real, cols] = (
                    (low_r * tail_r - low_i * tail_i + cross_r * head_r - cross_i * head_i) * scale
                ).astype(jnp.bfloat16)
                active[3, imag, cols] = (
                    (low_r * tail_i + low_i * tail_r + cross_r * head_i + cross_i * head_r) * scale
                ).astype(jnp.bfloat16)
                return carry

            lax.fori_loop(0, half // 256 * (feat // 256), spread_step, 0)
            loads["table_t"].wait()
            loads["w_out"].wait()

            def residual_step(index, carry):
                rows = rows_of(index)
                part_steps = half // step_rows
                which = index // part_steps
                of_part = pl.ds(pl.multiple_of(index % part_steps * step_rows, step_rows), step_rows)
                mixed = dot_nn(table_tv[of_part, :], active[2 + which])
                mixed_v[rows, :] = mixed.astype(jnp.bfloat16)
                branch = (mixed * gate_v[rows, :].astype(jnp.float32)).astype(jnp.bfloat16)
                branch_v[:, rows] = branch.T
                left = tokens_v[rows, :].astype(jnp.float32) + dot_nn(branch, w_out_v[...])
                running[rows, :] = left
                stash_copy(index).start()
                unit, _ = norm_of(left)
                low = (unit * ln2_gain[...][None, :] + ln2_shift[...][None, :]).astype(jnp.bfloat16)
                normed_2[rows, :] = low
                normed_2t[:, rows] = low.T
                return carry

            lax.fori_loop(0, row_steps, residual_step, 0)
            pltpu.make_async_copy(running, residual, load_sems.at[STORES + 5]).wait()

        pl.run_scoped(
            mix,
            pltpu.VMEM((tok_count, feat), jnp.bfloat16),
            pltpu.VMEM((tok_count, feat), jnp.bfloat16),
            pltpu.VMEM((feat, 2 * feat), jnp.bfloat16),
            pltpu.VMEM((tok_count, half), jnp.bfloat16),
            pltpu.VMEM((half, tok_count), jnp.bfloat16),
        )

        def feed_forward(d_hidden):
            loads["cot"].wait()

            for t in range(planes):
                up_tile, down_tile = up_tiles.at[t % 2], down_tiles.at[t % 2]
                loads["up", t].wait()
                loads["down", t].wait()
                if t + 1 < planes:
                    load_tile(t + 1)

                def rows_step(index, carry):
                    rows = rows_of(index)
                    hidden = dot_nn(normed_2[rows, :], up_tile[...])
                    d_active = dot_nt(cot[rows, :], down_tile[...])
                    value, slope = gelu_both(hidden)
                    active[t, rows, :] = value.astype(jnp.bfloat16)
                    d_value = (d_active * slope).astype(jnp.bfloat16)
                    d_hidden[rows, :] = d_value
                    back = dot_nt(d_value, up_tile[...])
                    if t == 0:
                        running[rows, :] = back
                    else:
                        running[rows, :] += back
                    return carry

                lax.fori_loop(0, row_steps // 2, rows_step, 0)
                if t >= 1:
                    ups[t - 1].over_core()
                    downs[t - 1].over_core()
                if t >= 2:
                    ups[t - 2].over_second()
                    downs[t - 2].over_second()
                lax.fori_loop(row_steps // 2, row_steps, rows_step, 0)
                if t >= FLIGHTS:
                    ups[t - FLIGHTS].sent()
                    downs[t - FLIGHTS].sent()
                for part in range(2):
                    cols = tile // 2
                    store_shards(
                        downs[t], dot_tn(active[t, :, part * cols : (part + 1) * cols], cot[...]), part * cols
                    )
                downs[t].start()
                if t >= 1:
                    ups[t - 1].over_first()
                    downs[t - 1].over_first()
                for part in range(2):
                    rows = feat // 2
                    store_rows(
                        ups[t], dot_nn(normed_2t[part * rows : (part + 1) * rows, :], d_hidden[...]), part * rows
                    )
                ups[t].start()

        pl.run_scoped(feed_forward, pltpu.VMEM((tok_count, tile), jnp.bfloat16))

    pl.run_scoped(
        forward_back,
        pltpu.VMEM((tok_count, feat), jnp.bfloat16),
        pltpu.VMEM((feat, tok_count), jnp.bfloat16),
        pltpu.VMEM((2, feat, tile), jnp.bfloat16),
        pltpu.VMEM((2, tile, feat), jnp.bfloat16),
    )

    out_chunk = chunk(2 * planes, planes, 0)
    gate_chunk = chunk(2 * planes + 1, planes, 1)
    signal_chunk = chunk(2 * planes + 2, planes + 1, 0)
    taps = Taps(
        place, taps_held, (taps0, taps1, taps2, taps3), taps_sum, (taps_send, taps_recv),
        tok_count // (8 * planes),
    )
    sums = Sums(place, levels, sums_inbox, (sums_send, sums_recv))

    def backward(d_out, d_gate, d_mix, d_signal):
        def norm_two_back(left_v):
            load("left", residual.at[0 : tok_count // 2, :], left_v.at[0 : tok_count // 2, :])
            load("left end", residual.at[tok_count // 2 :, :], left_v.at[tok_count // 2 :, :])
            loads["left"].wait()

            def back_step(index, carry):
                gain_sum, shift_sum = carry
                rows = rows_of(index)
                left = left_v[rows, :]
                centered = left - jnp.mean(left, axis=-1, keepdims=True)
                inverse = lax.rsqrt(jnp.mean(centered * centered, axis=-1, keepdims=True) + eps_norm)
                unit = centered * inverse
                grad = running[rows, :]
                scaled = grad * ln2_gain[...][None, :]
                d_left = cot[rows, :].astype(jnp.float32) + inverse * (
                    scaled
                    - jnp.mean(scaled, axis=-1, keepdims=True)
                    - unit * jnp.mean(scaled * unit, axis=-1, keepdims=True)
                )
                running[rows, :] = d_left
                d_low = d_left.astype(jnp.bfloat16)
                d_out[rows, :] = d_low
                d_branch = dot_nt(d_low, w_out_v[...])
                d_mix[rows, :] = (
                    d_branch * gate_v[rows, :].astype(jnp.float32) * (1.0 / half)
                ).astype(jnp.bfloat16)
                d_gate[rows, :] = (d_branch * mixed_v[rows, :].astype(jnp.float32)).astype(jnp.bfloat16)
                return gain_sum + column_sums(grad * unit), shift_sum + column_sums(grad)

            zero = jnp.zeros((8, feat), jnp.float32)
            carry = lax.fori_loop(0, row_steps // 2, back_step, (zero, zero))
            ups[planes - 1].over_core()
            downs[planes - 1].over_core()
            ups[planes - 2].over_second()
            downs[planes - 2].over_second()
            loads["left end"].wait()
            gain_sum, shift_sum = lax.fori_loop(row_steps // 2, row_steps, back_step, carry)
            levels[0] = jnp.zeros(levels.shape[1:], jnp.float32)
            levels[0, 0:1, :] = jnp.sum(gain_sum, axis=0, keepdims=True)
            levels[0, 1:2, :] = jnp.sum(shift_sum, axis=0, keepdims=True)

        pl.run_scoped(norm_two_back, pltpu.VMEM((tok_count, feat), jnp.float32))


        def weight_rows(target, left_t, right):
            for part in range(2):
                rows = feat // 2
                store_rows(target, dot_nn(left_t[part * rows : (part + 1) * rows, :], right[...]), part * rows)
            target.start()

        def mixer_back(table_v, table_tv, d_kernel, d_taps, d_waves):
            load("table again", table, table_v)
            load("table_t again", table_t, table_tv)
            ups[planes - 3].sent()
            downs[planes - 3].sent()
            weight_rows(out_chunk, branch_v, d_out)
            ups[planes - 1].over_first()
            downs[planes - 1].over_first()
            loads["table again"].wait()
            loads["table_t again"].wait()
            wave_rows, wave_cols = 256, 256

            def wave_step(down, cols):
                real = pl.ds(pl.multiple_of(down * wave_rows, wave_rows), wave_rows)
                imag = pl.ds(pl.multiple_of(half + down * wave_rows, wave_rows), wave_rows)
                first_r = dot_nn(table_v[real, :], d_mix[0:half, cols])
                first_i = dot_nn(table_v[imag, :], d_mix[0:half, cols])
                second_r = dot_nn(table_v[real, :], d_mix[half:, cols])
                second_i = dot_nn(table_v[imag, :], d_mix[half:, cols])

                def wide(ref, which, rows):
                    return ref[which, rows, cols].astype(jnp.float32)

                def keep(ref, which, rows, values):
                    at = cols if ref.shape[2] == feat else slice(None)
                    ref[which, rows, at] = values.astype(jnp.bfloat16)

                low_r, low_i = wide(kernels, 0, real), wide(kernels, 0, imag)
                cross_r, cross_i = wide(kernels, 1, real), wide(kernels, 1, imag)
                keep(d_waves, 0, real, low_r * first_r + low_i * first_i + cross_r * second_r + cross_i * second_i)
                keep(d_waves, 0, imag, low_r * first_i - low_i * first_r + cross_r * second_i - cross_i * second_r)
                keep(d_waves, 1, real, low_r * second_r + low_i * second_i)
                keep(d_waves, 1, imag, low_r * second_i - low_i * second_r)
                head_r, head_i = wide(waves, 0, real), wide(waves, 0, imag)
                tail_r, tail_i = wide(waves, 1, real), wide(waves, 1, imag)
                far_r = (head_r * second_r + head_i * second_i) * long
                far_i = (head_r * second_i - head_i * second_r) * long
                odd = lax.broadcasted_iota(jnp.int32, (wave_rows, 1), 0) % 2
                parity = (1 - 2 * odd).astype(jnp.float32)
                keep(d_kernel, 1, real, far_r)
                keep(d_kernel, 1, imag, far_i)
                keep(
                    d_kernel,
                    0,
                    real,
                    head_r * first_r + head_i * first_i + tail_r * second_r + tail_i * second_i + parity * far_i,
                )
                keep(
                    d_kernel,
                    0,
                    imag,
                    head_r * first_i - head_i * first_r + tail_r * second_i - tail_i * second_r - parity * far_r,
                )

            pad = 8
            d_taps[0:pad, :] = jnp.zeros((pad, wave_cols), jnp.float32)
            d_taps[pad + tok_count :, :] = jnp.zeros((pad, wave_cols), jnp.float32)
            pool_rows = 128

            def column_step(across, carry):
                cols = pl.ds(pl.multiple_of(across * wave_cols, wave_cols), wave_cols)
                for down in range(half // wave_rows):
                    wave_step(down, cols)
                for which in range(2):
                    d_taps[pad + which * half : pad + (which + 1) * half, :] = dot_nn(table_tv[...], d_kernel[which])
                for index in range(tok_count // pool_rows):
                    at = pad + index * pool_rows
                    taps_held[at - pad : at - pad + pool_rows, cols] = (
                        (
                            d_taps[at - 1 : at - 1 + pool_rows, :]
                            + d_taps[at : at + pool_rows, :]
                            + d_taps[at + 1 : at + 1 + pool_rows, :]
                        )
                        / 3.0
                    ).astype(jnp.bfloat16)
                return carry

            lax.fori_loop(0, feat // wave_cols, column_step, 0)
            taps.start()
            ups[planes - 1].over_second()
            downs[planes - 1].over_second()
            out_chunk.over_core()
            for which in range(2):

                def signal_step(index, carry):
                    at = pl.multiple_of(index * step_rows, step_rows)
                    d_signal[pl.ds(which * half + at, step_rows), :] = dot_nn(
                        table_tv[pl.ds(at, step_rows), :], d_waves[which]
                    ).astype(jnp.bfloat16)
                    return carry

                lax.fori_loop(0, half // step_rows, signal_step, 0)

        pl.run_scoped(
            mixer_back,
            pltpu.VMEM((tok_count, half), jnp.bfloat16),
            pltpu.VMEM((half, tok_count), jnp.bfloat16),
            pltpu.VMEM((2, tok_count, 256), jnp.bfloat16),
            pltpu.VMEM((tok_count + 16, 256), jnp.float32),
            pltpu.VMEM((2, tok_count, feat), jnp.bfloat16),
        )

        taps.over_core()
        ups[planes - 2].sent()
        weight_rows(signal_chunk, normed_v, d_signal)
        out_chunk.over_first()
        taps.over_x()
        weight_rows(gate_chunk, normed_v, d_gate)
        out_chunk.over_second()
        signal_chunk.over_core()
        taps.over_y()

        def finish(w_in_v, left_v, grad_stage, out_stage):
            def down_again(t):
                return (waves if t < 2 else kernels).at[t % 2, 0:tile, :]

            def load_again(t):
                rows = pl.ds(t * tile, tile)
                load(("again", t), lambda: w_down.at[rows, :], lambda: down_again(t))

            load("w_in again", w_in, w_in_v)
            load("tokens again", tokens, gate_v)
            for t in range(planes):
                load_again(t)
            load("left again", residual, left_v)
            loads["tokens again"].wait()
            loads["w_in again"].wait()
            gate_chunk.over_core()

            def grad_copy(index, slot):
                return pltpu.make_async_copy(
                    grad_stage.at[slot], input_grad.at[rows_of(index), :], load_sems.at[STORES + slot]
                )

            def input_step(index, carry):
                gain_sum, shift_sum = carry
                rows = rows_of(index)
                slot = index % 2
                d_normed = dot_nt(d_signal[rows, :], w_in_v[:, 0:feat]) + dot_nt(
                    d_gate[rows, :], w_in_v[:, feat:]
                )
                values = gate_v[rows, :].astype(jnp.float32)
                centered = values - jnp.mean(values, axis=-1, keepdims=True)
                inverse = lax.rsqrt(jnp.mean(centered * centered, axis=-1, keepdims=True) + eps_norm)
                unit = centered * inverse
                scaled = d_normed * ln1_gain[...][None, :]

                @pl.when(index >= 2)
                def _():
                    grad_copy(index - 2, slot).wait()

                grad_stage[slot] = running[rows, :] + inverse * (
                    scaled
                    - jnp.mean(scaled, axis=-1, keepdims=True)
                    - unit * jnp.mean(scaled * unit, axis=-1, keepdims=True)
                )
                grad_copy(index, slot).start()
                return gain_sum + column_sums(d_normed * unit), shift_sum + column_sums(d_normed)

            zero = jnp.zeros((8, feat), jnp.float32)
            carry = lax.fori_loop(0, row_steps // 2, input_step, (zero, zero))
            signal_chunk.over_first()
            taps.over_planes()
            gain_sum, shift_sum = lax.fori_loop(row_steps // 2, row_steps, input_step, carry)
            levels[0, 2:3, :] = jnp.sum(gain_sum, axis=0, keepdims=True)
            levels[0, 3:4, :] = jnp.sum(shift_sum, axis=0, keepdims=True)
            sums.start()
            gate_chunk.over_first()
            signal_chunk.over_second()
            taps.back_y()
            for t in range(planes):
                loads["again", t].wait()
            loads["left again"].wait()

            def out_copy(index, slot):
                return pltpu.make_async_copy(
                    out_stage.at[slot], block_out.at[rows_of(index), :], load_sems.at[STORES + 2 + slot]
                )

            def out_step(index, carry):
                rows = rows_of(index)
                slot = index % 2
                total = left_v[rows, :]
                for t in range(planes):
                    total = total + dot_nn(active[t, rows, :], down_again(t)[...])

                @pl.when(index >= 2)
                def _():
                    out_copy(index - 2, slot).wait()

                out_stage[slot] = total.astype(jnp.bfloat16)
                out_copy(index, slot).start()
                return carry

            lax.fori_loop(0, 1, out_step, 0)
            sums.over(0)
            gate_chunk.over_second()
            lax.fori_loop(1, 2, out_step, 0)
            sums.over(1)
            taps.back_core()
            lax.fori_loop(2, 3, out_step, 0)
            sums.over(2)
            lax.fori_loop(3, row_steps, out_step, 0)
            for index in (row_steps - 2, row_steps - 1):
                grad_copy(index, index % 2).wait()
                out_copy(index, index % 2).wait()

        pl.run_scoped(
            finish,
            pltpu.VMEM((feat, 2 * feat), jnp.bfloat16),
            pltpu.VMEM((tok_count, feat), jnp.float32),
            pltpu.VMEM((2, step_rows, feat), jnp.float32),
            pltpu.VMEM((2, step_rows, feat), jnp.bfloat16),
        )

    pl.run_scoped(backward, *[pltpu.VMEM((tok_count, feat), jnp.bfloat16)] * 4)

    def own_rows(target):
        target.arrived()
        return load_rows(target.total(0), feat)

    for t in range(planes):
        w_up_grad[:, t * tile : (t + 1) * tile] = own_rows(ups[t])
    w_out_grad[...] = own_rows(out_chunk)
    w_in_grad[:, 0:feat] = own_rows(signal_chunk)
    w_in_grad[:, feat:] = own_rows(gate_chunk)
    for t in range(planes):

        @pl.when(place.z == t)
        def _():
            downs[t].arrived()
            for index in range(planes):
                block = downs[t].total(index)
                for sub in range(6):
                    for first, line, at, count in tile_runs(sub, feat):
                        if line == index:
                            w_down_grad[16 * sub : 16 * sub + 16, 128 * first : 128 * (first + count)] = block[
                                :, 128 * at : 128 * (at + count)
                            ]

    sums_out[...] = sums.finish()
    taps.finish()
    taps_store = pltpu.make_async_copy(taps_sum, taps_out, load_sems.at[STORES + 4])
    taps_store.start()
    for one in (downs[planes - 2], ups[planes - 1], downs[planes - 1], out_chunk, gate_chunk, signal_chunk):
        one.sent()
    taps_store.wait()


def linked_block(
    planes,
    tokens,
    lengths,
    raw_taps,
    ln1_gain,
    ln1_shift,
    w_in,
    w_out,
    ln2_gain,
    ln2_shift,
    w_up,
    w_down,
    cotangent,
):
    tok_count, feat = tokens.shape
    half = tok_count // 2
    tile = w_up.shape[1] // planes
    table = jnp.asarray(wave_table(half), jnp.bfloat16)
    table_t = jnp.asarray(wave_table(half).T, jnp.bfloat16)
    shares = 8 * planes
    rows = feat // shares
    block = (16, 128 * PART)
    chunks = 2 * planes + 3
    bf16, f32 = jnp.bfloat16, jnp.float32
    whole = pl.BlockSpec(memory_space=pl.ANY)
    near = pl.BlockSpec(memory_space=pltpu.VMEM)
    results = pl.pallas_call(
        functools.partial(block_kernel, planes),
        out_shape=(
            jax.ShapeDtypeStruct((tok_count, feat), bf16),
            jax.ShapeDtypeStruct((tok_count, feat), f32),
            jax.ShapeDtypeStruct((half, feat), bf16),
            jax.ShapeDtypeStruct((tok_count, feat), f32),
            jax.ShapeDtypeStruct((8, feat), f32),
            jax.ShapeDtypeStruct((rows, 2 * feat), f32),
            jax.ShapeDtypeStruct((rows, feat), f32),
            jax.ShapeDtypeStruct((rows, planes * tile), f32),
            jax.ShapeDtypeStruct((tile // 8, feat), f32),
        ),
        in_specs=[pl.BlockSpec(memory_space=pltpu.SMEM)] + [whole] * 9 + [near] * 4,
        out_specs=(whole,) * 4 + (near,) * 5,
        scratch_shapes=[
            pltpu.VMEM((2 * FLIGHTS, shares) + block, bf16),
            pltpu.VMEM((4, 4 * planes) + block, bf16),
            pltpu.VMEM((4, 2 * planes) + block, bf16),
            pltpu.VMEM((4, planes) + block, bf16),
            pltpu.VMEM((planes + 3, planes) + block, bf16),
            pltpu.VMEM((planes, planes) + block, bf16),
            pltpu.VMEM((tok_count, feat), bf16),
            pltpu.VMEM((2, tok_count // 4, feat), bf16),
            pltpu.VMEM((tok_count // 4, feat), bf16),
            pltpu.VMEM((tok_count // 8, feat), bf16),
            pltpu.VMEM((planes - 1, tok_count // shares, feat), bf16),
            pltpu.VMEM((half, feat), bf16),
            pltpu.VMEM((4, 8, feat), f32),
            pltpu.VMEM((planes + 2, 8, feat), f32),
            pltpu.VMEM((tok_count, feat), bf16),
            pltpu.VMEM((planes, tok_count, tile), bf16),
            pltpu.VMEM((tok_count, feat), f32),
            pltpu.VMEM((feat, tok_count), bf16),
            pltpu.VMEM((feat, tok_count), bf16),
            pltpu.VMEM((feat, feat), bf16),
            pltpu.VMEM((tok_count, feat), bf16),
            pltpu.VMEM((tok_count, feat), bf16),
            pltpu.VMEM((2, tok_count, feat), bf16),
            pltpu.VMEM((2, tok_count, feat), bf16),
            pltpu.SemaphoreType.DMA((chunks, planes + 2)),
            pltpu.SemaphoreType.DMA((chunks, planes + 2)),
            pltpu.SemaphoreType.DMA((2 * planes + 4,)),
            pltpu.SemaphoreType.DMA((2 * planes + 4,)),
            pltpu.SemaphoreType.DMA((planes + 2,)),
            pltpu.SemaphoreType.DMA((planes + 2,)),
            pltpu.SemaphoreType.DMA((2,)),
            pltpu.SemaphoreType.DMA((2,)),
            pltpu.SemaphoreType.DMA((STORES + 6,)),
        ],
        compiler_params=pltpu.CompilerParams(
            collective_id=1, has_side_effects=True, vmem_limit_bytes=VMEM_BYTES
        ),
        cost_estimate=pl.CostEstimate(
            flops=2 * tok_count * feat * (5 * w_up.shape[1] + 9 * feat),
            bytes_accessed=40 * tok_count * feat,
            transcendentals=tok_count * w_up.shape[1],
        ),
    )(
        lengths,
        tokens,
        cotangent,
        raw_taps,
        w_in,
        w_out,
        w_up,
        w_down,
        table,
        table_t,
        ln1_gain,
        ln1_shift,
        ln2_gain,
        ln2_shift,
    )
    block_out, input_grad, taps_sum, _, sums, w_in_grad, w_out_grad, w_up_grad, w_down_grad = results
    raw_grad = taps_sum.astype(f32) * (jnp.abs(raw_taps) > shrink_level).astype(f32)
    share = lax.axis_index("wide") * 2 + lax.axis_index("narrow")
    mine = lax.dynamic_slice(sums, (0, share * rows), (8, rows))
    return (
        block_out,
        input_grad,
        raw_grad,
        mine[2],
        mine[3],
        w_in_grad,
        w_out_grad,
        mine[0],
        mine[1],
        w_up_grad,
        w_down_grad,
    )


def solution(mesh):
    spread = P(("wide", "narrow"))
    rows = P(("wide", "narrow"), None)
    placed = (rows, spread, P("narrow", None)) + (P(),) * 8 + (rows,)
    wide, narrow = mesh.shape["wide"], mesh.shape["narrow"]

    def block(tokens, lengths, raw_taps, *others):
        fits = (
            narrow == 2
            and wide == 4 * 4
            and lengths.shape[0] == 1
            and raw_taps.shape[0] * 2 == tokens.shape[0]
            and tokens.shape[1] == 24 * wide * narrow
            and others[-2].shape[0] == 96 * wide * narrow
            and tokens.shape[0] % 512 == 0
        )
        if fits:
            return linked_block(wide // 4, tokens, lengths, raw_taps, *others)
        return local(tokens, lengths, raw_taps, *others)

    return jax.shard_map(
        block,
        mesh=mesh,
        in_specs=placed,
        out_specs=(rows, rows, P("narrow", None), spread, spread, rows, rows, spread, spread, rows, rows),
        check_vma=False,
    )
```

```python
import functools

import jax
import jax.numpy as jnp
import numpy as np
from jax import lax
from jax.experimental import pallas as pl
from jax.experimental.pallas import tpu as pltpu
from jax.sharding import PartitionSpec as P

shrink_level = 0.003
eps_norm = 1e-05


def wave_table(half):
    period = 4 * half
    phase = (np.outer(2 * np.arange(half) + 1, np.arange(half)) % period) * (2 * np.pi / period)
    return np.concatenate([np.cos(phase), -np.sin(phase)], axis=0)


def to_waves(table, block):
    return jnp.einsum("kn,nc->kc", table, block, preferred_element_type=jnp.float32)


def from_waves(table, waves):
    return jnp.einsum(
        "kn,kc->nc", table, waves.astype(jnp.bfloat16), preferred_element_type=jnp.float32
    )


def norm_parts(values):
    centered = values - jnp.mean(values, axis=-1, keepdims=True)
    inverse = lax.rsqrt(jnp.mean(centered * centered, axis=-1, keepdims=True) + eps_norm)
    return (centered * inverse, inverse)


def norm_back(upstream, unit_vals, inverse, gain_vec):
    scaled = upstream * gain_vec
    return inverse * (
        scaled
        - jnp.mean(scaled, axis=-1, keepdims=True)
        - unit_vals * jnp.mean(scaled * unit_vals, axis=-1, keepdims=True)
    )


def split(waves):
    half = waves.shape[0] // 2
    return waves[:half], waves[half:]


def times(left, right):
    lr, li = split(left)
    rr, ri = split(right)
    return jnp.concatenate([lr * rr - li * ri, lr * ri + li * rr], axis=0)


def conj_times(left, right):
    lr, li = split(left)
    rr, ri = split(right)
    return jnp.concatenate([lr * rr + li * ri, lr * ri - li * rr], axis=0)


def turned(waves, sign):
    wr, wi = split(waves)
    index = lax.broadcasted_iota(jnp.int32, (wr.shape[0], 1), 0)
    parity = sign * (1.0 - 2.0 * (index % 2).astype(jnp.float32))
    return jnp.concatenate([-parity * wi, parity * wr], axis=0)


def pool(values):
    padded = jnp.pad(values, ((1, 1), (0, 0)))
    return (padded[:-2] + padded[1:-1] + padded[2:]) / 3.0


def local(
    tokens,
    lengths,
    raw_taps,
    ln1_gain,
    ln1_shift,
    w_in,
    w_out,
    ln2_gain,
    ln2_shift,
    w_up,
    w_down,
    cotangent,
):
    tok_count, feat_width = tokens.shape
    row_count = lengths.shape[0]
    row_len = tok_count // row_count
    half = row_len // 2
    table = jnp.asarray(wave_table(half), jnp.bfloat16)
    scale = 1.0 / half
    long_rows = (lengths > half).astype(jnp.float32)

    squashed = raw_taps - jnp.clip(raw_taps, -shrink_level, shrink_level)
    gathered = lax.all_gather(squashed.astype(jnp.bfloat16), "narrow", axis=0, tiled=True)
    kernel = pool(gathered.astype(jnp.float32)).astype(jnp.bfloat16)
    kernel_low = to_waves(table, kernel[:half])
    kernel_cross = to_waves(table, kernel[half : 2 * half]) + turned(kernel_low, 1.0)

    inputs = tokens.astype(jnp.float32)
    unit_one, inverse_one = norm_parts(inputs)
    normed = (unit_one * ln1_gain + ln1_shift).astype(jnp.bfloat16)
    projected = jnp.dot(normed, w_in, preferred_element_type=jnp.float32)
    signal = projected[:, :feat_width].astype(jnp.bfloat16)
    gate_vals = projected[:, feat_width:]
    signal_waves = []
    mixed = []
    for row in range(row_count):
        first = to_waves(table, signal[row * row_len : row * row_len + half])
        second = to_waves(table, signal[row * row_len + half : (row + 1) * row_len])
        signal_waves.append((first, second))
        mixed.append(from_waves(table, times(first, kernel_low) * scale))
        mixed.append(
            from_waves(
                table,
                (times(second, kernel_low) + long_rows[row] * times(first, kernel_cross)) * scale,
            )
        )
    mixed = jnp.concatenate(mixed, axis=0)
    branch = (mixed * gate_vals).astype(jnp.bfloat16)
    residual = inputs + jnp.dot(branch, w_out, preferred_element_type=jnp.float32)
    unit_two, inverse_two = norm_parts(residual)
    normed2 = (unit_two * ln2_gain + ln2_shift).astype(jnp.bfloat16)
    hidden = jnp.dot(normed2, w_up, preferred_element_type=jnp.float32)
    active = jax.nn.gelu(hidden).astype(jnp.bfloat16)
    block_out = (residual + jnp.dot(active, w_down, preferred_element_type=jnp.float32)).astype(
        jnp.bfloat16
    )
    w_down_grad = jnp.einsum("tf,td->fd", active, cotangent, preferred_element_type=jnp.float32)
    d_active = jnp.einsum("td,fd->tf", cotangent, w_down, preferred_element_type=jnp.float32)
    gelu_pull = jax.vjp(jax.nn.gelu, hidden)[1]
    d_hidden = gelu_pull(d_active)[0].astype(jnp.bfloat16)
    w_up_grad = jnp.einsum("td,tf->df", normed2, d_hidden, preferred_element_type=jnp.float32)
    d_normed2 = jnp.einsum("tf,df->td", d_hidden, w_up, preferred_element_type=jnp.float32)
    ln2_gain_grad = jnp.sum(d_normed2 * unit_two, axis=0)
    ln2_shift_grad = jnp.sum(d_normed2, axis=0)
    d_residual = cotangent.astype(jnp.float32) + norm_back(
        d_normed2, unit_two, inverse_two, ln2_gain
    )
    d_outproj = d_residual.astype(jnp.bfloat16)
    w_out_grad = jnp.einsum("td,te->de", branch, d_outproj, preferred_element_type=jnp.float32)
    d_branch = jnp.einsum("te,de->td", d_outproj, w_out, preferred_element_type=jnp.float32)
    d_mixed = (d_branch * gate_vals).astype(jnp.bfloat16)
    d_gate = d_branch * mixed
    d_signal = []
    low_grad = 0.0
    cross_grad = 0.0
    for row in range(row_count):
        first, second = signal_waves[row]
        d_first = to_waves(table, d_mixed[row * row_len : row * row_len + half]) * scale
        d_second = to_waves(table, d_mixed[row * row_len + half : (row + 1) * row_len]) * scale
        d_cross = d_second * long_rows[row]
        d_signal.append(
            from_waves(table, conj_times(kernel_low, d_first) + conj_times(kernel_cross, d_cross))
        )
        d_signal.append(from_waves(table, conj_times(kernel_low, d_second)))
        low_grad = low_grad + conj_times(first, d_first) + conj_times(second, d_second)
        cross_grad = cross_grad + conj_times(first, d_cross)
    low_grad = low_grad + turned(cross_grad, -1.0)
    d_kernel = jnp.concatenate([from_waves(table, low_grad), from_waves(table, cross_grad)], axis=0)
    d_signal = jnp.concatenate(d_signal, axis=0)
    d_projected = jnp.concatenate([d_signal, d_gate], axis=1).astype(jnp.bfloat16)
    w_in_grad = jnp.einsum("td,te->de", normed, d_projected, preferred_element_type=jnp.float32)
    d_normed = jnp.einsum("te,de->td", d_projected, w_in, preferred_element_type=jnp.float32)
    ln1_gain_grad = jnp.sum(d_normed * unit_one, axis=0)
    ln1_shift_grad = jnp.sum(d_normed, axis=0)
    input_grad = d_residual + norm_back(d_normed, unit_one, inverse_one, ln1_gain)

    shares = lax.psum_scatter(
        pool(d_kernel).astype(jnp.bfloat16), "narrow", scatter_dimension=0, tiled=True
    )
    summed = lax.psum(shares, "wide").astype(jnp.float32)
    raw_grad = summed * (jnp.abs(raw_taps) > shrink_level).astype(jnp.float32)

    def scatter(values):
        return lax.psum_scatter(
            values.astype(jnp.bfloat16), ("wide", "narrow"), scatter_dimension=0, tiled=True
        ).astype(jnp.float32)

    def scatter_wide(values):
        return lax.psum_scatter(values, ("wide", "narrow"), scatter_dimension=0, tiled=True)

    return (
        block_out,
        input_grad,
        raw_grad,
        scatter_wide(ln1_gain_grad),
        scatter_wide(ln1_shift_grad),
        scatter(w_in_grad),
        scatter(w_out_grad),
        scatter_wide(ln2_gain_grad),
        scatter_wide(ln2_shift_grad),
        scatter(w_up_grad),
        scatter(w_down_grad),
    )


MESH = pl.DeviceIdType.MESH
PART = 9
STORES = 30
VMEM_BYTES = 60 * 2**20
FLIGHTS = 3


def dot_nn(left, right):
    return lax.dot_general(left, right, (((1,), (0,)), ((), ())), preferred_element_type=jnp.float32)


def dot_nt(left, right):
    return lax.dot_general(left, right, (((1,), (1,)), ((), ())), preferred_element_type=jnp.float32)


def dot_tn(left, right):
    return lax.dot_general(left, right, (((0,), (0,)), ((), ())), preferred_element_type=jnp.float32)


def gelu_both(hidden):
    inner = 0.7978845608028654
    cubic = inner * 0.044715
    square = hidden * hidden
    bent = jnp.tanh(hidden * (inner + cubic * square))
    share = 0.5 + 0.5 * bent
    slope = share + (0.5 * hidden) * (1.0 - bent * bent) * (inner + (3.0 * cubic) * square)
    return hidden * share, slope


def column_sums(values):
    rows, width = values.shape
    return jnp.sum(values.reshape(rows // 8, 8, width), axis=0)


class Place:
    def __init__(self, planes):
        wide = lax.axis_index("wide")
        self.narrow = lax.axis_index("narrow")
        self.wide = wide
        self.core = wide % 2
        self.y = (wide // 2) % 2
        self.z = wide // 4
        self.x = self.narrow
        self.planes = planes
        self.sibling = (wide + 1 - 2 * self.core, self.narrow)
        self.next_x = (wide, 1 - self.narrow)
        self.next_y = (wide + 2 - 4 * self.y, self.narrow)

    def plane(self, step):
        other = (self.z + step) % self.planes
        return (self.wide + 4 * (other - self.z), self.narrow), other


class Chunk:
    def __init__(self, place, held, inbox, sems, x_first, target=None):
        self.place = place
        self.views = (held, inbox, sems)
        self.target = target
        self.first, self.second = (place.x, place.y) if x_first else (place.y, place.x)
        self.to_first, self.to_second = (
            (place.next_x, place.next_y) if x_first else (place.next_y, place.next_x)
        )
        self.x_first = x_first

    @property
    def held(self):
        ref, at = self.views[0]
        return ref.at[at]

    @property
    def inbox(self):
        return [ref if at is None else ref.at[at] for ref, at in self.views[1]]

    @property
    def sems(self):
        return [ref.at[at] for ref, at in self.views[2]]

    def slot(self, y, core, x):
        first, second = (x, y) if self.x_first else (y, x)
        return ((core * 2 + first) * 2 + second) * self.place.planes

    def copy(self, stage):
        planes, core = self.place.planes, self.place.core
        first, second = self.first, self.second
        start, count, device = (
            (4 * planes * (1 - core), 4 * planes, self.place.sibling),
            (4 * planes * core + 2 * planes * (1 - first), 2 * planes, self.to_first),
            (4 * planes * core + 2 * planes * first + planes * (1 - second), planes, self.to_second),
        )[stage]
        return pltpu.make_async_remote_copy(
            src_ref=self.held.at[pl.ds(start, count)],
            dst_ref=self.inbox[stage],
            send_sem=self.sems[0].at[stage],
            recv_sem=self.sems[1].at[stage],
            device_id=device,
            device_id_type=MESH,
        )

    def add(self, start, landing, count):
        def body(index, carry):
            at = start + index
            self.held[at] = (
                self.held[at].astype(jnp.float32) + landing[index].astype(jnp.float32)
            ).astype(self.held.dtype)
            return carry

        lax.fori_loop(0, count, body, 0)

    def start(self):
        self.copy(0).start()

    def over_core(self):
        planes = self.place.planes
        self.copy(0).wait()
        self.add(4 * planes * self.place.core, self.inbox[0], 4 * planes)
        self.copy(1).start()

    def over_first(self):
        planes = self.place.planes
        self.copy(1).wait()
        self.add(4 * planes * self.place.core + 2 * planes * self.first, self.inbox[1], 2 * planes)
        self.copy(2).start()

    def base(self):
        planes, place = self.place.planes, self.place
        return 4 * planes * place.core + 2 * planes * self.first + planes * self.second

    def plane_copy(self, step):
        device, other = self.place.plane(step)
        if self.target is None:
            return pltpu.make_async_remote_copy(
                src_ref=self.held.at[self.base() + other],
                dst_ref=self.inbox[3].at[step - 1],
                send_sem=self.sems[0].at[2 + step],
                recv_sem=self.sems[1].at[2 + step],
                device_id=device,
                device_id_type=MESH,
            )
        return pltpu.make_async_remote_copy(
            src_ref=self.held.at[pl.ds(self.base(), self.place.planes)],
            dst_ref=self.inbox[3].at[step - 1],
            send_sem=self.sems[0].at[2 + step],
            recv_sem=self.sems[1].at[2 + step],
            device_id=device,
            device_id_type=MESH,
        )

    def each_plane(self, act):
        for step in range(1, self.place.planes):
            if self.target is None:
                act(self.plane_copy(step))
            else:

                @pl.when((self.place.z + step) % self.place.planes == self.target)
                def _():
                    act(self.plane_copy(step))

    def over_second(self):
        self.copy(2).wait()
        planes = self.place.planes
        self.add(self.base(), self.inbox[2], planes)
        if self.target is None:
            self.inbox[3][planes - 1] = self.held[self.base() + self.place.z]
        else:

            @pl.when(self.place.z == self.target)
            def _():
                for index in range(planes):
                    self.inbox[3][planes - 1, index] = self.held[self.base() + index]

        self.each_plane(lambda copy: copy.start())

    def sent(self):
        self.each_plane(lambda copy: copy.wait_send())

    def arrived(self):
        for step in range(1, self.place.planes):
            self.plane_copy(step).wait_recv()

    def total(self, index):
        terms = [
            self.inbox[3][step] if self.target is None else self.inbox[3][step, index]
            for step in range(self.place.planes)
        ]
        return sum(term.astype(jnp.float32) for term in terms)


def store_rows(chunk, values, first_row):
    width = values.shape[1]
    for k in range(values.shape[0] // 24):
        shard = first_row // 24 + k
        z, y, core, x = shard // 8, shard // 4 % 2, shard // 2 % 2, shard % 2
        at = chunk.slot(y, core, x) + z
        block = values[24 * k : 24 * k + 24]
        rest = block[16:24]
        chunk.held[at, :, 0:width] = block[0:16].astype(jnp.bfloat16)
        chunk.held[at, :, width : width + width // 2] = jnp.concatenate(
            [rest[:, : width // 2], rest[:, width // 2 :]], axis=0
        ).astype(jnp.bfloat16)


def load_rows(block, width):
    rest = block[:, width:]
    return jnp.concatenate(
        [block[:, :width], jnp.concatenate([rest[0:8], rest[8:16]], axis=1)], axis=0
    )


def tile_runs(sub, width):
    tiles = width // 128
    runs, tile = [], 0
    while tile < tiles:
        line = sub * tiles + tile
        count = min(tiles - tile, PART - line % PART)
        runs.append((tile, line // PART, line % PART, count))
        tile += count
    return runs


def store_shards(chunk, values, first_row):
    width = values.shape[1]
    for k in range(values.shape[0] // 16):
        row = first_row + 16 * k
        shard, sub = row // 96, row % 96 // 16
        base = chunk.slot(shard // 4, shard // 2 % 2, shard % 2)
        for tile, block, at, count in tile_runs(sub, width):
            chunk.held[base + block, :, 128 * at : 128 * (at + count)] = values[
                16 * k : 16 * k + 16, 128 * tile : 128 * (tile + count)
            ].astype(jnp.bfloat16)


class Taps:
    def __init__(self, place, held, inbox, result, sems, rows):
        self.place, self.held, self.inbox, self.result, self.sems = place, held, inbox, result, sems
        self.rows = rows

    def part(self, x, core, y, plane, count):
        planes = self.place.planes
        return pl.ds((((x * 2 + core) * 2 + y) * planes + plane) * self.rows, count * self.rows)

    def add(self, target, landing):
        self.held[target, :] = (
            self.held[target, :].astype(jnp.float32) + landing[...].astype(jnp.float32)
        ).astype(self.held.dtype)

    def copy(self, kind, step=0):
        place, planes = self.place, self.place.planes
        x, core, y, z = place.x, place.core, place.y, place.z
        if kind == "core":
            source, landing = self.part(step, 1 - core, 0, 0, 2 * planes), self.inbox[0].at[step]
            stage, device = step, place.sibling
        elif kind == "x":
            source, landing = self.part(1 - x, core, 0, 0, 2 * planes), self.inbox[1]
            stage, device = 2, place.next_x
        elif kind == "y":
            source, landing = self.part(x, core, 1 - y, 0, planes), self.inbox[2]
            stage, device = 3, place.next_y
        elif kind == "plane":
            device, other = place.plane(step)
            source, landing = self.part(x, core, y, other, 1), self.inbox[3].at[step - 1]
            stage = 3 + step
        else:
            if kind == "back plane":
                mine, stage, device = (0, core, y, z, 1), 2 + planes + step, place.plane(step)[0]
            elif kind == "back y":
                mine, stage, device = (0, core, y, 0, planes), 2 + 2 * planes, place.next_y
            else:
                mine, stage, device = (0, core, 0, 0, 2 * planes), 3 + 2 * planes, place.sibling
            landing = self.result.at[self.part(*mine), :]
        return pltpu.make_async_remote_copy(
            src_ref=landing if kind.startswith("back") else self.held.at[source, :],
            dst_ref=landing,
            send_sem=self.sems[0].at[stage],
            recv_sem=self.sems[1].at[stage],
            device_id=device,
            device_id_type=MESH,
        )

    def start(self):
        for x in range(2):
            self.copy("core", x).start()

    def over_core(self):
        for x in range(2):
            self.copy("core", x).wait()
            self.add(self.part(x, self.place.core, 0, 0, 2 * self.place.planes), self.inbox[0].at[x])
        self.copy("x").start()

    def over_x(self):
        place = self.place
        self.copy("x").wait()
        self.add(self.part(place.x, place.core, 0, 0, 2 * place.planes), self.inbox[1])
        self.copy("y").start()

    def over_y(self):
        place = self.place
        self.copy("y").wait()
        self.add(self.part(place.x, place.core, place.y, 0, place.planes), self.inbox[2])
        for step in range(1, place.planes):
            self.copy("plane", step).start()

    def over_planes(self):
        place = self.place
        total = self.held[self.part(place.x, place.core, place.y, place.z, 1), :].astype(jnp.float32)
        for step in range(1, place.planes):
            self.copy("plane", step).wait()
            total = total + self.inbox[3][step - 1].astype(jnp.float32)
        self.result[self.part(0, place.core, place.y, place.z, 1), :] = total.astype(self.result.dtype)
        for step in range(1, place.planes):
            self.copy("back plane", step).start()

    def back_y(self):
        for step in range(1, self.place.planes):
            self.copy("back plane", step).wait()
        self.copy("back y").start()

    def back_core(self):
        self.copy("back y").wait()
        self.copy("back core").start()

    def finish(self):
        self.copy("back core").wait()


class Sums:
    def __init__(self, place, levels, inbox, sems):
        self.place, self.levels, self.inbox, self.sems = place, levels, inbox, sems

    def copy(self, level, step=0):
        place = self.place
        device = (place.sibling, place.next_x, place.next_y)[level] if level < 3 else place.plane(step)[0]
        landing = level + max(step - 1, 0)
        return pltpu.make_async_remote_copy(
            src_ref=self.levels.at[level],
            dst_ref=self.inbox.at[landing],
            send_sem=self.sems[0].at[landing],
            recv_sem=self.sems[1].at[landing],
            device_id=device,
            device_id_type=MESH,
        )

    def start(self):
        self.copy(0).start()

    def over(self, level):
        self.copy(level).wait()
        self.levels[level + 1] = self.levels[level] + self.inbox[level]
        if level < 2:
            self.copy(level + 1).start()
        else:
            for step in range(1, self.place.planes):
                self.copy(3, step).start()

    def finish(self):
        total = self.levels[3]
        for step in range(1, self.place.planes):
            self.copy(3, step).wait()
            total = total + self.inbox[2 + step]
        return total


def block_kernel(
    planes,
    lengths,
    tokens, cotangent, raw_taps, w_in, w_out, w_up, w_down, table, table_t,
    ln1_gain, ln1_shift, ln2_gain, ln2_shift,
    block_out, input_grad, taps_out, residual, sums_out, w_in_grad, w_out_grad, w_up_grad, w_down_grad,
    held, inbox0, inbox1, inbox2, inbox_u, inbox_n, taps_held, taps0, taps1, taps2, taps3, taps_sum,
    levels, sums_inbox, cot, active, running, branch_v, normed_v, w_out_v,
    gate_v, mixed_v, waves, kernels,
    send_sems, recv_sems, taps_send, taps_recv, sums_send, sums_recv, share_send, share_recv, load_sems,
):
    tok_count, feat = cot.shape
    half = tok_count // 2
    tile = active.shape[2]
    step_rows = 256
    row_steps = tok_count // step_rows
    place = Place(planes)

    loads = {}

    class Load:
        def __init__(self, source, target):
            self.ends, self.at = (source, target), len(loads)

        def copy(self):
            source, target = (end() if callable(end) else end for end in self.ends)
            return pltpu.make_async_copy(source, target, load_sems.at[self.at])

        def wait(self):
            self.copy().wait()

    def load(name, source, target):
        loads[name] = Load(source, target)
        loads[name].copy().start()

    barrier = pltpu.get_barrier_semaphore()
    partners = [place.sibling, place.next_x, place.next_y] + [
        place.plane(step)[0] for step in range(1, planes)
    ]
    for partner in partners:
        pl.semaphore_signal(barrier, inc=1, device_id=partner, device_id_type=MESH)
    long = jnp.where(lengths[0] > half, 1.0, 0.0).astype(jnp.float32)

    def chunk(index, step, kind, target=None):
        at = step % FLIGHTS * 2 + kind
        ring = step % 2 * 2 + kind
        if target is None:
            far = (inbox_u, index // 2 if index < 2 * planes else index - planes)
        else:
            far = (inbox_n, None)
        return Chunk(
            place,
            (held, at),
            ((inbox0, ring), (inbox1, ring), (inbox2, ring), far),
            ((send_sems, index), (recv_sems, index)),
            kind == 0,
            target,
        )

    ups = [chunk(2 * t, t, 0) for t in range(planes)]
    downs = [chunk(2 * t + 1, t, 1, t) for t in range(planes)]

    def rows_of(index):
        return pl.ds(index * step_rows, step_rows)

    def unrolled(first, last, body, carry):
        for index in range(first, last):
            carry = body(index, carry)
        return carry

    def norm_of(values):
        centered = values - jnp.mean(values, axis=-1, keepdims=True)
        inverse = lax.rsqrt(jnp.mean(centered * centered, axis=-1, keepdims=True) + eps_norm)
        return centered * inverse, inverse

    def stash_copy(index):
        rows = rows_of(index)
        return pltpu.make_async_copy(running.at[rows, :], residual.at[rows, :], load_sems.at[STORES - 2])

    def share_copy(which):
        block = half // 2
        block_x = place.x if which == 0 else 1 - place.x
        rows = pl.ds(pl.multiple_of(block_x * half + place.core * block, block), block)
        return pltpu.make_async_remote_copy(
            src_ref=taps_held.at[rows, :],
            dst_ref=taps_held.at[rows, :],
            send_sem=share_send.at[which],
            recv_sem=share_recv.at[which],
            device_id=place.next_x if which == 0 else place.sibling,
            device_id_type=MESH,
        )

    def forward_back(normed_2, normed_2t, up_tiles, down_tiles):
        def load_tile(t):
            cols = pl.ds(t * tile, tile)
            load(("up", t), lambda: w_up.at[:, cols], lambda: up_tiles.at[t % 2])
            load(("down", t), lambda: w_down.at[cols, :], lambda: down_tiles.at[t % 2])

        def mix(w_in_v, table_v, table_tv):
            kernel = mixed_v
            load("taps", raw_taps, running.at[0:half, :])
            load("tokens", tokens, lambda: active.at[0])
            load("w_in", w_in, w_in_v)
            load("table", table, table_v)
            load("table_t", table_t, table_tv)
            load("w_out", w_out, w_out_v)
            load_tile(0)
            load("cot", cotangent, cot)

            loads["taps"].wait()

            def squash_step(index, carry):
                rows = pl.ds(pl.multiple_of(index * 128, 128), 128)
                raw = running[rows, :]
                taps_held[pl.ds(pl.multiple_of(place.x * half + index * 128, 128), 128), :] = (
                    raw - jnp.clip(raw, -shrink_level, shrink_level)
                ).astype(jnp.bfloat16)
                return carry

            lax.fori_loop(0, half // 128, squash_step, 0)
            pl.semaphore_wait(barrier, len(partners))
            share_copy(0).start()
            loads["tokens"].wait()
            loads["w_in"].wait()

            def project_step(index, carry):
                rows = rows_of(index)
                unit, _ = norm_of(active[0, rows, :].astype(jnp.float32))
                low = (unit * ln1_gain[...][None, :] + ln1_shift[...][None, :]).astype(jnp.bfloat16)
                normed_v[:, rows] = low.T
                active[1, rows, :] = dot_nn(low, w_in_v[:, 0:feat]).astype(jnp.bfloat16)
                gate_v[rows, :] = dot_nn(low, w_in_v[:, feat:]).astype(jnp.bfloat16)
                return carry

            unrolled(0, row_steps, project_step, 0)
            share_copy(0).wait()
            share_copy(1).start()
            loads["table"].wait()

            def signal_wave_step(index, carry):
                rows = rows_of(index)
                for which in range(2):
                    waves[which, rows, :] = dot_nn(
                        table_v[rows, :], active[1, which * half : (which + 1) * half, :]
                    ).astype(jnp.bfloat16)
                return carry

            unrolled(0, row_steps, signal_wave_step, 0)
            share_copy(1).wait()
            pool_rows = 128
            for index in range(tok_count // pool_rows):
                at = index * pool_rows
                first, last = max(at - 16, 0), min(at + pool_rows + 16, tok_count)
                around = taps_held[first:last, :].astype(jnp.float32)
                if at == 0:
                    around = jnp.concatenate([jnp.zeros((16, feat), jnp.float32), around], axis=0)
                if last == tok_count:
                    around = jnp.concatenate([around, jnp.zeros((16, feat), jnp.float32)], axis=0)
                kernel[at : at + pool_rows, :] = (
                    (around[15 : 15 + pool_rows] + around[16 : 16 + pool_rows] + around[17 : 17 + pool_rows])
                    / 3.0
                ).astype(jnp.bfloat16)

            def spread_step(index, carry):
                down, across = index // (feat // 256), index % (feat // 256)
                real = pl.ds(pl.multiple_of(down * 256, 256), 256)
                imag = pl.ds(pl.multiple_of(half + down * 256, 256), 256)
                cols = pl.ds(pl.multiple_of(across * 256, 256), 256)
                low_r = dot_nn(table_v[real, :], kernel[0:half, cols])
                low_i = dot_nn(table_v[imag, :], kernel[0:half, cols])
                high_r = dot_nn(table_v[real, :], kernel[half:, cols])
                high_i = dot_nn(table_v[imag, :], kernel[half:, cols])
                odd = lax.broadcasted_iota(jnp.int32, (256, 1), 0) % 2
                parity = (1 - 2 * odd).astype(jnp.float32)
                cross_r = long * (high_r - parity * low_i)
                cross_i = long * (high_i + parity * low_r)
                kernels[0, real, cols] = low_r.astype(jnp.bfloat16)
                kernels[0, imag, cols] = low_i.astype(jnp.bfloat16)
                kernels[1, real, cols] = cross_r.astype(jnp.bfloat16)
                kernels[1, imag, cols] = cross_i.astype(jnp.bfloat16)
                head_r = waves[0, real, cols].astype(jnp.float32)
                head_i = waves[0, imag, cols].astype(jnp.float32)
                tail_r = waves[1, real, cols].astype(jnp.float32)
                tail_i = waves[1, imag, cols].astype(jnp.float32)
                scale = 1.0 / half
                active[2, real, cols] = ((low_r * head_r - low_i * head_i) * scale).astype(jnp.bfloat16)
                active[2, imag, cols] = ((low_r * head_i + low_i * head_r) * scale).astype(jnp.bfloat16)
                active[3, real, cols] = (
                    (low_r * tail_r - low_i * tail_i + cross_r * head_r - cross_i * head_i) * scale
                ).astype(jnp.bfloat16)
                active[3, imag, cols] = (
                    (low_r * tail_i + low_i * tail_r + cross_r * head_i + cross_i * head_r) * scale
                ).astype(jnp.bfloat16)
                return carry

            lax.fori_loop(0, half // 256 * (feat // 256), spread_step, 0)
            loads["table_t"].wait()
            loads["w_out"].wait()

            def residual_step(index, carry):
                rows = rows_of(index)
                part_steps = half // step_rows
                which = index // part_steps
                of_part = pl.ds(index % part_steps * step_rows, step_rows)
                mixed = dot_nn(table_tv[of_part, :], active[2 + which])
                mixed_v[rows, :] = mixed.astype(jnp.bfloat16)
                branch = (mixed * gate_v[rows, :].astype(jnp.float32)).astype(jnp.bfloat16)
                branch_v[:, rows] = branch.T
                left = active[0, rows, :].astype(jnp.float32) + dot_nn(branch, w_out_v[...])
                running[rows, :] = left
                stash_copy(index).start()
                unit, _ = norm_of(left)
                low = (unit * ln2_gain[...][None, :] + ln2_shift[...][None, :]).astype(jnp.bfloat16)
                normed_2[rows, :] = low
                normed_2t[:, rows] = low.T
                return carry

            unrolled(0, row_steps, residual_step, 0)
            pltpu.make_async_copy(running, residual, load_sems.at[STORES - 2]).wait()

        pl.run_scoped(
            mix,
            pltpu.VMEM((feat, 2 * feat), jnp.bfloat16),
            pltpu.VMEM((tok_count, half), jnp.bfloat16),
            pltpu.VMEM((half, tok_count), jnp.bfloat16),
        )

        def feed_forward(d_hidden):
            loads["cot"].wait()

            for t in range(planes):
                up_tile, down_tile = up_tiles.at[t % 2], down_tiles.at[t % 2]
                loads["up", t].wait()
                loads["down", t].wait()
                if t + 1 < planes:
                    load_tile(t + 1)

                def rows_step(index, carry):
                    rows = rows_of(index)
                    hidden = dot_nn(normed_2[rows, :], up_tile[...])
                    d_active = dot_nt(cot[rows, :], down_tile[...])
                    value, slope = gelu_both(hidden)
                    active[t, rows, :] = value.astype(jnp.bfloat16)
                    d_value = (d_active * slope).astype(jnp.bfloat16)
                    d_hidden[rows, :] = d_value
                    back = dot_nt(d_value, up_tile[...])
                    if t == 0:
                        running[rows, :] = back
                    else:
                        running[rows, :] += back
                    return carry

                unrolled(0, row_steps // 2, rows_step, 0)
                if t >= 1:
                    ups[t - 1].over_core()
                    downs[t - 1].over_core()
                if t >= 2:
                    ups[t - 2].over_second()
                    downs[t - 2].over_second()
                unrolled(row_steps // 2, row_steps, rows_step, 0)
                if t >= FLIGHTS:
                    ups[t - FLIGHTS].sent()
                    downs[t - FLIGHTS].sent()
                for part in range(2):
                    cols = tile // 2
                    store_shards(
                        downs[t], dot_tn(active[t, :, part * cols : (part + 1) * cols], cot[...]), part * cols
                    )
                downs[t].start()
                if t >= 1:
                    ups[t - 1].over_first()
                    downs[t - 1].over_first()
                for part in range(2):
                    rows = feat // 2
                    store_rows(
                        ups[t], dot_nn(normed_2t[part * rows : (part + 1) * rows, :], d_hidden[...]), part * rows
                    )
                ups[t].start()

        pl.run_scoped(feed_forward, pltpu.VMEM((tok_count, tile), jnp.bfloat16))

    pl.run_scoped(
        forward_back,
        pltpu.VMEM((tok_count, feat), jnp.bfloat16),
        pltpu.VMEM((feat, tok_count), jnp.bfloat16),
        pltpu.VMEM((2, feat, tile), jnp.bfloat16),
        pltpu.VMEM((2, tile, feat), jnp.bfloat16),
    )

    out_chunk = chunk(2 * planes, planes, 0)
    gate_chunk = chunk(2 * planes + 1, planes, 1)
    signal_chunk = chunk(2 * planes + 2, planes + 1, 0)
    taps = Taps(
        place, taps_held, (taps0, taps1, taps2, taps3), taps_sum, (taps_send, taps_recv),
        tok_count // (8 * planes),
    )
    sums = Sums(place, levels, sums_inbox, (sums_send, sums_recv))

    def backward(d_out, d_gate, d_mix, d_signal):
        def norm_two_back(left_v):
            load("left", residual.at[0 : tok_count // 2, :], left_v.at[0 : tok_count // 2, :])
            load("left end", residual.at[tok_count // 2 :, :], left_v.at[tok_count // 2 :, :])
            loads["left"].wait()

            def back_step(index, carry):
                gain_sum, shift_sum = carry
                rows = rows_of(index)
                left = left_v[rows, :]
                centered = left - jnp.mean(left, axis=-1, keepdims=True)
                inverse = lax.rsqrt(jnp.mean(centered * centered, axis=-1, keepdims=True) + eps_norm)
                unit = centered * inverse
                grad = running[rows, :]
                scaled = grad * ln2_gain[...][None, :]
                d_left = cot[rows, :].astype(jnp.float32) + inverse * (
                    scaled
                    - jnp.mean(scaled, axis=-1, keepdims=True)
                    - unit * jnp.mean(scaled * unit, axis=-1, keepdims=True)
                )
                running[rows, :] = d_left
                d_low = d_left.astype(jnp.bfloat16)
                d_out[rows, :] = d_low
                d_branch = dot_nt(d_low, w_out_v[...])
                d_mix[rows, :] = (
                    d_branch * gate_v[rows, :].astype(jnp.float32) * (1.0 / half)
                ).astype(jnp.bfloat16)
                d_gate[rows, :] = (d_branch * mixed_v[rows, :].astype(jnp.float32)).astype(jnp.bfloat16)
                return gain_sum + column_sums(grad * unit), shift_sum + column_sums(grad)

            zero = jnp.zeros((8, feat), jnp.float32)
            carry = unrolled(0, row_steps // 2, back_step, (zero, zero))
            ups[planes - 1].over_core()
            downs[planes - 1].over_core()
            ups[planes - 2].over_second()
            downs[planes - 2].over_second()
            loads["left end"].wait()
            gain_sum, shift_sum = unrolled(row_steps // 2, row_steps, back_step, carry)
            levels[0] = jnp.zeros(levels.shape[1:], jnp.float32)
            levels[0, 0:1, :] = jnp.sum(gain_sum, axis=0, keepdims=True)
            levels[0, 1:2, :] = jnp.sum(shift_sum, axis=0, keepdims=True)

        pl.run_scoped(norm_two_back, pltpu.VMEM((tok_count, feat), jnp.float32))


        def weight_rows(target, left_t, right):
            for part in range(2):
                rows = feat // 2
                store_rows(target, dot_nn(left_t[part * rows : (part + 1) * rows, :], right[...]), part * rows)
            target.start()

        def mixer_back(table_v, table_tv, d_kernel, d_taps):
            d_waves = waves
            load("table again", table, table_v)
            load("table_t again", table_t, table_tv)
            ups[planes - 3].sent()
            downs[planes - 3].sent()
            weight_rows(out_chunk, branch_v, d_out)
            ups[planes - 1].over_first()
            downs[planes - 1].over_first()
            loads["table again"].wait()
            loads["table_t again"].wait()
            wave_rows, wave_cols = 256, 256

            def wave_step(down, cols):
                real = pl.ds(pl.multiple_of(down * wave_rows, wave_rows), wave_rows)
                imag = pl.ds(pl.multiple_of(half + down * wave_rows, wave_rows), wave_rows)
                first_r = dot_nn(table_v[real, :], d_mix[0:half, cols])
                first_i = dot_nn(table_v[imag, :], d_mix[0:half, cols])
                second_r = dot_nn(table_v[real, :], d_mix[half:, cols])
                second_i = dot_nn(table_v[imag, :], d_mix[half:, cols])

                def wide(ref, which, rows):
                    return ref[which, rows, cols].astype(jnp.float32)

                def keep(ref, which, rows, values):
                    at = cols if ref.shape[2] == feat else slice(None)
                    ref[which, rows, at] = values.astype(jnp.bfloat16)

                low_r, low_i = wide(kernels, 0, real), wide(kernels, 0, imag)
                cross_r, cross_i = wide(kernels, 1, real), wide(kernels, 1, imag)
                head_r, head_i = wide(waves, 0, real), wide(waves, 0, imag)
                tail_r, tail_i = wide(waves, 1, real), wide(waves, 1, imag)
                keep(d_waves, 0, real, low_r * first_r + low_i * first_i + cross_r * second_r + cross_i * second_i)
                keep(d_waves, 0, imag, low_r * first_i - low_i * first_r + cross_r * second_i - cross_i * second_r)
                keep(d_waves, 1, real, low_r * second_r + low_i * second_i)
                keep(d_waves, 1, imag, low_r * second_i - low_i * second_r)
                far_r = (head_r * second_r + head_i * second_i) * long
                far_i = (head_r * second_i - head_i * second_r) * long
                odd = lax.broadcasted_iota(jnp.int32, (wave_rows, 1), 0) % 2
                parity = (1 - 2 * odd).astype(jnp.float32)
                keep(d_kernel, 1, real, far_r)
                keep(d_kernel, 1, imag, far_i)
                keep(
                    d_kernel,
                    0,
                    real,
                    head_r * first_r + head_i * first_i + tail_r * second_r + tail_i * second_i + parity * far_i,
                )
                keep(
                    d_kernel,
                    0,
                    imag,
                    head_r * first_i - head_i * first_r + tail_r * second_i - tail_i * second_r - parity * far_r,
                )

            pad = 8
            d_taps[0:pad, :] = jnp.zeros((pad, wave_cols), jnp.float32)
            d_taps[pad + tok_count :, :] = jnp.zeros((pad, wave_cols), jnp.float32)
            pool_rows = 128

            def column_step(across, carry):
                cols = pl.ds(pl.multiple_of(across * wave_cols, wave_cols), wave_cols)
                for down in range(half // wave_rows):
                    wave_step(down, cols)
                for which in range(2):
                    d_taps[pad + which * half : pad + (which + 1) * half, :] = dot_nn(table_tv[...], d_kernel[which])
                for index in range(tok_count // pool_rows):
                    at = pad + index * pool_rows
                    taps_held[at - pad : at - pad + pool_rows, cols] = (
                        (
                            d_taps[at - 1 : at - 1 + pool_rows, :]
                            + d_taps[at : at + pool_rows, :]
                            + d_taps[at + 1 : at + 1 + pool_rows, :]
                        )
                        / 3.0
                    ).astype(jnp.bfloat16)
                return carry

            lax.fori_loop(0, feat // wave_cols, column_step, 0)
            taps.start()
            ups[planes - 1].over_second()
            downs[planes - 1].over_second()
            out_chunk.over_core()
            for which in range(2):

                def signal_step(index, carry):
                    at = index * step_rows
                    d_signal[pl.ds(which * half + at, step_rows), :] = dot_nn(
                        table_tv[pl.ds(at, step_rows), :], d_waves[which]
                    ).astype(jnp.bfloat16)
                    return carry

                unrolled(0, half // step_rows, signal_step, 0)

        pl.run_scoped(
            mixer_back,
            pltpu.VMEM((tok_count, half), jnp.bfloat16),
            pltpu.VMEM((half, tok_count), jnp.bfloat16),
            pltpu.VMEM((2, tok_count, 256), jnp.bfloat16),
            pltpu.VMEM((tok_count + 16, 256), jnp.float32),
        )

        taps.over_core()
        ups[planes - 2].sent()
        weight_rows(signal_chunk, normed_v, d_signal)
        out_chunk.over_first()
        taps.over_x()
        weight_rows(gate_chunk, normed_v, d_gate)
        out_chunk.over_second()
        signal_chunk.over_core()
        taps.over_y()

        def finish(w_in_v, left_v):
            def down_again(t):
                return (waves if t < 2 else kernels).at[t % 2, 0:tile, :]

            def load_again(t):
                rows = pl.ds(t * tile, tile)
                load(("again", t), lambda: w_down.at[rows, :], lambda: down_again(t))

            load("w_in again", w_in, w_in_v)
            load("tokens again", tokens, gate_v)
            for t in range(planes):
                load_again(t)
            load("left again", residual, left_v)
            loads["tokens again"].wait()
            loads["w_in again"].wait()
            gate_chunk.over_core()

            def grad_copy(index):
                rows = rows_of(index)
                return pltpu.make_async_copy(
                    running.at[rows, :], input_grad.at[rows, :], load_sems.at[STORES + index]
                )

            def input_step(index, carry):
                gain_sum, shift_sum = carry
                rows = rows_of(index)
                d_normed = dot_nt(d_signal[rows, :], w_in_v[:, 0:feat]) + dot_nt(
                    d_gate[rows, :], w_in_v[:, feat:]
                )
                values = gate_v[rows, :].astype(jnp.float32)
                centered = values - jnp.mean(values, axis=-1, keepdims=True)
                inverse = lax.rsqrt(jnp.mean(centered * centered, axis=-1, keepdims=True) + eps_norm)
                unit = centered * inverse
                scaled = d_normed * ln1_gain[...][None, :]

                running[rows, :] = running[rows, :] + inverse * (
                    scaled
                    - jnp.mean(scaled, axis=-1, keepdims=True)
                    - unit * jnp.mean(scaled * unit, axis=-1, keepdims=True)
                )
                grad_copy(index).start()
                return gain_sum + column_sums(d_normed * unit), shift_sum + column_sums(d_normed)

            zero = jnp.zeros((8, feat), jnp.float32)
            carry = unrolled(0, row_steps // 2, input_step, (zero, zero))
            signal_chunk.over_first()
            taps.over_planes()
            gain_sum, shift_sum = unrolled(row_steps // 2, row_steps, input_step, carry)
            levels[0, 2:3, :] = jnp.sum(gain_sum, axis=0, keepdims=True)
            levels[0, 3:4, :] = jnp.sum(shift_sum, axis=0, keepdims=True)
            sums.start()
            gate_chunk.over_first()
            signal_chunk.over_second()
            taps.back_y()
            for t in range(planes):
                loads["again", t].wait()
            loads["left again"].wait()

            def out_copy(index):
                rows = rows_of(index)
                return pltpu.make_async_copy(
                    mixed_v.at[rows, :], block_out.at[rows, :], load_sems.at[STORES + row_steps + index]
                )

            def out_step(index, carry):
                rows = rows_of(index)
                total = left_v[rows, :]
                for t in range(planes):
                    total = total + dot_nn(active[t, rows, :], down_again(t)[...])

                mixed_v[rows, :] = total.astype(jnp.bfloat16)
                out_copy(index).start()
                return carry

            unrolled(0, 1, out_step, 0)
            sums.over(0)
            gate_chunk.over_second()
            unrolled(1, 2, out_step, 0)
            sums.over(1)
            taps.back_core()
            unrolled(2, 3, out_step, 0)
            sums.over(2)
            unrolled(3, row_steps, out_step, 0)
            for index in range(row_steps):
                grad_copy(index).wait()
                out_copy(index).wait()

        pl.run_scoped(
            finish,
            pltpu.VMEM((feat, 2 * feat), jnp.bfloat16),
            pltpu.VMEM((tok_count, feat), jnp.float32),
        )

    pl.run_scoped(backward, *[pltpu.VMEM((tok_count, feat), jnp.bfloat16)] * 4)

    def own_rows(target):
        target.arrived()
        return load_rows(target.total(0), feat)

    for t in range(planes):
        w_up_grad[:, t * tile : (t + 1) * tile] = own_rows(ups[t])
    w_out_grad[...] = own_rows(out_chunk)
    w_in_grad[:, 0:feat] = own_rows(signal_chunk)
    w_in_grad[:, feat:] = own_rows(gate_chunk)
    for t in range(planes):

        @pl.when(place.z == t)
        def _():
            downs[t].arrived()
            for index in range(planes):
                block = downs[t].total(index)
                for sub in range(6):
                    for first, line, at, count in tile_runs(sub, feat):
                        if line == index:
                            w_down_grad[16 * sub : 16 * sub + 16, 128 * first : 128 * (first + count)] = block[
                                :, 128 * at : 128 * (at + count)
                            ]

    sums_out[...] = sums.finish()
    taps.finish()
    taps_store = pltpu.make_async_copy(taps_sum, taps_out, load_sems.at[STORES - 1])
    taps_store.start()
    for one in (downs[planes - 2], ups[planes - 1], downs[planes - 1], out_chunk, gate_chunk, signal_chunk):
        one.sent()
    taps_store.wait()


def linked_block(
    planes,
    tokens,
    lengths,
    raw_taps,
    ln1_gain,
    ln1_shift,
    w_in,
    w_out,
    ln2_gain,
    ln2_shift,
    w_up,
    w_down,
    cotangent,
):
    tok_count, feat = tokens.shape
    half = tok_count // 2
    tile = w_up.shape[1] // planes
    table = jnp.asarray(wave_table(half), jnp.bfloat16)
    table_t = jnp.asarray(wave_table(half).T, jnp.bfloat16)
    shares = 8 * planes
    rows = feat // shares
    block = (16, 128 * PART)
    chunks = 2 * planes + 3
    bf16, f32 = jnp.bfloat16, jnp.float32
    whole = pl.BlockSpec(memory_space=pl.ANY)
    near = pl.BlockSpec(memory_space=pltpu.VMEM)
    results = pl.pallas_call(
        functools.partial(block_kernel, planes),
        out_shape=(
            jax.ShapeDtypeStruct((tok_count, feat), bf16),
            jax.ShapeDtypeStruct((tok_count, feat), f32),
            jax.ShapeDtypeStruct((half, feat), bf16),
            jax.ShapeDtypeStruct((tok_count, feat), f32),
            jax.ShapeDtypeStruct((8, feat), f32),
            jax.ShapeDtypeStruct((rows, 2 * feat), f32),
            jax.ShapeDtypeStruct((rows, feat), f32),
            jax.ShapeDtypeStruct((rows, planes * tile), f32),
            jax.ShapeDtypeStruct((tile // 8, feat), f32),
        ),
        in_specs=[pl.BlockSpec(memory_space=pltpu.SMEM)] + [whole] * 9 + [near] * 4,
        out_specs=(whole,) * 4 + (near,) * 5,
        scratch_shapes=[
            pltpu.VMEM((2 * FLIGHTS, shares) + block, bf16),
            pltpu.VMEM((4, 4 * planes) + block, bf16),
            pltpu.VMEM((4, 2 * planes) + block, bf16),
            pltpu.VMEM((4, planes) + block, bf16),
            pltpu.VMEM((planes + 3, planes) + block, bf16),
            pltpu.VMEM((planes, planes) + block, bf16),
            pltpu.VMEM((tok_count, feat), bf16),
            pltpu.VMEM((2, tok_count // 4, feat), bf16),
            pltpu.VMEM((tok_count // 4, feat), bf16),
            pltpu.VMEM((tok_count // 8, feat), bf16),
            pltpu.VMEM((planes - 1, tok_count // shares, feat), bf16),
            pltpu.VMEM((half, feat), bf16),
            pltpu.VMEM((4, 8, feat), f32),
            pltpu.VMEM((planes + 2, 8, feat), f32),
            pltpu.VMEM((tok_count, feat), bf16),
            pltpu.VMEM((planes, tok_count, tile), bf16),
            pltpu.VMEM((tok_count, feat), f32),
            pltpu.VMEM((feat, tok_count), bf16),
            pltpu.VMEM((feat, tok_count), bf16),
            pltpu.VMEM((feat, feat), bf16),
            pltpu.VMEM((tok_count, feat), bf16),
            pltpu.VMEM((tok_count, feat), bf16),
            pltpu.VMEM((2, tok_count, feat), bf16),
            pltpu.VMEM((2, tok_count, feat), bf16),
            pltpu.SemaphoreType.DMA((chunks, planes + 2)),
            pltpu.SemaphoreType.DMA((chunks, planes + 2)),
            pltpu.SemaphoreType.DMA((2 * planes + 4,)),
            pltpu.SemaphoreType.DMA((2 * planes + 4,)),
            pltpu.SemaphoreType.DMA((planes + 2,)),
            pltpu.SemaphoreType.DMA((planes + 2,)),
            pltpu.SemaphoreType.DMA((2,)),
            pltpu.SemaphoreType.DMA((2,)),
            pltpu.SemaphoreType.DMA((STORES + 2 * tok_count // 256,)),
        ],
        compiler_params=pltpu.CompilerParams(
            collective_id=1, has_side_effects=True, vmem_limit_bytes=VMEM_BYTES
        ),
        cost_estimate=pl.CostEstimate(
            flops=2 * tok_count * feat * (5 * w_up.shape[1] + 9 * feat),
            bytes_accessed=40 * tok_count * feat,
            transcendentals=tok_count * w_up.shape[1],
        ),
    )(
        lengths,
        tokens,
        cotangent,
        raw_taps,
        w_in,
        w_out,
        w_up,
        w_down,
        table,
        table_t,
        ln1_gain,
        ln1_shift,
        ln2_gain,
        ln2_shift,
    )
    block_out, input_grad, taps_sum, _, sums, w_in_grad, w_out_grad, w_up_grad, w_down_grad = results
    raw_grad = taps_sum.astype(f32) * (jnp.abs(raw_taps) > shrink_level).astype(f32)
    share = lax.axis_index("wide") * 2 + lax.axis_index("narrow")
    mine = lax.dynamic_slice(sums, (0, share * rows), (8, rows))
    return (
        block_out,
        input_grad,
        raw_grad,
        mine[2],
        mine[3],
        w_in_grad,
        w_out_grad,
        mine[0],
        mine[1],
        w_up_grad,
        w_down_grad,
    )


def solution(mesh):
    spread = P(("wide", "narrow"))
    rows = P(("wide", "narrow"), None)
    placed = (rows, spread, P("narrow", None)) + (P(),) * 8 + (rows,)
    wide, narrow = mesh.shape["wide"], mesh.shape["narrow"]

    def block(tokens, lengths, raw_taps, *others):
        fits = (
            narrow == 2
            and wide == 4 * 4
            and lengths.shape[0] == 1
            and raw_taps.shape[0] * 2 == tokens.shape[0]
            and tokens.shape[1] == 24 * wide * narrow
            and others[-2].shape[0] == 96 * wide * narrow
            and tokens.shape[0] % 512 == 0
        )
        if fits:
            return linked_block(wide // 4, tokens, lengths, raw_taps, *others)
        return local(tokens, lengths, raw_taps, *others)

    return jax.shard_map(
        block,
        mesh=mesh,
        in_specs=placed,
        out_specs=(rows, rows, P("narrow", None), spread, spread, rows, rows, spread, spread, rows, rows),
        check_vma=False,
    )
```

```python
import functools

import jax
import jax.numpy as jnp
import numpy as np
from jax import lax
from jax.experimental import pallas as pl
from jax.experimental.pallas import tpu as pltpu
from jax.sharding import PartitionSpec as P

shrink_level = 0.003
eps_norm = 1e-05


def wave_table(half):
    period = 4 * half
    phase = (np.outer(2 * np.arange(half) + 1, np.arange(half)) % period) * (2 * np.pi / period)
    return np.concatenate([np.cos(phase), -np.sin(phase)], axis=0)


def to_waves(table, block):
    return jnp.einsum("kn,nc->kc", table, block, preferred_element_type=jnp.float32)


def from_waves(table, waves):
    return jnp.einsum(
        "kn,kc->nc", table, waves.astype(jnp.bfloat16), preferred_element_type=jnp.float32
    )


def norm_parts(values):
    centered = values - jnp.mean(values, axis=-1, keepdims=True)
    inverse = lax.rsqrt(jnp.mean(centered * centered, axis=-1, keepdims=True) + eps_norm)
    return (centered * inverse, inverse)


def norm_back(upstream, unit_vals, inverse, gain_vec):
    scaled = upstream * gain_vec
    return inverse * (
        scaled
        - jnp.mean(scaled, axis=-1, keepdims=True)
        - unit_vals * jnp.mean(scaled * unit_vals, axis=-1, keepdims=True)
    )


def split(waves):
    half = waves.shape[0] // 2
    return waves[:half], waves[half:]


def times(left, right):
    lr, li = split(left)
    rr, ri = split(right)
    return jnp.concatenate([lr * rr - li * ri, lr * ri + li * rr], axis=0)


def conj_times(left, right):
    lr, li = split(left)
    rr, ri = split(right)
    return jnp.concatenate([lr * rr + li * ri, lr * ri - li * rr], axis=0)


def turned(waves, sign):
    wr, wi = split(waves)
    index = lax.broadcasted_iota(jnp.int32, (wr.shape[0], 1), 0)
    parity = sign * (1.0 - 2.0 * (index % 2).astype(jnp.float32))
    return jnp.concatenate([-parity * wi, parity * wr], axis=0)


def pool(values):
    padded = jnp.pad(values, ((1, 1), (0, 0)))
    return (padded[:-2] + padded[1:-1] + padded[2:]) / 3.0


def local(
    tokens,
    lengths,
    raw_taps,
    ln1_gain,
    ln1_shift,
    w_in,
    w_out,
    ln2_gain,
    ln2_shift,
    w_up,
    w_down,
    cotangent,
):
    tok_count, feat_width = tokens.shape
    row_count = lengths.shape[0]
    row_len = tok_count // row_count
    half = row_len // 2
    table = jnp.asarray(wave_table(half), jnp.bfloat16)
    scale = 1.0 / half
    long_rows = (lengths > half).astype(jnp.float32)

    squashed = raw_taps - jnp.clip(raw_taps, -shrink_level, shrink_level)
    gathered = lax.all_gather(squashed.astype(jnp.bfloat16), "narrow", axis=0, tiled=True)
    kernel = pool(gathered.astype(jnp.float32)).astype(jnp.bfloat16)
    kernel_low = to_waves(table, kernel[:half])
    kernel_cross = to_waves(table, kernel[half : 2 * half]) + turned(kernel_low, 1.0)

    inputs = tokens.astype(jnp.float32)
    unit_one, inverse_one = norm_parts(inputs)
    normed = (unit_one * ln1_gain + ln1_shift).astype(jnp.bfloat16)
    projected = jnp.dot(normed, w_in, preferred_element_type=jnp.float32)
    signal = projected[:, :feat_width].astype(jnp.bfloat16)
    gate_vals = projected[:, feat_width:]
    signal_waves = []
    mixed = []
    for row in range(row_count):
        first = to_waves(table, signal[row * row_len : row * row_len + half])
        second = to_waves(table, signal[row * row_len + half : (row + 1) * row_len])
        signal_waves.append((first, second))
        mixed.append(from_waves(table, times(first, kernel_low) * scale))
        mixed.append(
            from_waves(
                table,
                (times(second, kernel_low) + long_rows[row] * times(first, kernel_cross)) * scale,
            )
        )
    mixed = jnp.concatenate(mixed, axis=0)
    branch = (mixed * gate_vals).astype(jnp.bfloat16)
    residual = inputs + jnp.dot(branch, w_out, preferred_element_type=jnp.float32)
    unit_two, inverse_two = norm_parts(residual)
    normed2 = (unit_two * ln2_gain + ln2_shift).astype(jnp.bfloat16)
    hidden = jnp.dot(normed2, w_up, preferred_element_type=jnp.float32)
    active = jax.nn.gelu(hidden).astype(jnp.bfloat16)
    block_out = (residual + jnp.dot(active, w_down, preferred_element_type=jnp.float32)).astype(
        jnp.bfloat16
    )
    w_down_grad = jnp.einsum("tf,td->fd", active, cotangent, preferred_element_type=jnp.float32)
    d_active = jnp.einsum("td,fd->tf", cotangent, w_down, preferred_element_type=jnp.float32)
    gelu_pull = jax.vjp(jax.nn.gelu, hidden)[1]
    d_hidden = gelu_pull(d_active)[0].astype(jnp.bfloat16)
    w_up_grad = jnp.einsum("td,tf->df", normed2, d_hidden, preferred_element_type=jnp.float32)
    d_normed2 = jnp.einsum("tf,df->td", d_hidden, w_up, preferred_element_type=jnp.float32)
    ln2_gain_grad = jnp.sum(d_normed2 * unit_two, axis=0)
    ln2_shift_grad = jnp.sum(d_normed2, axis=0)
    d_residual = cotangent.astype(jnp.float32) + norm_back(
        d_normed2, unit_two, inverse_two, ln2_gain
    )
    d_outproj = d_residual.astype(jnp.bfloat16)
    w_out_grad = jnp.einsum("td,te->de", branch, d_outproj, preferred_element_type=jnp.float32)
    d_branch = jnp.einsum("te,de->td", d_outproj, w_out, preferred_element_type=jnp.float32)
    d_mixed = (d_branch * gate_vals).astype(jnp.bfloat16)
    d_gate = d_branch * mixed
    d_signal = []
    low_grad = 0.0
    cross_grad = 0.0
    for row in range(row_count):
        first, second = signal_waves[row]
        d_first = to_waves(table, d_mixed[row * row_len : row * row_len + half]) * scale
        d_second = to_waves(table, d_mixed[row * row_len + half : (row + 1) * row_len]) * scale
        d_cross = d_second * long_rows[row]
        d_signal.append(
            from_waves(table, conj_times(kernel_low, d_first) + conj_times(kernel_cross, d_cross))
        )
        d_signal.append(from_waves(table, conj_times(kernel_low, d_second)))
        low_grad = low_grad + conj_times(first, d_first) + conj_times(second, d_second)
        cross_grad = cross_grad + conj_times(first, d_cross)
    low_grad = low_grad + turned(cross_grad, -1.0)
    d_kernel = jnp.concatenate([from_waves(table, low_grad), from_waves(table, cross_grad)], axis=0)
    d_signal = jnp.concatenate(d_signal, axis=0)
    d_projected = jnp.concatenate([d_signal, d_gate], axis=1).astype(jnp.bfloat16)
    w_in_grad = jnp.einsum("td,te->de", normed, d_projected, preferred_element_type=jnp.float32)
    d_normed = jnp.einsum("te,de->td", d_projected, w_in, preferred_element_type=jnp.float32)
    ln1_gain_grad = jnp.sum(d_normed * unit_one, axis=0)
    ln1_shift_grad = jnp.sum(d_normed, axis=0)
    input_grad = d_residual + norm_back(d_normed, unit_one, inverse_one, ln1_gain)

    shares = lax.psum_scatter(
        pool(d_kernel).astype(jnp.bfloat16), "narrow", scatter_dimension=0, tiled=True
    )
    summed = lax.psum(shares, "wide").astype(jnp.float32)
    raw_grad = summed * (jnp.abs(raw_taps) > shrink_level).astype(jnp.float32)

    def scatter(values):
        return lax.psum_scatter(
            values.astype(jnp.bfloat16), ("wide", "narrow"), scatter_dimension=0, tiled=True
        ).astype(jnp.float32)

    def scatter_wide(values):
        return lax.psum_scatter(values, ("wide", "narrow"), scatter_dimension=0, tiled=True)

    return (
        block_out,
        input_grad,
        raw_grad,
        scatter_wide(ln1_gain_grad),
        scatter_wide(ln1_shift_grad),
        scatter(w_in_grad),
        scatter(w_out_grad),
        scatter_wide(ln2_gain_grad),
        scatter_wide(ln2_shift_grad),
        scatter(w_up_grad),
        scatter(w_down_grad),
    )


MESH = pl.DeviceIdType.MESH
PART = 9
STORES = 30
VMEM_BYTES = 60 * 2**20
FLIGHTS = 3


def dot_nn(left, right):
    return lax.dot_general(left, right, (((1,), (0,)), ((), ())), preferred_element_type=jnp.float32)


def dot_nt(left, right):
    return lax.dot_general(left, right, (((1,), (1,)), ((), ())), preferred_element_type=jnp.float32)


def dot_tn(left, right):
    return lax.dot_general(left, right, (((0,), (0,)), ((), ())), preferred_element_type=jnp.float32)


def gelu_both(hidden):
    inner = 0.7978845608028654
    cubic = inner * 0.044715
    square = hidden * hidden
    bent = jnp.tanh(hidden * (inner + cubic * square))
    share = 0.5 + 0.5 * bent
    slope = share + (0.5 * hidden) * (1.0 - bent * bent) * (inner + (3.0 * cubic) * square)
    return hidden * share, slope


def column_sums(values):
    rows, width = values.shape
    return jnp.sum(values.reshape(rows // 8, 8, width), axis=0)


class Place:
    def __init__(self, planes):
        wide = lax.axis_index("wide")
        self.narrow = lax.axis_index("narrow")
        self.wide = wide
        self.core = wide % 2
        self.y = (wide // 2) % 2
        self.z = wide // 4
        self.x = self.narrow
        self.planes = planes
        self.sibling = (wide + 1 - 2 * self.core, self.narrow)
        self.next_x = (wide, 1 - self.narrow)
        self.next_y = (wide + 2 - 4 * self.y, self.narrow)

    def plane(self, step):
        other = (self.z + step) % self.planes
        return (self.wide + 4 * (other - self.z), self.narrow), other


class Chunk:
    def __init__(self, place, held, inbox, sems, x_first, target=None):
        self.place = place
        self.views = (held, inbox, sems)
        self.target = target
        self.first, self.second = (place.x, place.y) if x_first else (place.y, place.x)
        self.to_first, self.to_second = (
            (place.next_x, place.next_y) if x_first else (place.next_y, place.next_x)
        )
        self.x_first = x_first

    @property
    def held(self):
        ref, at = self.views[0]
        return ref.at[at]

    @property
    def inbox(self):
        return [ref if at is None else ref.at[at] for ref, at in self.views[1]]

    @property
    def sems(self):
        return [ref.at[at] for ref, at in self.views[2]]

    def slot(self, y, core, x):
        first, second = (x, y) if self.x_first else (y, x)
        return ((core * 2 + first) * 2 + second) * self.place.planes

    def copy(self, stage):
        planes, core = self.place.planes, self.place.core
        first, second = self.first, self.second
        start, count, device = (
            (4 * planes * (1 - core), 4 * planes, self.place.sibling),
            (4 * planes * core + 2 * planes * (1 - first), 2 * planes, self.to_first),
            (4 * planes * core + 2 * planes * first + planes * (1 - second), planes, self.to_second),
        )[stage]
        return pltpu.make_async_remote_copy(
            src_ref=self.held.at[pl.ds(start, count)],
            dst_ref=self.inbox[stage],
            send_sem=self.sems[0].at[stage],
            recv_sem=self.sems[1].at[stage],
            device_id=device,
            device_id_type=MESH,
        )

    def add(self, start, landing, count):
        def body(index, carry):
            at = start + index
            self.held[at] = (
                self.held[at].astype(jnp.float32) + landing[index].astype(jnp.float32)
            ).astype(self.held.dtype)
            return carry

        lax.fori_loop(0, count, body, 0)

    def start(self):
        self.copy(0).start()

    def over_core(self):
        planes = self.place.planes
        self.copy(0).wait()
        self.add(4 * planes * self.place.core, self.inbox[0], 4 * planes)
        self.copy(1).start()

    def over_first(self):
        planes = self.place.planes
        self.copy(1).wait()
        self.add(4 * planes * self.place.core + 2 * planes * self.first, self.inbox[1], 2 * planes)
        self.copy(2).start()

    def base(self):
        planes, place = self.place.planes, self.place
        return 4 * planes * place.core + 2 * planes * self.first + planes * self.second

    def plane_copy(self, step):
        device, other = self.place.plane(step)
        if self.target is None:
            return pltpu.make_async_remote_copy(
                src_ref=self.held.at[self.base() + other],
                dst_ref=self.inbox[3].at[step - 1],
                send_sem=self.sems[0].at[2 + step],
                recv_sem=self.sems[1].at[2 + step],
                device_id=device,
                device_id_type=MESH,
            )
        return pltpu.make_async_remote_copy(
            src_ref=self.held.at[pl.ds(self.base(), self.place.planes)],
            dst_ref=self.inbox[3].at[step - 1],
            send_sem=self.sems[0].at[2 + step],
            recv_sem=self.sems[1].at[2 + step],
            device_id=device,
            device_id_type=MESH,
        )

    def each_plane(self, act):
        for step in range(1, self.place.planes):
            if self.target is None:
                act(self.plane_copy(step))
            else:

                @pl.when((self.place.z + step) % self.place.planes == self.target)
                def _():
                    act(self.plane_copy(step))

    def over_second(self):
        self.copy(2).wait()
        planes = self.place.planes
        self.add(self.base(), self.inbox[2], planes)
        if self.target is None:
            self.inbox[3][planes - 1] = self.held[self.base() + self.place.z]
        else:

            @pl.when(self.place.z == self.target)
            def _():
                for index in range(planes):
                    self.inbox[3][planes - 1, index] = self.held[self.base() + index]

        self.each_plane(lambda copy: copy.start())

    def sent(self):
        self.each_plane(lambda copy: copy.wait_send())

    def arrived(self):
        for step in range(1, self.place.planes):
            self.plane_copy(step).wait_recv()

    def total(self, index):
        terms = [
            self.inbox[3][step] if self.target is None else self.inbox[3][step, index]
            for step in range(self.place.planes)
        ]
        return sum(term.astype(jnp.float32) for term in terms)


def store_rows(chunk, values, first_row):
    width = values.shape[1]
    for k in range(values.shape[0] // 24):
        shard = first_row // 24 + k
        z, y, core, x = shard // 8, shard // 4 % 2, shard // 2 % 2, shard % 2
        at = chunk.slot(y, core, x) + z
        block = values[24 * k : 24 * k + 24]
        rest = block[16:24]
        chunk.held[at, :, 0:width] = block[0:16].astype(jnp.bfloat16)
        chunk.held[at, :, width : width + width // 2] = jnp.concatenate(
            [rest[:, : width // 2], rest[:, width // 2 :]], axis=0
        ).astype(jnp.bfloat16)


def load_rows(block, width):
    rest = block[:, width:]
    return jnp.concatenate(
        [block[:, :width], jnp.concatenate([rest[0:8], rest[8:16]], axis=1)], axis=0
    )


def tile_runs(sub, width):
    tiles = width // 128
    runs, tile = [], 0
    while tile < tiles:
        line = sub * tiles + tile
        count = min(tiles - tile, PART - line % PART)
        runs.append((tile, line // PART, line % PART, count))
        tile += count
    return runs


def store_shards(chunk, values, first_row):
    width = values.shape[1]
    for k in range(values.shape[0] // 16):
        row = first_row + 16 * k
        shard, sub = row // 96, row % 96 // 16
        base = chunk.slot(shard // 4, shard // 2 % 2, shard % 2)
        for tile, block, at, count in tile_runs(sub, width):
            chunk.held[base + block, :, 128 * at : 128 * (at + count)] = values[
                16 * k : 16 * k + 16, 128 * tile : 128 * (tile + count)
            ].astype(jnp.bfloat16)


class Taps:
    def __init__(self, place, held, inbox, result, sems, index, rows, cols, x_first):
        self.place, self.held, self.inbox, self.result = place, held, inbox, result
        self.sems, self.index = sems, index
        self.rows = rows
        self.cols = cols
        self.x_first = x_first

    def part(self, x, core, y, plane, count):
        planes = self.place.planes
        return pl.ds((((x * 2 + core) * 2 + y) * planes + plane) * self.rows, count * self.rows)

    def add(self, target, landing):
        self.held[target, self.cols] = (
            self.held[target, self.cols].astype(jnp.float32) + landing[...].astype(jnp.float32)
        ).astype(self.held.dtype)

    def landing(self, level, first, count):
        return self.inbox[level].at[pl.ds(first * self.rows, count * self.rows), self.cols]

    def copy(self, kind, step=0):
        place, planes = self.place, self.place.planes
        x, core, y, z = place.x, place.core, place.y, place.z
        if kind == "core":
            source, landing = self.part(step, 1 - core, 0, 0, 2 * planes), self.landing(0, step * 2 * planes, 2 * planes)
            stage, device = step, place.sibling
        elif kind == "first" and self.x_first:
            source, landing = self.part(1 - x, core, 0, 0, 2 * planes), self.landing(1, 0, 2 * planes)
            stage, device = 2, place.next_x
        elif kind == "first":
            source, landing = self.part(step, core, 1 - y, 0, planes), self.landing(1, step * planes, planes)
            stage, device = 2 + step, place.next_y
        elif kind == "second":
            first = self.part(x, core, 1 - y, 0, planes) if self.x_first else self.part(1 - x, core, y, 0, planes)
            source, landing = first, self.landing(2, 0, planes)
            stage, device = 4, place.next_y if self.x_first else place.next_x
        elif kind == "plane":
            device, other = place.plane(step)
            source, landing = self.part(x, core, y, other, 1), self.landing(3, step - 1, 1)
            stage = 4 + step
        else:
            if kind == "back plane":
                mine, stage, device = (0, core, y, z, 1), 3 + planes + step, place.plane(step)[0]
            elif kind == "back y":
                mine, stage, device = (0, core, y, 0, planes), 3 + 2 * planes, place.next_y
            else:
                mine, stage, device = (0, core, 0, 0, 2 * planes), 4 + 2 * planes, place.sibling
            landing = self.result.at[self.part(*mine), self.cols]
        return pltpu.make_async_remote_copy(
            src_ref=landing if kind.startswith("back") else self.held.at[source, self.cols],
            dst_ref=landing,
            send_sem=self.sems[0].at[self.index, stage],
            recv_sem=self.sems[1].at[self.index, stage],
            device_id=device,
            device_id_type=MESH,
        )

    def start(self):
        for x in range(2):
            self.copy("core", x).start()

    def over_core(self):
        for x in range(2):
            self.copy("core", x).wait()
            self.add(
                self.part(x, self.place.core, 0, 0, 2 * self.place.planes),
                self.landing(0, x * 2 * self.place.planes, 2 * self.place.planes),
            )
        for step in range(1 if self.x_first else 2):
            self.copy("first", step).start()

    def over_first(self):
        place, planes = self.place, self.place.planes
        if self.x_first:
            self.copy("first").wait()
            self.add(self.part(place.x, place.core, 0, 0, 2 * planes), self.landing(1, 0, 2 * planes))
        else:
            for x in range(2):
                self.copy("first", x).wait()
                self.add(self.part(x, place.core, place.y, 0, planes), self.landing(1, x * planes, planes))
        self.copy("second").start()

    def over_second(self):
        place = self.place
        self.copy("second").wait()
        self.add(self.part(place.x, place.core, place.y, 0, place.planes), self.landing(2, 0, place.planes))
        for step in range(1, place.planes):
            self.copy("plane", step).start()

    def over_planes(self):
        place = self.place
        mine = self.part(place.x, place.core, place.y, place.z, 1)
        total = self.held[mine, self.cols].astype(jnp.float32)
        for step in range(1, place.planes):
            self.copy("plane", step).wait()
            total = total + self.landing(3, step - 1, 1)[...].astype(jnp.float32)
        self.result[self.part(0, place.core, place.y, place.z, 1), self.cols] = total.astype(self.result.dtype)
        for step in range(1, place.planes):
            self.copy("back plane", step).start()

    def back_y(self):
        for step in range(1, self.place.planes):
            self.copy("back plane", step).wait()
        self.copy("back y").start()

    def back_core(self):
        self.copy("back y").wait()
        self.copy("back core").start()

    def finish(self):
        self.copy("back core").wait()


class Sums:
    def __init__(self, place, levels, inbox, sems):
        self.place, self.levels, self.inbox, self.sems = place, levels, inbox, sems

    def copy(self, level, step=0):
        place = self.place
        device = (place.sibling, place.next_x, place.next_y)[level] if level < 3 else place.plane(step)[0]
        landing = level + max(step - 1, 0)
        return pltpu.make_async_remote_copy(
            src_ref=self.levels.at[level],
            dst_ref=self.inbox.at[landing],
            send_sem=self.sems[0].at[landing],
            recv_sem=self.sems[1].at[landing],
            device_id=device,
            device_id_type=MESH,
        )

    def start(self):
        self.copy(0).start()

    def over(self, level):
        self.copy(level).wait()
        self.levels[level + 1] = self.levels[level] + self.inbox[level]
        if level < 2:
            self.copy(level + 1).start()
        else:
            for step in range(1, self.place.planes):
                self.copy(3, step).start()

    def finish(self):
        total = self.levels[3]
        for step in range(1, self.place.planes):
            self.copy(3, step).wait()
            total = total + self.inbox[2 + step]
        return total


def block_kernel(
    planes,
    lengths,
    tokens, cotangent, raw_taps, w_in, w_out, w_up, w_down, table, table_t,
    ln1_gain, ln1_shift, ln2_gain, ln2_shift,
    block_out, input_grad, taps_out, residual, sums_out, w_in_grad, w_out_grad, w_up_grad, w_down_grad,
    held, inbox0, inbox1, inbox2, inbox_u, inbox_n, taps_held, taps0, taps1, taps2, taps3, taps_sum,
    levels, sums_inbox, cot, active, running, branch_v, normed_v, w_out_v,
    gate_v, mixed_v, waves, kernels,
    send_sems, recv_sems, taps_send, taps_recv, sums_send, sums_recv, share_send, share_recv, load_sems,
):
    tok_count, feat = cot.shape
    half = tok_count // 2
    tile = active.shape[2]
    step_rows = 256
    row_steps = tok_count // step_rows
    place = Place(planes)

    loads = {}

    class Load:
        def __init__(self, source, target):
            self.ends, self.at = (source, target), len(loads)

        def copy(self):
            source, target = (end() if callable(end) else end for end in self.ends)
            return pltpu.make_async_copy(source, target, load_sems.at[self.at])

        def wait(self):
            self.copy().wait()

    def load(name, source, target):
        loads[name] = Load(source, target)
        loads[name].copy().start()

    barrier = pltpu.get_barrier_semaphore()
    partners = [place.sibling, place.next_x, place.next_y] + [
        place.plane(step)[0] for step in range(1, planes)
    ]
    for partner in partners:
        pl.semaphore_signal(barrier, inc=1, device_id=partner, device_id_type=MESH)
    long = jnp.where(lengths[0] > half, 1.0, 0.0).astype(jnp.float32)

    def chunk(index, step, kind, target=None):
        at = step % FLIGHTS * 2 + kind
        ring = step % 2 * 2 + kind
        if target is None:
            far = (inbox_u, index // 2 if index < 2 * planes else index - planes)
        else:
            far = (inbox_n, None)
        return Chunk(
            place,
            (held, at),
            ((inbox0, ring), (inbox1, ring), (inbox2, ring), far),
            ((send_sems, index), (recv_sems, index)),
            kind == 0,
            target,
        )

    ups = [chunk(2 * t, t, 0) for t in range(planes)]
    downs = [chunk(2 * t + 1, t, 1, t) for t in range(planes)]

    def rows_of(index):
        return pl.ds(index * step_rows, step_rows)

    def unrolled(first, last, body, carry):
        for index in range(first, last):
            carry = body(index, carry)
        return carry

    def norm_of(values):
        centered = values - jnp.mean(values, axis=-1, keepdims=True)
        inverse = lax.rsqrt(jnp.mean(centered * centered, axis=-1, keepdims=True) + eps_norm)
        return centered * inverse, inverse

    def stash_copy(index):
        rows = rows_of(index)
        return pltpu.make_async_copy(running.at[rows, :], residual.at[rows, :], load_sems.at[STORES - 2])

    def share_copy(which):
        block = half // 2
        block_x = place.x if which == 0 else 1 - place.x
        rows = pl.ds(pl.multiple_of(block_x * half + place.core * block, block), block)
        return pltpu.make_async_remote_copy(
            src_ref=taps_held.at[rows, :],
            dst_ref=taps_held.at[rows, :],
            send_sem=share_send.at[which],
            recv_sem=share_recv.at[which],
            device_id=place.next_x if which == 0 else place.sibling,
            device_id_type=MESH,
        )

    def forward_back(normed_2, normed_2t, up_tiles, down_tiles):
        def load_tile(t):
            cols = pl.ds(t * tile, tile)
            load(("up", t), lambda: w_up.at[:, cols], lambda: up_tiles.at[t % 2])
            load(("down", t), lambda: w_down.at[cols, :], lambda: down_tiles.at[t % 2])

        def mix(w_in_v, table_v, table_tv):
            kernel = mixed_v
            load("taps", raw_taps, running.at[0:half, :])
            load("tokens", tokens, lambda: active.at[0])
            load("w_in", w_in, w_in_v)
            load("table", table, table_v)
            load("table_t", table_t, table_tv)
            load("w_out", w_out, w_out_v)
            load_tile(0)
            load("cot", cotangent, cot)

            loads["taps"].wait()

            def squash_step(index, carry):
                rows = pl.ds(pl.multiple_of(index * 128, 128), 128)
                raw = running[rows, :]
                taps_held[pl.ds(pl.multiple_of(place.x * half + index * 128, 128), 128), :] = (
                    raw - jnp.clip(raw, -shrink_level, shrink_level)
                ).astype(jnp.bfloat16)
                return carry

            lax.fori_loop(0, half // 128, squash_step, 0)
            pl.semaphore_wait(barrier, len(partners))
            share_copy(0).start()
            loads["tokens"].wait()
            loads["w_in"].wait()

            def project_step(index, carry):
                rows = rows_of(index)
                unit, _ = norm_of(active[0, rows, :].astype(jnp.float32))
                low = (unit * ln1_gain[...][None, :] + ln1_shift[...][None, :]).astype(jnp.bfloat16)
                normed_v[:, rows] = low.T
                active[1, rows, :] = dot_nn(low, w_in_v[:, 0:feat]).astype(jnp.bfloat16)
                gate_v[rows, :] = dot_nn(low, w_in_v[:, feat:]).astype(jnp.bfloat16)
                return carry

            unrolled(0, row_steps, project_step, 0)
            share_copy(0).wait()
            share_copy(1).start()
            loads["table"].wait()

            def signal_wave_step(index, carry):
                rows = rows_of(index)
                for which in range(2):
                    waves[which, rows, :] = dot_nn(
                        table_v[rows, :], active[1, which * half : (which + 1) * half, :]
                    ).astype(jnp.bfloat16)
                return carry

            unrolled(0, row_steps, signal_wave_step, 0)
            share_copy(1).wait()
            pool_rows = 128
            for index in range(tok_count // pool_rows):
                at = index * pool_rows
                first, last = max(at - 16, 0), min(at + pool_rows + 16, tok_count)
                around = taps_held[first:last, :].astype(jnp.float32)
                if at == 0:
                    around = jnp.concatenate([jnp.zeros((16, feat), jnp.float32), around], axis=0)
                if last == tok_count:
                    around = jnp.concatenate([around, jnp.zeros((16, feat), jnp.float32)], axis=0)
                kernel[at : at + pool_rows, :] = (
                    (around[15 : 15 + pool_rows] + around[16 : 16 + pool_rows] + around[17 : 17 + pool_rows])
                    / 3.0
                ).astype(jnp.bfloat16)

            def spread_step(index, carry):
                down, across = index // (feat // 256), index % (feat // 256)
                real, imag = pl.ds(down * 256, 256), pl.ds(half + down * 256, 256)
                cols = pl.ds(across * 256, 256)
                low_r = dot_nn(table_v[real, :], kernel[0:half, cols])
                low_i = dot_nn(table_v[imag, :], kernel[0:half, cols])
                high_r = dot_nn(table_v[real, :], kernel[half:, cols])
                high_i = dot_nn(table_v[imag, :], kernel[half:, cols])
                odd = lax.broadcasted_iota(jnp.int32, (256, 1), 0) % 2
                parity = (1 - 2 * odd).astype(jnp.float32)
                cross_r = long * (high_r - parity * low_i)
                cross_i = long * (high_i + parity * low_r)
                kernels[0, real, cols] = low_r.astype(jnp.bfloat16)
                kernels[0, imag, cols] = low_i.astype(jnp.bfloat16)
                kernels[1, real, cols] = cross_r.astype(jnp.bfloat16)
                kernels[1, imag, cols] = cross_i.astype(jnp.bfloat16)
                head_r = waves[0, real, cols].astype(jnp.float32)
                head_i = waves[0, imag, cols].astype(jnp.float32)
                tail_r = waves[1, real, cols].astype(jnp.float32)
                tail_i = waves[1, imag, cols].astype(jnp.float32)
                scale = 1.0 / half
                active[2, real, cols] = ((low_r * head_r - low_i * head_i) * scale).astype(jnp.bfloat16)
                active[2, imag, cols] = ((low_r * head_i + low_i * head_r) * scale).astype(jnp.bfloat16)
                active[3, real, cols] = (
                    (low_r * tail_r - low_i * tail_i + cross_r * head_r - cross_i * head_i) * scale
                ).astype(jnp.bfloat16)
                active[3, imag, cols] = (
                    (low_r * tail_i + low_i * tail_r + cross_r * head_i + cross_i * head_r) * scale
                ).astype(jnp.bfloat16)
                return carry

            unrolled(0, half // 256 * (feat // 256), spread_step, 0)
            loads["table_t"].wait()
            loads["w_out"].wait()

            def residual_step(index, carry):
                rows = rows_of(index)
                part_steps = half // step_rows
                which = index // part_steps
                of_part = pl.ds(index % part_steps * step_rows, step_rows)
                mixed = dot_nn(table_tv[of_part, :], active[2 + which])
                mixed_v[rows, :] = mixed.astype(jnp.bfloat16)
                branch = (mixed * gate_v[rows, :].astype(jnp.float32)).astype(jnp.bfloat16)
                branch_v[:, rows] = branch.T
                left = active[0, rows, :].astype(jnp.float32) + dot_nn(branch, w_out_v[...])
                running[rows, :] = left
                stash_copy(index).start()
                unit, _ = norm_of(left)
                low = (unit * ln2_gain[...][None, :] + ln2_shift[...][None, :]).astype(jnp.bfloat16)
                normed_2[rows, :] = low
                normed_2t[:, rows] = low.T
                return carry

            unrolled(0, row_steps, residual_step, 0)
            pltpu.make_async_copy(running, residual, load_sems.at[STORES - 2]).wait()

        pl.run_scoped(
            mix,
            pltpu.VMEM((feat, 2 * feat), jnp.bfloat16),
            pltpu.VMEM((tok_count, half), jnp.bfloat16),
            pltpu.VMEM((half, tok_count), jnp.bfloat16),
        )

        def feed_forward(d_hidden):
            loads["cot"].wait()

            for t in range(planes):
                up_tile, down_tile = up_tiles.at[t % 2], down_tiles.at[t % 2]
                loads["up", t].wait()
                loads["down", t].wait()
                if t + 1 < planes:
                    load_tile(t + 1)

                def rows_step(index, carry):
                    rows = rows_of(index)
                    hidden = dot_nn(normed_2[rows, :], up_tile[...])
                    d_active = dot_nt(cot[rows, :], down_tile[...])
                    value, slope = gelu_both(hidden)
                    active[t, rows, :] = value.astype(jnp.bfloat16)
                    d_value = (d_active * slope).astype(jnp.bfloat16)
                    d_hidden[rows, :] = d_value
                    back = dot_nt(d_value, up_tile[...])
                    if t == 0:
                        running[rows, :] = back
                    else:
                        running[rows, :] += back
                    return carry

                unrolled(0, row_steps // 2, rows_step, 0)
                if t >= 1:
                    ups[t - 1].over_core()
                    downs[t - 1].over_core()
                if t >= 2:
                    ups[t - 2].over_second()
                    downs[t - 2].over_second()
                unrolled(row_steps // 2, row_steps, rows_step, 0)
                if t >= FLIGHTS:
                    ups[t - FLIGHTS].sent()
                    downs[t - FLIGHTS].sent()
                for part in range(2):
                    cols = tile // 2
                    store_shards(
                        downs[t], dot_tn(active[t, :, part * cols : (part + 1) * cols], cot[...]), part * cols
                    )
                downs[t].start()
                if t >= 1:
                    ups[t - 1].over_first()
                    downs[t - 1].over_first()
                for part in range(2):
                    rows = feat // 2
                    store_rows(
                        ups[t], dot_nn(normed_2t[part * rows : (part + 1) * rows, :], d_hidden[...]), part * rows
                    )
                ups[t].start()

        pl.run_scoped(feed_forward, pltpu.VMEM((tok_count, tile), jnp.bfloat16))

    pl.run_scoped(
        forward_back,
        pltpu.VMEM((tok_count, feat), jnp.bfloat16),
        pltpu.VMEM((feat, tok_count), jnp.bfloat16),
        pltpu.VMEM((2, feat, tile), jnp.bfloat16),
        pltpu.VMEM((2, tile, feat), jnp.bfloat16),
    )

    out_chunk = chunk(2 * planes, planes, 0)
    gate_chunk = chunk(2 * planes + 1, planes, 1)
    signal_chunk = chunk(2 * planes + 2, planes + 1, 0)
    tap_cols = 256
    taps = [
        Taps(
            place, taps_held, (taps0, taps1, taps2, taps3), taps_sum, (taps_send, taps_recv), index,
            tok_count // (8 * planes), pl.ds(index * tap_cols, tap_cols), index % 2 == 0,
        )
        for index in range(feat // tap_cols)
    ]
    sums = Sums(place, levels, sums_inbox, (sums_send, sums_recv))

    def own_rows(target):
        target.arrived()
        return load_rows(target.total(0), feat)

    def own_down():
        for t in range(planes):

            @pl.when(place.z == t)
            def _():
                downs[t].arrived()
                for index in range(planes):
                    block = downs[t].total(index)
                    for sub in range(6):
                        for first, line, at, count in tile_runs(sub, feat):
                            if line == index:
                                w_down_grad[16 * sub : 16 * sub + 16, 128 * first : 128 * (first + count)] = block[
                                    :, 128 * at : 128 * (at + count)
                                ]

    def backward(d_out, d_gate, d_mix, d_signal):
        def norm_two_back(left_v):
            load("left", residual.at[0 : tok_count // 2, :], left_v.at[0 : tok_count // 2, :])
            load("left end", residual.at[tok_count // 2 :, :], left_v.at[tok_count // 2 :, :])
            loads["left"].wait()

            def back_step(index, carry):
                gain_sum, shift_sum = carry
                rows = rows_of(index)
                left = left_v[rows, :]
                centered = left - jnp.mean(left, axis=-1, keepdims=True)
                inverse = lax.rsqrt(jnp.mean(centered * centered, axis=-1, keepdims=True) + eps_norm)
                unit = centered * inverse
                grad = running[rows, :]
                scaled = grad * ln2_gain[...][None, :]
                d_left = cot[rows, :].astype(jnp.float32) + inverse * (
                    scaled
                    - jnp.mean(scaled, axis=-1, keepdims=True)
                    - unit * jnp.mean(scaled * unit, axis=-1, keepdims=True)
                )
                running[rows, :] = d_left
                d_low = d_left.astype(jnp.bfloat16)
                d_out[rows, :] = d_low
                d_branch = dot_nt(d_low, w_out_v[...])
                d_mix[rows, :] = (
                    d_branch * gate_v[rows, :].astype(jnp.float32) * (1.0 / half)
                ).astype(jnp.bfloat16)
                d_gate[rows, :] = (d_branch * mixed_v[rows, :].astype(jnp.float32)).astype(jnp.bfloat16)
                return gain_sum + column_sums(grad * unit), shift_sum + column_sums(grad)

            zero = jnp.zeros((8, feat), jnp.float32)
            carry = unrolled(0, row_steps // 2, back_step, (zero, zero))
            ups[planes - 1].over_core()
            downs[planes - 1].over_core()
            ups[planes - 2].over_second()
            downs[planes - 2].over_second()
            loads["left end"].wait()
            gain_sum, shift_sum = unrolled(row_steps // 2, row_steps, back_step, carry)
            levels[0] = jnp.zeros(levels.shape[1:], jnp.float32)
            levels[0, 0:1, :] = jnp.sum(gain_sum, axis=0, keepdims=True)
            levels[0, 1:2, :] = jnp.sum(shift_sum, axis=0, keepdims=True)

        pl.run_scoped(norm_two_back, pltpu.VMEM((tok_count, feat), jnp.float32))


        def weight_rows(target, left_t, right):
            for part in range(2):
                rows = feat // 2
                store_rows(target, dot_nn(left_t[part * rows : (part + 1) * rows, :], right[...]), part * rows)
            target.start()

        def mixer_back(table_v, table_tv, d_kernel, d_taps):
            d_waves = waves
            load("table again", table, table_v)
            load("table_t again", table_t, table_tv)
            downs[planes - 3].sent()
            weight_rows(gate_chunk, normed_v, d_gate)
            ups[planes - 1].over_first()
            downs[planes - 1].over_first()
            ups[planes - 3].sent()
            weight_rows(out_chunk, branch_v, d_out)
            loads["table again"].wait()
            loads["table_t again"].wait()
            wave_rows, wave_cols = 256, 256

            def wave_step(down, cols):
                real, imag = pl.ds(down * wave_rows, wave_rows), pl.ds(half + down * wave_rows, wave_rows)
                first_r = dot_nn(table_v[real, :], d_mix[0:half, cols])
                first_i = dot_nn(table_v[imag, :], d_mix[0:half, cols])
                second_r = dot_nn(table_v[real, :], d_mix[half:, cols])
                second_i = dot_nn(table_v[imag, :], d_mix[half:, cols])

                def wide(ref, which, rows):
                    return ref[which, rows, cols].astype(jnp.float32)

                def keep(ref, which, rows, values):
                    at = cols if ref.shape[2] == feat else slice(None)
                    ref[which, rows, at] = values.astype(jnp.bfloat16)

                low_r, low_i = wide(kernels, 0, real), wide(kernels, 0, imag)
                cross_r, cross_i = wide(kernels, 1, real), wide(kernels, 1, imag)
                head_r, head_i = wide(waves, 0, real), wide(waves, 0, imag)
                tail_r, tail_i = wide(waves, 1, real), wide(waves, 1, imag)
                keep(d_waves, 0, real, low_r * first_r + low_i * first_i + cross_r * second_r + cross_i * second_i)
                keep(d_waves, 0, imag, low_r * first_i - low_i * first_r + cross_r * second_i - cross_i * second_r)
                keep(d_waves, 1, real, low_r * second_r + low_i * second_i)
                keep(d_waves, 1, imag, low_r * second_i - low_i * second_r)
                far_r = (head_r * second_r + head_i * second_i) * long
                far_i = (head_r * second_i - head_i * second_r) * long
                odd = lax.broadcasted_iota(jnp.int32, (wave_rows, 1), 0) % 2
                parity = (1 - 2 * odd).astype(jnp.float32)
                keep(d_kernel, 1, real, far_r)
                keep(d_kernel, 1, imag, far_i)
                keep(
                    d_kernel,
                    0,
                    real,
                    head_r * first_r + head_i * first_i + tail_r * second_r + tail_i * second_i + parity * far_i,
                )
                keep(
                    d_kernel,
                    0,
                    imag,
                    head_r * first_i - head_i * first_r + tail_r * second_i - tail_i * second_r - parity * far_r,
                )

            pad = 8
            d_taps[0:pad, :] = jnp.zeros((pad, wave_cols), jnp.float32)
            d_taps[pad + tok_count :, :] = jnp.zeros((pad, wave_cols), jnp.float32)
            pool_rows = 128

            def column_step(across):
                cols = pl.ds(across * wave_cols, wave_cols)
                for down in range(half // wave_rows):
                    wave_step(down, cols)
                for which in range(2):
                    d_taps[pad + which * half : pad + (which + 1) * half, :] = dot_nn(table_tv[...], d_kernel[which])
                for index in range(tok_count // pool_rows):
                    at = pad + index * pool_rows
                    taps_held[at - pad : at - pad + pool_rows, cols] = (
                        (
                            d_taps[at - 1 : at - 1 + pool_rows, :]
                            + d_taps[at : at + pool_rows, :]
                            + d_taps[at + 1 : at + 1 + pool_rows, :]
                        )
                        / 3.0
                    ).astype(jnp.bfloat16)

            column_step(0)
            taps[0].start()
            ups[planes - 1].over_second()
            downs[planes - 1].over_second()
            gate_chunk.over_core()
            column_step(1)
            taps[1].start()
            taps[0].over_core()
            out_chunk.over_core()
            column_step(2)
            taps[2].start()
            taps[1].over_core()
            gate_chunk.over_first()
            taps[0].over_first()

            def signal_step(which, index):
                at = index * step_rows
                d_signal[which * half + at : which * half + at + step_rows, :] = dot_nn(
                    table_tv[at : at + step_rows, :], d_waves[which]
                ).astype(jnp.bfloat16)

            for index in range(half // step_rows):
                signal_step(0, index)
            taps[2].over_core()
            out_chunk.over_first()
            taps[0].over_second()
            for index in range(half // step_rows):
                signal_step(1, index)
            taps[1].over_first()

        pl.run_scoped(
            mixer_back,
            pltpu.VMEM((tok_count, half), jnp.bfloat16),
            pltpu.VMEM((half, tok_count), jnp.bfloat16),
            pltpu.VMEM((2, tok_count, 256), jnp.bfloat16),
            pltpu.VMEM((tok_count + 16, 256), jnp.float32),
        )

        ups[planes - 2].sent()
        weight_rows(signal_chunk, normed_v, d_signal)
        gate_chunk.over_second()
        taps[2].over_first()
        taps[1].over_second()
        taps[0].over_planes()

        def finish(w_in_v, left_v):
            def down_again(t):
                return (waves if t < 2 else kernels).at[t % 2, 0:tile, :]

            def load_again(t):
                rows = pl.ds(t * tile, tile)
                load(("again", t), lambda: w_down.at[rows, :], lambda: down_again(t))

            load("w_in again", w_in, w_in_v)
            load("tokens again", tokens, gate_v)
            for t in range(planes):
                load_again(t)
            load("left again", residual, left_v)
            loads["tokens again"].wait()
            loads["w_in again"].wait()

            def grad_copy(index):
                rows = rows_of(index)
                return pltpu.make_async_copy(
                    running.at[rows, :], input_grad.at[rows, :], load_sems.at[STORES + index]
                )

            def input_step(index, carry):
                gain_sum, shift_sum = carry
                rows = rows_of(index)
                d_normed = dot_nt(d_signal[rows, :], w_in_v[:, 0:feat]) + dot_nt(
                    d_gate[rows, :], w_in_v[:, feat:]
                )
                values = gate_v[rows, :].astype(jnp.float32)
                centered = values - jnp.mean(values, axis=-1, keepdims=True)
                inverse = lax.rsqrt(jnp.mean(centered * centered, axis=-1, keepdims=True) + eps_norm)
                unit = centered * inverse
                scaled = d_normed * ln1_gain[...][None, :]

                running[rows, :] = running[rows, :] + inverse * (
                    scaled
                    - jnp.mean(scaled, axis=-1, keepdims=True)
                    - unit * jnp.mean(scaled * unit, axis=-1, keepdims=True)
                )
                grad_copy(index).start()
                return gain_sum + column_sums(d_normed * unit), shift_sum + column_sums(d_normed)

            zero = jnp.zeros((8, feat), jnp.float32)
            carry = unrolled(0, 1, input_step, (zero, zero))
            signal_chunk.over_core()
            out_chunk.over_second()
            carry = unrolled(1, 2, input_step, carry)
            taps[2].over_second()
            taps[1].over_planes()
            taps[0].back_y()
            carry = unrolled(2, 3, input_step, carry)
            signal_chunk.over_first()
            gain_sum, shift_sum = unrolled(3, row_steps, input_step, carry)
            levels[0, 2:3, :] = jnp.sum(gain_sum, axis=0, keepdims=True)
            levels[0, 3:4, :] = jnp.sum(shift_sum, axis=0, keepdims=True)
            sums.start()
            taps[2].over_planes()
            taps[1].back_y()
            taps[0].back_core()
            for t in range(planes):
                loads["again", t].wait()
            loads["left again"].wait()

            def out_copy(index):
                rows = rows_of(index)
                return pltpu.make_async_copy(
                    mixed_v.at[rows, :], block_out.at[rows, :], load_sems.at[STORES + row_steps + index]
                )

            def out_step(index, carry):
                rows = rows_of(index)
                total = left_v[rows, :]
                for t in range(planes):
                    total = total + dot_nn(active[t, rows, :], down_again(t)[...])

                mixed_v[rows, :] = total.astype(jnp.bfloat16)
                out_copy(index).start()
                return carry

            unrolled(0, 1, out_step, 0)
            sums.over(0)
            signal_chunk.over_second()
            unrolled(1, 2, out_step, 0)
            sums.over(1)
            taps[2].back_y()
            taps[1].back_core()
            unrolled(2, 3, out_step, 0)
            sums.over(2)
            taps[2].back_core()
            for t in range(planes):
                w_up_grad[:, t * tile : (t + 1) * tile] = own_rows(ups[t])
            w_in_grad[:, feat:] = own_rows(gate_chunk)
            unrolled(3, row_steps, out_step, 0)
            w_out_grad[...] = own_rows(out_chunk)
            own_down()
            for index in range(row_steps):
                grad_copy(index).wait()
                out_copy(index).wait()

        pl.run_scoped(
            finish,
            pltpu.VMEM((feat, 2 * feat), jnp.bfloat16),
            pltpu.VMEM((tok_count, feat), jnp.float32),
        )

    pl.run_scoped(backward, *[pltpu.VMEM((tok_count, feat), jnp.bfloat16)] * 4)

    w_in_grad[:, 0:feat] = own_rows(signal_chunk)
    sums_out[...] = sums.finish()
    for part in taps:
        part.finish()
    taps_store = pltpu.make_async_copy(taps_sum, taps_out, load_sems.at[STORES - 1])
    taps_store.start()
    for one in (downs[planes - 2], ups[planes - 1], downs[planes - 1], out_chunk, gate_chunk, signal_chunk):
        one.sent()
    taps_store.wait()


def linked_block(
    planes,
    tokens,
    lengths,
    raw_taps,
    ln1_gain,
    ln1_shift,
    w_in,
    w_out,
    ln2_gain,
    ln2_shift,
    w_up,
    w_down,
    cotangent,
):
    tok_count, feat = tokens.shape
    half = tok_count // 2
    tile = w_up.shape[1] // planes
    table = jnp.asarray(wave_table(half), jnp.bfloat16)
    table_t = jnp.asarray(wave_table(half).T, jnp.bfloat16)
    shares = 8 * planes
    rows = feat // shares
    block = (16, 128 * PART)
    chunks = 2 * planes + 3
    bf16, f32 = jnp.bfloat16, jnp.float32
    whole = pl.BlockSpec(memory_space=pl.ANY)
    near = pl.BlockSpec(memory_space=pltpu.VMEM)
    results = pl.pallas_call(
        functools.partial(block_kernel, planes),
        out_shape=(
            jax.ShapeDtypeStruct((tok_count, feat), bf16),
            jax.ShapeDtypeStruct((tok_count, feat), f32),
            jax.ShapeDtypeStruct((half, feat), bf16),
            jax.ShapeDtypeStruct((tok_count, feat), f32),
            jax.ShapeDtypeStruct((8, feat), f32),
            jax.ShapeDtypeStruct((rows, 2 * feat), f32),
            jax.ShapeDtypeStruct((rows, feat), f32),
            jax.ShapeDtypeStruct((rows, planes * tile), f32),
            jax.ShapeDtypeStruct((tile // 8, feat), f32),
        ),
        in_specs=[pl.BlockSpec(memory_space=pltpu.SMEM)] + [whole] * 9 + [near] * 4,
        out_specs=(whole,) * 4 + (near,) * 5,
        scratch_shapes=[
            pltpu.VMEM((2 * FLIGHTS, shares) + block, bf16),
            pltpu.VMEM((4, 4 * planes) + block, bf16),
            pltpu.VMEM((4, 2 * planes) + block, bf16),
            pltpu.VMEM((4, planes) + block, bf16),
            pltpu.VMEM((planes + 3, planes) + block, bf16),
            pltpu.VMEM((planes, planes) + block, bf16),
            pltpu.VMEM((tok_count, feat), bf16),
            pltpu.VMEM((tok_count // 2, feat), bf16),
            pltpu.VMEM((tok_count // 4, feat), bf16),
            pltpu.VMEM((tok_count // 8, feat), bf16),
            pltpu.VMEM(((planes - 1) * (tok_count // shares), feat), bf16),
            pltpu.VMEM((half, feat), bf16),
            pltpu.VMEM((4, 8, feat), f32),
            pltpu.VMEM((planes + 2, 8, feat), f32),
            pltpu.VMEM((tok_count, feat), bf16),
            pltpu.VMEM((planes, tok_count, tile), bf16),
            pltpu.VMEM((tok_count, feat), f32),
            pltpu.VMEM((feat, tok_count), bf16),
            pltpu.VMEM((feat, tok_count), bf16),
            pltpu.VMEM((feat, feat), bf16),
            pltpu.VMEM((tok_count, feat), bf16),
            pltpu.VMEM((tok_count, feat), bf16),
            pltpu.VMEM((2, tok_count, feat), bf16),
            pltpu.VMEM((2, tok_count, feat), bf16),
            pltpu.SemaphoreType.DMA((chunks, planes + 2)),
            pltpu.SemaphoreType.DMA((chunks, planes + 2)),
            pltpu.SemaphoreType.DMA((feat // 256, 2 * planes + 5)),
            pltpu.SemaphoreType.DMA((feat // 256, 2 * planes + 5)),
            pltpu.SemaphoreType.DMA((planes + 2,)),
            pltpu.SemaphoreType.DMA((planes + 2,)),
            pltpu.SemaphoreType.DMA((2,)),
            pltpu.SemaphoreType.DMA((2,)),
            pltpu.SemaphoreType.DMA((STORES + 2 * tok_count // 256,)),
        ],
        compiler_params=pltpu.CompilerParams(
            collective_id=1, has_side_effects=True, vmem_limit_bytes=VMEM_BYTES
        ),
        cost_estimate=pl.CostEstimate(
            flops=2 * tok_count * feat * (5 * w_up.shape[1] + 9 * feat),
            bytes_accessed=40 * tok_count * feat,
            transcendentals=tok_count * w_up.shape[1],
        ),
    )(
        lengths,
        tokens,
        cotangent,
        raw_taps,
        w_in,
        w_out,
        w_up,
        w_down,
        table,
        table_t,
        ln1_gain,
        ln1_shift,
        ln2_gain,
        ln2_shift,
    )
    block_out, input_grad, taps_sum, _, sums, w_in_grad, w_out_grad, w_up_grad, w_down_grad = results
    raw_grad = taps_sum.astype(f32) * (jnp.abs(raw_taps) > shrink_level).astype(f32)
    share = lax.axis_index("wide") * 2 + lax.axis_index("narrow")
    mine = lax.dynamic_slice(sums, (0, share * rows), (8, rows))
    return (
        block_out,
        input_grad,
        raw_grad,
        mine[2],
        mine[3],
        w_in_grad,
        w_out_grad,
        mine[0],
        mine[1],
        w_up_grad,
        w_down_grad,
    )


def solution(mesh):
    spread = P(("wide", "narrow"))
    rows = P(("wide", "narrow"), None)
    placed = (rows, spread, P("narrow", None)) + (P(),) * 8 + (rows,)
    wide, narrow = mesh.shape["wide"], mesh.shape["narrow"]

    def block(tokens, lengths, raw_taps, *others):
        fits = (
            narrow == 2
            and wide == 4 * 4
            and lengths.shape[0] == 1
            and raw_taps.shape[0] * 2 == tokens.shape[0]
            and tokens.shape[1] == 24 * wide * narrow
            and others[-2].shape[0] == 96 * wide * narrow
            and tokens.shape[0] % 512 == 0
        )
        if fits:
            return linked_block(wide // 4, tokens, lengths, raw_taps, *others)
        return local(tokens, lengths, raw_taps, *others)

    return jax.shard_map(
        block,
        mesh=mesh,
        in_specs=placed,
        out_specs=(rows, rows, P("narrow", None), spread, spread, rows, rows, spread, spread, rows, rows),
        check_vma=False,
    )
```

```python
import functools

import jax
import jax.numpy as jnp
import numpy as np
from jax import lax
from jax.experimental import pallas as pl
from jax.experimental.pallas import tpu as pltpu
from jax.sharding import PartitionSpec as P

shrink_level = 0.003
eps_norm = 1e-05


def wave_table(half):
    period = 4 * half
    phase = (np.outer(2 * np.arange(half) + 1, np.arange(half)) % period) * (2 * np.pi / period)
    return np.concatenate([np.cos(phase), -np.sin(phase)], axis=0)


def to_waves(table, block):
    return jnp.einsum("kn,nc->kc", table, block, preferred_element_type=jnp.float32)


def from_waves(table, waves):
    return jnp.einsum(
        "kn,kc->nc", table, waves.astype(jnp.bfloat16), preferred_element_type=jnp.float32
    )


def norm_parts(values):
    centered = values - jnp.mean(values, axis=-1, keepdims=True)
    inverse = lax.rsqrt(jnp.mean(centered * centered, axis=-1, keepdims=True) + eps_norm)
    return (centered * inverse, inverse)


def norm_back(upstream, unit_vals, inverse, gain_vec):
    scaled = upstream * gain_vec
    return inverse * (
        scaled
        - jnp.mean(scaled, axis=-1, keepdims=True)
        - unit_vals * jnp.mean(scaled * unit_vals, axis=-1, keepdims=True)
    )


def split(waves):
    half = waves.shape[0] // 2
    return waves[:half], waves[half:]


def times(left, right):
    lr, li = split(left)
    rr, ri = split(right)
    return jnp.concatenate([lr * rr - li * ri, lr * ri + li * rr], axis=0)


def conj_times(left, right):
    lr, li = split(left)
    rr, ri = split(right)
    return jnp.concatenate([lr * rr + li * ri, lr * ri - li * rr], axis=0)


def turned(waves, sign):
    wr, wi = split(waves)
    index = lax.broadcasted_iota(jnp.int32, (wr.shape[0], 1), 0)
    parity = sign * (1.0 - 2.0 * (index % 2).astype(jnp.float32))
    return jnp.concatenate([-parity * wi, parity * wr], axis=0)


def pool(values):
    padded = jnp.pad(values, ((1, 1), (0, 0)))
    return (padded[:-2] + padded[1:-1] + padded[2:]) / 3.0


def local(
    tokens,
    lengths,
    raw_taps,
    ln1_gain,
    ln1_shift,
    w_in,
    w_out,
    ln2_gain,
    ln2_shift,
    w_up,
    w_down,
    cotangent,
):
    tok_count, feat_width = tokens.shape
    row_count = lengths.shape[0]
    row_len = tok_count // row_count
    half = row_len // 2
    table = jnp.asarray(wave_table(half), jnp.bfloat16)
    scale = 1.0 / half
    long_rows = (lengths > half).astype(jnp.float32)

    squashed = raw_taps - jnp.clip(raw_taps, -shrink_level, shrink_level)
    gathered = lax.all_gather(squashed.astype(jnp.bfloat16), "narrow", axis=0, tiled=True)
    kernel = pool(gathered.astype(jnp.float32)).astype(jnp.bfloat16)
    kernel_low = to_waves(table, kernel[:half])
    kernel_cross = to_waves(table, kernel[half : 2 * half]) + turned(kernel_low, 1.0)

    inputs = tokens.astype(jnp.float32)
    unit_one, inverse_one = norm_parts(inputs)
    normed = (unit_one * ln1_gain + ln1_shift).astype(jnp.bfloat16)
    projected = jnp.dot(normed, w_in, preferred_element_type=jnp.float32)
    signal = projected[:, :feat_width].astype(jnp.bfloat16)
    gate_vals = projected[:, feat_width:]
    signal_waves = []
    mixed = []
    for row in range(row_count):
        first = to_waves(table, signal[row * row_len : row * row_len + half])
        second = to_waves(table, signal[row * row_len + half : (row + 1) * row_len])
        signal_waves.append((first, second))
        mixed.append(from_waves(table, times(first, kernel_low) * scale))
        mixed.append(
            from_waves(
                table,
                (times(second, kernel_low) + long_rows[row] * times(first, kernel_cross)) * scale,
            )
        )
    mixed = jnp.concatenate(mixed, axis=0)
    branch = (mixed * gate_vals).astype(jnp.bfloat16)
    residual = inputs + jnp.dot(branch, w_out, preferred_element_type=jnp.float32)
    unit_two, inverse_two = norm_parts(residual)
    normed2 = (unit_two * ln2_gain + ln2_shift).astype(jnp.bfloat16)
    hidden = jnp.dot(normed2, w_up, preferred_element_type=jnp.float32)
    active = jax.nn.gelu(hidden).astype(jnp.bfloat16)
    block_out = (residual + jnp.dot(active, w_down, preferred_element_type=jnp.float32)).astype(
        jnp.bfloat16
    )
    w_down_grad = jnp.einsum("tf,td->fd", active, cotangent, preferred_element_type=jnp.float32)
    d_active = jnp.einsum("td,fd->tf", cotangent, w_down, preferred_element_type=jnp.float32)
    gelu_pull = jax.vjp(jax.nn.gelu, hidden)[1]
    d_hidden = gelu_pull(d_active)[0].astype(jnp.bfloat16)
    w_up_grad = jnp.einsum("td,tf->df", normed2, d_hidden, preferred_element_type=jnp.float32)
    d_normed2 = jnp.einsum("tf,df->td", d_hidden, w_up, preferred_element_type=jnp.float32)
    ln2_gain_grad = jnp.sum(d_normed2 * unit_two, axis=0)
    ln2_shift_grad = jnp.sum(d_normed2, axis=0)
    d_residual = cotangent.astype(jnp.float32) + norm_back(
        d_normed2, unit_two, inverse_two, ln2_gain
    )
    d_outproj = d_residual.astype(jnp.bfloat16)
    w_out_grad = jnp.einsum("td,te->de", branch, d_outproj, preferred_element_type=jnp.float32)
    d_branch = jnp.einsum("te,de->td", d_outproj, w_out, preferred_element_type=jnp.float32)
    d_mixed = (d_branch * gate_vals).astype(jnp.bfloat16)
    d_gate = d_branch * mixed
    d_signal = []
    low_grad = 0.0
    cross_grad = 0.0
    for row in range(row_count):
        first, second = signal_waves[row]
        d_first = to_waves(table, d_mixed[row * row_len : row * row_len + half]) * scale
        d_second = to_waves(table, d_mixed[row * row_len + half : (row + 1) * row_len]) * scale
        d_cross = d_second * long_rows[row]
        d_signal.append(
            from_waves(table, conj_times(kernel_low, d_first) + conj_times(kernel_cross, d_cross))
        )
        d_signal.append(from_waves(table, conj_times(kernel_low, d_second)))
        low_grad = low_grad + conj_times(first, d_first) + conj_times(second, d_second)
        cross_grad = cross_grad + conj_times(first, d_cross)
    low_grad = low_grad + turned(cross_grad, -1.0)
    d_kernel = jnp.concatenate([from_waves(table, low_grad), from_waves(table, cross_grad)], axis=0)
    d_signal = jnp.concatenate(d_signal, axis=0)
    d_projected = jnp.concatenate([d_signal, d_gate], axis=1).astype(jnp.bfloat16)
    w_in_grad = jnp.einsum("td,te->de", normed, d_projected, preferred_element_type=jnp.float32)
    d_normed = jnp.einsum("te,de->td", d_projected, w_in, preferred_element_type=jnp.float32)
    ln1_gain_grad = jnp.sum(d_normed * unit_one, axis=0)
    ln1_shift_grad = jnp.sum(d_normed, axis=0)
    input_grad = d_residual + norm_back(d_normed, unit_one, inverse_one, ln1_gain)

    shares = lax.psum_scatter(
        pool(d_kernel).astype(jnp.bfloat16), "narrow", scatter_dimension=0, tiled=True
    )
    summed = lax.psum(shares, "wide").astype(jnp.float32)
    raw_grad = summed * (jnp.abs(raw_taps) > shrink_level).astype(jnp.float32)

    def scatter(values):
        return lax.psum_scatter(
            values.astype(jnp.bfloat16), ("wide", "narrow"), scatter_dimension=0, tiled=True
        ).astype(jnp.float32)

    def scatter_wide(values):
        return lax.psum_scatter(values, ("wide", "narrow"), scatter_dimension=0, tiled=True)

    return (
        block_out,
        input_grad,
        raw_grad,
        scatter_wide(ln1_gain_grad),
        scatter_wide(ln1_shift_grad),
        scatter(w_in_grad),
        scatter(w_out_grad),
        scatter_wide(ln2_gain_grad),
        scatter_wide(ln2_shift_grad),
        scatter(w_up_grad),
        scatter(w_down_grad),
    )


MESH = pl.DeviceIdType.MESH
PART = 9
STORES = 30
VMEM_BYTES = 60 * 2**20
FLIGHTS = 3


def dot_nn(left, right):
    return lax.dot_general(left, right, (((1,), (0,)), ((), ())), preferred_element_type=jnp.float32)


def dot_nt(left, right):
    return lax.dot_general(left, right, (((1,), (1,)), ((), ())), preferred_element_type=jnp.float32)


def dot_tn(left, right):
    return lax.dot_general(left, right, (((0,), (0,)), ((), ())), preferred_element_type=jnp.float32)


def gelu_both(hidden):
    inner = 0.7978845608028654
    cubic = inner * 0.044715
    square = hidden * hidden
    bent = jnp.tanh(hidden * (inner + cubic * square))
    share = 0.5 + 0.5 * bent
    slope = share + (0.5 * hidden) * (1.0 - bent * bent) * (inner + (3.0 * cubic) * square)
    return hidden * share, slope


def column_sums(values):
    rows, width = values.shape
    return jnp.sum(values.reshape(rows // 8, 8, width), axis=0)


class Place:
    def __init__(self, planes):
        wide = lax.axis_index("wide")
        self.narrow = lax.axis_index("narrow")
        self.wide = wide
        self.core = wide % 2
        self.y = (wide // 2) % 2
        self.z = wide // 4
        self.x = self.narrow
        self.planes = planes
        self.sibling = (wide + 1 - 2 * self.core, self.narrow)
        self.next_x = (wide, 1 - self.narrow)
        self.next_y = (wide + 2 - 4 * self.y, self.narrow)

    def plane(self, step):
        other = (self.z + step) % self.planes
        return (self.wide + 4 * (other - self.z), self.narrow), other


class Chunk:
    def __init__(self, place, held, inbox, sems, x_first, target=None):
        self.place = place
        self.views = (held, inbox, sems)
        self.target = target
        self.first, self.second = (place.x, place.y) if x_first else (place.y, place.x)
        self.to_first, self.to_second = (
            (place.next_x, place.next_y) if x_first else (place.next_y, place.next_x)
        )
        self.x_first = x_first

    @property
    def held(self):
        ref, at = self.views[0]
        return ref.at[at]

    @property
    def inbox(self):
        return [ref if at is None else ref.at[at] for ref, at in self.views[1]]

    @property
    def sems(self):
        return [ref.at[at] for ref, at in self.views[2]]

    def slot(self, y, core, x):
        first, second = (x, y) if self.x_first else (y, x)
        return ((core * 2 + first) * 2 + second) * self.place.planes

    def copy(self, stage):
        planes, core = self.place.planes, self.place.core
        first, second = self.first, self.second
        start, count, device = (
            (4 * planes * (1 - core), 4 * planes, self.place.sibling),
            (4 * planes * core + 2 * planes * (1 - first), 2 * planes, self.to_first),
            (4 * planes * core + 2 * planes * first + planes * (1 - second), planes, self.to_second),
        )[stage]
        return pltpu.make_async_remote_copy(
            src_ref=self.held.at[pl.ds(start, count)],
            dst_ref=self.inbox[stage],
            send_sem=self.sems[0].at[stage],
            recv_sem=self.sems[1].at[stage],
            device_id=device,
            device_id_type=MESH,
        )

    def add(self, start, landing, count):
        for index in range(count):
            self.held[start + index] += landing[index]

    def start(self):
        self.copy(0).start()

    def over_core(self):
        planes = self.place.planes
        self.copy(0).wait()
        self.add(4 * planes * self.place.core, self.inbox[0], 4 * planes)
        self.copy(1).start()

    def over_first(self):
        planes = self.place.planes
        self.copy(1).wait()
        self.add(4 * planes * self.place.core + 2 * planes * self.first, self.inbox[1], 2 * planes)
        self.copy(2).start()

    def base(self):
        planes, place = self.place.planes, self.place
        return 4 * planes * place.core + 2 * planes * self.first + planes * self.second

    def plane_copy(self, step):
        device, other = self.place.plane(step)
        if self.target is None:
            return pltpu.make_async_remote_copy(
                src_ref=self.held.at[self.base() + other],
                dst_ref=self.inbox[3].at[step - 1],
                send_sem=self.sems[0].at[2 + step],
                recv_sem=self.sems[1].at[2 + step],
                device_id=device,
                device_id_type=MESH,
            )
        return pltpu.make_async_remote_copy(
            src_ref=self.held.at[pl.ds(self.base(), self.place.planes)],
            dst_ref=self.inbox[3].at[step - 1],
            send_sem=self.sems[0].at[2 + step],
            recv_sem=self.sems[1].at[2 + step],
            device_id=device,
            device_id_type=MESH,
        )

    def each_plane(self, act):
        for step in range(1, self.place.planes):
            if self.target is None:
                act(self.plane_copy(step))
            else:

                @pl.when((self.place.z + step) % self.place.planes == self.target)
                def _():
                    act(self.plane_copy(step))

    def over_second(self):
        self.copy(2).wait()
        planes = self.place.planes
        self.add(self.base(), self.inbox[2], planes)
        if self.target is None:
            self.inbox[3][planes - 1] = self.held[self.base() + self.place.z]
        else:

            @pl.when(self.place.z == self.target)
            def _():
                for index in range(planes):
                    self.inbox[3][planes - 1, index] = self.held[self.base() + index]

        self.each_plane(lambda copy: copy.start())

    def sent(self):
        self.each_plane(lambda copy: copy.wait_send())

    def arrived(self):
        for step in range(1, self.place.planes):
            self.plane_copy(step).wait_recv()

    def total(self, index):
        terms = [
            self.inbox[3][step] if self.target is None else self.inbox[3][step, index]
            for step in range(self.place.planes)
        ]
        return sum(term.astype(jnp.float32) for term in terms)


def store_rows(chunk, values, first_row):
    width = values.shape[1]
    for k in range(values.shape[0] // 24):
        shard = first_row // 24 + k
        z, y, core, x = shard // 8, shard // 4 % 2, shard // 2 % 2, shard % 2
        at = chunk.slot(y, core, x) + z
        block = values[24 * k : 24 * k + 24]
        rest = block[16:24]
        chunk.held[at, :, 0:width] = block[0:16].astype(jnp.bfloat16)
        chunk.held[at, :, width : width + width // 2] = jnp.concatenate(
            [rest[:, : width // 2], rest[:, width // 2 :]], axis=0
        ).astype(jnp.bfloat16)


def load_rows(block, width):
    rest = block[:, width:]
    return jnp.concatenate(
        [block[:, :width], jnp.concatenate([rest[0:8], rest[8:16]], axis=1)], axis=0
    )


def tile_runs(sub, width):
    tiles = width // 128
    runs, tile = [], 0
    while tile < tiles:
        line = sub * tiles + tile
        count = min(tiles - tile, PART - line % PART)
        runs.append((tile, line // PART, line % PART, count))
        tile += count
    return runs


def store_shards(chunk, values, first_row):
    width = values.shape[1]
    for k in range(values.shape[0] // 16):
        row = first_row + 16 * k
        shard, sub = row // 96, row % 96 // 16
        base = chunk.slot(shard // 4, shard // 2 % 2, shard % 2)
        for tile, block, at, count in tile_runs(sub, width):
            chunk.held[base + block, :, 128 * at : 128 * (at + count)] = values[
                16 * k : 16 * k + 16, 128 * tile : 128 * (tile + count)
            ].astype(jnp.bfloat16)


class Taps:
    def __init__(self, place, held, inbox, result, sems, index, rows, cols, x_first):
        self.place, self.held, self.inbox, self.result = place, held, inbox, result
        self.sems, self.index = sems, index
        self.rows = rows
        self.cols = cols
        self.x_first = x_first

    def part(self, x, core, y, plane, count):
        planes = self.place.planes
        return pl.ds((((x * 2 + core) * 2 + y) * planes + plane) * self.rows, count * self.rows)

    def add(self, target, landing):
        self.held[target, self.cols] += landing[...]

    def landing(self, level, first, count):
        return self.inbox[level].at[pl.ds(first * self.rows, count * self.rows), self.cols]

    def copy(self, kind, step=0):
        place, planes = self.place, self.place.planes
        x, core, y, z = place.x, place.core, place.y, place.z
        if kind == "core":
            source, landing = self.part(step, 1 - core, 0, 0, 2 * planes), self.landing(0, step * 2 * planes, 2 * planes)
            stage, device = step, place.sibling
        elif kind == "first" and self.x_first:
            source, landing = self.part(1 - x, core, 0, 0, 2 * planes), self.landing(1, 0, 2 * planes)
            stage, device = 2, place.next_x
        elif kind == "first":
            source, landing = self.part(step, core, 1 - y, 0, planes), self.landing(1, step * planes, planes)
            stage, device = 2 + step, place.next_y
        elif kind == "second":
            first = self.part(x, core, 1 - y, 0, planes) if self.x_first else self.part(1 - x, core, y, 0, planes)
            source, landing = first, self.landing(2, 0, planes)
            stage, device = 4, place.next_y if self.x_first else place.next_x
        elif kind == "plane":
            device, other = place.plane(step)
            source, landing = self.part(x, core, y, other, 1), self.landing(3, step - 1, 1)
            stage = 4 + step
        else:
            if kind == "back plane":
                mine, stage, device = (0, core, y, z, 1), 3 + planes + step, place.plane(step)[0]
            elif kind == "back y":
                mine, stage, device = (0, core, y, 0, planes), 3 + 2 * planes, place.next_y
            else:
                mine, stage, device = (0, core, 0, 0, 2 * planes), 4 + 2 * planes, place.sibling
            landing = self.result.at[self.part(*mine), self.cols]
        return pltpu.make_async_remote_copy(
            src_ref=landing if kind.startswith("back") else self.held.at[source, self.cols],
            dst_ref=landing,
            send_sem=self.sems[0].at[self.index, stage],
            recv_sem=self.sems[1].at[self.index, stage],
            device_id=device,
            device_id_type=MESH,
        )

    def start(self):
        for x in range(2):
            self.copy("core", x).start()

    def over_core(self):
        for x in range(2):
            self.copy("core", x).wait()
            self.add(
                self.part(x, self.place.core, 0, 0, 2 * self.place.planes),
                self.landing(0, x * 2 * self.place.planes, 2 * self.place.planes),
            )
        for step in range(1 if self.x_first else 2):
            self.copy("first", step).start()

    def over_first(self):
        place, planes = self.place, self.place.planes
        if self.x_first:
            self.copy("first").wait()
            self.add(self.part(place.x, place.core, 0, 0, 2 * planes), self.landing(1, 0, 2 * planes))
        else:
            for x in range(2):
                self.copy("first", x).wait()
                self.add(self.part(x, place.core, place.y, 0, planes), self.landing(1, x * planes, planes))
        self.copy("second").start()

    def over_second(self):
        place = self.place
        self.copy("second").wait()
        self.add(self.part(place.x, place.core, place.y, 0, place.planes), self.landing(2, 0, place.planes))
        for step in range(1, place.planes):
            self.copy("plane", step).start()

    def over_planes(self):
        place = self.place
        mine = self.part(place.x, place.core, place.y, place.z, 1)
        total = self.held[mine, self.cols].astype(jnp.float32)
        for step in range(1, place.planes):
            self.copy("plane", step).wait()
            total = total + self.landing(3, step - 1, 1)[...].astype(jnp.float32)
        self.result[self.part(0, place.core, place.y, place.z, 1), self.cols] = total.astype(self.result.dtype)
        for step in range(1, place.planes):
            self.copy("back plane", step).start()

    def back_y(self):
        for step in range(1, self.place.planes):
            self.copy("back plane", step).wait()
        self.copy("back y").start()

    def back_core(self):
        self.copy("back y").wait()
        self.copy("back core").start()

    def finish(self):
        self.copy("back core").wait()


class Sums:
    def __init__(self, place, levels, inbox, sems):
        self.place, self.levels, self.inbox, self.sems = place, levels, inbox, sems

    def copy(self, level, step=0):
        place = self.place
        device = (place.sibling, place.next_x, place.next_y)[level] if level < 3 else place.plane(step)[0]
        landing = level + max(step - 1, 0)
        return pltpu.make_async_remote_copy(
            src_ref=self.levels.at[level],
            dst_ref=self.inbox.at[landing],
            send_sem=self.sems[0].at[landing],
            recv_sem=self.sems[1].at[landing],
            device_id=device,
            device_id_type=MESH,
        )

    def start(self):
        self.copy(0).start()

    def over(self, level):
        self.copy(level).wait()
        self.levels[level + 1] = self.levels[level] + self.inbox[level]
        if level < 2:
            self.copy(level + 1).start()
        else:
            for step in range(1, self.place.planes):
                self.copy(3, step).start()

    def finish(self):
        total = self.levels[3]
        for step in range(1, self.place.planes):
            self.copy(3, step).wait()
            total = total + self.inbox[2 + step]
        return total


def block_kernel(
    planes,
    lengths,
    tokens, cotangent, raw_taps, w_in, w_out, w_up, w_down, table, table_t,
    ln1_gain, ln1_shift, ln2_gain, ln2_shift,
    block_out, input_grad, taps_out, residual, sums_out, w_in_grad, w_out_grad, w_up_grad, w_down_grad,
    held, inbox0, inbox1, inbox2, inbox_u, inbox_n, taps_held, taps0, taps1, taps2, taps3, taps_sum,
    levels, sums_inbox, cot, active, running, branch_v, normed_v, w_out_v,
    gate_v, mixed_v, waves, kernels,
    send_sems, recv_sems, taps_send, taps_recv, sums_send, sums_recv, share_send, share_recv, load_sems,
):
    tok_count, feat = cot.shape
    half = tok_count // 2
    tile = active.shape[2]
    step_rows = 256
    row_steps = tok_count // step_rows
    place = Place(planes)

    loads = {}

    class Load:
        def __init__(self, source, target):
            self.ends, self.at = (source, target), len(loads)

        def copy(self):
            source, target = (end() if callable(end) else end for end in self.ends)
            return pltpu.make_async_copy(source, target, load_sems.at[self.at])

        def wait(self):
            self.copy().wait()

    def load(name, source, target):
        loads[name] = Load(source, target)
        loads[name].copy().start()

    barrier = pltpu.get_barrier_semaphore()
    partners = [place.sibling, place.next_x, place.next_y] + [
        place.plane(step)[0] for step in range(1, planes)
    ]
    for partner in partners:
        pl.semaphore_signal(barrier, inc=1, device_id=partner, device_id_type=MESH)
    long = jnp.where(lengths[0] > half, 1.0, 0.0).astype(jnp.float32)

    def chunk(index, step, kind, target=None):
        at = step % FLIGHTS * 2 + kind
        ring = step % 2 * 2 + kind
        if target is None:
            far = (inbox_u, index // 2 if index < 2 * planes else index - planes)
        else:
            far = (inbox_n, None)
        return Chunk(
            place,
            (held, at),
            ((inbox0, ring), (inbox1, ring), (inbox2, ring), far),
            ((send_sems, index), (recv_sems, index)),
            kind == 0,
            target,
        )

    ups = [chunk(2 * t, t, 0) for t in range(planes)]
    downs = [chunk(2 * t + 1, t, 1, t) for t in range(planes)]

    def rows_of(index):
        return pl.ds(index * step_rows, step_rows)

    def unrolled(first, last, body, carry):
        for index in range(first, last):
            carry = body(index, carry)
        return carry

    def norm_of(values):
        centered = values - jnp.mean(values, axis=-1, keepdims=True)
        inverse = lax.rsqrt(jnp.mean(centered * centered, axis=-1, keepdims=True) + eps_norm)
        return centered * inverse, inverse

    def stash_copy(index):
        rows = rows_of(index)
        return pltpu.make_async_copy(running.at[rows, :], residual.at[rows, :], load_sems.at[STORES - 2])

    def share_copy(which):
        block = half // 2
        block_x = place.x if which == 0 else 1 - place.x
        rows = pl.ds(pl.multiple_of(block_x * half + place.core * block, block), block)
        return pltpu.make_async_remote_copy(
            src_ref=taps_held.at[rows, :],
            dst_ref=taps_held.at[rows, :],
            send_sem=share_send.at[which],
            recv_sem=share_recv.at[which],
            device_id=place.next_x if which == 0 else place.sibling,
            device_id_type=MESH,
        )

    def forward_back(normed_2, normed_2t, up_tiles, down_tiles):
        def load_tile(t):
            cols = pl.ds(t * tile, tile)
            load(("up", t), lambda: w_up.at[:, cols], lambda: up_tiles.at[t % 2])
            load(("down", t), lambda: w_down.at[cols, :], lambda: down_tiles.at[t % 2])

        def mix(w_in_v, table_v, table_tv):
            kernel = mixed_v
            load("taps", raw_taps, running.at[0:half, :])
            load("tokens", tokens, lambda: active.at[0])
            load("w_in", w_in, w_in_v)
            load("table", table, table_v)
            load("table_t", table_t, table_tv)
            load("w_out", w_out, w_out_v)
            load_tile(0)
            load("cot", cotangent, cot)

            loads["taps"].wait()

            def squash_step(index, carry):
                rows = pl.ds(pl.multiple_of(index * 128, 128), 128)
                raw = running[rows, :]
                taps_held[pl.ds(pl.multiple_of(place.x * half + index * 128, 128), 128), :] = (
                    raw - jnp.clip(raw, -shrink_level, shrink_level)
                ).astype(jnp.bfloat16)
                return carry

            lax.fori_loop(0, half // 128, squash_step, 0)
            pl.semaphore_wait(barrier, len(partners))
            share_copy(0).start()
            loads["tokens"].wait()
            loads["w_in"].wait()

            def project_step(index, carry):
                rows = rows_of(index)
                unit, _ = norm_of(active[0, rows, :].astype(jnp.float32))
                low = (unit * ln1_gain[...][None, :] + ln1_shift[...][None, :]).astype(jnp.bfloat16)
                normed_v[:, rows] = low.T
                active[1, rows, :] = dot_nn(low, w_in_v[:, 0:feat]).astype(jnp.bfloat16)
                gate_v[rows, :] = dot_nn(low, w_in_v[:, feat:]).astype(jnp.bfloat16)
                return carry

            unrolled(0, row_steps, project_step, 0)
            share_copy(0).wait()
            share_copy(1).start()
            loads["table"].wait()

            def signal_wave_step(index, carry):
                rows = rows_of(index)
                for which in range(2):
                    waves[which, rows, :] = dot_nn(
                        table_v[rows, :], active[1, which * half : (which + 1) * half, :]
                    ).astype(jnp.bfloat16)
                return carry

            unrolled(0, row_steps, signal_wave_step, 0)
            share_copy(1).wait()
            pool_rows = 128
            for index in range(tok_count // pool_rows):
                at = index * pool_rows
                first, last = max(at - 16, 0), min(at + pool_rows + 16, tok_count)
                around = taps_held[first:last, :].astype(jnp.float32)
                if at == 0:
                    around = jnp.concatenate([jnp.zeros((16, feat), jnp.float32), around], axis=0)
                if last == tok_count:
                    around = jnp.concatenate([around, jnp.zeros((16, feat), jnp.float32)], axis=0)
                kernel[at : at + pool_rows, :] = (
                    (around[15 : 15 + pool_rows] + around[16 : 16 + pool_rows] + around[17 : 17 + pool_rows])
                    / 3.0
                ).astype(jnp.bfloat16)

            def spread_step(index, carry):
                down, across = index // (feat // 256), index % (feat // 256)
                real, imag = pl.ds(down * 256, 256), pl.ds(half + down * 256, 256)
                cols = pl.ds(across * 256, 256)
                low_r = dot_nn(table_v[real, :], kernel[0:half, cols])
                low_i = dot_nn(table_v[imag, :], kernel[0:half, cols])
                high_r = dot_nn(table_v[real, :], kernel[half:, cols])
                high_i = dot_nn(table_v[imag, :], kernel[half:, cols])
                odd = lax.broadcasted_iota(jnp.int32, (256, 1), 0) % 2
                parity = (1 - 2 * odd).astype(jnp.float32)
                cross_r = long * (high_r - parity * low_i)
                cross_i = long * (high_i + parity * low_r)
                kernels[0, real, cols] = low_r.astype(jnp.bfloat16)
                kernels[0, imag, cols] = low_i.astype(jnp.bfloat16)
                kernels[1, real, cols] = cross_r.astype(jnp.bfloat16)
                kernels[1, imag, cols] = cross_i.astype(jnp.bfloat16)
                head_r = waves[0, real, cols].astype(jnp.float32)
                head_i = waves[0, imag, cols].astype(jnp.float32)
                tail_r = waves[1, real, cols].astype(jnp.float32)
                tail_i = waves[1, imag, cols].astype(jnp.float32)
                scale = 1.0 / half
                active[2, real, cols] = ((low_r * head_r - low_i * head_i) * scale).astype(jnp.bfloat16)
                active[2, imag, cols] = ((low_r * head_i + low_i * head_r) * scale).astype(jnp.bfloat16)
                active[3, real, cols] = (
                    (low_r * tail_r - low_i * tail_i + cross_r * head_r - cross_i * head_i) * scale
                ).astype(jnp.bfloat16)
                active[3, imag, cols] = (
                    (low_r * tail_i + low_i * tail_r + cross_r * head_i + cross_i * head_r) * scale
                ).astype(jnp.bfloat16)
                return carry

            unrolled(0, half // 256 * (feat // 256), spread_step, 0)
            loads["table_t"].wait()
            loads["w_out"].wait()

            def residual_step(index, carry):
                rows = rows_of(index)
                part_steps = half // step_rows
                which = index // part_steps
                of_part = pl.ds(index % part_steps * step_rows, step_rows)
                mixed = dot_nn(table_tv[of_part, :], active[2 + which])
                mixed_v[rows, :] = mixed.astype(jnp.bfloat16)
                branch = (mixed * gate_v[rows, :].astype(jnp.float32)).astype(jnp.bfloat16)
                branch_v[:, rows] = branch.T
                left = active[0, rows, :].astype(jnp.float32) + dot_nn(branch, w_out_v[...])
                running[rows, :] = left
                stash_copy(index).start()
                unit, _ = norm_of(left)
                low = (unit * ln2_gain[...][None, :] + ln2_shift[...][None, :]).astype(jnp.bfloat16)
                normed_2[rows, :] = low
                normed_2t[:, rows] = low.T
                return carry

            unrolled(0, row_steps, residual_step, 0)
            pltpu.make_async_copy(running, residual, load_sems.at[STORES - 2]).wait()

        pl.run_scoped(
            mix,
            pltpu.VMEM((feat, 2 * feat), jnp.bfloat16),
            pltpu.VMEM((tok_count, half), jnp.bfloat16),
            pltpu.VMEM((half, tok_count), jnp.bfloat16),
        )

        def feed_forward(d_hidden):
            loads["cot"].wait()

            for t in range(planes):
                up_tile, down_tile = up_tiles.at[t % 2], down_tiles.at[t % 2]
                loads["up", t].wait()
                loads["down", t].wait()
                if t + 1 < planes:
                    load_tile(t + 1)

                def rows_step(index, carry):
                    rows = rows_of(index)
                    hidden = dot_nn(normed_2[rows, :], up_tile[...])
                    d_active = dot_nt(cot[rows, :], down_tile[...])
                    value, slope = gelu_both(hidden)
                    active[t, rows, :] = value.astype(jnp.bfloat16)
                    d_value = (d_active * slope).astype(jnp.bfloat16)
                    d_hidden[rows, :] = d_value
                    back = dot_nt(d_value, up_tile[...])
                    if t == 0:
                        running[rows, :] = back
                    else:
                        running[rows, :] += back
                    return carry

                unrolled(0, row_steps // 2, rows_step, 0)
                if t >= 2:
                    ups[t - 2].over_first()
                    downs[t - 2].over_first()
                if t >= 1:
                    ups[t - 1].over_core()
                    downs[t - 1].over_core()
                unrolled(row_steps // 2, row_steps, rows_step, 0)
                if t >= FLIGHTS:
                    ups[t - FLIGHTS].sent()
                    downs[t - FLIGHTS].sent()
                for part in range(2):
                    cols = tile // 2
                    store_shards(
                        downs[t], dot_tn(active[t, :, part * cols : (part + 1) * cols], cot[...]), part * cols
                    )
                downs[t].start()
                if t >= 2:
                    ups[t - 2].over_second()
                    downs[t - 2].over_second()
                for part in range(2):
                    rows = feat // 2
                    store_rows(
                        ups[t], dot_nn(normed_2t[part * rows : (part + 1) * rows, :], d_hidden[...]), part * rows
                    )
                ups[t].start()

        pl.run_scoped(feed_forward, pltpu.VMEM((tok_count, tile), jnp.bfloat16))

    pl.run_scoped(
        forward_back,
        pltpu.VMEM((tok_count, feat), jnp.bfloat16),
        pltpu.VMEM((feat, tok_count), jnp.bfloat16),
        pltpu.VMEM((2, feat, tile), jnp.bfloat16),
        pltpu.VMEM((2, tile, feat), jnp.bfloat16),
    )

    out_chunk = chunk(2 * planes, planes, 0)
    gate_chunk = chunk(2 * planes + 1, planes, 1)
    signal_chunk = chunk(2 * planes + 2, planes + 1, 0)
    tap_cols = 256
    taps = [
        Taps(
            place, taps_held, (taps0, taps1, taps2, taps3), taps_sum, (taps_send, taps_recv), index,
            tok_count // (8 * planes), pl.ds(index * tap_cols, tap_cols), index % 2 == 0,
        )
        for index in range(feat // tap_cols)
    ]
    sums = Sums(place, levels, sums_inbox, (sums_send, sums_recv))

    def own_rows(target):
        target.arrived()
        return load_rows(target.total(0), feat)

    def own_down():
        for t in range(planes):

            @pl.when(place.z == t)
            def _():
                downs[t].arrived()
                for index in range(planes):
                    block = downs[t].total(index)
                    for sub in range(6):
                        for first, line, at, count in tile_runs(sub, feat):
                            if line == index:
                                w_down_grad[16 * sub : 16 * sub + 16, 128 * first : 128 * (first + count)] = block[
                                    :, 128 * at : 128 * (at + count)
                                ]

    def backward(d_out, d_gate, d_mix, d_signal):
        def norm_two_back(left_v):
            load("left", residual.at[0 : tok_count // 2, :], left_v.at[0 : tok_count // 2, :])
            load("left end", residual.at[tok_count // 2 :, :], left_v.at[tok_count // 2 :, :])
            loads["left"].wait()

            def back_step(index, carry):
                gain_sum, shift_sum = carry
                rows = rows_of(index)
                left = left_v[rows, :]
                centered = left - jnp.mean(left, axis=-1, keepdims=True)
                inverse = lax.rsqrt(jnp.mean(centered * centered, axis=-1, keepdims=True) + eps_norm)
                unit = centered * inverse
                grad = running[rows, :]
                scaled = grad * ln2_gain[...][None, :]
                d_left = cot[rows, :].astype(jnp.float32) + inverse * (
                    scaled
                    - jnp.mean(scaled, axis=-1, keepdims=True)
                    - unit * jnp.mean(scaled * unit, axis=-1, keepdims=True)
                )
                running[rows, :] = d_left
                d_low = d_left.astype(jnp.bfloat16)
                d_out[rows, :] = d_low
                d_branch = dot_nt(d_low, w_out_v[...])
                d_mix[rows, :] = (
                    d_branch * gate_v[rows, :].astype(jnp.float32) * (1.0 / half)
                ).astype(jnp.bfloat16)
                d_gate[rows, :] = (d_branch * mixed_v[rows, :].astype(jnp.float32)).astype(jnp.bfloat16)
                return gain_sum + column_sums(grad * unit), shift_sum + column_sums(grad)

            zero = jnp.zeros((8, feat), jnp.float32)
            carry = unrolled(0, row_steps // 2, back_step, (zero, zero))
            ups[planes - 2].over_first()
            downs[planes - 2].over_first()
            ups[planes - 1].over_core()
            downs[planes - 1].over_core()
            loads["left end"].wait()
            gain_sum, shift_sum = unrolled(row_steps // 2, row_steps, back_step, carry)
            levels[0] = jnp.zeros(levels.shape[1:], jnp.float32)
            levels[0, 0:1, :] = jnp.sum(gain_sum, axis=0, keepdims=True)
            levels[0, 1:2, :] = jnp.sum(shift_sum, axis=0, keepdims=True)

        pl.run_scoped(norm_two_back, pltpu.VMEM((tok_count, feat), jnp.float32))


        def weight_rows(target, left_t, right):
            for part in range(2):
                rows = feat // 2
                store_rows(target, dot_nn(left_t[part * rows : (part + 1) * rows, :], right[...]), part * rows)
            target.start()

        def mixer_back(table_v, table_tv, d_kernel, d_taps):
            d_waves = waves
            load("table again", table, table_v)
            load("table_t again", table_t, table_tv)
            downs[planes - 3].sent()
            weight_rows(gate_chunk, normed_v, d_gate)
            ups[planes - 2].over_second()
            downs[planes - 2].over_second()
            ups[planes - 1].over_first()
            downs[planes - 1].over_first()
            ups[planes - 3].sent()
            weight_rows(out_chunk, branch_v, d_out)
            loads["table again"].wait()
            loads["table_t again"].wait()
            wave_rows, wave_cols = 256, 256

            def wave_step(down, cols):
                real, imag = pl.ds(down * wave_rows, wave_rows), pl.ds(half + down * wave_rows, wave_rows)
                first_r = dot_nn(table_v[real, :], d_mix[0:half, cols])
                first_i = dot_nn(table_v[imag, :], d_mix[0:half, cols])
                second_r = dot_nn(table_v[real, :], d_mix[half:, cols])
                second_i = dot_nn(table_v[imag, :], d_mix[half:, cols])

                def wide(ref, which, rows):
                    return ref[which, rows, cols].astype(jnp.float32)

                def keep(ref, which, rows, values):
                    at = cols if ref.shape[2] == feat else slice(None)
                    ref[which, rows, at] = values.astype(jnp.bfloat16)

                low_r, low_i = wide(kernels, 0, real), wide(kernels, 0, imag)
                cross_r, cross_i = wide(kernels, 1, real), wide(kernels, 1, imag)
                head_r, head_i = wide(waves, 0, real), wide(waves, 0, imag)
                tail_r, tail_i = wide(waves, 1, real), wide(waves, 1, imag)
                keep(d_waves, 0, real, low_r * first_r + low_i * first_i + cross_r * second_r + cross_i * second_i)
                keep(d_waves, 0, imag, low_r * first_i - low_i * first_r + cross_r * second_i - cross_i * second_r)
                keep(d_waves, 1, real, low_r * second_r + low_i * second_i)
                keep(d_waves, 1, imag, low_r * second_i - low_i * second_r)
                far_r = (head_r * second_r + head_i * second_i) * long
                far_i = (head_r * second_i - head_i * second_r) * long
                odd = lax.broadcasted_iota(jnp.int32, (wave_rows, 1), 0) % 2
                parity = (1 - 2 * odd).astype(jnp.float32)
                keep(d_kernel, 1, real, far_r)
                keep(d_kernel, 1, imag, far_i)
                keep(
                    d_kernel,
                    0,
                    real,
                    head_r * first_r + head_i * first_i + tail_r * second_r + tail_i * second_i + parity * far_i,
                )
                keep(
                    d_kernel,
                    0,
                    imag,
                    head_r * first_i - head_i * first_r + tail_r * second_i - tail_i * second_r - parity * far_r,
                )

            pad = 8
            d_taps[0:pad, :] = jnp.zeros((pad, wave_cols), jnp.float32)
            d_taps[pad + tok_count :, :] = jnp.zeros((pad, wave_cols), jnp.float32)
            pool_rows = 128

            def column_step(across):
                cols = pl.ds(across * wave_cols, wave_cols)
                for down in range(half // wave_rows):
                    wave_step(down, cols)
                for which in range(2):
                    d_taps[pad + which * half : pad + (which + 1) * half, :] = dot_nn(table_tv[...], d_kernel[which])
                for index in range(tok_count // pool_rows):
                    at = pad + index * pool_rows
                    taps_held[at - pad : at - pad + pool_rows, cols] = (
                        (
                            d_taps[at - 1 : at - 1 + pool_rows, :]
                            + d_taps[at : at + pool_rows, :]
                            + d_taps[at + 1 : at + 1 + pool_rows, :]
                        )
                        / 3.0
                    ).astype(jnp.bfloat16)

            column_step(0)
            taps[0].start()
            ups[planes - 1].over_second()
            downs[planes - 1].over_second()
            gate_chunk.over_core()
            column_step(1)
            taps[1].start()
            taps[0].over_core()
            out_chunk.over_core()
            column_step(2)
            taps[2].start()
            taps[1].over_core()
            gate_chunk.over_first()
            taps[0].over_first()

            def signal_step(which, index):
                at = index * step_rows
                d_signal[which * half + at : which * half + at + step_rows, :] = dot_nn(
                    table_tv[at : at + step_rows, :], d_waves[which]
                ).astype(jnp.bfloat16)

            for index in range(half // step_rows):
                signal_step(0, index)
            taps[2].over_core()
            out_chunk.over_first()
            taps[0].over_second()
            for index in range(half // step_rows):
                signal_step(1, index)
            taps[1].over_first()

        pl.run_scoped(
            mixer_back,
            pltpu.VMEM((tok_count, half), jnp.bfloat16),
            pltpu.VMEM((half, tok_count), jnp.bfloat16),
            pltpu.VMEM((2, tok_count, 256), jnp.bfloat16),
            pltpu.VMEM((tok_count + 16, 256), jnp.float32),
        )

        ups[planes - 2].sent()
        weight_rows(signal_chunk, normed_v, d_signal)
        gate_chunk.over_second()
        taps[2].over_first()
        taps[1].over_second()
        taps[0].over_planes()

        def finish(w_in_v, left_v):
            def down_again(t):
                return (waves if t < 2 else kernels).at[t % 2, 0:tile, :]

            def load_again(t):
                rows = pl.ds(t * tile, tile)
                load(("again", t), lambda: w_down.at[rows, :], lambda: down_again(t))

            load("w_in again", w_in, w_in_v)
            load("tokens again", tokens, gate_v)
            for t in range(planes):
                load_again(t)
            load("left again", residual, left_v)
            loads["tokens again"].wait()
            loads["w_in again"].wait()

            def grad_copy(index):
                rows = rows_of(index)
                return pltpu.make_async_copy(
                    running.at[rows, :], input_grad.at[rows, :], load_sems.at[STORES + index]
                )

            def input_step(index, carry):
                gain_sum, shift_sum = carry
                rows = rows_of(index)
                d_normed = dot_nt(d_signal[rows, :], w_in_v[:, 0:feat]) + dot_nt(
                    d_gate[rows, :], w_in_v[:, feat:]
                )
                values = gate_v[rows, :].astype(jnp.float32)
                centered = values - jnp.mean(values, axis=-1, keepdims=True)
                inverse = lax.rsqrt(jnp.mean(centered * centered, axis=-1, keepdims=True) + eps_norm)
                unit = centered * inverse
                scaled = d_normed * ln1_gain[...][None, :]

                running[rows, :] = running[rows, :] + inverse * (
                    scaled
                    - jnp.mean(scaled, axis=-1, keepdims=True)
                    - unit * jnp.mean(scaled * unit, axis=-1, keepdims=True)
                )
                grad_copy(index).start()
                return gain_sum + column_sums(d_normed * unit), shift_sum + column_sums(d_normed)

            zero = jnp.zeros((8, feat), jnp.float32)
            carry = unrolled(0, 1, input_step, (zero, zero))
            signal_chunk.over_core()
            out_chunk.over_second()
            carry = unrolled(1, 2, input_step, carry)
            taps[2].over_second()
            taps[1].over_planes()
            taps[0].back_y()
            carry = unrolled(2, 3, input_step, carry)
            signal_chunk.over_first()
            gain_sum, shift_sum = unrolled(3, row_steps, input_step, carry)
            levels[0, 2:3, :] = jnp.sum(gain_sum, axis=0, keepdims=True)
            levels[0, 3:4, :] = jnp.sum(shift_sum, axis=0, keepdims=True)
            sums.start()
            taps[2].over_planes()
            taps[1].back_y()
            taps[0].back_core()
            for t in range(planes):
                loads["again", t].wait()
            loads["left again"].wait()

            def out_copy(index):
                rows = rows_of(index)
                return pltpu.make_async_copy(
                    mixed_v.at[rows, :], block_out.at[rows, :], load_sems.at[STORES + row_steps + index]
                )

            def out_step(index, carry):
                rows = rows_of(index)
                total = left_v[rows, :]
                for t in range(planes):
                    total = total + dot_nn(active[t, rows, :], down_again(t)[...])

                mixed_v[rows, :] = total.astype(jnp.bfloat16)
                out_copy(index).start()
                return carry

            unrolled(0, 1, out_step, 0)
            sums.over(0)
            signal_chunk.over_second()
            unrolled(1, 2, out_step, 0)
            sums.over(1)
            taps[2].back_y()
            taps[1].back_core()
            unrolled(2, 3, out_step, 0)
            sums.over(2)
            taps[2].back_core()
            for t in range(planes):
                w_up_grad[:, t * tile : (t + 1) * tile] = own_rows(ups[t])
            w_in_grad[:, feat:] = own_rows(gate_chunk)
            unrolled(3, row_steps, out_step, 0)
            w_out_grad[...] = own_rows(out_chunk)
            own_down()
            for index in range(row_steps):
                grad_copy(index).wait()
                out_copy(index).wait()

        pl.run_scoped(
            finish,
            pltpu.VMEM((feat, 2 * feat), jnp.bfloat16),
            pltpu.VMEM((tok_count, feat), jnp.float32),
        )

    pl.run_scoped(backward, *[pltpu.VMEM((tok_count, feat), jnp.bfloat16)] * 4)

    w_in_grad[:, 0:feat] = own_rows(signal_chunk)
    sums_out[...] = sums.finish()
    for part in taps:
        part.finish()
    taps_store = pltpu.make_async_copy(taps_sum, taps_out, load_sems.at[STORES - 1])
    taps_store.start()
    for one in (downs[planes - 2], ups[planes - 1], downs[planes - 1], out_chunk, gate_chunk, signal_chunk):
        one.sent()
    taps_store.wait()


def linked_block(
    planes,
    tokens,
    lengths,
    raw_taps,
    ln1_gain,
    ln1_shift,
    w_in,
    w_out,
    ln2_gain,
    ln2_shift,
    w_up,
    w_down,
    cotangent,
):
    tok_count, feat = tokens.shape
    half = tok_count // 2
    tile = w_up.shape[1] // planes
    table = jnp.asarray(wave_table(half), jnp.bfloat16)
    table_t = jnp.asarray(wave_table(half).T, jnp.bfloat16)
    shares = 8 * planes
    rows = feat // shares
    block = (16, 128 * PART)
    chunks = 2 * planes + 3
    bf16, f32 = jnp.bfloat16, jnp.float32
    whole = pl.BlockSpec(memory_space=pl.ANY)
    near = pl.BlockSpec(memory_space=pltpu.VMEM)
    results = pl.pallas_call(
        functools.partial(block_kernel, planes),
        out_shape=(
            jax.ShapeDtypeStruct((tok_count, feat), bf16),
            jax.ShapeDtypeStruct((tok_count, feat), f32),
            jax.ShapeDtypeStruct((half, feat), bf16),
            jax.ShapeDtypeStruct((tok_count, feat), f32),
            jax.ShapeDtypeStruct((8, feat), f32),
            jax.ShapeDtypeStruct((rows, 2 * feat), f32),
            jax.ShapeDtypeStruct((rows, feat), f32),
            jax.ShapeDtypeStruct((rows, planes * tile), f32),
            jax.ShapeDtypeStruct((tile // 8, feat), f32),
        ),
        in_specs=[pl.BlockSpec(memory_space=pltpu.SMEM)] + [whole] * 9 + [near] * 4,
        out_specs=(whole,) * 4 + (near,) * 5,
        scratch_shapes=[
            pltpu.VMEM((2 * FLIGHTS, shares) + block, bf16),
            pltpu.VMEM((4, 4 * planes) + block, bf16),
            pltpu.VMEM((4, 2 * planes) + block, bf16),
            pltpu.VMEM((4, planes) + block, bf16),
            pltpu.VMEM((planes + 3, planes) + block, bf16),
            pltpu.VMEM((planes, planes) + block, bf16),
            pltpu.VMEM((tok_count, feat), bf16),
            pltpu.VMEM((tok_count // 2, feat), bf16),
            pltpu.VMEM((tok_count // 4, feat), bf16),
            pltpu.VMEM((tok_count // 8, feat), bf16),
            pltpu.VMEM(((planes - 1) * (tok_count // shares), feat), bf16),
            pltpu.VMEM((half, feat), bf16),
            pltpu.VMEM((4, 8, feat), f32),
            pltpu.VMEM((planes + 2, 8, feat), f32),
            pltpu.VMEM((tok_count, feat), bf16),
            pltpu.VMEM((planes, tok_count, tile), bf16),
            pltpu.VMEM((tok_count, feat), f32),
            pltpu.VMEM((feat, tok_count), bf16),
            pltpu.VMEM((feat, tok_count), bf16),
            pltpu.VMEM((feat, feat), bf16),
            pltpu.VMEM((tok_count, feat), bf16),
            pltpu.VMEM((tok_count, feat), bf16),
            pltpu.VMEM((2, tok_count, feat), bf16),
            pltpu.VMEM((2, tok_count, feat), bf16),
            pltpu.SemaphoreType.DMA((chunks, planes + 2)),
            pltpu.SemaphoreType.DMA((chunks, planes + 2)),
            pltpu.SemaphoreType.DMA((feat // 256, 2 * planes + 5)),
            pltpu.SemaphoreType.DMA((feat // 256, 2 * planes + 5)),
            pltpu.SemaphoreType.DMA((planes + 2,)),
            pltpu.SemaphoreType.DMA((planes + 2,)),
            pltpu.SemaphoreType.DMA((2,)),
            pltpu.SemaphoreType.DMA((2,)),
            pltpu.SemaphoreType.DMA((STORES + 2 * tok_count // 256,)),
        ],
        compiler_params=pltpu.CompilerParams(
            collective_id=1, has_side_effects=True, vmem_limit_bytes=VMEM_BYTES
        ),
        cost_estimate=pl.CostEstimate(
            flops=2 * tok_count * feat * (5 * w_up.shape[1] + 9 * feat),
            bytes_accessed=40 * tok_count * feat,
            transcendentals=tok_count * w_up.shape[1],
        ),
    )(
        lengths,
        tokens,
        cotangent,
        raw_taps,
        w_in,
        w_out,
        w_up,
        w_down,
        table,
        table_t,
        ln1_gain,
        ln1_shift,
        ln2_gain,
        ln2_shift,
    )
    block_out, input_grad, taps_sum, _, sums, w_in_grad, w_out_grad, w_up_grad, w_down_grad = results
    raw_grad = taps_sum.astype(f32) * (jnp.abs(raw_taps) > shrink_level).astype(f32)
    share = lax.axis_index("wide") * 2 + lax.axis_index("narrow")
    mine = lax.dynamic_slice(sums, (0, share * rows), (8, rows))
    return (
        block_out,
        input_grad,
        raw_grad,
        mine[2],
        mine[3],
        w_in_grad,
        w_out_grad,
        mine[0],
        mine[1],
        w_up_grad,
        w_down_grad,
    )


def solution(mesh):
    spread = P(("wide", "narrow"))
    rows = P(("wide", "narrow"), None)
    placed = (rows, spread, P("narrow", None)) + (P(),) * 8 + (rows,)
    wide, narrow = mesh.shape["wide"], mesh.shape["narrow"]

    def block(tokens, lengths, raw_taps, *others):
        fits = (
            narrow == 2
            and wide == 4 * 4
            and lengths.shape[0] == 1
            and raw_taps.shape[0] * 2 == tokens.shape[0]
            and tokens.shape[1] == 24 * wide * narrow
            and others[-2].shape[0] == 96 * wide * narrow
            and tokens.shape[0] % 512 == 0
        )
        if fits:
            return linked_block(wide // 4, tokens, lengths, raw_taps, *others)
        return local(tokens, lengths, raw_taps, *others)

    return jax.shard_map(
        block,
        mesh=mesh,
        in_specs=placed,
        out_specs=(rows, rows, P("narrow", None), spread, spread, rows, rows, spread, spread, rows, rows),
        check_vma=False,
    )
```

```python
import functools

import jax
import jax.numpy as jnp
import numpy as np
from jax import lax
from jax.experimental import pallas as pl
from jax.experimental.pallas import tpu as pltpu
from jax.sharding import PartitionSpec as P

shrink_level = 0.003
eps_norm = 1e-05


def wave_table(half):
    period = 4 * half
    phase = (np.outer(2 * np.arange(half) + 1, np.arange(half)) % period) * (2 * np.pi / period)
    return np.concatenate([np.cos(phase), -np.sin(phase)], axis=0)


def to_waves(table, block):
    return jnp.einsum("kn,nc->kc", table, block, preferred_element_type=jnp.float32)


def from_waves(table, waves):
    return jnp.einsum(
        "kn,kc->nc", table, waves.astype(jnp.bfloat16), preferred_element_type=jnp.float32
    )


def norm_parts(values):
    centered = values - jnp.mean(values, axis=-1, keepdims=True)
    inverse = lax.rsqrt(jnp.mean(centered * centered, axis=-1, keepdims=True) + eps_norm)
    return (centered * inverse, inverse)


def norm_back(upstream, unit_vals, inverse, gain_vec):
    scaled = upstream * gain_vec
    return inverse * (
        scaled
        - jnp.mean(scaled, axis=-1, keepdims=True)
        - unit_vals * jnp.mean(scaled * unit_vals, axis=-1, keepdims=True)
    )


def split(waves):
    half = waves.shape[0] // 2
    return waves[:half], waves[half:]


def times(left, right):
    lr, li = split(left)
    rr, ri = split(right)
    return jnp.concatenate([lr * rr - li * ri, lr * ri + li * rr], axis=0)


def conj_times(left, right):
    lr, li = split(left)
    rr, ri = split(right)
    return jnp.concatenate([lr * rr + li * ri, lr * ri - li * rr], axis=0)


def turned(waves, sign):
    wr, wi = split(waves)
    index = lax.broadcasted_iota(jnp.int32, (wr.shape[0], 1), 0)
    parity = sign * (1.0 - 2.0 * (index % 2).astype(jnp.float32))
    return jnp.concatenate([-parity * wi, parity * wr], axis=0)


def pool(values):
    padded = jnp.pad(values, ((1, 1), (0, 0)))
    return (padded[:-2] + padded[1:-1] + padded[2:]) / 3.0


def local(
    tokens,
    lengths,
    raw_taps,
    ln1_gain,
    ln1_shift,
    w_in,
    w_out,
    ln2_gain,
    ln2_shift,
    w_up,
    w_down,
    cotangent,
):
    tok_count, feat_width = tokens.shape
    row_count = lengths.shape[0]
    row_len = tok_count // row_count
    half = row_len // 2
    table = jnp.asarray(wave_table(half), jnp.bfloat16)
    scale = 1.0 / half
    long_rows = (lengths > half).astype(jnp.float32)

    squashed = raw_taps - jnp.clip(raw_taps, -shrink_level, shrink_level)
    gathered = lax.all_gather(squashed.astype(jnp.bfloat16), "narrow", axis=0, tiled=True)
    kernel = pool(gathered.astype(jnp.float32)).astype(jnp.bfloat16)
    kernel_low = to_waves(table, kernel[:half])
    kernel_cross = to_waves(table, kernel[half : 2 * half]) + turned(kernel_low, 1.0)

    inputs = tokens.astype(jnp.float32)
    unit_one, inverse_one = norm_parts(inputs)
    normed = (unit_one * ln1_gain + ln1_shift).astype(jnp.bfloat16)
    projected = jnp.dot(normed, w_in, preferred_element_type=jnp.float32)
    signal = projected[:, :feat_width].astype(jnp.bfloat16)
    gate_vals = projected[:, feat_width:]
    signal_waves = []
    mixed = []
    for row in range(row_count):
        first = to_waves(table, signal[row * row_len : row * row_len + half])
        second = to_waves(table, signal[row * row_len + half : (row + 1) * row_len])
        signal_waves.append((first, second))
        mixed.append(from_waves(table, times(first, kernel_low) * scale))
        mixed.append(
            from_waves(
                table,
                (times(second, kernel_low) + long_rows[row] * times(first, kernel_cross)) * scale,
            )
        )
    mixed = jnp.concatenate(mixed, axis=0)
    branch = (mixed * gate_vals).astype(jnp.bfloat16)
    residual = inputs + jnp.dot(branch, w_out, preferred_element_type=jnp.float32)
    unit_two, inverse_two = norm_parts(residual)
    normed2 = (unit_two * ln2_gain + ln2_shift).astype(jnp.bfloat16)
    hidden = jnp.dot(normed2, w_up, preferred_element_type=jnp.float32)
    active = jax.nn.gelu(hidden).astype(jnp.bfloat16)
    block_out = (residual + jnp.dot(active, w_down, preferred_element_type=jnp.float32)).astype(
        jnp.bfloat16
    )
    w_down_grad = jnp.einsum("tf,td->fd", active, cotangent, preferred_element_type=jnp.float32)
    d_active = jnp.einsum("td,fd->tf", cotangent, w_down, preferred_element_type=jnp.float32)
    gelu_pull = jax.vjp(jax.nn.gelu, hidden)[1]
    d_hidden = gelu_pull(d_active)[0].astype(jnp.bfloat16)
    w_up_grad = jnp.einsum("td,tf->df", normed2, d_hidden, preferred_element_type=jnp.float32)
    d_normed2 = jnp.einsum("tf,df->td", d_hidden, w_up, preferred_element_type=jnp.float32)
    ln2_gain_grad = jnp.sum(d_normed2 * unit_two, axis=0)
    ln2_shift_grad = jnp.sum(d_normed2, axis=0)
    d_residual = cotangent.astype(jnp.float32) + norm_back(
        d_normed2, unit_two, inverse_two, ln2_gain
    )
    d_outproj = d_residual.astype(jnp.bfloat16)
    w_out_grad = jnp.einsum("td,te->de", branch, d_outproj, preferred_element_type=jnp.float32)
    d_branch = jnp.einsum("te,de->td", d_outproj, w_out, preferred_element_type=jnp.float32)
    d_mixed = (d_branch * gate_vals).astype(jnp.bfloat16)
    d_gate = d_branch * mixed
    d_signal = []
    low_grad = 0.0
    cross_grad = 0.0
    for row in range(row_count):
        first, second = signal_waves[row]
        d_first = to_waves(table, d_mixed[row * row_len : row * row_len + half]) * scale
        d_second = to_waves(table, d_mixed[row * row_len + half : (row + 1) * row_len]) * scale
        d_cross = d_second * long_rows[row]
        d_signal.append(
            from_waves(table, conj_times(kernel_low, d_first) + conj_times(kernel_cross, d_cross))
        )
        d_signal.append(from_waves(table, conj_times(kernel_low, d_second)))
        low_grad = low_grad + conj_times(first, d_first) + conj_times(second, d_second)
        cross_grad = cross_grad + conj_times(first, d_cross)
    low_grad = low_grad + turned(cross_grad, -1.0)
    d_kernel = jnp.concatenate([from_waves(table, low_grad), from_waves(table, cross_grad)], axis=0)
    d_signal = jnp.concatenate(d_signal, axis=0)
    d_projected = jnp.concatenate([d_signal, d_gate], axis=1).astype(jnp.bfloat16)
    w_in_grad = jnp.einsum("td,te->de", normed, d_projected, preferred_element_type=jnp.float32)
    d_normed = jnp.einsum("te,de->td", d_projected, w_in, preferred_element_type=jnp.float32)
    ln1_gain_grad = jnp.sum(d_normed * unit_one, axis=0)
    ln1_shift_grad = jnp.sum(d_normed, axis=0)
    input_grad = d_residual + norm_back(d_normed, unit_one, inverse_one, ln1_gain)

    shares = lax.psum_scatter(
        pool(d_kernel).astype(jnp.bfloat16), "narrow", scatter_dimension=0, tiled=True
    )
    summed = lax.psum(shares, "wide").astype(jnp.float32)
    raw_grad = summed * (jnp.abs(raw_taps) > shrink_level).astype(jnp.float32)

    def scatter(values):
        return lax.psum_scatter(
            values.astype(jnp.bfloat16), ("wide", "narrow"), scatter_dimension=0, tiled=True
        ).astype(jnp.float32)

    def scatter_wide(values):
        return lax.psum_scatter(values, ("wide", "narrow"), scatter_dimension=0, tiled=True)

    return (
        block_out,
        input_grad,
        raw_grad,
        scatter_wide(ln1_gain_grad),
        scatter_wide(ln1_shift_grad),
        scatter(w_in_grad),
        scatter(w_out_grad),
        scatter_wide(ln2_gain_grad),
        scatter_wide(ln2_shift_grad),
        scatter(w_up_grad),
        scatter(w_down_grad),
    )


MESH = pl.DeviceIdType.MESH
PART = 9
STORES = 30
VMEM_BYTES = 60 * 2**20
FLIGHTS = 3


def dot_nn(left, right):
    return lax.dot_general(left, right, (((1,), (0,)), ((), ())), preferred_element_type=jnp.float32)


def dot_nt(left, right):
    return lax.dot_general(left, right, (((1,), (1,)), ((), ())), preferred_element_type=jnp.float32)


def dot_tn(left, right):
    return lax.dot_general(left, right, (((0,), (0,)), ((), ())), preferred_element_type=jnp.float32)


def gelu_both(hidden):
    inner = 0.7978845608028654
    cubic = inner * 0.044715
    square = hidden * hidden
    bent = jnp.tanh(hidden * (inner + cubic * square))
    share = 0.5 + 0.5 * bent
    slope = share + (0.5 * hidden) * (1.0 - bent * bent) * (inner + (3.0 * cubic) * square)
    return hidden * share, slope


def column_sums(values):
    rows, width = values.shape
    return jnp.sum(values.reshape(rows // 8, 8, width), axis=0)


class Place:
    def __init__(self, planes):
        wide = lax.axis_index("wide")
        self.narrow = lax.axis_index("narrow")
        self.wide = wide
        self.core = wide % 2
        self.y = (wide // 2) % 2
        self.z = wide // 4
        self.x = self.narrow
        self.planes = planes
        self.sibling = (wide + 1 - 2 * self.core, self.narrow)
        self.next_x = (wide, 1 - self.narrow)
        self.next_y = (wide + 2 - 4 * self.y, self.narrow)

    def plane(self, step):
        other = (self.z + step) % self.planes
        return (self.wide + 4 * (other - self.z), self.narrow), other


class Chunk:
    def __init__(self, place, held, inbox, sems, x_first, target=None):
        self.place = place
        self.views = (held, inbox, sems)
        self.target = target
        self.first, self.second = (place.x, place.y) if x_first else (place.y, place.x)
        self.to_first, self.to_second = (
            (place.next_x, place.next_y) if x_first else (place.next_y, place.next_x)
        )
        self.x_first = x_first

    @property
    def held(self):
        ref, at = self.views[0]
        return ref.at[at]

    @property
    def inbox(self):
        return [ref if at is None else ref.at[at] for ref, at in self.views[1]]

    @property
    def sems(self):
        return [ref.at[at] for ref, at in self.views[2]]

    def slot(self, y, core, x):
        first, second = (x, y) if self.x_first else (y, x)
        return ((core * 2 + first) * 2 + second) * self.place.planes

    def copy(self, stage):
        planes, core = self.place.planes, self.place.core
        first, second = self.first, self.second
        start, count, device = (
            (4 * planes * (1 - core), 4 * planes, self.place.sibling),
            (4 * planes * core + 2 * planes * (1 - first), 2 * planes, self.to_first),
            (4 * planes * core + 2 * planes * first + planes * (1 - second), planes, self.to_second),
        )[stage]
        return pltpu.make_async_remote_copy(
            src_ref=self.held.at[pl.ds(start, count)],
            dst_ref=self.inbox[stage],
            send_sem=self.sems[0].at[stage],
            recv_sem=self.sems[1].at[stage],
            device_id=device,
            device_id_type=MESH,
        )

    def add(self, start, landing, count):
        for index in range(count):
            self.held[start + index] += landing[index]

    def start(self):
        self.copy(0).start()

    def over_core(self):
        planes = self.place.planes
        self.copy(0).wait()
        self.add(4 * planes * self.place.core, self.inbox[0], 4 * planes)
        self.copy(1).start()

    def over_first(self):
        planes = self.place.planes
        self.copy(1).wait()
        self.add(4 * planes * self.place.core + 2 * planes * self.first, self.inbox[1], 2 * planes)
        self.copy(2).start()

    def base(self):
        planes, place = self.place.planes, self.place
        return 4 * planes * place.core + 2 * planes * self.first + planes * self.second

    def plane_copy(self, step):
        device, other = self.place.plane(step)
        if self.target is None:
            return pltpu.make_async_remote_copy(
                src_ref=self.held.at[self.base() + other],
                dst_ref=self.inbox[3].at[step - 1],
                send_sem=self.sems[0].at[2 + step],
                recv_sem=self.sems[1].at[2 + step],
                device_id=device,
                device_id_type=MESH,
            )
        return pltpu.make_async_remote_copy(
            src_ref=self.held.at[pl.ds(self.base(), self.place.planes)],
            dst_ref=self.inbox[3].at[step - 1],
            send_sem=self.sems[0].at[2 + step],
            recv_sem=self.sems[1].at[2 + step],
            device_id=device,
            device_id_type=MESH,
        )

    def each_plane(self, act):
        for step in range(1, self.place.planes):
            if self.target is None:
                act(self.plane_copy(step))
            else:

                @pl.when((self.place.z + step) % self.place.planes == self.target)
                def _():
                    act(self.plane_copy(step))

    def over_second(self):
        self.copy(2).wait()
        planes = self.place.planes
        self.add(self.base(), self.inbox[2], planes)
        if self.target is None:
            self.inbox[3][planes - 1] = self.held[self.base() + self.place.z]
        else:

            @pl.when(self.place.z == self.target)
            def _():
                for index in range(planes):
                    self.inbox[3][planes - 1, index] = self.held[self.base() + index]

        self.each_plane(lambda copy: copy.start())

    def sent(self):
        self.each_plane(lambda copy: copy.wait_send())

    def arrived(self):
        for step in range(1, self.place.planes):
            self.plane_copy(step).wait_recv()

    def total(self, index):
        terms = [
            self.inbox[3][step] if self.target is None else self.inbox[3][step, index]
            for step in range(self.place.planes)
        ]
        return sum(term.astype(jnp.float32) for term in terms)


def store_rows(chunk, values, first_row):
    width = values.shape[1]
    for k in range(values.shape[0] // 24):
        shard = first_row // 24 + k
        z, y, core, x = shard // 8, shard // 4 % 2, shard // 2 % 2, shard % 2
        at = chunk.slot(y, core, x) + z
        block = values[24 * k : 24 * k + 24]
        rest = block[16:24]
        chunk.held[at, :, 0:width] = block[0:16].astype(jnp.bfloat16)
        chunk.held[at, :, width : width + width // 2] = jnp.concatenate(
            [rest[:, : width // 2], rest[:, width // 2 :]], axis=0
        ).astype(jnp.bfloat16)


def load_rows(block, width):
    rest = block[:, width:]
    return jnp.concatenate(
        [block[:, :width], jnp.concatenate([rest[0:8], rest[8:16]], axis=1)], axis=0
    )


def tile_runs(sub, width):
    tiles = width // 128
    runs, tile = [], 0
    while tile < tiles:
        line = sub * tiles + tile
        count = min(tiles - tile, PART - line % PART)
        runs.append((tile, line // PART, line % PART, count))
        tile += count
    return runs


def store_shards(chunk, values, first_row):
    width = values.shape[1]
    for k in range(values.shape[0] // 16):
        row = first_row + 16 * k
        shard, sub = row // 96, row % 96 // 16
        base = chunk.slot(shard // 4, shard // 2 % 2, shard % 2)
        for tile, block, at, count in tile_runs(sub, width):
            chunk.held[base + block, :, 128 * at : 128 * (at + count)] = values[
                16 * k : 16 * k + 16, 128 * tile : 128 * (tile + count)
            ].astype(jnp.bfloat16)


class Taps:
    def __init__(self, place, held, inbox, result, sems, index, rows, cols, x_first):
        self.place, self.held, self.inbox, self.result = place, held, inbox, result
        self.sems, self.index = sems, index
        self.rows = rows
        self.cols = cols
        self.x_first = x_first

    def part(self, x, core, y, plane, count):
        planes = self.place.planes
        return pl.ds((((x * 2 + core) * 2 + y) * planes + plane) * self.rows, count * self.rows)

    def add(self, target, landing):
        self.held[target, self.cols] += landing[...]

    def landing(self, level, first, count):
        return self.inbox[level].at[pl.ds(first * self.rows, count * self.rows), self.cols]

    def copy(self, kind, step=0):
        place, planes = self.place, self.place.planes
        x, core, y, z = place.x, place.core, place.y, place.z
        if kind == "core":
            source, landing = self.part(step, 1 - core, 0, 0, 2 * planes), self.landing(0, step * 2 * planes, 2 * planes)
            stage, device = step, place.sibling
        elif kind == "first" and self.x_first:
            source, landing = self.part(1 - x, core, 0, 0, 2 * planes), self.landing(1, 0, 2 * planes)
            stage, device = 2, place.next_x
        elif kind == "first":
            source, landing = self.part(step, core, 1 - y, 0, planes), self.landing(1, step * planes, planes)
            stage, device = 2 + step, place.next_y
        elif kind == "second":
            first = self.part(x, core, 1 - y, 0, planes) if self.x_first else self.part(1 - x, core, y, 0, planes)
            source, landing = first, self.landing(2, 0, planes)
            stage, device = 4, place.next_y if self.x_first else place.next_x
        elif kind == "plane":
            device, other = place.plane(step)
            source, landing = self.part(x, core, y, other, 1), self.landing(3, step - 1, 1)
            stage = 4 + step
        else:
            if kind == "back plane":
                mine, stage, device = (0, core, y, z, 1), 3 + planes + step, place.plane(step)[0]
            elif kind == "back y":
                mine, stage, device = (0, core, y, 0, planes), 3 + 2 * planes, place.next_y
            else:
                mine, stage, device = (0, core, 0, 0, 2 * planes), 4 + 2 * planes, place.sibling
            landing = self.result.at[self.part(*mine), self.cols]
        return pltpu.make_async_remote_copy(
            src_ref=landing if kind.startswith("back") else self.held.at[source, self.cols],
            dst_ref=landing,
            send_sem=self.sems[0].at[self.index, stage],
            recv_sem=self.sems[1].at[self.index, stage],
            device_id=device,
            device_id_type=MESH,
        )

    def start(self):
        for x in range(2):
            self.copy("core", x).start()

    def over_core(self):
        for x in range(2):
            self.copy("core", x).wait()
            self.add(
                self.part(x, self.place.core, 0, 0, 2 * self.place.planes),
                self.landing(0, x * 2 * self.place.planes, 2 * self.place.planes),
            )
        for step in range(1 if self.x_first else 2):
            self.copy("first", step).start()

    def over_first(self):
        place, planes = self.place, self.place.planes
        if self.x_first:
            self.copy("first").wait()
            self.add(self.part(place.x, place.core, 0, 0, 2 * planes), self.landing(1, 0, 2 * planes))
        else:
            for x in range(2):
                self.copy("first", x).wait()
                self.add(self.part(x, place.core, place.y, 0, planes), self.landing(1, x * planes, planes))
        self.copy("second").start()

    def over_second(self):
        place = self.place
        self.copy("second").wait()
        self.add(self.part(place.x, place.core, place.y, 0, place.planes), self.landing(2, 0, place.planes))
        for step in range(1, place.planes):
            self.copy("plane", step).start()

    def over_planes(self):
        place = self.place
        mine = self.part(place.x, place.core, place.y, place.z, 1)
        total = self.held[mine, self.cols].astype(jnp.float32)
        for step in range(1, place.planes):
            self.copy("plane", step).wait()
            total = total + self.landing(3, step - 1, 1)[...].astype(jnp.float32)
        self.result[self.part(0, place.core, place.y, place.z, 1), self.cols] = total.astype(self.result.dtype)
        for step in range(1, place.planes):
            self.copy("back plane", step).start()

    def back_y(self):
        for step in range(1, self.place.planes):
            self.copy("back plane", step).wait()
        self.copy("back y").start()

    def back_core(self):
        self.copy("back y").wait()
        self.copy("back core").start()

    def finish(self):
        self.copy("back core").wait()


class Sums:
    def __init__(self, place, levels, inbox, sems):
        self.place, self.levels, self.inbox, self.sems = place, levels, inbox, sems

    def copy(self, level, step=0):
        place = self.place
        device = (place.sibling, place.next_x, place.next_y)[level] if level < 3 else place.plane(step)[0]
        landing = level + max(step - 1, 0)
        return pltpu.make_async_remote_copy(
            src_ref=self.levels.at[level],
            dst_ref=self.inbox.at[landing],
            send_sem=self.sems[0].at[landing],
            recv_sem=self.sems[1].at[landing],
            device_id=device,
            device_id_type=MESH,
        )

    def start(self):
        self.copy(0).start()

    def over(self, level):
        self.copy(level).wait()
        self.levels[level + 1] = self.levels[level] + self.inbox[level]
        if level < 2:
            self.copy(level + 1).start()
        else:
            for step in range(1, self.place.planes):
                self.copy(3, step).start()

    def finish(self):
        total = self.levels[3]
        for step in range(1, self.place.planes):
            self.copy(3, step).wait()
            total = total + self.inbox[2 + step]
        return total


def block_kernel(
    planes,
    lengths,
    tokens, cotangent, raw_taps, w_in, w_out, w_up, w_down, table, table_t,
    ln1_gain, ln1_shift, ln2_gain, ln2_shift,
    block_out, input_grad, taps_out, sums_out, w_in_grad, w_out_grad, w_up_grad, w_down_grad,
    held, inbox0, inbox1, inbox2, inbox_u, inbox_n, taps_held, taps0, taps1, taps2, taps3, taps_sum,
    levels, sums_inbox, cot, active, running, branch_v, normed_v, w_out_v,
    gate_v, mixed_v, left_v, waves, kernels,
    send_sems, recv_sems, taps_send, taps_recv, sums_send, sums_recv, share_send, share_recv, load_sems,
):
    tok_count, feat = cot.shape
    half = tok_count // 2
    tile = active.shape[2]
    step_rows = tap_cols = 256
    blocks = feat // tap_cols
    row_steps = tok_count // step_rows
    place = Place(planes)

    loads = {}

    class Load:
        def __init__(self, source, target):
            self.ends, self.at = (source, target), len(loads)

        def copy(self):
            source, target = (end() if callable(end) else end for end in self.ends)
            return pltpu.make_async_copy(source, target, load_sems.at[self.at])

        def wait(self):
            self.copy().wait()

    def load(name, source, target):
        loads[name] = Load(source, target)
        loads[name].copy().start()

    barrier = pltpu.get_barrier_semaphore()
    partners = [place.sibling, place.next_x, place.next_y] + [
        place.plane(step)[0] for step in range(1, planes)
    ]
    for partner in partners:
        pl.semaphore_signal(barrier, inc=1, device_id=partner, device_id_type=MESH)
    long = jnp.where(lengths[0] > half, 1.0, 0.0).astype(jnp.float32)

    def chunk(index, step, kind, target=None):
        at = step % FLIGHTS * 2 + kind
        ring = step % 2 * 2 + kind
        if target is None:
            far = (inbox_u, index // 2 if index < 2 * planes else index - planes)
        else:
            far = (inbox_n, None)
        return Chunk(
            place,
            (held, at),
            ((inbox0, ring), (inbox1, ring), (inbox2, ring), far),
            ((send_sems, index), (recv_sems, index)),
            kind == 0,
            target,
        )

    ups = [chunk(2 * t, t, 0) for t in range(planes)]
    downs = [chunk(2 * t + 1, t, 1, t) for t in range(planes)]

    def rows_of(index):
        return pl.ds(index * step_rows, step_rows)

    def unrolled(first, last, body, carry):
        for index in range(first, last):
            carry = body(index, carry)
        return carry

    def norm_of(values):
        centered = values - jnp.mean(values, axis=-1, keepdims=True)
        inverse = lax.rsqrt(jnp.mean(centered * centered, axis=-1, keepdims=True) + eps_norm)
        return centered * inverse, inverse

    out_chunk = chunk(2 * planes, planes, 0)
    gate_chunk = chunk(2 * planes + 1, planes, 1)
    signal_chunk = chunk(2 * planes + 2, planes + 1, 0)
    taps = [
        Taps(
            place, taps_held, (taps0, taps1, taps2, taps3), taps_sum, (taps_send, taps_recv), index,
            tok_count // (8 * planes), pl.ds(index * tap_cols, tap_cols), index % 2 == 0,
        )
        for index in range(feat // tap_cols)
    ]
    sums = Sums(place, levels, sums_inbox, (sums_send, sums_recv))

    def own_rows(target):
        target.arrived()
        return load_rows(target.total(0), feat)

    def own_down(t):
        @pl.when(place.z == t)
        def _():
            downs[t].arrived()
            for index in range(planes):
                block = downs[t].total(index)
                for sub in range(6):
                    for first, line, at, count in tile_runs(sub, feat):
                        if line == index:
                            w_down_grad[16 * sub : 16 * sub + 16, 128 * first : 128 * (first + count)] = block[
                                :, 128 * at : 128 * (at + count)
                            ]

    def weight_rows(target, left_t, right):
        for part in range(2):
            rows = feat // 2
            store_rows(target, dot_nn(left_t[part * rows : (part + 1) * rows, :], right[...]), part * rows)
        target.start()

    def own_up(t):
        w_up_grad[:, t * tile : (t + 1) * tile] = own_rows(ups[t])

    def own_out():
        w_out_grad[...] = own_rows(out_chunk)

    def own_gate():
        w_in_grad[:, feat:] = own_rows(gate_chunk)

    def own_signal():
        w_in_grad[:, 0:feat] = own_rows(signal_chunk)

    def taps_copy(index):
        cols = pl.ds(index * tap_cols, tap_cols)
        return pltpu.make_async_copy(taps_sum.at[:, cols], taps_out.at[:, cols], load_sems.at[STORES - 1 - index])

    def own_taps(index):
        taps[index].finish()
        taps_copy(index).start()

    def share_copy(which, across):
        block = half // 2
        block_x = place.x if which == 0 else 1 - place.x
        rows = pl.ds(pl.multiple_of(block_x * half + place.core * block, block), block)
        part = taps_held.at[rows, pl.ds(across * tap_cols, tap_cols)]
        return pltpu.make_async_remote_copy(
            src_ref=part,
            dst_ref=part,
            send_sem=share_send.at[which, across],
            recv_sem=share_recv.at[which, across],
            device_id=place.next_x if which == 0 else place.sibling,
            device_id_type=MESH,
        )

    def share_on(across):
        share_copy(0, across).wait()
        share_copy(1, across).start()

    def forward_back(normed_2, normed_2t, up_tiles, down_tiles):
        def load_tile(t):
            cols = pl.ds(t * tile, tile)
            load(("up", t), lambda: w_up.at[:, cols], lambda: up_tiles.at[t % 2])
            load(("down", t), lambda: w_down.at[cols, :], lambda: down_tiles.at[t % 2])

        def mix(w_in_v, table_v, table_tv):
            kernel = mixed_v
            load("taps", raw_taps, running.at[0:half, :])
            load("tokens", tokens, lambda: active.at[0])
            load("w_in", w_in, w_in_v)
            load("table", table, table_v)
            load("table_t", table_t, table_tv)
            load("w_out", w_out, w_out_v)
            load_tile(0)
            load("cot", cotangent, cot)

            loads["taps"].wait()

            def squash_step(index, carry):
                rows = pl.ds(pl.multiple_of(index * 128, 128), 128)
                raw = running[rows, :]
                taps_held[pl.ds(pl.multiple_of(place.x * half + index * 128, 128), 128), :] = (
                    raw - jnp.clip(raw, -shrink_level, shrink_level)
                ).astype(jnp.bfloat16)
                return carry

            lax.fori_loop(0, half // 128, squash_step, 0)
            pl.semaphore_wait(barrier, len(partners))
            for across in range(blocks):
                share_copy(0, across).start()
            loads["tokens"].wait()
            loads["w_in"].wait()

            def project_step(index, carry):
                rows = rows_of(index)
                unit, _ = norm_of(active[0, rows, :].astype(jnp.float32))
                low = (unit * ln1_gain[...][None, :] + ln1_shift[...][None, :]).astype(jnp.bfloat16)
                normed_v[:, rows] = low.T
                active[1, rows, :] = dot_nn(low, w_in_v[:, 0:feat]).astype(jnp.bfloat16)
                gate_v[rows, :] = dot_nn(low, w_in_v[:, feat:]).astype(jnp.bfloat16)
                return carry

            unrolled(0, row_steps, project_step, 0)
            share_on(0)
            loads["table"].wait()

            def signal_wave_step(index, carry):
                rows = rows_of(index)
                for which in range(2):
                    waves[which, rows, :] = dot_nn(
                        table_v[rows, :], active[1, which * half : (which + 1) * half, :]
                    ).astype(jnp.bfloat16)
                return carry

            unrolled(0, row_steps, signal_wave_step, 0)
            pool_rows = 128

            def pool_step(across):
                cols = slice(across * tap_cols, (across + 1) * tap_cols)
                rim = jnp.zeros((16, tap_cols), jnp.float32)
                for index in range(tok_count // pool_rows):
                    at = index * pool_rows
                    first, last = max(at - 16, 0), min(at + pool_rows + 16, tok_count)
                    around = taps_held[first:last, cols].astype(jnp.float32)
                    if at == 0:
                        around = jnp.concatenate([rim, around], axis=0)
                    if last == tok_count:
                        around = jnp.concatenate([around, rim], axis=0)
                    kernel[at : at + pool_rows, cols] = (
                        (around[15 : 15 + pool_rows] + around[16 : 16 + pool_rows] + around[17 : 17 + pool_rows])
                        / 3.0
                    ).astype(jnp.bfloat16)

            def spread_step(down, across):
                real, imag = pl.ds(down * 256, 256), pl.ds(half + down * 256, 256)
                cols = pl.ds(across * 256, 256)
                low_r = dot_nn(table_v[real, :], kernel[0:half, cols])
                low_i = dot_nn(table_v[imag, :], kernel[0:half, cols])
                high_r = dot_nn(table_v[real, :], kernel[half:, cols])
                high_i = dot_nn(table_v[imag, :], kernel[half:, cols])
                odd = lax.broadcasted_iota(jnp.int32, (256, 1), 0) % 2
                parity = (1 - 2 * odd).astype(jnp.float32)
                cross_r = long * (high_r - parity * low_i)
                cross_i = long * (high_i + parity * low_r)
                kernels[0, real, cols] = low_r.astype(jnp.bfloat16)
                kernels[0, imag, cols] = low_i.astype(jnp.bfloat16)
                kernels[1, real, cols] = cross_r.astype(jnp.bfloat16)
                kernels[1, imag, cols] = cross_i.astype(jnp.bfloat16)
                head_r = waves[0, real, cols].astype(jnp.float32)
                head_i = waves[0, imag, cols].astype(jnp.float32)
                tail_r = waves[1, real, cols].astype(jnp.float32)
                tail_i = waves[1, imag, cols].astype(jnp.float32)
                scale = 1.0 / half
                active[2, real, cols] = ((low_r * head_r - low_i * head_i) * scale).astype(jnp.bfloat16)
                active[2, imag, cols] = ((low_r * head_i + low_i * head_r) * scale).astype(jnp.bfloat16)
                active[3, real, cols] = (
                    (low_r * tail_r - low_i * tail_i + cross_r * head_r - cross_i * head_i) * scale
                ).astype(jnp.bfloat16)
                active[3, imag, cols] = (
                    (low_r * tail_i + low_i * tail_r + cross_r * head_i + cross_i * head_r) * scale
                ).astype(jnp.bfloat16)

            share_on(1)
            for across in range(blocks):
                share_copy(1, across).wait()
                pool_step(across)
                for down in range(half // 256):
                    spread_step(down, across)
                if across + 2 < blocks:
                    share_on(across + 2)
            loads["table_t"].wait()
            loads["w_out"].wait()

            def residual_step(index, carry):
                rows = rows_of(index)
                part_steps = half // step_rows
                which = index // part_steps
                of_part = pl.ds(index % part_steps * step_rows, step_rows)
                mixed = dot_nn(table_tv[of_part, :], active[2 + which])
                mixed_v[rows, :] = mixed.astype(jnp.bfloat16)
                branch = (mixed * gate_v[rows, :].astype(jnp.float32)).astype(jnp.bfloat16)
                branch_v[:, rows] = branch.T
                left = active[0, rows, :].astype(jnp.float32) + dot_nn(branch, w_out_v[...])
                left_v[rows, :] = left
                unit, _ = norm_of(left)
                low = (unit * ln2_gain[...][None, :] + ln2_shift[...][None, :]).astype(jnp.bfloat16)
                normed_2[rows, :] = low
                normed_2t[:, rows] = low.T
                return carry

            unrolled(0, row_steps, residual_step, 0)

        pl.run_scoped(
            mix,
            pltpu.VMEM((feat, 2 * feat), jnp.bfloat16),
            pltpu.VMEM((tok_count, half), jnp.bfloat16),
            pltpu.VMEM((half, tok_count), jnp.bfloat16),
        )

        def feed_forward(d_hidden):
            loads["cot"].wait()

            def rows_piece(t, index):
                up_tile, down_tile = up_tiles.at[t % 2], down_tiles.at[t % 2]
                if index == 0:
                    loads["up", t].wait()
                    loads["down", t].wait()
                    if t + 1 < planes:
                        load_tile(t + 1)
                rows = rows_of(index)
                hidden = dot_nn(normed_2[rows, :], up_tile[...])
                d_active = dot_nt(cot[rows, :], down_tile[...])
                value, slope = gelu_both(hidden)
                active[t, rows, :] = value.astype(jnp.bfloat16)
                d_value = (d_active * slope).astype(jnp.bfloat16)
                d_hidden[rows, :] = d_value
                back = dot_nt(d_value, up_tile[...])
                if t == 0:
                    running[rows, :] = back
                else:
                    running[rows, :] += back

            def up_piece(t):
                if t >= FLIGHTS:
                    ups[t - FLIGHTS].sent()
                weight_rows(ups[t], normed_2t, d_hidden)

            def down_piece(t):
                if t >= FLIGHTS:
                    downs[t - FLIGHTS].sent()
                for part in range(2):
                    cols = slice(part * (tile // 2), (part + 1) * (tile // 2))
                    store_shards(downs[t], dot_tn(active[t, :, cols], cot[...]), part * (tile // 2))
                downs[t].start()

            rows_piece(0, 0)
            rows_piece(0, 1)
            rows_piece(0, 2)
            rows_piece(0, 3)
            down_piece(0)
            up_piece(0)
            rows_piece(1, 0)
            rows_piece(1, 1)
            downs[0].over_core()
            ups[0].over_core()
            rows_piece(1, 2)
            rows_piece(1, 3)
            down_piece(1)
            up_piece(1)
            rows_piece(2, 0)
            downs[0].over_first()
            downs[1].over_core()
            ups[0].over_first()
            ups[1].over_core()
            rows_piece(2, 1)
            rows_piece(2, 2)
            rows_piece(2, 3)
            down_piece(2)
            up_piece(2)
            rows_piece(3, 0)
            downs[0].over_second()
            downs[1].over_first()
            downs[2].over_core()
            rows_piece(3, 1)
            rows_piece(3, 2)
            ups[0].over_second()
            ups[1].over_first()
            ups[2].over_core()
            rows_piece(3, 3)
            down_piece(3)
            up_piece(3)

        pl.run_scoped(feed_forward, pltpu.VMEM((tok_count, tile), jnp.bfloat16))

    pl.run_scoped(
        forward_back,
        pltpu.VMEM((tok_count, feat), jnp.bfloat16),
        pltpu.VMEM((feat, tok_count), jnp.bfloat16),
        pltpu.VMEM((2, feat, tile), jnp.bfloat16),
        pltpu.VMEM((2, tile, feat), jnp.bfloat16),
    )

    def backward(d_out, d_gate, d_mix, d_signal, table_v, table_tv, d_kernel, d_taps):
        d_waves = waves
        load("table again", table, table_v)
        load("table_t again", table_t, table_tv)
        totals = {}

        def sum_rows(at, index, values):
            totals[at] = column_sums(values) + (totals[at] if index > 0 else 0.0)
            if index == row_steps - 1:
                levels[0, at : at + 1, :] = jnp.sum(totals[at], axis=0, keepdims=True)

        def back_piece(index):
            if index == 0:
                levels[0] = jnp.zeros(levels.shape[1:], jnp.float32)
            rows = rows_of(index)
            left = left_v[rows, :]
            centered = left - jnp.mean(left, axis=-1, keepdims=True)
            inverse = lax.rsqrt(jnp.mean(centered * centered, axis=-1, keepdims=True) + eps_norm)
            unit = centered * inverse
            grad = running[rows, :]
            scaled = grad * ln2_gain[...][None, :]
            d_left = cot[rows, :].astype(jnp.float32) + inverse * (
                scaled
                - jnp.mean(scaled, axis=-1, keepdims=True)
                - unit * jnp.mean(scaled * unit, axis=-1, keepdims=True)
            )
            running[rows, :] = d_left
            d_low = d_left.astype(jnp.bfloat16)
            d_out[rows, :] = d_low
            d_branch = dot_nt(d_low, w_out_v[...])
            d_mix[rows, :] = (
                d_branch * gate_v[rows, :].astype(jnp.float32) * (1.0 / half)
            ).astype(jnp.bfloat16)
            d_gate[rows, :] = (d_branch * mixed_v[rows, :].astype(jnp.float32)).astype(jnp.bfloat16)
            sum_rows(0, index, grad * unit)
            sum_rows(1, index, grad)
            if index == row_steps - 1:
                load("tokens again", tokens, gate_v)

        def gate_piece():
            downs[planes - 3].sent()
            weight_rows(gate_chunk, normed_v, d_gate)

        def out_piece():
            ups[planes - 3].sent()
            weight_rows(out_chunk, branch_v, d_out)

        def signal_piece():
            ups[planes - 2].sent()
            weight_rows(signal_chunk, normed_v, d_signal)

        wave_rows, wave_cols = 256, 256

        def wave_step(down, cols):
            real, imag = pl.ds(down * wave_rows, wave_rows), pl.ds(half + down * wave_rows, wave_rows)
            first_r = dot_nn(table_v[real, :], d_mix[0:half, cols])
            first_i = dot_nn(table_v[imag, :], d_mix[0:half, cols])
            second_r = dot_nn(table_v[real, :], d_mix[half:, cols])
            second_i = dot_nn(table_v[imag, :], d_mix[half:, cols])

            def wide(ref, which, rows):
                return ref[which, rows, cols].astype(jnp.float32)

            def keep(ref, which, rows, values):
                at = cols if ref.shape[2] == feat else slice(None)
                ref[which, rows, at] = values.astype(jnp.bfloat16)

            low_r, low_i = wide(kernels, 0, real), wide(kernels, 0, imag)
            cross_r, cross_i = wide(kernels, 1, real), wide(kernels, 1, imag)
            head_r, head_i = wide(waves, 0, real), wide(waves, 0, imag)
            tail_r, tail_i = wide(waves, 1, real), wide(waves, 1, imag)
            keep(d_waves, 0, real, low_r * first_r + low_i * first_i + cross_r * second_r + cross_i * second_i)
            keep(d_waves, 0, imag, low_r * first_i - low_i * first_r + cross_r * second_i - cross_i * second_r)
            keep(d_waves, 1, real, low_r * second_r + low_i * second_i)
            keep(d_waves, 1, imag, low_r * second_i - low_i * second_r)
            far_r = (head_r * second_r + head_i * second_i) * long
            far_i = (head_r * second_i - head_i * second_r) * long
            odd = lax.broadcasted_iota(jnp.int32, (wave_rows, 1), 0) % 2
            parity = (1 - 2 * odd).astype(jnp.float32)
            keep(d_kernel, 1, real, far_r)
            keep(d_kernel, 1, imag, far_i)
            keep(
                d_kernel,
                0,
                real,
                head_r * first_r + head_i * first_i + tail_r * second_r + tail_i * second_i + parity * far_i,
            )
            keep(
                d_kernel,
                0,
                imag,
                head_r * first_i - head_i * first_r + tail_r * second_i - tail_i * second_r - parity * far_r,
            )

        pad = 8
        d_taps[0:pad, :] = jnp.zeros((pad, wave_cols), jnp.float32)
        d_taps[pad + tok_count :, :] = jnp.zeros((pad, wave_cols), jnp.float32)
        pool_rows = 128

        def column_step(across):
            cols = pl.ds(across * wave_cols, wave_cols)
            for down in range(half // wave_rows):
                wave_step(down, cols)
            for which in range(2):
                d_taps[pad + which * half : pad + (which + 1) * half, :] = dot_nn(table_tv[...], d_kernel[which])
            for index in range(tok_count // pool_rows):
                at = pad + index * pool_rows
                taps_held[at - pad : at - pad + pool_rows, cols] = (
                    (
                        d_taps[at - 1 : at - 1 + pool_rows, :]
                        + d_taps[at : at + pool_rows, :]
                        + d_taps[at + 1 : at + 1 + pool_rows, :]
                    )
                    / 3.0
                ).astype(jnp.bfloat16)


        def column_piece(across):
            if across == 0:
                loads["table again"].wait()
                loads["table_t again"].wait()
            column_step(across)
            taps[across].start()
            if across == blocks - 1:
                load("w_in signal", w_in.at[:, 0:feat], cot.at[0:feat, :])
                load("w_in gate", w_in.at[:, feat : 2 * feat], d_mix.at[0:feat, :])

        def down_again(t):
            return (waves if t < 2 else kernels).at[t % 2, 0:tile, :]

        def load_again(t):
            rows = pl.ds(t * tile, tile)
            load(("again", t), lambda: w_down.at[rows, :], lambda: down_again(t))

        def unwave_piece(which):
            for at in range(0, half, step_rows):
                d_signal[which * half + at : which * half + at + step_rows, :] = dot_nn(
                    table_tv[at : at + step_rows, :], d_waves[which]
                ).astype(jnp.bfloat16)
            if which == 1:
                for t in range(planes):
                    load_again(t)

        def grad_copy(index):
            rows = rows_of(index)
            return pltpu.make_async_copy(
                running.at[rows, :], input_grad.at[rows, :], load_sems.at[STORES + index]
            )

        def out_copy(index):
            rows = rows_of(index)
            return pltpu.make_async_copy(
                mixed_v.at[rows, :], block_out.at[rows, :], load_sems.at[STORES + row_steps + index]
            )

        def input_piece(index):
            if index == 0:
                loads["tokens again"].wait()
                loads["w_in signal"].wait()
                loads["w_in gate"].wait()
            rows = rows_of(index)
            d_normed = dot_nt(d_signal[rows, :], cot[0:feat, :]) + dot_nt(
                d_gate[rows, :], d_mix[0:feat, :]
            )
            values = gate_v[rows, :].astype(jnp.float32)
            centered = values - jnp.mean(values, axis=-1, keepdims=True)
            inverse = lax.rsqrt(jnp.mean(centered * centered, axis=-1, keepdims=True) + eps_norm)
            unit = centered * inverse
            scaled = d_normed * ln1_gain[...][None, :]

            running[rows, :] = running[rows, :] + inverse * (
                scaled
                - jnp.mean(scaled, axis=-1, keepdims=True)
                - unit * jnp.mean(scaled * unit, axis=-1, keepdims=True)
            )
            grad_copy(index).start()
            sum_rows(2, index, d_normed * unit)
            sum_rows(3, index, d_normed)

        def output_piece(index):
            if index == 0:
                for t in range(planes):
                    loads["again", t].wait()
            rows = rows_of(index)
            total = left_v[rows, :]
            for t in range(planes):
                total = total + dot_nn(active[t, rows, :], down_again(t)[...])
            mixed_v[rows, :] = total.astype(jnp.bfloat16)
            out_copy(index).start()

        back_piece(0)
        downs[1].over_second()
        downs[2].over_first()
        downs[3].over_core()
        back_piece(1)
        back_piece(2)
        ups[1].over_second()
        ups[2].over_first()
        ups[3].over_core()
        back_piece(3)
        column_piece(0)
        downs[2].over_second()
        out_piece()
        taps[0].over_core()
        column_piece(1)
        ups[2].over_second()
        downs[3].over_first()
        ups[3].over_first()
        column_piece(2)
        taps[1].over_core()
        out_chunk.over_core()
        gate_piece()
        taps[2].over_core()
        taps[0].over_first()
        ups[3].over_second()
        unwave_piece(0)
        gate_chunk.over_core()
        taps[1].over_first()
        taps[0].over_second()
        downs[3].over_second()
        unwave_piece(1)
        signal_piece()
        input_piece(0)
        out_chunk.over_first()
        taps[0].over_planes()
        own_up(3)
        signal_chunk.over_core()
        taps[2].over_first()
        input_piece(1)
        output_piece(0)
        input_piece(2)
        taps[1].over_second()
        taps[2].over_second()
        out_chunk.over_second()
        gate_chunk.over_first()
        taps[0].back_y()
        input_piece(3)
        sums.start()
        taps[1].over_planes()
        own_up(1)
        own_down(2)
        own_up(2)
        own_down(0)
        signal_chunk.over_first()
        taps[0].back_core()
        taps[2].over_planes()
        output_piece(1)
        gate_chunk.over_second()
        own_taps(0)
        taps[1].back_y()
        sums.over(0)
        own_down(1)
        sums.over(1)
        signal_chunk.over_second()
        own_out()
        taps[2].back_y()
        own_up(0)
        output_piece(2)
        taps[1].back_core()
        sums.over(2)
        own_gate()
        taps[2].back_core()
        own_down(3)
        output_piece(3)
        own_taps(1)
        own_taps(2)
        own_signal()
        for index in range(row_steps):
            grad_copy(index).wait()
            out_copy(index).wait()

    pl.run_scoped(
        backward,
        *[pltpu.VMEM((tok_count, feat), jnp.bfloat16)] * 4,
        pltpu.VMEM((tok_count, half), jnp.bfloat16),
        pltpu.VMEM((half, tok_count), jnp.bfloat16),
        pltpu.VMEM((2, tok_count, tap_cols), jnp.bfloat16),
        pltpu.VMEM((tok_count + 16, tap_cols), jnp.float32),
    )

    sums_out[...] = sums.finish()
    for one in (downs[planes - 2], ups[planes - 1], downs[planes - 1], out_chunk, gate_chunk, signal_chunk):
        one.sent()
    for index in range(blocks):
        taps_copy(index).wait()


def hand_on_kernel(raw_taps, taps_sum, *others):
    count = (len(others) - 5) // 2
    sources, raw_grad, targets = others[:count], others[count], others[count + 1 : 2 * count + 1]
    raw_v, taps_v, grad_v, sems = others[2 * count + 1 :]
    fetch = [
        pltpu.make_async_copy(source, target, sems.at[index])
        for index, (source, target) in enumerate(((taps_sum, taps_v), (raw_taps, raw_v)))
    ]
    copies = []
    for source, target in zip(sources, targets):
        rows = source.shape[0]
        parts = 4 if rows % 64 == 0 else 1
        for part in range(parts):
            at = pl.ds(part * (rows // parts), rows // parts)
            copies.append(pltpu.make_async_copy(source.at[at, :], target.at[at, :], sems.at[3 + len(copies)]))
    for copy in fetch + copies:
        copy.start()
    for copy in fetch:
        copy.wait()
    grad_v[...] = jnp.where(jnp.abs(raw_v[...]) > shrink_level, taps_v[...].astype(jnp.float32), 0.0)
    store = pltpu.make_async_copy(grad_v, raw_grad, sems.at[2])
    store.start()
    for copy in copies + [store]:
        copy.wait()


def hand_on(raw_taps, taps_sum, *sources):
    whole = pl.BlockSpec(memory_space=pl.ANY)
    return pl.pallas_call(
        hand_on_kernel,
        out_shape=[jax.ShapeDtypeStruct(raw_taps.shape, jnp.float32)]
        + [jax.ShapeDtypeStruct(source.shape, source.dtype) for source in sources],
        in_specs=[whole] * (2 + len(sources)),
        out_specs=[whole] * (1 + len(sources)),
        scratch_shapes=[
            pltpu.VMEM(raw_taps.shape, jnp.float32),
            pltpu.VMEM(taps_sum.shape, taps_sum.dtype),
            pltpu.VMEM(raw_taps.shape, jnp.float32),
            pltpu.SemaphoreType.DMA((3 + 4 * len(sources),)),
        ],
        compiler_params=pltpu.CompilerParams(vmem_limit_bytes=VMEM_BYTES),
    )(raw_taps, taps_sum, *sources)


def linked_block(
    planes,
    tokens,
    lengths,
    raw_taps,
    ln1_gain,
    ln1_shift,
    w_in,
    w_out,
    ln2_gain,
    ln2_shift,
    w_up,
    w_down,
    cotangent,
):
    tok_count, feat = tokens.shape
    half = tok_count // 2
    tile = w_up.shape[1] // planes
    table = jnp.asarray(wave_table(half), jnp.bfloat16)
    table_t = jnp.asarray(wave_table(half).T, jnp.bfloat16)
    shares = 8 * planes
    rows = feat // shares
    block = (16, 128 * PART)
    chunks = 2 * planes + 3
    bf16, f32 = jnp.bfloat16, jnp.float32
    whole = pl.BlockSpec(memory_space=pl.ANY)
    near = pl.BlockSpec(memory_space=pltpu.VMEM)
    results = pl.pallas_call(
        functools.partial(block_kernel, planes),
        out_shape=(
            jax.ShapeDtypeStruct((tok_count, feat), bf16),
            jax.ShapeDtypeStruct((tok_count, feat), f32),
            jax.ShapeDtypeStruct((half, feat), bf16),
            jax.ShapeDtypeStruct((8, feat), f32),
            jax.ShapeDtypeStruct((rows, 2 * feat), f32),
            jax.ShapeDtypeStruct((rows, feat), f32),
            jax.ShapeDtypeStruct((rows, planes * tile), f32),
            jax.ShapeDtypeStruct((tile // 8, feat), f32),
        ),
        in_specs=[pl.BlockSpec(memory_space=pltpu.SMEM)] + [whole] * 9 + [near] * 4,
        out_specs=(whole,) * 3 + (near,) * 5,
        scratch_shapes=[
            pltpu.VMEM((2 * FLIGHTS, shares) + block, bf16),
            pltpu.VMEM((4, 4 * planes) + block, bf16),
            pltpu.VMEM((4, 2 * planes) + block, bf16),
            pltpu.VMEM((4, planes) + block, bf16),
            pltpu.VMEM((planes + 3, planes) + block, bf16),
            pltpu.VMEM((planes, planes) + block, bf16),
            pltpu.VMEM((tok_count, feat), bf16),
            pltpu.VMEM((tok_count // 2, feat), bf16),
            pltpu.VMEM((tok_count // 4, feat), bf16),
            pltpu.VMEM((tok_count // 8, feat), bf16),
            pltpu.VMEM(((planes - 1) * (tok_count // shares), feat), bf16),
            pltpu.VMEM((half, feat), bf16),
            pltpu.VMEM((4, 8, feat), f32),
            pltpu.VMEM((planes + 2, 8, feat), f32),
            pltpu.VMEM((tok_count, feat), bf16),
            pltpu.VMEM((planes, tok_count, tile), bf16),
            pltpu.VMEM((tok_count, feat), f32),
            pltpu.VMEM((feat, tok_count), bf16),
            pltpu.VMEM((feat, tok_count), bf16),
            pltpu.VMEM((feat, feat), bf16),
            pltpu.VMEM((tok_count, feat), bf16),
            pltpu.VMEM((tok_count, feat), bf16),
            pltpu.VMEM((tok_count, feat), f32),
            pltpu.VMEM((2, tok_count, feat), bf16),
            pltpu.VMEM((2, tok_count, feat), bf16),
            pltpu.SemaphoreType.DMA((chunks, planes + 2)),
            pltpu.SemaphoreType.DMA((chunks, planes + 2)),
            pltpu.SemaphoreType.DMA((feat // 256, 2 * planes + 5)),
            pltpu.SemaphoreType.DMA((feat // 256, 2 * planes + 5)),
            pltpu.SemaphoreType.DMA((planes + 2,)),
            pltpu.SemaphoreType.DMA((planes + 2,)),
            pltpu.SemaphoreType.DMA((2, feat // 256)),
            pltpu.SemaphoreType.DMA((2, feat // 256)),
            pltpu.SemaphoreType.DMA((STORES + 2 * tok_count // 256,)),
        ],
        compiler_params=pltpu.CompilerParams(
            collective_id=1, has_side_effects=True, vmem_limit_bytes=VMEM_BYTES
        ),
        cost_estimate=pl.CostEstimate(
            flops=2 * tok_count * feat * (5 * w_up.shape[1] + 9 * feat),
            bytes_accessed=40 * tok_count * feat,
            transcendentals=tok_count * w_up.shape[1],
        ),
    )(
        lengths,
        tokens,
        cotangent,
        raw_taps,
        w_in,
        w_out,
        w_up,
        w_down,
        table,
        table_t,
        ln1_gain,
        ln1_shift,
        ln2_gain,
        ln2_shift,
    )
    block_out, input_grad, taps_sum, sums, w_in_grad, w_out_grad, w_up_grad, w_down_grad = results
    raw_grad, block_out, input_grad, w_in_grad, w_out_grad, w_up_grad, w_down_grad = hand_on(
        raw_taps, taps_sum, block_out, input_grad, w_in_grad, w_out_grad, w_up_grad, w_down_grad
    )
    share = lax.axis_index("wide") * 2 + lax.axis_index("narrow")
    mine = lax.dynamic_slice(sums, (0, share * rows), (8, rows))
    return (
        block_out,
        input_grad,
        raw_grad,
        mine[2],
        mine[3],
        w_in_grad,
        w_out_grad,
        mine[0],
        mine[1],
        w_up_grad,
        w_down_grad,
    )


def solution(mesh):
    spread = P(("wide", "narrow"))
    rows = P(("wide", "narrow"), None)
    placed = (rows, spread, P("narrow", None)) + (P(),) * 8 + (rows,)
    wide, narrow = mesh.shape["wide"], mesh.shape["narrow"]

    def block(tokens, lengths, raw_taps, *others):
        fits = (
            narrow == 2
            and wide == 4 * 4
            and lengths.shape[0] == 1
            and raw_taps.shape[0] * 2 == tokens.shape[0]
            and tokens.shape[1] == 24 * wide * narrow
            and others[-2].shape[0] == 96 * wide * narrow
            and tokens.shape[0] % 512 == 0
        )
        if fits:
            return linked_block(wide // 4, tokens, lengths, raw_taps, *others)
        return local(tokens, lengths, raw_taps, *others)

    return jax.shard_map(
        block,
        mesh=mesh,
        in_specs=placed,
        out_specs=(rows, rows, P("narrow", None), spread, spread, rows, rows, spread, spread, rows, rows),
        check_vma=False,
    )
```

```python
import functools

import jax
import jax.numpy as jnp
import numpy as np
from jax import lax
from jax.experimental import pallas as pl
from jax.experimental.pallas import tpu as pltpu
from jax.sharding import PartitionSpec as P

shrink_level = 0.003
eps_norm = 1e-05


def wave_table(half):
    period = 4 * half
    phase = (np.outer(2 * np.arange(half) + 1, np.arange(half)) % period) * (2 * np.pi / period)
    return np.concatenate([np.cos(phase), -np.sin(phase)], axis=0)


def to_waves(table, block):
    return jnp.einsum("kn,nc->kc", table, block, preferred_element_type=jnp.float32)


def from_waves(table, waves):
    return jnp.einsum(
        "kn,kc->nc", table, waves.astype(jnp.bfloat16), preferred_element_type=jnp.float32
    )


def norm_parts(values):
    centered = values - jnp.mean(values, axis=-1, keepdims=True)
    inverse = lax.rsqrt(jnp.mean(centered * centered, axis=-1, keepdims=True) + eps_norm)
    return (centered * inverse, inverse)


def norm_back(upstream, unit_vals, inverse, gain_vec):
    scaled = upstream * gain_vec
    return inverse * (
        scaled
        - jnp.mean(scaled, axis=-1, keepdims=True)
        - unit_vals * jnp.mean(scaled * unit_vals, axis=-1, keepdims=True)
    )


def split(waves):
    half = waves.shape[0] // 2
    return waves[:half], waves[half:]


def times(left, right):
    lr, li = split(left)
    rr, ri = split(right)
    return jnp.concatenate([lr * rr - li * ri, lr * ri + li * rr], axis=0)


def conj_times(left, right):
    lr, li = split(left)
    rr, ri = split(right)
    return jnp.concatenate([lr * rr + li * ri, lr * ri - li * rr], axis=0)


def turned(waves, sign):
    wr, wi = split(waves)
    index = lax.broadcasted_iota(jnp.int32, (wr.shape[0], 1), 0)
    parity = sign * (1.0 - 2.0 * (index % 2).astype(jnp.float32))
    return jnp.concatenate([-parity * wi, parity * wr], axis=0)


def pool(values):
    padded = jnp.pad(values, ((1, 1), (0, 0)))
    return (padded[:-2] + padded[1:-1] + padded[2:]) / 3.0


def local(
    tokens,
    lengths,
    raw_taps,
    ln1_gain,
    ln1_shift,
    w_in,
    w_out,
    ln2_gain,
    ln2_shift,
    w_up,
    w_down,
    cotangent,
):
    tok_count, feat_width = tokens.shape
    row_count = lengths.shape[0]
    row_len = tok_count // row_count
    half = row_len // 2
    table = jnp.asarray(wave_table(half), jnp.bfloat16)
    scale = 1.0 / half
    long_rows = (lengths > half).astype(jnp.float32)

    squashed = raw_taps - jnp.clip(raw_taps, -shrink_level, shrink_level)
    gathered = lax.all_gather(squashed.astype(jnp.bfloat16), "narrow", axis=0, tiled=True)
    kernel = pool(gathered.astype(jnp.float32)).astype(jnp.bfloat16)
    kernel_low = to_waves(table, kernel[:half])
    kernel_cross = to_waves(table, kernel[half : 2 * half]) + turned(kernel_low, 1.0)

    inputs = tokens.astype(jnp.float32)
    unit_one, inverse_one = norm_parts(inputs)
    normed = (unit_one * ln1_gain + ln1_shift).astype(jnp.bfloat16)
    projected = jnp.dot(normed, w_in, preferred_element_type=jnp.float32)
    signal = projected[:, :feat_width].astype(jnp.bfloat16)
    gate_vals = projected[:, feat_width:]
    signal_waves = []
    mixed = []
    for row in range(row_count):
        first = to_waves(table, signal[row * row_len : row * row_len + half])
        second = to_waves(table, signal[row * row_len + half : (row + 1) * row_len])
        signal_waves.append((first, second))
        mixed.append(from_waves(table, times(first, kernel_low) * scale))
        mixed.append(
            from_waves(
                table,
                (times(second, kernel_low) + long_rows[row] * times(first, kernel_cross)) * scale,
            )
        )
    mixed = jnp.concatenate(mixed, axis=0)
    branch = (mixed * gate_vals).astype(jnp.bfloat16)
    residual = inputs + jnp.dot(branch, w_out, preferred_element_type=jnp.float32)
    unit_two, inverse_two = norm_parts(residual)
    normed2 = (unit_two * ln2_gain + ln2_shift).astype(jnp.bfloat16)
    hidden = jnp.dot(normed2, w_up, preferred_element_type=jnp.float32)
    active = jax.nn.gelu(hidden).astype(jnp.bfloat16)
    block_out = (residual + jnp.dot(active, w_down, preferred_element_type=jnp.float32)).astype(
        jnp.bfloat16
    )
    w_down_grad = jnp.einsum("tf,td->fd", active, cotangent, preferred_element_type=jnp.float32)
    d_active = jnp.einsum("td,fd->tf", cotangent, w_down, preferred_element_type=jnp.float32)
    gelu_pull = jax.vjp(jax.nn.gelu, hidden)[1]
    d_hidden = gelu_pull(d_active)[0].astype(jnp.bfloat16)
    w_up_grad = jnp.einsum("td,tf->df", normed2, d_hidden, preferred_element_type=jnp.float32)
    d_normed2 = jnp.einsum("tf,df->td", d_hidden, w_up, preferred_element_type=jnp.float32)
    ln2_gain_grad = jnp.sum(d_normed2 * unit_two, axis=0)
    ln2_shift_grad = jnp.sum(d_normed2, axis=0)
    d_residual = cotangent.astype(jnp.float32) + norm_back(
        d_normed2, unit_two, inverse_two, ln2_gain
    )
    d_outproj = d_residual.astype(jnp.bfloat16)
    w_out_grad = jnp.einsum("td,te->de", branch, d_outproj, preferred_element_type=jnp.float32)
    d_branch = jnp.einsum("te,de->td", d_outproj, w_out, preferred_element_type=jnp.float32)
    d_mixed = (d_branch * gate_vals).astype(jnp.bfloat16)
    d_gate = d_branch * mixed
    d_signal = []
    low_grad = 0.0
    cross_grad = 0.0
    for row in range(row_count):
        first, second = signal_waves[row]
        d_first = to_waves(table, d_mixed[row * row_len : row * row_len + half]) * scale
        d_second = to_waves(table, d_mixed[row * row_len + half : (row + 1) * row_len]) * scale
        d_cross = d_second * long_rows[row]
        d_signal.append(
            from_waves(table, conj_times(kernel_low, d_first) + conj_times(kernel_cross, d_cross))
        )
        d_signal.append(from_waves(table, conj_times(kernel_low, d_second)))
        low_grad = low_grad + conj_times(first, d_first) + conj_times(second, d_second)
        cross_grad = cross_grad + conj_times(first, d_cross)
    low_grad = low_grad + turned(cross_grad, -1.0)
    d_kernel = jnp.concatenate([from_waves(table, low_grad), from_waves(table, cross_grad)], axis=0)
    d_signal = jnp.concatenate(d_signal, axis=0)
    d_projected = jnp.concatenate([d_signal, d_gate], axis=1).astype(jnp.bfloat16)
    w_in_grad = jnp.einsum("td,te->de", normed, d_projected, preferred_element_type=jnp.float32)
    d_normed = jnp.einsum("te,de->td", d_projected, w_in, preferred_element_type=jnp.float32)
    ln1_gain_grad = jnp.sum(d_normed * unit_one, axis=0)
    ln1_shift_grad = jnp.sum(d_normed, axis=0)
    input_grad = d_residual + norm_back(d_normed, unit_one, inverse_one, ln1_gain)

    shares = lax.psum_scatter(
        pool(d_kernel).astype(jnp.bfloat16), "narrow", scatter_dimension=0, tiled=True
    )
    summed = lax.psum(shares, "wide").astype(jnp.float32)
    raw_grad = summed * (jnp.abs(raw_taps) > shrink_level).astype(jnp.float32)

    def scatter(values):
        return lax.psum_scatter(
            values.astype(jnp.bfloat16), ("wide", "narrow"), scatter_dimension=0, tiled=True
        ).astype(jnp.float32)

    def scatter_wide(values):
        return lax.psum_scatter(values, ("wide", "narrow"), scatter_dimension=0, tiled=True)

    return (
        block_out,
        input_grad,
        raw_grad,
        scatter_wide(ln1_gain_grad),
        scatter_wide(ln1_shift_grad),
        scatter(w_in_grad),
        scatter(w_out_grad),
        scatter_wide(ln2_gain_grad),
        scatter_wide(ln2_shift_grad),
        scatter(w_up_grad),
        scatter(w_down_grad),
    )


MESH = pl.DeviceIdType.MESH
PART = 9
STORES = 30
VMEM_BYTES = 60 * 2**20
FLIGHTS = 3


def dot_nn(left, right):
    return lax.dot_general(left, right, (((1,), (0,)), ((), ())), preferred_element_type=jnp.float32)


def dot_nt(left, right):
    return lax.dot_general(left, right, (((1,), (1,)), ((), ())), preferred_element_type=jnp.float32)


def dot_tn(left, right):
    return lax.dot_general(left, right, (((0,), (0,)), ((), ())), preferred_element_type=jnp.float32)


def gelu_both(hidden):
    inner = 0.7978845608028654
    cubic = inner * 0.044715
    square = hidden * hidden
    bent = jnp.tanh(hidden * (inner + cubic * square))
    share = 0.5 + 0.5 * bent
    slope = share + (0.5 * hidden) * (1.0 - bent * bent) * (inner + (3.0 * cubic) * square)
    return hidden * share, slope


def column_sums(values):
    rows, width = values.shape
    return jnp.sum(values.reshape(rows // 8, 8, width), axis=0)


class Place:
    def __init__(self, planes):
        wide = lax.axis_index("wide")
        self.narrow = lax.axis_index("narrow")
        self.wide = wide
        self.core = wide % 2
        self.y = (wide // 2) % 2
        self.z = wide // 4
        self.x = self.narrow
        self.planes = planes
        self.sibling = (wide + 1 - 2 * self.core, self.narrow)
        self.next_x = (wide, 1 - self.narrow)
        self.next_y = (wide + 2 - 4 * self.y, self.narrow)

    def plane(self, step):
        other = (self.z + step) % self.planes
        return (self.wide + 4 * (other - self.z), self.narrow), other


class Chunk:
    def __init__(self, place, held, inbox, sems, x_first, target=None):
        self.place = place
        self.views = (held, inbox, sems)
        self.target = target
        self.first, self.second = (place.x, place.y) if x_first else (place.y, place.x)
        self.to_first, self.to_second = (
            (place.next_x, place.next_y) if x_first else (place.next_y, place.next_x)
        )
        self.x_first = x_first

    @property
    def held(self):
        ref, at = self.views[0]
        return ref.at[at]

    @property
    def inbox(self):
        return [ref if at is None else ref.at[at] for ref, at in self.views[1]]

    @property
    def sems(self):
        return [ref.at[at] for ref, at in self.views[2]]

    def slot(self, y, core, x):
        first, second = (x, y) if self.x_first else (y, x)
        return ((core * 2 + first) * 2 + second) * self.place.planes

    def copy(self, stage):
        planes, core = self.place.planes, self.place.core
        first, second = self.first, self.second
        start, count, device = (
            (4 * planes * (1 - core), 4 * planes, self.place.sibling),
            (4 * planes * core + 2 * planes * (1 - first), 2 * planes, self.to_first),
            (4 * planes * core + 2 * planes * first + planes * (1 - second), planes, self.to_second),
        )[stage]
        return pltpu.make_async_remote_copy(
            src_ref=self.held.at[pl.ds(start, count)],
            dst_ref=self.inbox[stage],
            send_sem=self.sems[0].at[stage],
            recv_sem=self.sems[1].at[stage],
            device_id=device,
            device_id_type=MESH,
        )

    def add(self, start, landing, count):
        for index in range(count):
            self.held[start + index] += landing[index]

    def start(self):
        self.copy(0).start()

    def over_core(self):
        planes = self.place.planes
        self.copy(0).wait()
        self.add(4 * planes * self.place.core, self.inbox[0], 4 * planes)
        self.copy(1).start()

    def over_first(self):
        planes = self.place.planes
        self.copy(1).wait()
        self.add(4 * planes * self.place.core + 2 * planes * self.first, self.inbox[1], 2 * planes)
        self.copy(2).start()

    def base(self):
        planes, place = self.place.planes, self.place
        return 4 * planes * place.core + 2 * planes * self.first + planes * self.second

    def plane_copy(self, step):
        device, other = self.place.plane(step)
        if self.target is None:
            return pltpu.make_async_remote_copy(
                src_ref=self.held.at[self.base() + other],
                dst_ref=self.inbox[3].at[step - 1],
                send_sem=self.sems[0].at[2 + step],
                recv_sem=self.sems[1].at[2 + step],
                device_id=device,
                device_id_type=MESH,
            )
        return pltpu.make_async_remote_copy(
            src_ref=self.held.at[pl.ds(self.base(), self.place.planes)],
            dst_ref=self.inbox[3].at[step - 1],
            send_sem=self.sems[0].at[2 + step],
            recv_sem=self.sems[1].at[2 + step],
            device_id=device,
            device_id_type=MESH,
        )

    def each_plane(self, act):
        for step in range(1, self.place.planes):
            if self.target is None:
                act(self.plane_copy(step))
            else:

                @pl.when((self.place.z + step) % self.place.planes == self.target)
                def _():
                    act(self.plane_copy(step))

    def over_second(self):
        self.copy(2).wait()
        planes = self.place.planes
        self.add(self.base(), self.inbox[2], planes)
        if self.target is None:
            self.inbox[3][planes - 1] = self.held[self.base() + self.place.z]
        else:

            @pl.when(self.place.z == self.target)
            def _():
                for index in range(planes):
                    self.inbox[3][planes - 1, index] = self.held[self.base() + index]

        self.each_plane(lambda copy: copy.start())

    def sent(self):
        self.each_plane(lambda copy: copy.wait_send())

    def arrived(self):
        for step in range(1, self.place.planes):
            self.plane_copy(step).wait_recv()

    def total(self, index):
        terms = [
            self.inbox[3][step] if self.target is None else self.inbox[3][step, index]
            for step in range(self.place.planes)
        ]
        return sum(term.astype(jnp.float32) for term in terms)


def store_rows(chunk, values, first_row):
    width = values.shape[1]
    for k in range(values.shape[0] // 24):
        shard = first_row // 24 + k
        z, y, core, x = shard // 8, shard // 4 % 2, shard // 2 % 2, shard % 2
        at = chunk.slot(y, core, x) + z
        block = values[24 * k : 24 * k + 24]
        rest = block[16:24]
        chunk.held[at, :, 0:width] = block[0:16].astype(jnp.bfloat16)
        chunk.held[at, :, width : width + width // 2] = jnp.concatenate(
            [rest[:, : width // 2], rest[:, width // 2 :]], axis=0
        ).astype(jnp.bfloat16)


def load_rows(block, width):
    rest = block[:, width:]
    return jnp.concatenate(
        [block[:, :width], jnp.concatenate([rest[0:8], rest[8:16]], axis=1)], axis=0
    )


def tile_runs(sub, width):
    tiles = width // 128
    runs, tile = [], 0
    while tile < tiles:
        line = sub * tiles + tile
        count = min(tiles - tile, PART - line % PART)
        runs.append((tile, line // PART, line % PART, count))
        tile += count
    return runs


def store_shards(chunk, values, first_row):
    width = values.shape[1]
    for k in range(values.shape[0] // 16):
        row = first_row + 16 * k
        shard, sub = row // 96, row % 96 // 16
        base = chunk.slot(shard // 4, shard // 2 % 2, shard % 2)
        for tile, block, at, count in tile_runs(sub, width):
            chunk.held[base + block, :, 128 * at : 128 * (at + count)] = values[
                16 * k : 16 * k + 16, 128 * tile : 128 * (tile + count)
            ].astype(jnp.bfloat16)


class Taps:
    def __init__(self, place, held, inbox, result, sems, index, rows, cols, x_first):
        self.place, self.held, self.inbox, self.result = place, held, inbox, result
        self.sems, self.index = sems, index
        self.rows = rows
        self.cols = cols
        self.x_first = x_first

    def part(self, x, core, y, plane, count):
        planes = self.place.planes
        return pl.ds((((x * 2 + core) * 2 + y) * planes + plane) * self.rows, count * self.rows)

    def add(self, target, landing):
        self.held[target, self.cols] += landing[...]

    def landing(self, level, first, count):
        return self.inbox[level].at[pl.ds(first * self.rows, count * self.rows), self.cols]

    def copy(self, kind, step=0):
        place, planes = self.place, self.place.planes
        x, core, y, z = place.x, place.core, place.y, place.z
        if kind == "core":
            source, landing = self.part(step, 1 - core, 0, 0, 2 * planes), self.landing(0, step * 2 * planes, 2 * planes)
            stage, device = step, place.sibling
        elif kind == "first" and self.x_first:
            source, landing = self.part(1 - x, core, 0, 0, 2 * planes), self.landing(1, 0, 2 * planes)
            stage, device = 2, place.next_x
        elif kind == "first":
            source, landing = self.part(step, core, 1 - y, 0, planes), self.landing(1, step * planes, planes)
            stage, device = 2 + step, place.next_y
        elif kind == "second":
            first = self.part(x, core, 1 - y, 0, planes) if self.x_first else self.part(1 - x, core, y, 0, planes)
            source, landing = first, self.landing(2, 0, planes)
            stage, device = 4, place.next_y if self.x_first else place.next_x
        elif kind == "plane":
            device, other = place.plane(step)
            source, landing = self.part(x, core, y, other, 1), self.landing(3, step - 1, 1)
            stage = 4 + step
        else:
            if kind == "back plane":
                mine, stage, device = (0, core, y, z, 1), 3 + planes + step, place.plane(step)[0]
            elif kind == "back y":
                mine, stage, device = (0, core, y, 0, planes), 3 + 2 * planes, place.next_y
            else:
                mine, stage, device = (0, core, 0, 0, 2 * planes), 4 + 2 * planes, place.sibling
            landing = self.result.at[self.part(*mine), self.cols]
        return pltpu.make_async_remote_copy(
            src_ref=landing if kind.startswith("back") else self.held.at[source, self.cols],
            dst_ref=landing,
            send_sem=self.sems[0].at[self.index, stage],
            recv_sem=self.sems[1].at[self.index, stage],
            device_id=device,
            device_id_type=MESH,
        )

    def start(self):
        for x in range(2):
            self.copy("core", x).start()

    def over_core(self):
        for x in range(2):
            self.copy("core", x).wait()
            self.add(
                self.part(x, self.place.core, 0, 0, 2 * self.place.planes),
                self.landing(0, x * 2 * self.place.planes, 2 * self.place.planes),
            )
        for step in range(1 if self.x_first else 2):
            self.copy("first", step).start()

    def over_first(self):
        place, planes = self.place, self.place.planes
        if self.x_first:
            self.copy("first").wait()
            self.add(self.part(place.x, place.core, 0, 0, 2 * planes), self.landing(1, 0, 2 * planes))
        else:
            for x in range(2):
                self.copy("first", x).wait()
                self.add(self.part(x, place.core, place.y, 0, planes), self.landing(1, x * planes, planes))
        self.copy("second").start()

    def over_second(self):
        place = self.place
        self.copy("second").wait()
        self.add(self.part(place.x, place.core, place.y, 0, place.planes), self.landing(2, 0, place.planes))
        for step in range(1, place.planes):
            self.copy("plane", step).start()

    def over_planes(self):
        place = self.place
        mine = self.part(place.x, place.core, place.y, place.z, 1)
        total = self.held[mine, self.cols].astype(jnp.float32)
        for step in range(1, place.planes):
            self.copy("plane", step).wait()
            total = total + self.landing(3, step - 1, 1)[...].astype(jnp.float32)
        self.result[self.part(0, place.core, place.y, place.z, 1), self.cols] = total.astype(self.result.dtype)
        for step in range(1, place.planes):
            self.copy("back plane", step).start()

    def back_y(self):
        for step in range(1, self.place.planes):
            self.copy("back plane", step).wait()
        self.copy("back y").start()

    def back_core(self):
        self.copy("back y").wait()
        self.copy("back core").start()

    def finish(self):
        self.copy("back core").wait()


class Sums:
    def __init__(self, place, levels, inbox, sems):
        self.place, self.levels, self.inbox, self.sems = place, levels, inbox, sems

    def copy(self, level, step=0):
        place = self.place
        device = (place.sibling, place.next_x, place.next_y)[level] if level < 3 else place.plane(step)[0]
        landing = level + max(step - 1, 0)
        return pltpu.make_async_remote_copy(
            src_ref=self.levels.at[level],
            dst_ref=self.inbox.at[landing],
            send_sem=self.sems[0].at[landing],
            recv_sem=self.sems[1].at[landing],
            device_id=device,
            device_id_type=MESH,
        )

    def start(self):
        self.copy(0).start()

    def over(self, level):
        self.copy(level).wait()
        self.levels[level + 1] = self.levels[level] + self.inbox[level]
        if level < 2:
            self.copy(level + 1).start()
        else:
            for step in range(1, self.place.planes):
                self.copy(3, step).start()

    def finish(self):
        total = self.levels[3]
        for step in range(1, self.place.planes):
            self.copy(3, step).wait()
            total = total + self.inbox[2 + step]
        return total


def block_kernel(
    planes,
    lengths,
    tokens, cotangent, raw_taps, w_in, w_out, w_up, w_down, table, table_t,
    ln1_gain, ln1_shift, ln2_gain, ln2_shift,
    block_out, input_grad, taps_out, sums_out, w_in_grad, w_out_grad, w_up_grad, w_down_grad,
    held, inbox0, inbox1, inbox2, inbox_u, inbox_n, taps_held, taps0, taps1, taps2, taps3, taps_sum,
    levels, sums_inbox, cot, active, running, branch_v, normed_v, w_out_v,
    gate_v, mixed_v, left_v, waves, kernels,
    send_sems, recv_sems, taps_send, taps_recv, sums_send, sums_recv, share_send, share_recv, load_sems,
):
    tok_count, feat = cot.shape
    half = tok_count // 2
    tile = active.shape[2]
    step_rows, tap_cols = 512, 256
    blocks = feat // tap_cols
    row_steps = tok_count // step_rows
    place = Place(planes)

    loads = {}

    class Load:
        def __init__(self, source, target):
            self.ends, self.at = (source, target), len(loads)

        def copy(self):
            source, target = (end() if callable(end) else end for end in self.ends)
            return pltpu.make_async_copy(source, target, load_sems.at[self.at])

        def wait(self):
            self.copy().wait()

    def load(name, source, target):
        loads[name] = Load(source, target)
        loads[name].copy().start()

    barrier = pltpu.get_barrier_semaphore()
    partners = [place.sibling, place.next_x, place.next_y] + [
        place.plane(step)[0] for step in range(1, planes)
    ]
    for partner in partners:
        pl.semaphore_signal(barrier, inc=1, device_id=partner, device_id_type=MESH)
    long = jnp.where(lengths[0] > half, 1.0, 0.0).astype(jnp.float32)

    def chunk(index, step, kind, target=None):
        at = step % FLIGHTS * 2 + kind
        ring = step % 2 * 2 + kind
        if target is None:
            far = (inbox_u, index // 2 if index < 2 * planes else index - planes)
        else:
            far = (inbox_n, None)
        return Chunk(
            place,
            (held, at),
            ((inbox0, ring), (inbox1, ring), (inbox2, ring), far),
            ((send_sems, index), (recv_sems, index)),
            kind == 0,
            target,
        )

    ups = [chunk(2 * t, t, 0) for t in range(planes)]
    downs = [chunk(2 * t + 1, t, 1, t) for t in range(planes)]

    def rows_of(index):
        return pl.ds(index * step_rows, step_rows)

    def unrolled(first, last, body, carry):
        for index in range(first, last):
            carry = body(index, carry)
        return carry

    def norm_of(values):
        centered = values - jnp.mean(values, axis=-1, keepdims=True)
        inverse = lax.rsqrt(jnp.mean(centered * centered, axis=-1, keepdims=True) + eps_norm)
        return centered * inverse, inverse

    out_chunk = chunk(2 * planes, planes, 0)
    gate_chunk = chunk(2 * planes + 1, planes, 1)
    signal_chunk = chunk(2 * planes + 2, planes + 1, 0)
    taps = [
        Taps(
            place, taps_held, (taps0, taps1, taps2, taps3), taps_sum, (taps_send, taps_recv), index,
            tok_count // (8 * planes), pl.ds(index * tap_cols, tap_cols), index % 2 == 0,
        )
        for index in range(feat // tap_cols)
    ]
    sums = Sums(place, levels, sums_inbox, (sums_send, sums_recv))

    def own_rows(target):
        target.arrived()
        return load_rows(target.total(0), feat)

    def own_down(t):
        @pl.when(place.z == t)
        def _():
            downs[t].arrived()
            for index in range(planes):
                block = downs[t].total(index)
                for sub in range(6):
                    for first, line, at, count in tile_runs(sub, feat):
                        if line == index:
                            w_down_grad[16 * sub : 16 * sub + 16, 128 * first : 128 * (first + count)] = block[
                                :, 128 * at : 128 * (at + count)
                            ]

    def weight_rows(target, left_t, right):
        for part in range(2):
            rows = feat // 2
            store_rows(target, dot_nn(left_t[part * rows : (part + 1) * rows, :], right[...]), part * rows)
        target.start()

    def own_up(t):
        w_up_grad[:, t * tile : (t + 1) * tile] = own_rows(ups[t])

    def own_out():
        w_out_grad[...] = own_rows(out_chunk)

    def own_gate():
        w_in_grad[:, feat:] = own_rows(gate_chunk)

    def own_signal():
        w_in_grad[:, 0:feat] = own_rows(signal_chunk)

    def taps_copy(index):
        cols = pl.ds(index * tap_cols, tap_cols)
        return pltpu.make_async_copy(taps_sum.at[:, cols], taps_out.at[:, cols], load_sems.at[STORES - 1 - index])

    def own_taps(index):
        taps[index].finish()
        taps_copy(index).start()

    def share_copy(which, across):
        block = half // 2
        block_x = place.x if which == 0 else 1 - place.x
        rows = pl.ds(pl.multiple_of(block_x * half + place.core * block, block), block)
        part = taps_held.at[rows, pl.ds(across * tap_cols, tap_cols)]
        return pltpu.make_async_remote_copy(
            src_ref=part,
            dst_ref=part,
            send_sem=share_send.at[which, across],
            recv_sem=share_recv.at[which, across],
            device_id=place.next_x if which == 0 else place.sibling,
            device_id_type=MESH,
        )

    def share_on(across):
        share_copy(0, across).wait()
        share_copy(1, across).start()

    def forward_back(normed_2, normed_2t, up_tiles, down_tiles):
        def load_tile(t):
            cols = pl.ds(t * tile, tile)
            load(("up", t), lambda: w_up.at[:, cols], lambda: up_tiles.at[t % 2])
            load(("down", t), lambda: w_down.at[cols, :], lambda: down_tiles.at[t % 2])

        def mix(table_v, table_tv):
            kernel = mixed_v
            load("taps", raw_taps, running.at[0:half, :])
            load("tokens", tokens, lambda: active.at[0])
            load("w_in", w_in.at[:, 0:feat], normed_2.at[0:feat, :])
            load("w_in end", w_in.at[:, feat : 2 * feat], normed_2t.at[:, 0:feat])
            load("table", table, table_v)
            load("table_t", table_t, table_tv)
            load("w_out", w_out, w_out_v)
            load_tile(0)
            load("cot", cotangent, cot)

            loads["taps"].wait()

            def squash_step(index, carry):
                rows = pl.ds(pl.multiple_of(index * 128, 128), 128)
                raw = running[rows, :]
                taps_held[pl.ds(pl.multiple_of(place.x * half + index * 128, 128), 128), :] = (
                    raw - jnp.clip(raw, -shrink_level, shrink_level)
                ).astype(jnp.bfloat16)
                return carry

            lax.fori_loop(0, half // 128, squash_step, 0)
            pl.semaphore_wait(barrier, len(partners))
            for across in range(blocks):
                share_copy(0, across).start()
            loads["tokens"].wait()
            loads["w_in"].wait()
            loads["w_in end"].wait()

            def project_step(index, carry):
                rows = rows_of(index)
                unit, _ = norm_of(active[0, rows, :].astype(jnp.float32))
                low = (unit * ln1_gain[...][None, :] + ln1_shift[...][None, :]).astype(jnp.bfloat16)
                normed_v[:, rows] = low.T
                active[1, rows, :] = dot_nn(low, normed_2[0:feat, :]).astype(jnp.bfloat16)
                gate_v[rows, :] = dot_nn(low, normed_2t[:, 0:feat]).astype(jnp.bfloat16)
                return carry

            unrolled(0, row_steps, project_step, 0)
            share_on(0)
            loads["table"].wait()

            def signal_wave_step(index, carry):
                rows = rows_of(index)
                for which in range(2):
                    waves[which, rows, :] = dot_nn(
                        table_v[rows, :], active[1, which * half : (which + 1) * half, :]
                    ).astype(jnp.bfloat16)
                return carry

            unrolled(0, row_steps, signal_wave_step, 0)
            pool_rows, wave_rows = 128, 256

            def pool_step(across):
                cols = slice(across * tap_cols, (across + 1) * tap_cols)
                rim = jnp.zeros((16, tap_cols), jnp.float32)
                for index in range(tok_count // pool_rows):
                    at = index * pool_rows
                    first, last = max(at - 16, 0), min(at + pool_rows + 16, tok_count)
                    around = taps_held[first:last, cols].astype(jnp.float32)
                    if at == 0:
                        around = jnp.concatenate([rim, around], axis=0)
                    if last == tok_count:
                        around = jnp.concatenate([around, rim], axis=0)
                    kernel[at : at + pool_rows, cols] = (
                        (around[15 : 15 + pool_rows] + around[16 : 16 + pool_rows] + around[17 : 17 + pool_rows])
                        / 3.0
                    ).astype(jnp.bfloat16)

            def spread_step(down, across):
                real, imag = pl.ds(down * wave_rows, wave_rows), pl.ds(half + down * wave_rows, wave_rows)
                cols = pl.ds(across * 256, 256)
                low_r = dot_nn(table_v[real, :], kernel[0:half, cols])
                low_i = dot_nn(table_v[imag, :], kernel[0:half, cols])
                high_r = dot_nn(table_v[real, :], kernel[half:, cols])
                high_i = dot_nn(table_v[imag, :], kernel[half:, cols])
                odd = lax.broadcasted_iota(jnp.int32, (wave_rows, 1), 0) % 2
                parity = (1 - 2 * odd).astype(jnp.float32)
                cross_r = long * (high_r - parity * low_i)
                cross_i = long * (high_i + parity * low_r)
                kernels[0, real, cols] = low_r.astype(jnp.bfloat16)
                kernels[0, imag, cols] = low_i.astype(jnp.bfloat16)
                kernels[1, real, cols] = cross_r.astype(jnp.bfloat16)
                kernels[1, imag, cols] = cross_i.astype(jnp.bfloat16)
                head_r = waves[0, real, cols].astype(jnp.float32)
                head_i = waves[0, imag, cols].astype(jnp.float32)
                tail_r = waves[1, real, cols].astype(jnp.float32)
                tail_i = waves[1, imag, cols].astype(jnp.float32)
                scale = 1.0 / half
                active[2, real, cols] = ((low_r * head_r - low_i * head_i) * scale).astype(jnp.bfloat16)
                active[2, imag, cols] = ((low_r * head_i + low_i * head_r) * scale).astype(jnp.bfloat16)
                active[3, real, cols] = (
                    (low_r * tail_r - low_i * tail_i + cross_r * head_r - cross_i * head_i) * scale
                ).astype(jnp.bfloat16)
                active[3, imag, cols] = (
                    (low_r * tail_i + low_i * tail_r + cross_r * head_i + cross_i * head_r) * scale
                ).astype(jnp.bfloat16)

            share_on(1)
            for across in range(blocks):
                share_copy(1, across).wait()
                pool_step(across)
                for down in range(half // wave_rows):
                    spread_step(down, across)
                if across + 2 < blocks:
                    share_on(across + 2)
            loads["table_t"].wait()
            loads["w_out"].wait()

            def residual_step(index, carry):
                rows = rows_of(index)
                part_steps = half // step_rows
                which = index // part_steps
                of_part = pl.ds(index % part_steps * step_rows, step_rows)
                mixed = dot_nn(table_tv[of_part, :], active[2 + which])
                mixed_v[rows, :] = mixed.astype(jnp.bfloat16)
                branch = (mixed * gate_v[rows, :].astype(jnp.float32)).astype(jnp.bfloat16)
                branch_v[:, rows] = branch.T
                left = active[0, rows, :].astype(jnp.float32) + dot_nn(branch, w_out_v[...])
                left_v[rows, :] = left
                unit, _ = norm_of(left)
                low = (unit * ln2_gain[...][None, :] + ln2_shift[...][None, :]).astype(jnp.bfloat16)
                normed_2[rows, :] = low
                normed_2t[:, rows] = low.T
                return carry

            unrolled(0, row_steps, residual_step, 0)

        pl.run_scoped(
            mix,
            pltpu.VMEM((tok_count, half), jnp.bfloat16),
            pltpu.VMEM((half, tok_count), jnp.bfloat16),
        )

        def feed_forward(d_hidden):
            loads["cot"].wait()

            def rows_piece(t, index):
                up_tile, down_tile = up_tiles.at[t % 2], down_tiles.at[t % 2]
                if index == 0:
                    loads["up", t].wait()
                    loads["down", t].wait()
                    if t + 1 < planes:
                        load_tile(t + 1)
                rows = rows_of(index)
                hidden = dot_nn(normed_2[rows, :], up_tile[...])
                d_active = dot_nt(cot[rows, :], down_tile[...])
                value, slope = gelu_both(hidden)
                active[t, rows, :] = value.astype(jnp.bfloat16)
                d_value = (d_active * slope).astype(jnp.bfloat16)
                d_hidden[rows, :] = d_value
                back = dot_nt(d_value, up_tile[...])
                if t == 0:
                    running[rows, :] = back
                else:
                    running[rows, :] += back

            def up_piece(t):
                if t >= FLIGHTS:
                    ups[t - FLIGHTS].sent()
                weight_rows(ups[t], normed_2t, d_hidden)

            def down_piece(t):
                if t >= FLIGHTS:
                    downs[t - FLIGHTS].sent()
                for part in range(2):
                    cols = slice(part * (tile // 2), (part + 1) * (tile // 2))
                    store_shards(downs[t], dot_tn(active[t, :, cols], cot[...]), part * (tile // 2))
                downs[t].start()

            rows_piece(0, 0)
            rows_piece(0, 1)
            down_piece(0)
            up_piece(0)
            rows_piece(1, 0)
            downs[0].over_core()
            ups[0].over_core()
            rows_piece(1, 1)
            down_piece(1)
            up_piece(1)
            downs[0].over_first()
            downs[1].over_core()
            ups[0].over_first()
            ups[1].over_core()
            rows_piece(2, 0)
            rows_piece(2, 1)
            down_piece(2)
            up_piece(2)
            downs[0].over_second()
            downs[1].over_first()
            downs[2].over_core()
            rows_piece(3, 0)
            ups[0].over_second()
            ups[1].over_first()
            ups[2].over_core()
            rows_piece(3, 1)
            down_piece(3)
            up_piece(3)

        pl.run_scoped(feed_forward, pltpu.VMEM((tok_count, tile), jnp.bfloat16))

    pl.run_scoped(
        forward_back,
        pltpu.VMEM((tok_count, feat), jnp.bfloat16),
        pltpu.VMEM((feat, tok_count), jnp.bfloat16),
        pltpu.VMEM((2, feat, tile), jnp.bfloat16),
        pltpu.VMEM((2, tile, feat), jnp.bfloat16),
    )

    def backward(d_out, d_gate, d_mix, d_signal, table_v, table_tv, d_kernel, d_taps):
        d_waves = waves
        load("table again", table, table_v)
        load("table_t again", table_t, table_tv)
        totals = {}

        def sum_rows(at, index, values):
            totals[at] = column_sums(values) + (totals[at] if index > 0 else 0.0)
            if index == row_steps - 1:
                levels[0, at : at + 1, :] = jnp.sum(totals[at], axis=0, keepdims=True)

        def back_piece(index):
            if index == 0:
                levels[0] = jnp.zeros(levels.shape[1:], jnp.float32)
            rows = rows_of(index)
            left = left_v[rows, :]
            centered = left - jnp.mean(left, axis=-1, keepdims=True)
            inverse = lax.rsqrt(jnp.mean(centered * centered, axis=-1, keepdims=True) + eps_norm)
            unit = centered * inverse
            grad = running[rows, :]
            scaled = grad * ln2_gain[...][None, :]
            d_left = cot[rows, :].astype(jnp.float32) + inverse * (
                scaled
                - jnp.mean(scaled, axis=-1, keepdims=True)
                - unit * jnp.mean(scaled * unit, axis=-1, keepdims=True)
            )
            running[rows, :] = d_left
            d_low = d_left.astype(jnp.bfloat16)
            d_out[rows, :] = d_low
            d_branch = dot_nt(d_low, w_out_v[...])
            d_mix[rows, :] = (
                d_branch * gate_v[rows, :].astype(jnp.float32) * (1.0 / half)
            ).astype(jnp.bfloat16)
            d_gate[rows, :] = (d_branch * mixed_v[rows, :].astype(jnp.float32)).astype(jnp.bfloat16)
            sum_rows(0, index, grad * unit)
            sum_rows(1, index, grad)
            if index == row_steps - 1:
                load("tokens again", tokens, gate_v)

        def gate_piece():
            downs[planes - 3].sent()
            weight_rows(gate_chunk, normed_v, d_gate)

        def out_piece():
            ups[planes - 3].sent()
            weight_rows(out_chunk, branch_v, d_out)

        def signal_piece():
            ups[planes - 2].sent()
            weight_rows(signal_chunk, normed_v, d_signal)

        wave_rows, wave_cols = half, 256

        def wave_step(down, cols):
            real, imag = pl.ds(down * wave_rows, wave_rows), pl.ds(half + down * wave_rows, wave_rows)
            first_r = dot_nn(table_v[real, :], d_mix[0:half, cols])
            first_i = dot_nn(table_v[imag, :], d_mix[0:half, cols])
            second_r = dot_nn(table_v[real, :], d_mix[half:, cols])
            second_i = dot_nn(table_v[imag, :], d_mix[half:, cols])

            def wide(ref, which, rows):
                return ref[which, rows, cols].astype(jnp.float32)

            def keep(ref, which, rows, values):
                at = cols if ref.shape[2] == feat else slice(None)
                ref[which, rows, at] = values.astype(jnp.bfloat16)

            low_r, low_i = wide(kernels, 0, real), wide(kernels, 0, imag)
            cross_r, cross_i = wide(kernels, 1, real), wide(kernels, 1, imag)
            head_r, head_i = wide(waves, 0, real), wide(waves, 0, imag)
            tail_r, tail_i = wide(waves, 1, real), wide(waves, 1, imag)
            keep(d_waves, 0, real, low_r * first_r + low_i * first_i + cross_r * second_r + cross_i * second_i)
            keep(d_waves, 0, imag, low_r * first_i - low_i * first_r + cross_r * second_i - cross_i * second_r)
            keep(d_waves, 1, real, low_r * second_r + low_i * second_i)
            keep(d_waves, 1, imag, low_r * second_i - low_i * second_r)
            far_r = (head_r * second_r + head_i * second_i) * long
            far_i = (head_r * second_i - head_i * second_r) * long
            odd = lax.broadcasted_iota(jnp.int32, (wave_rows, 1), 0) % 2
            parity = (1 - 2 * odd).astype(jnp.float32)
            keep(d_kernel, 1, real, far_r)
            keep(d_kernel, 1, imag, far_i)
            keep(
                d_kernel,
                0,
                real,
                head_r * first_r + head_i * first_i + tail_r * second_r + tail_i * second_i + parity * far_i,
            )
            keep(
                d_kernel,
                0,
                imag,
                head_r * first_i - head_i * first_r + tail_r * second_i - tail_i * second_r - parity * far_r,
            )

        pad = 8
        d_taps[0:pad, :] = jnp.zeros((pad, wave_cols), jnp.float32)
        d_taps[pad + tok_count :, :] = jnp.zeros((pad, wave_cols), jnp.float32)
        pool_rows = 128

        def column_step(across):
            cols = pl.ds(across * wave_cols, wave_cols)
            for down in range(half // wave_rows):
                wave_step(down, cols)
            for which in range(2):
                d_taps[pad + which * half : pad + (which + 1) * half, :] = dot_nn(table_tv[...], d_kernel[which])
            for index in range(tok_count // pool_rows):
                at = pad + index * pool_rows
                taps_held[at - pad : at - pad + pool_rows, cols] = (
                    (
                        d_taps[at - 1 : at - 1 + pool_rows, :]
                        + d_taps[at : at + pool_rows, :]
                        + d_taps[at + 1 : at + 1 + pool_rows, :]
                    )
                    / 3.0
                ).astype(jnp.bfloat16)


        def column_piece(across):
            if across == 0:
                loads["table again"].wait()
                loads["table_t again"].wait()
            column_step(across)
            taps[across].start()
            if across == blocks - 1:
                load("w_in signal", w_in.at[:, 0:feat], cot.at[0:feat, :])
                load("w_in gate", w_in.at[:, feat : 2 * feat], d_mix.at[0:feat, :])

        def down_again(t):
            return (waves if t < 2 else kernels).at[t % 2, 0:tile, :]

        def load_again(t):
            rows = pl.ds(t * tile, tile)
            load(("again", t), lambda: w_down.at[rows, :], lambda: down_again(t))

        def unwave_piece(which):
            for at in range(0, half, step_rows):
                d_signal[which * half + at : which * half + at + step_rows, :] = dot_nn(
                    table_tv[at : at + step_rows, :], d_waves[which]
                ).astype(jnp.bfloat16)
            if which == 1:
                for t in range(planes):
                    load_again(t)

        def grad_copy(index):
            rows = rows_of(index)
            return pltpu.make_async_copy(
                running.at[rows, :], input_grad.at[rows, :], load_sems.at[STORES + index]
            )

        def out_copy(index):
            rows = rows_of(index)
            return pltpu.make_async_copy(
                mixed_v.at[rows, :], block_out.at[rows, :], load_sems.at[STORES + row_steps + index]
            )

        def input_piece(index):
            if index == 0:
                loads["tokens again"].wait()
                loads["w_in signal"].wait()
                loads["w_in gate"].wait()
            rows = rows_of(index)
            d_normed = dot_nt(d_signal[rows, :], cot[0:feat, :]) + dot_nt(
                d_gate[rows, :], d_mix[0:feat, :]
            )
            values = gate_v[rows, :].astype(jnp.float32)
            centered = values - jnp.mean(values, axis=-1, keepdims=True)
            inverse = lax.rsqrt(jnp.mean(centered * centered, axis=-1, keepdims=True) + eps_norm)
            unit = centered * inverse
            scaled = d_normed * ln1_gain[...][None, :]

            running[rows, :] = running[rows, :] + inverse * (
                scaled
                - jnp.mean(scaled, axis=-1, keepdims=True)
                - unit * jnp.mean(scaled * unit, axis=-1, keepdims=True)
            )
            grad_copy(index).start()
            sum_rows(2, index, d_normed * unit)
            sum_rows(3, index, d_normed)

        def output_piece(index):
            if index == 0:
                for t in range(planes):
                    loads["again", t].wait()
            rows = rows_of(index)
            total = left_v[rows, :]
            for t in range(planes):
                total = total + dot_nn(active[t, rows, :], down_again(t)[...])
            mixed_v[rows, :] = total.astype(jnp.bfloat16)
            out_copy(index).start()

        downs[1].over_second()
        downs[2].over_first()
        downs[3].over_core()
        back_piece(0)
        ups[1].over_second()
        ups[2].over_first()
        ups[3].over_core()
        back_piece(1)
        column_piece(0)
        downs[2].over_second()
        out_piece()
        taps[0].over_core()
        column_piece(1)
        ups[2].over_second()
        downs[3].over_first()
        ups[3].over_first()
        column_piece(2)
        taps[1].over_core()
        out_chunk.over_core()
        gate_piece()
        taps[2].over_core()
        taps[0].over_first()
        ups[3].over_second()
        unwave_piece(0)
        gate_chunk.over_core()
        taps[1].over_first()
        taps[0].over_second()
        downs[3].over_second()
        unwave_piece(1)
        signal_piece()
        out_chunk.over_first()
        taps[0].over_planes()
        own_up(3)
        signal_chunk.over_core()
        taps[2].over_first()
        input_piece(0)
        taps[1].over_second()
        taps[2].over_second()
        out_chunk.over_second()
        gate_chunk.over_first()
        taps[0].back_y()
        input_piece(1)
        sums.start()
        taps[1].over_planes()
        own_up(1)
        own_down(2)
        own_up(2)
        own_down(0)
        signal_chunk.over_first()
        taps[0].back_core()
        taps[2].over_planes()
        output_piece(0)
        gate_chunk.over_second()
        own_taps(0)
        taps[1].back_y()
        sums.over(0)
        own_down(1)
        sums.over(1)
        signal_chunk.over_second()
        own_out()
        taps[2].back_y()
        own_up(0)
        taps[1].back_core()
        sums.over(2)
        own_gate()
        taps[2].back_core()
        own_down(3)
        output_piece(1)
        own_taps(1)
        own_taps(2)
        own_signal()
        for index in range(row_steps):
            grad_copy(index).wait()
            out_copy(index).wait()

    pl.run_scoped(
        backward,
        *[pltpu.VMEM((tok_count, feat), jnp.bfloat16)] * 4,
        pltpu.VMEM((tok_count, half), jnp.bfloat16),
        pltpu.VMEM((half, tok_count), jnp.bfloat16),
        pltpu.VMEM((2, tok_count, tap_cols), jnp.bfloat16),
        pltpu.VMEM((tok_count + 16, tap_cols), jnp.float32),
    )

    sums_out[...] = sums.finish()
    for one in (downs[planes - 2], ups[planes - 1], downs[planes - 1], out_chunk, gate_chunk, signal_chunk):
        one.sent()
    for index in range(blocks):
        taps_copy(index).wait()


def hand_on_kernel(raw_taps, taps_sum, *others):
    count = (len(others) - 5) // 3
    sources, raw_grad, targets = others[:count], others[count], others[count + 1 : 2 * count + 1]
    raw_v, taps_v, grad_v = others[2 * count + 1 : 2 * count + 4]
    rooms, sems = others[2 * count + 4 : -1], others[-1]
    fetches = [pltpu.make_async_copy(taps_sum, taps_v, sems.at[0]), pltpu.make_async_copy(raw_taps, raw_v, sems.at[1])]
    stores = []
    for source, room, target in zip(sources, rooms, targets):
        rows = source.shape[0]
        parts = 4 if rows % 64 == 0 else 1
        for part in range(parts):
            at = pl.ds(part * (rows // parts), rows // parts)
            sem = sems.at[1 + len(fetches)]
            fetches.append(pltpu.make_async_copy(source.at[at, :], room.at[at, :], sem))
            stores.append(pltpu.make_async_copy(room.at[at, :], target.at[at, :], sem))
    for fetch in fetches:
        fetch.start()
    for fetch in fetches[:2]:
        fetch.wait()
    grad_v[...] = jnp.where(jnp.abs(raw_v[...]) > shrink_level, taps_v[...].astype(jnp.float32), 0.0)
    mask = pltpu.make_async_copy(grad_v, raw_grad, sems.at[2])
    mask.start()
    for fetch, store in zip(fetches[2:], stores):
        fetch.wait()
        store.start()
    for store in [mask] + stores:
        store.wait()


def hand_on(raw_taps, taps_sum, *sources):
    whole = pl.BlockSpec(memory_space=pl.ANY)
    return pl.pallas_call(
        hand_on_kernel,
        out_shape=[jax.ShapeDtypeStruct(raw_taps.shape, jnp.float32)]
        + [jax.ShapeDtypeStruct(source.shape, source.dtype) for source in sources],
        in_specs=[whole] * (2 + len(sources)),
        out_specs=[whole] * (1 + len(sources)),
        scratch_shapes=[
            pltpu.VMEM(raw_taps.shape, jnp.float32),
            pltpu.VMEM(taps_sum.shape, taps_sum.dtype),
            pltpu.VMEM(raw_taps.shape, jnp.float32),
        ]
        + [pltpu.VMEM(source.shape, source.dtype) for source in sources]
        + [pltpu.SemaphoreType.DMA((3 + 4 * len(sources),))],
        compiler_params=pltpu.CompilerParams(vmem_limit_bytes=VMEM_BYTES),
    )(raw_taps, taps_sum, *sources)


def linked_block(
    planes,
    tokens,
    lengths,
    raw_taps,
    ln1_gain,
    ln1_shift,
    w_in,
    w_out,
    ln2_gain,
    ln2_shift,
    w_up,
    w_down,
    cotangent,
):
    tok_count, feat = tokens.shape
    half = tok_count // 2
    tile = w_up.shape[1] // planes
    table = jnp.asarray(wave_table(half), jnp.bfloat16)
    table_t = jnp.asarray(wave_table(half).T, jnp.bfloat16)
    shares = 8 * planes
    rows = feat // shares
    block = (16, 128 * PART)
    chunks = 2 * planes + 3
    bf16, f32 = jnp.bfloat16, jnp.float32
    whole = pl.BlockSpec(memory_space=pl.ANY)
    near = pl.BlockSpec(memory_space=pltpu.VMEM)
    results = pl.pallas_call(
        functools.partial(block_kernel, planes),
        out_shape=(
            jax.ShapeDtypeStruct((tok_count, feat), bf16),
            jax.ShapeDtypeStruct((tok_count, feat), f32),
            jax.ShapeDtypeStruct((half, feat), bf16),
            jax.ShapeDtypeStruct((8, feat), f32),
            jax.ShapeDtypeStruct((rows, 2 * feat), f32),
            jax.ShapeDtypeStruct((rows, feat), f32),
            jax.ShapeDtypeStruct((rows, planes * tile), f32),
            jax.ShapeDtypeStruct((tile // 8, feat), f32),
        ),
        in_specs=[pl.BlockSpec(memory_space=pltpu.SMEM)] + [whole] * 9 + [near] * 4,
        out_specs=(whole,) * 3 + (near,) * 5,
        scratch_shapes=[
            pltpu.VMEM((2 * FLIGHTS, shares) + block, bf16),
            pltpu.VMEM((4, 4 * planes) + block, bf16),
            pltpu.VMEM((4, 2 * planes) + block, bf16),
            pltpu.VMEM((4, planes) + block, bf16),
            pltpu.VMEM((planes + 3, planes) + block, bf16),
            pltpu.VMEM((planes, planes) + block, bf16),
            pltpu.VMEM((tok_count, feat), bf16),
            pltpu.VMEM((tok_count // 2, feat), bf16),
            pltpu.VMEM((tok_count // 4, feat), bf16),
            pltpu.VMEM((tok_count // 8, feat), bf16),
            pltpu.VMEM(((planes - 1) * (tok_count // shares), feat), bf16),
            pltpu.VMEM((half, feat), bf16),
            pltpu.VMEM((4, 8, feat), f32),
            pltpu.VMEM((planes + 2, 8, feat), f32),
            pltpu.VMEM((tok_count, feat), bf16),
            pltpu.VMEM((planes, tok_count, tile), bf16),
            pltpu.VMEM((tok_count, feat), f32),
            pltpu.VMEM((feat, tok_count), bf16),
            pltpu.VMEM((feat, tok_count), bf16),
            pltpu.VMEM((feat, feat), bf16),
            pltpu.VMEM((tok_count, feat), bf16),
            pltpu.VMEM((tok_count, feat), bf16),
            pltpu.VMEM((tok_count, feat), f32),
            pltpu.VMEM((2, tok_count, feat), bf16),
            pltpu.VMEM((2, tok_count, feat), bf16),
            pltpu.SemaphoreType.DMA((chunks, planes + 2)),
            pltpu.SemaphoreType.DMA((chunks, planes + 2)),
            pltpu.SemaphoreType.DMA((feat // 256, 2 * planes + 5)),
            pltpu.SemaphoreType.DMA((feat // 256, 2 * planes + 5)),
            pltpu.SemaphoreType.DMA((planes + 2,)),
            pltpu.SemaphoreType.DMA((planes + 2,)),
            pltpu.SemaphoreType.DMA((2, feat // 256)),
            pltpu.SemaphoreType.DMA((2, feat // 256)),
            pltpu.SemaphoreType.DMA((STORES + 2 * tok_count // 512,)),
        ],
        compiler_params=pltpu.CompilerParams(
            collective_id=1, has_side_effects=True, vmem_limit_bytes=VMEM_BYTES
        ),
        cost_estimate=pl.CostEstimate(
            flops=2 * tok_count * feat * (5 * w_up.shape[1] + 9 * feat),
            bytes_accessed=40 * tok_count * feat,
            transcendentals=tok_count * w_up.shape[1],
        ),
    )(
        lengths,
        tokens,
        cotangent,
        raw_taps,
        w_in,
        w_out,
        w_up,
        w_down,
        table,
        table_t,
        ln1_gain,
        ln1_shift,
        ln2_gain,
        ln2_shift,
    )
    block_out, input_grad, taps_sum, sums, w_in_grad, w_out_grad, w_up_grad, w_down_grad = results
    raw_grad, block_out, input_grad, w_in_grad, w_out_grad, w_up_grad, w_down_grad = hand_on(
        raw_taps, taps_sum, block_out, input_grad, w_in_grad, w_out_grad, w_up_grad, w_down_grad
    )
    share = lax.axis_index("wide") * 2 + lax.axis_index("narrow")
    mine = lax.dynamic_slice(sums, (0, share * rows), (8, rows))
    return (
        block_out,
        input_grad,
        raw_grad,
        mine[2],
        mine[3],
        w_in_grad,
        w_out_grad,
        mine[0],
        mine[1],
        w_up_grad,
        w_down_grad,
    )


def solution(mesh):
    spread = P(("wide", "narrow"))
    rows = P(("wide", "narrow"), None)
    placed = (rows, spread, P("narrow", None)) + (P(),) * 8 + (rows,)
    wide, narrow = mesh.shape["wide"], mesh.shape["narrow"]

    def block(tokens, lengths, raw_taps, *others):
        fits = (
            narrow == 2
            and wide == 4 * 4
            and lengths.shape[0] == 1
            and raw_taps.shape[0] * 2 == tokens.shape[0]
            and tokens.shape[1] == 24 * wide * narrow
            and others[-2].shape[0] == 96 * wide * narrow
            and tokens.shape[0] % 512 == 0
        )
        if fits:
            return linked_block(wide // 4, tokens, lengths, raw_taps, *others)
        return local(tokens, lengths, raw_taps, *others)

    return jax.shard_map(
        block,
        mesh=mesh,
        in_specs=placed,
        out_specs=(rows, rows, P("narrow", None), spread, spread, rows, rows, spread, spread, rows, rows),
        check_vma=False,
    )
```

```python
import functools

import jax
import jax.numpy as jnp
import numpy as np
from jax import lax
from jax.experimental import pallas as pl
from jax.experimental.pallas import tpu as pltpu
from jax.sharding import PartitionSpec as P

shrink_level = 0.003
eps_norm = 1e-05


def wave_table(half):
    period = 4 * half
    phase = (np.outer(2 * np.arange(half) + 1, np.arange(half)) % period) * (2 * np.pi / period)
    return np.concatenate([np.cos(phase), -np.sin(phase)], axis=0)


def to_waves(table, block):
    return jnp.einsum("kn,nc->kc", table, block, preferred_element_type=jnp.float32)


def from_waves(table, waves):
    return jnp.einsum(
        "kn,kc->nc", table, waves.astype(jnp.bfloat16), preferred_element_type=jnp.float32
    )


def norm_parts(values):
    centered = values - jnp.mean(values, axis=-1, keepdims=True)
    inverse = lax.rsqrt(jnp.mean(centered * centered, axis=-1, keepdims=True) + eps_norm)
    return (centered * inverse, inverse)


def norm_back(upstream, unit_vals, inverse, gain_vec):
    scaled = upstream * gain_vec
    return inverse * (
        scaled
        - jnp.mean(scaled, axis=-1, keepdims=True)
        - unit_vals * jnp.mean(scaled * unit_vals, axis=-1, keepdims=True)
    )


def split(waves):
    half = waves.shape[0] // 2
    return waves[:half], waves[half:]


def times(left, right):
    lr, li = split(left)
    rr, ri = split(right)
    return jnp.concatenate([lr * rr - li * ri, lr * ri + li * rr], axis=0)


def conj_times(left, right):
    lr, li = split(left)
    rr, ri = split(right)
    return jnp.concatenate([lr * rr + li * ri, lr * ri - li * rr], axis=0)


def turned(waves, sign):
    wr, wi = split(waves)
    index = lax.broadcasted_iota(jnp.int32, (wr.shape[0], 1), 0)
    parity = sign * (1.0 - 2.0 * (index % 2).astype(jnp.float32))
    return jnp.concatenate([-parity * wi, parity * wr], axis=0)


def pool(values):
    padded = jnp.pad(values, ((1, 1), (0, 0)))
    return (padded[:-2] + padded[1:-1] + padded[2:]) / 3.0


def local(
    tokens,
    lengths,
    raw_taps,
    ln1_gain,
    ln1_shift,
    w_in,
    w_out,
    ln2_gain,
    ln2_shift,
    w_up,
    w_down,
    cotangent,
):
    tok_count, feat_width = tokens.shape
    row_count = lengths.shape[0]
    row_len = tok_count // row_count
    half = row_len // 2
    table = jnp.asarray(wave_table(half), jnp.bfloat16)
    scale = 1.0 / half
    long_rows = (lengths > half).astype(jnp.float32)

    squashed = raw_taps - jnp.clip(raw_taps, -shrink_level, shrink_level)
    gathered = lax.all_gather(squashed.astype(jnp.bfloat16), "narrow", axis=0, tiled=True)
    kernel = pool(gathered.astype(jnp.float32)).astype(jnp.bfloat16)
    kernel_low = to_waves(table, kernel[:half])
    kernel_cross = to_waves(table, kernel[half : 2 * half]) + turned(kernel_low, 1.0)

    inputs = tokens.astype(jnp.float32)
    unit_one, inverse_one = norm_parts(inputs)
    normed = (unit_one * ln1_gain + ln1_shift).astype(jnp.bfloat16)
    projected = jnp.dot(normed, w_in, preferred_element_type=jnp.float32)
    signal = projected[:, :feat_width].astype(jnp.bfloat16)
    gate_vals = projected[:, feat_width:]
    signal_waves = []
    mixed = []
    for row in range(row_count):
        first = to_waves(table, signal[row * row_len : row * row_len + half])
        second = to_waves(table, signal[row * row_len + half : (row + 1) * row_len])
        signal_waves.append((first, second))
        mixed.append(from_waves(table, times(first, kernel_low) * scale))
        mixed.append(
            from_waves(
                table,
                (times(second, kernel_low) + long_rows[row] * times(first, kernel_cross)) * scale,
            )
        )
    mixed = jnp.concatenate(mixed, axis=0)
    branch = (mixed * gate_vals).astype(jnp.bfloat16)
    residual = inputs + jnp.dot(branch, w_out, preferred_element_type=jnp.float32)
    unit_two, inverse_two = norm_parts(residual)
    normed2 = (unit_two * ln2_gain + ln2_shift).astype(jnp.bfloat16)
    hidden = jnp.dot(normed2, w_up, preferred_element_type=jnp.float32)
    active = jax.nn.gelu(hidden).astype(jnp.bfloat16)
    block_out = (residual + jnp.dot(active, w_down, preferred_element_type=jnp.float32)).astype(
        jnp.bfloat16
    )
    w_down_grad = jnp.einsum("tf,td->fd", active, cotangent, preferred_element_type=jnp.float32)
    d_active = jnp.einsum("td,fd->tf", cotangent, w_down, preferred_element_type=jnp.float32)
    gelu_pull = jax.vjp(jax.nn.gelu, hidden)[1]
    d_hidden = gelu_pull(d_active)[0].astype(jnp.bfloat16)
    w_up_grad = jnp.einsum("td,tf->df", normed2, d_hidden, preferred_element_type=jnp.float32)
    d_normed2 = jnp.einsum("tf,df->td", d_hidden, w_up, preferred_element_type=jnp.float32)
    ln2_gain_grad = jnp.sum(d_normed2 * unit_two, axis=0)
    ln2_shift_grad = jnp.sum(d_normed2, axis=0)
    d_residual = cotangent.astype(jnp.float32) + norm_back(
        d_normed2, unit_two, inverse_two, ln2_gain
    )
    d_outproj = d_residual.astype(jnp.bfloat16)
    w_out_grad = jnp.einsum("td,te->de", branch, d_outproj, preferred_element_type=jnp.float32)
    d_branch = jnp.einsum("te,de->td", d_outproj, w_out, preferred_element_type=jnp.float32)
    d_mixed = (d_branch * gate_vals).astype(jnp.bfloat16)
    d_gate = d_branch * mixed
    d_signal = []
    low_grad = 0.0
    cross_grad = 0.0
    for row in range(row_count):
        first, second = signal_waves[row]
        d_first = to_waves(table, d_mixed[row * row_len : row * row_len + half]) * scale
        d_second = to_waves(table, d_mixed[row * row_len + half : (row + 1) * row_len]) * scale
        d_cross = d_second * long_rows[row]
        d_signal.append(
            from_waves(table, conj_times(kernel_low, d_first) + conj_times(kernel_cross, d_cross))
        )
        d_signal.append(from_waves(table, conj_times(kernel_low, d_second)))
        low_grad = low_grad + conj_times(first, d_first) + conj_times(second, d_second)
        cross_grad = cross_grad + conj_times(first, d_cross)
    low_grad = low_grad + turned(cross_grad, -1.0)
    d_kernel = jnp.concatenate([from_waves(table, low_grad), from_waves(table, cross_grad)], axis=0)
    d_signal = jnp.concatenate(d_signal, axis=0)
    d_projected = jnp.concatenate([d_signal, d_gate], axis=1).astype(jnp.bfloat16)
    w_in_grad = jnp.einsum("td,te->de", normed, d_projected, preferred_element_type=jnp.float32)
    d_normed = jnp.einsum("te,de->td", d_projected, w_in, preferred_element_type=jnp.float32)
    ln1_gain_grad = jnp.sum(d_normed * unit_one, axis=0)
    ln1_shift_grad = jnp.sum(d_normed, axis=0)
    input_grad = d_residual + norm_back(d_normed, unit_one, inverse_one, ln1_gain)

    shares = lax.psum_scatter(
        pool(d_kernel).astype(jnp.bfloat16), "narrow", scatter_dimension=0, tiled=True
    )
    summed = lax.psum(shares, "wide").astype(jnp.float32)
    raw_grad = summed * (jnp.abs(raw_taps) > shrink_level).astype(jnp.float32)

    def scatter(values):
        return lax.psum_scatter(
            values.astype(jnp.bfloat16), ("wide", "narrow"), scatter_dimension=0, tiled=True
        ).astype(jnp.float32)

    def scatter_wide(values):
        return lax.psum_scatter(values, ("wide", "narrow"), scatter_dimension=0, tiled=True)

    return (
        block_out,
        input_grad,
        raw_grad,
        scatter_wide(ln1_gain_grad),
        scatter_wide(ln1_shift_grad),
        scatter(w_in_grad),
        scatter(w_out_grad),
        scatter_wide(ln2_gain_grad),
        scatter_wide(ln2_shift_grad),
        scatter(w_up_grad),
        scatter(w_down_grad),
    )


MESH = pl.DeviceIdType.MESH
PART = 9
STORES = 30
VMEM_BYTES = 60 * 2**20
FLIGHTS = 3


def dot_nn(left, right):
    return lax.dot_general(left, right, (((1,), (0,)), ((), ())), preferred_element_type=jnp.float32)


def dot_nt(left, right):
    return lax.dot_general(left, right, (((1,), (1,)), ((), ())), preferred_element_type=jnp.float32)


def dot_tn(left, right):
    return lax.dot_general(left, right, (((0,), (0,)), ((), ())), preferred_element_type=jnp.float32)


def gelu_both(hidden):
    inner = 0.7978845608028654
    cubic = inner * 0.044715
    square = hidden * hidden
    bent = jnp.tanh(hidden * (inner + cubic * square))
    share = 0.5 + 0.5 * bent
    slope = share + (0.5 * hidden) * (1.0 - bent * bent) * (inner + (3.0 * cubic) * square)
    return hidden * share, slope


def blocks_of(rows, columns, height=16, width=768):
    return [
        (slice(at, at + height), slice(left, min(left + width, columns)))
        for at in range(0, rows, height)
        for left in range(0, columns, width)
    ]


def column_sums(values):
    rows, width = values.shape
    return jnp.sum(values.reshape(rows // 8, 8, width), axis=0)


class Place:
    def __init__(self, planes):
        wide = lax.axis_index("wide")
        self.narrow = lax.axis_index("narrow")
        self.wide = wide
        self.core = wide % 2
        self.y = (wide // 2) % 2
        self.z = wide // 4
        self.x = self.narrow
        self.planes = planes
        self.sibling = (wide + 1 - 2 * self.core, self.narrow)
        self.next_x = (wide, 1 - self.narrow)
        self.next_y = (wide + 2 - 4 * self.y, self.narrow)

    def plane(self, step):
        other = (self.z + step) % self.planes
        return (self.wide + 4 * (other - self.z), self.narrow), other


class Chunk:
    def __init__(self, place, held, inbox, sems, x_first, target=None):
        self.place = place
        self.views = (held, inbox, sems)
        self.target = target
        self.first, self.second = (place.x, place.y) if x_first else (place.y, place.x)
        self.to_first, self.to_second = (
            (place.next_x, place.next_y) if x_first else (place.next_y, place.next_x)
        )
        self.x_first = x_first

    @property
    def held(self):
        ref, at = self.views[0]
        return ref.at[at]

    @property
    def inbox(self):
        return [ref if at is None else ref.at[at] for ref, at in self.views[1]]

    @property
    def sems(self):
        return [ref.at[at] for ref, at in self.views[2]]

    def slot(self, y, core, x):
        first, second = (x, y) if self.x_first else (y, x)
        return ((core * 2 + first) * 2 + second) * self.place.planes

    def copy(self, stage):
        planes, core = self.place.planes, self.place.core
        first, second = self.first, self.second
        start, count, device = (
            (4 * planes * (1 - core), 4 * planes, self.place.sibling),
            (4 * planes * core + 2 * planes * (1 - first), 2 * planes, self.to_first),
            (4 * planes * core + 2 * planes * first + planes * (1 - second), planes, self.to_second),
        )[stage]
        return pltpu.make_async_remote_copy(
            src_ref=self.held.at[pl.ds(start, count)],
            dst_ref=self.inbox[stage],
            send_sem=self.sems[0].at[stage],
            recv_sem=self.sems[1].at[stage],
            device_id=device,
            device_id_type=MESH,
        )

    def add(self, start, landing, count):
        for index in range(count):
            self.held[start + index] += landing[index]

    def start(self):
        self.copy(0).start()

    def over_core(self):
        planes = self.place.planes
        self.copy(0).wait()
        self.add(4 * planes * self.place.core, self.inbox[0], 4 * planes)
        self.copy(1).start()

    def over_first(self):
        planes = self.place.planes
        self.copy(1).wait()
        self.add(4 * planes * self.place.core + 2 * planes * self.first, self.inbox[1], 2 * planes)
        self.copy(2).start()

    def base(self):
        planes, place = self.place.planes, self.place
        return 4 * planes * place.core + 2 * planes * self.first + planes * self.second

    def plane_copy(self, step):
        device, other = self.place.plane(step)
        if self.target is None:
            return pltpu.make_async_remote_copy(
                src_ref=self.held.at[self.base() + other],
                dst_ref=self.inbox[3].at[step - 1],
                send_sem=self.sems[0].at[2 + step],
                recv_sem=self.sems[1].at[2 + step],
                device_id=device,
                device_id_type=MESH,
            )
        return pltpu.make_async_remote_copy(
            src_ref=self.held.at[pl.ds(self.base(), self.place.planes)],
            dst_ref=self.inbox[3].at[step - 1],
            send_sem=self.sems[0].at[2 + step],
            recv_sem=self.sems[1].at[2 + step],
            device_id=device,
            device_id_type=MESH,
        )

    def each_plane(self, act):
        for step in range(1, self.place.planes):
            if self.target is None:
                act(self.plane_copy(step))
            else:

                @pl.when((self.place.z + step) % self.place.planes == self.target)
                def _():
                    act(self.plane_copy(step))

    def over_second(self):
        self.copy(2).wait()
        planes = self.place.planes
        self.add(self.base(), self.inbox[2], planes)
        if self.target is None:
            self.inbox[3][planes - 1] = self.held[self.base() + self.place.z]
        else:

            @pl.when(self.place.z == self.target)
            def _():
                for index in range(planes):
                    self.inbox[3][planes - 1, index] = self.held[self.base() + index]

        self.each_plane(lambda copy: copy.start())

    def sent(self):
        self.each_plane(lambda copy: copy.wait_send())

    def arrived(self):
        for step in range(1, self.place.planes):
            self.plane_copy(step).wait_recv()

    def total(self, index):
        terms = [
            self.inbox[3][step] if self.target is None else self.inbox[3][step, index]
            for step in range(self.place.planes)
        ]
        return sum(term.astype(jnp.float32) for term in terms)


def store_rows(chunk, values, first_row):
    width = values.shape[1]
    for k in range(values.shape[0] // 24):
        shard = first_row // 24 + k
        z, y, core, x = shard // 8, shard // 4 % 2, shard // 2 % 2, shard % 2
        at = chunk.slot(y, core, x) + z
        block = values[24 * k : 24 * k + 24]
        rest = block[16:24]
        chunk.held[at, :, 0:width] = block[0:16].astype(jnp.bfloat16)
        chunk.held[at, :, width : width + width // 2] = jnp.concatenate(
            [rest[:, : width // 2], rest[:, width // 2 :]], axis=0
        ).astype(jnp.bfloat16)


def load_rows(block, width):
    rest = block[:, width:]
    return jnp.concatenate(
        [block[:, :width], jnp.concatenate([rest[0:8], rest[8:16]], axis=1)], axis=0
    )


def tile_runs(sub, width):
    tiles = width // 128
    runs, tile = [], 0
    while tile < tiles:
        line = sub * tiles + tile
        count = min(tiles - tile, PART - line % PART)
        runs.append((tile, line // PART, line % PART, count))
        tile += count
    return runs


def store_shards(chunk, values, first_row):
    width = values.shape[1]
    for k in range(values.shape[0] // 16):
        row = first_row + 16 * k
        shard, sub = row // 96, row % 96 // 16
        base = chunk.slot(shard // 4, shard // 2 % 2, shard % 2)
        for tile, block, at, count in tile_runs(sub, width):
            chunk.held[base + block, :, 128 * at : 128 * (at + count)] = values[
                16 * k : 16 * k + 16, 128 * tile : 128 * (tile + count)
            ].astype(jnp.bfloat16)


class Taps:
    def __init__(self, place, held, inbox, result, sems, index, rows, cols, x_first):
        self.place, self.held, self.inbox, self.result = place, held, inbox, result
        self.sems, self.index = sems, index
        self.rows = rows
        self.cols = cols
        self.x_first = x_first

    def part(self, x, core, y, plane, count):
        planes = self.place.planes
        return pl.ds((((x * 2 + core) * 2 + y) * planes + plane) * self.rows, count * self.rows)

    def add(self, target, landing):
        self.held[target, self.cols] += landing[...]

    def landing(self, level, first, count):
        return self.inbox[level].at[pl.ds(first * self.rows, count * self.rows), self.cols]

    def copy(self, kind, step=0):
        place, planes = self.place, self.place.planes
        x, core, y, z = place.x, place.core, place.y, place.z
        if kind == "core":
            source, landing = self.part(step, 1 - core, 0, 0, 2 * planes), self.landing(0, step * 2 * planes, 2 * planes)
            stage, device = step, place.sibling
        elif kind == "first" and self.x_first:
            source, landing = self.part(1 - x, core, 0, 0, 2 * planes), self.landing(1, 0, 2 * planes)
            stage, device = 2, place.next_x
        elif kind == "first":
            source, landing = self.part(step, core, 1 - y, 0, planes), self.landing(1, step * planes, planes)
            stage, device = 2 + step, place.next_y
        elif kind == "second":
            first = self.part(x, core, 1 - y, 0, planes) if self.x_first else self.part(1 - x, core, y, 0, planes)
            source, landing = first, self.landing(2, 0, planes)
            stage, device = 4, place.next_y if self.x_first else place.next_x
        elif kind == "plane":
            device, other = place.plane(step)
            source, landing = self.part(x, core, y, other, 1), self.landing(3, step - 1, 1)
            stage = 4 + step
        else:
            if kind == "back plane":
                mine, stage, device = (0, core, y, z, 1), 3 + planes + step, place.plane(step)[0]
            elif kind == "back y":
                mine, stage, device = (0, core, y, 0, planes), 3 + 2 * planes, place.next_y
            else:
                mine, stage, device = (0, core, 0, 0, 2 * planes), 4 + 2 * planes, place.sibling
            landing = self.result.at[self.part(*mine), self.cols]
        return pltpu.make_async_remote_copy(
            src_ref=landing if kind.startswith("back") else self.held.at[source, self.cols],
            dst_ref=landing,
            send_sem=self.sems[0].at[self.index, stage],
            recv_sem=self.sems[1].at[self.index, stage],
            device_id=device,
            device_id_type=MESH,
        )

    def start(self):
        for x in range(2):
            self.copy("core", x).start()

    def over_core(self):
        for x in range(2):
            self.copy("core", x).wait()
            self.add(
                self.part(x, self.place.core, 0, 0, 2 * self.place.planes),
                self.landing(0, x * 2 * self.place.planes, 2 * self.place.planes),
            )
        for step in range(1 if self.x_first else 2):
            self.copy("first", step).start()

    def over_first(self):
        place, planes = self.place, self.place.planes
        if self.x_first:
            self.copy("first").wait()
            self.add(self.part(place.x, place.core, 0, 0, 2 * planes), self.landing(1, 0, 2 * planes))
        else:
            for x in range(2):
                self.copy("first", x).wait()
                self.add(self.part(x, place.core, place.y, 0, planes), self.landing(1, x * planes, planes))
        self.copy("second").start()

    def over_second(self):
        place = self.place
        self.copy("second").wait()
        self.add(self.part(place.x, place.core, place.y, 0, place.planes), self.landing(2, 0, place.planes))
        for step in range(1, place.planes):
            self.copy("plane", step).start()

    def over_planes(self):
        place = self.place
        mine = self.part(place.x, place.core, place.y, place.z, 1)
        total = self.held[mine, self.cols].astype(jnp.float32)
        for step in range(1, place.planes):
            self.copy("plane", step).wait()
            total = total + self.landing(3, step - 1, 1)[...].astype(jnp.float32)
        self.result[self.part(0, place.core, place.y, place.z, 1), self.cols] = total.astype(self.result.dtype)
        for step in range(1, place.planes):
            self.copy("back plane", step).start()

    def back_y(self):
        for step in range(1, self.place.planes):
            self.copy("back plane", step).wait()
        self.copy("back y").start()

    def back_core(self):
        self.copy("back y").wait()
        self.copy("back core").start()

    def finish(self):
        self.copy("back core").wait()


class Sums:
    def __init__(self, place, levels, inbox, sems):
        self.place, self.levels, self.inbox, self.sems = place, levels, inbox, sems

    def copy(self, level, step=0):
        place = self.place
        device = (place.sibling, place.next_x, place.next_y)[level] if level < 3 else place.plane(step)[0]
        landing = level + max(step - 1, 0)
        return pltpu.make_async_remote_copy(
            src_ref=self.levels.at[level],
            dst_ref=self.inbox.at[landing],
            send_sem=self.sems[0].at[landing],
            recv_sem=self.sems[1].at[landing],
            device_id=device,
            device_id_type=MESH,
        )

    def start(self):
        self.copy(0).start()

    def over(self, level):
        self.copy(level).wait()
        self.levels[level + 1] = self.levels[level] + self.inbox[level]
        if level < 2:
            self.copy(level + 1).start()
        else:
            for step in range(1, self.place.planes):
                self.copy(3, step).start()

    def finish(self):
        total = self.levels[3]
        for step in range(1, self.place.planes):
            self.copy(3, step).wait()
            total = total + self.inbox[2 + step]
        return total


def block_kernel(
    planes,
    lengths,
    tokens, cotangent, raw_taps, w_in, w_out, w_up, w_down, table, table_t,
    ln1_gain, ln1_shift, ln2_gain, ln2_shift,
    block_out, input_grad, taps_out, sums_out, w_in_grad, w_out_grad, w_up_grad, w_down_grad,
    held, inbox0, inbox1, inbox2, inbox_u, inbox_n, taps_held, taps0, taps1, taps2, taps3, taps_sum,
    levels, sums_inbox, cot, active, running, branch_v, normed_v, w_out_v,
    gate_v, mixed_v, left_v, waves, kernels,
    send_sems, recv_sems, taps_send, taps_recv, sums_send, sums_recv, share_send, share_recv, load_sems,
):
    tok_count, feat = cot.shape
    half = tok_count // 2
    tile = active.shape[2]
    step_rows = tap_cols = 256
    blocks = feat // tap_cols
    row_steps = tok_count // step_rows
    place = Place(planes)

    loads = {}

    class Load:
        def __init__(self, source, target):
            self.ends, self.at = (source, target), len(loads)

        def copy(self):
            source, target = (end() if callable(end) else end for end in self.ends)
            return pltpu.make_async_copy(source, target, load_sems.at[self.at])

        def wait(self):
            self.copy().wait()

    def load(name, source, target):
        loads[name] = Load(source, target)
        loads[name].copy().start()

    barrier = pltpu.get_barrier_semaphore()
    partners = [place.sibling, place.next_x, place.next_y] + [
        place.plane(step)[0] for step in range(1, planes)
    ]
    for partner in partners:
        pl.semaphore_signal(barrier, inc=1, device_id=partner, device_id_type=MESH)
    long = jnp.where(lengths[0] > half, 1.0, 0.0).astype(jnp.float32)

    def chunk(index, step, kind, target=None):
        at = step % FLIGHTS * 2 + kind
        ring = step % 2 * 2 + kind
        if target is None:
            far = (inbox_u, index // 2 if index < 2 * planes else index - planes)
        else:
            far = (inbox_n, None)
        return Chunk(
            place,
            (held, at),
            ((inbox0, ring), (inbox1, ring), (inbox2, ring), far),
            ((send_sems, index), (recv_sems, index)),
            kind == 0,
            target,
        )

    ups = [chunk(2 * t, t, 0) for t in range(planes)]
    downs = [chunk(2 * t + 1, t, 1, t) for t in range(planes)]

    def rows_of(index):
        return pl.ds(index * step_rows, step_rows)

    def under(index, part):
        return pl.ds(index * step_rows + part.start, part.stop - part.start)

    def unrolled(first, last, body, carry):
        for index in range(first, last):
            carry = body(index, carry)
        return carry

    def norm_of(values):
        centered = values - jnp.mean(values, axis=-1, keepdims=True)
        inverse = lax.rsqrt(jnp.mean(centered * centered, axis=-1, keepdims=True) + eps_norm)
        return centered * inverse, inverse

    out_chunk = chunk(2 * planes, planes, 0)
    gate_chunk = chunk(2 * planes + 1, planes, 1)
    signal_chunk = chunk(2 * planes + 2, planes + 1, 0)
    taps = [
        Taps(
            place, taps_held, (taps0, taps1, taps2, taps3), taps_sum, (taps_send, taps_recv), index,
            tok_count // (8 * planes), pl.ds(index * tap_cols, tap_cols), index % 2 == 0,
        )
        for index in range(feat // tap_cols)
    ]
    sums = Sums(place, levels, sums_inbox, (sums_send, sums_recv))

    def own_rows(target):
        target.arrived()
        return load_rows(target.total(0), feat)

    def own_down(t):
        @pl.when(place.z == t)
        def _():
            downs[t].arrived()
            for index in range(planes):
                block = downs[t].total(index)
                for sub in range(6):
                    for first, line, at, count in tile_runs(sub, feat):
                        if line == index:
                            w_down_grad[16 * sub : 16 * sub + 16, 128 * first : 128 * (first + count)] = block[
                                :, 128 * at : 128 * (at + count)
                            ]

    def weight_rows(target, left_t, right):
        for part in range(2):
            rows = feat // 2
            store_rows(target, dot_nn(left_t[part * rows : (part + 1) * rows, :], right[...]), part * rows)
        target.start()

    def own_up(t):
        w_up_grad[:, t * tile : (t + 1) * tile] = own_rows(ups[t])

    def own_out():
        w_out_grad[...] = own_rows(out_chunk)

    def own_gate():
        w_in_grad[:, feat:] = own_rows(gate_chunk)

    def own_signal():
        w_in_grad[:, 0:feat] = own_rows(signal_chunk)

    def taps_copy(index):
        cols = pl.ds(index * tap_cols, tap_cols)
        return pltpu.make_async_copy(taps_sum.at[:, cols], taps_out.at[:, cols], load_sems.at[STORES - 1 - index])

    def own_taps(index):
        taps[index].finish()
        taps_copy(index).start()

    def share_copy(which, across):
        block = half // 2
        block_x = place.x if which == 0 else 1 - place.x
        rows = pl.ds(pl.multiple_of(block_x * half + place.core * block, block), block)
        part = taps_held.at[rows, pl.ds(across * tap_cols, tap_cols)]
        return pltpu.make_async_remote_copy(
            src_ref=part,
            dst_ref=part,
            send_sem=share_send.at[which, across],
            recv_sem=share_recv.at[which, across],
            device_id=place.next_x if which == 0 else place.sibling,
            device_id_type=MESH,
        )

    def share_on(across):
        share_copy(0, across).wait()
        share_copy(1, across).start()

    def forward_back(normed_2, normed_2t, up_tiles, down_tiles):
        def load_tile(t):
            cols = pl.ds(t * tile, tile)
            load(("up", t), lambda: w_up.at[:, cols], lambda: up_tiles.at[t % 2])
            load(("down", t), lambda: w_down.at[cols, :], lambda: down_tiles.at[t % 2])

        def mix(table_v, table_tv):
            kernel = mixed_v
            load("taps", raw_taps, running.at[0:half, :])
            load("tokens", tokens, lambda: active.at[0])
            load("w_in", w_in.at[:, 0:feat], normed_2.at[0:feat, :])
            load("w_in end", w_in.at[:, feat : 2 * feat], normed_2t.at[:, 0:feat])
            load("table", table, table_v)
            load("table_t", table_t, table_tv)
            load("w_out", w_out, w_out_v)
            load_tile(0)
            load("cot", cotangent, cot)

            loads["taps"].wait()

            def squash_step(index, carry):
                rows = pl.ds(pl.multiple_of(index * 128, 128), 128)
                raw = running[rows, :]
                taps_held[pl.ds(pl.multiple_of(place.x * half + index * 128, 128), 128), :] = (
                    raw - jnp.clip(raw, -shrink_level, shrink_level)
                ).astype(jnp.bfloat16)
                return carry

            lax.fori_loop(0, half // 128, squash_step, 0)
            pl.semaphore_wait(barrier, len(partners))
            for across in range(blocks):
                share_copy(0, across).start()
            loads["tokens"].wait()
            loads["w_in"].wait()
            loads["w_in end"].wait()

            def project_step(index, carry):
                rows = rows_of(index)
                for part, _ in blocks_of(step_rows, feat):
                    at = under(index, part)
                    unit, _ = norm_of(active[0, at, :].astype(jnp.float32))
                    mixed_v[at, :] = (unit * ln1_gain[...][None, :] + ln1_shift[...][None, :]).astype(jnp.bfloat16)
                low = mixed_v[rows, :]
                normed_v[:, rows] = low.T
                active[1, rows, :] = dot_nn(low, normed_2[0:feat, :]).astype(jnp.bfloat16)
                gate_v[rows, :] = dot_nn(low, normed_2t[:, 0:feat]).astype(jnp.bfloat16)
                return carry

            unrolled(0, row_steps, project_step, 0)
            share_on(0)
            loads["table"].wait()

            def signal_wave_step(index, carry):
                rows = rows_of(index)
                for which in range(2):
                    waves[which, rows, :] = dot_nn(
                        table_v[rows, :], active[1, which * half : (which + 1) * half, :]
                    ).astype(jnp.bfloat16)
                return carry

            unrolled(0, row_steps, signal_wave_step, 0)
            pool_rows = 16

            def pool_step(across):
                cols = slice(across * tap_cols, (across + 1) * tap_cols)
                rim = jnp.zeros((16, tap_cols), jnp.float32)
                for index in range(tok_count // pool_rows):
                    at = index * pool_rows
                    first, last = max(at - 16, 0), min(at + pool_rows + 16, tok_count)
                    around = taps_held[first:last, cols].astype(jnp.float32)
                    if at == 0:
                        around = jnp.concatenate([rim, around], axis=0)
                    if last == tok_count:
                        around = jnp.concatenate([around, rim], axis=0)
                    kernel[at : at + pool_rows, cols] = (
                        (around[15 : 15 + pool_rows] + around[16 : 16 + pool_rows] + around[17 : 17 + pool_rows])
                        / 3.0
                    ).astype(jnp.bfloat16)

            def spread_step(down, across):
                real, imag = pl.ds(down * 256, 256), pl.ds(half + down * 256, 256)
                cols = pl.ds(across * 256, 256)
                low_r = dot_nn(table_v[real, :], kernel[0:half, cols])
                low_i = dot_nn(table_v[imag, :], kernel[0:half, cols])
                high_r = dot_nn(table_v[real, :], kernel[half:, cols])
                high_i = dot_nn(table_v[imag, :], kernel[half:, cols])
                odd = lax.broadcasted_iota(jnp.int32, (16, 1), 0) % 2
                parity = (1 - 2 * odd).astype(jnp.float32)
                scale = 1.0 / half
                for part, _ in blocks_of(256, tap_cols):
                    re, im = under(down, part), pl.ds(half + down * 256 + part.start, 16)

                    def keep(ref, which, at, values):
                        ref[which, at, cols] = values.astype(jnp.bfloat16)

                    lr, li = low_r[part], low_i[part]
                    cr, ci = long * (high_r[part] - parity * li), long * (high_i[part] + parity * lr)
                    keep(kernels, 0, re, lr)
                    keep(kernels, 0, im, li)
                    keep(kernels, 1, re, cr)
                    keep(kernels, 1, im, ci)
                    hr, hi, tr, ti = (
                        waves[which, at, cols].astype(jnp.float32) * scale for which in range(2) for at in (re, im)
                    )
                    keep(active, 2, re, lr * hr - li * hi)
                    keep(active, 2, im, lr * hi + li * hr)
                    keep(active, 3, re, lr * tr - li * ti + cr * hr - ci * hi)
                    keep(active, 3, im, lr * ti + li * tr + cr * hi + ci * hr)

            share_on(1)
            for across in range(blocks):
                share_copy(1, across).wait()
                pool_step(across)
                for down in range(half // 256):
                    spread_step(down, across)
                if across + 2 < blocks:
                    share_on(across + 2)
            loads["table_t"].wait()
            loads["w_out"].wait()

            def residual_step(index, carry):
                rows = rows_of(index)
                part_steps = half // step_rows
                which = index // part_steps
                of_part = pl.ds(index % part_steps * step_rows, step_rows)
                mixed = dot_nn(table_tv[of_part, :], active[2 + which])
                for part, columns in blocks_of(step_rows, feat):
                    at = under(index, part)
                    mixed_v[at, columns] = mixed[part, columns].astype(jnp.bfloat16)
                    active[1, at, columns] = (
                        mixed[part, columns] * gate_v[at, columns].astype(jnp.float32)
                    ).astype(jnp.bfloat16)
                branch = active[1, rows, :]
                branch_v[:, rows] = branch.T
                added = dot_nn(branch, w_out_v[...])
                for part, _ in blocks_of(step_rows, feat):
                    at = under(index, part)
                    left = active[0, at, :].astype(jnp.float32) + added[part]
                    left_v[at, :] = left
                    unit, _ = norm_of(left)
                    normed_2[at, :] = (unit * ln2_gain[...][None, :] + ln2_shift[...][None, :]).astype(jnp.bfloat16)
                normed_2t[:, rows] = normed_2[rows, :].T
                return carry

            unrolled(0, row_steps, residual_step, 0)

        pl.run_scoped(
            mix,
            pltpu.VMEM((tok_count, half), jnp.bfloat16),
            pltpu.VMEM((half, tok_count), jnp.bfloat16),
        )

        def feed_forward(d_hidden):
            loads["cot"].wait()

            def rows_piece(t, index):
                up_tile, down_tile = up_tiles.at[t % 2], down_tiles.at[t % 2]
                if index == 0:
                    loads["up", t].wait()
                    loads["down", t].wait()
                    if t + 1 < planes:
                        load_tile(t + 1)
                rows = rows_of(index)
                hidden = dot_nn(normed_2[rows, :], up_tile[...])
                d_active = dot_nt(cot[rows, :], down_tile[...])
                for part, columns in blocks_of(step_rows, tile, 16, 384):
                    at = under(index, part)
                    value, slope = gelu_both(hidden[part, columns])
                    active[t, at, columns] = value.astype(jnp.bfloat16)
                    d_hidden[t % 2, at, columns] = (d_active[part, columns] * slope).astype(jnp.bfloat16)
                back = dot_nt(d_hidden[t % 2, rows, :], up_tile[...])
                if t == 0:
                    running[rows, :] = back
                else:
                    running[rows, :] += back

            def up_piece(t):
                if t >= FLIGHTS:
                    ups[t - FLIGHTS].sent()
                weight_rows(ups[t], normed_2t, d_hidden.at[t % 2])

            def down_piece(t):
                if t >= FLIGHTS:
                    downs[t - FLIGHTS].sent()
                for part in range(2):
                    cols = slice(part * (tile // 2), (part + 1) * (tile // 2))
                    store_shards(downs[t], dot_tn(active[t, :, cols], cot[...]), part * (tile // 2))
                downs[t].start()

            rows_piece(0, 0)
            rows_piece(0, 1)
            rows_piece(0, 2)
            rows_piece(0, 3)
            up_piece(0)
            down_piece(0)
            rows_piece(1, 0)
            ups[0].over_core()
            downs[0].over_core()
            rows_piece(1, 1)
            rows_piece(1, 2)
            rows_piece(1, 3)
            down_piece(1)
            up_piece(1)
            rows_piece(2, 0)
            downs[0].over_first()
            downs[1].over_core()
            ups[0].over_first()
            ups[1].over_core()
            rows_piece(2, 1)
            rows_piece(2, 2)
            rows_piece(2, 3)
            rows_piece(3, 0)
            down_piece(2)
            up_piece(2)
            rows_piece(3, 1)
            downs[0].over_second()
            downs[1].over_first()
            downs[2].over_core()
            ups[0].over_second()
            ups[1].over_first()
            ups[2].over_core()
            rows_piece(3, 2)
            rows_piece(3, 3)
            down_piece(3)
            up_piece(3)

        pl.run_scoped(feed_forward, pltpu.VMEM((2, tok_count, tile), jnp.bfloat16))

    pl.run_scoped(
        forward_back,
        pltpu.VMEM((tok_count, feat), jnp.bfloat16),
        pltpu.VMEM((feat, tok_count), jnp.bfloat16),
        pltpu.VMEM((2, feat, tile), jnp.bfloat16),
        pltpu.VMEM((2, tile, feat), jnp.bfloat16),
    )

    def backward(d_out, d_gate, d_mix, d_signal, table_v, table_tv, d_kernel, d_taps):
        d_waves = waves
        load("table again", table, table_v)
        load("table_t again", table_t, table_tv)
        totals = {}

        def sum_rows(at, index, values):
            totals[at] = values + (totals[at] if index > 0 else 0.0)
            if index == row_steps - 1:
                levels[0, at : at + 1, :] = jnp.sum(totals[at], axis=0, keepdims=True)

        def back_piece(index):
            if index == 0:
                levels[0] = jnp.zeros(levels.shape[1:], jnp.float32)
            rows = rows_of(index)
            sums_of = [0.0, 0.0]
            for part, _ in blocks_of(step_rows, feat):
                at = under(index, part)
                unit, inverse = norm_of(left_v[at, :])
                grad = running[at, :]
                sums_of = [sums_of[0] + column_sums(grad * unit), sums_of[1] + column_sums(grad)]
                scaled = grad * ln2_gain[...][None, :]
                d_left = cot[at, :].astype(jnp.float32) + inverse * (
                    scaled
                    - jnp.mean(scaled, axis=-1, keepdims=True)
                    - unit * jnp.mean(scaled * unit, axis=-1, keepdims=True)
                )
                running[at, :] = d_left
                d_out[at, :] = d_left.astype(jnp.bfloat16)
            d_branch = dot_nt(d_out[rows, :], w_out_v[...])
            for part, columns in blocks_of(step_rows, feat):
                at = under(index, part)
                values = d_branch[part, columns]
                d_mix[at, columns] = (
                    values * gate_v[at, columns].astype(jnp.float32) * (1.0 / half)
                ).astype(jnp.bfloat16)
                d_gate[at, columns] = (values * mixed_v[at, columns].astype(jnp.float32)).astype(jnp.bfloat16)
            sum_rows(0, index, sums_of[0])
            sum_rows(1, index, sums_of[1])
            if index == row_steps - 1:
                load("tokens again", tokens, gate_v)

        def gate_piece():
            downs[planes - 3].sent()
            weight_rows(gate_chunk, normed_v, d_gate)

        def out_piece():
            ups[planes - 3].sent()
            weight_rows(out_chunk, branch_v, d_out)

        def signal_piece():
            ups[planes - 2].sent()
            weight_rows(signal_chunk, normed_v, d_signal)

        wave_rows, wave_cols = 256, 256

        def wave_step(down, cols):
            real, imag = pl.ds(down * wave_rows, wave_rows), pl.ds(half + down * wave_rows, wave_rows)
            first_r = dot_nn(table_v[real, :], d_mix[0:half, cols])
            first_i = dot_nn(table_v[imag, :], d_mix[0:half, cols])
            second_r = dot_nn(table_v[real, :], d_mix[half:, cols])
            second_i = dot_nn(table_v[imag, :], d_mix[half:, cols])

            odd = lax.broadcasted_iota(jnp.int32, (16, 1), 0) % 2
            parity = (1 - 2 * odd).astype(jnp.float32)
            for part, _ in blocks_of(wave_rows, wave_cols):
                re = pl.ds(down * wave_rows + part.start, 16)
                im = pl.ds(half + down * wave_rows + part.start, 16)

                def wide(ref, which, at):
                    return ref[which, at, cols].astype(jnp.float32)

                def keep(ref, which, at, values):
                    ref[which, at, cols if ref.shape[2] == feat else slice(None)] = values.astype(jnp.bfloat16)

                fr, fi, sr, si = first_r[part], first_i[part], second_r[part], second_i[part]
                hr, hi = wide(waves, 0, re), wide(waves, 0, im)
                far_r, far_i = (hr * sr + hi * si) * long, (hr * si - hi * sr) * long
                keep(d_kernel, 1, re, far_r)
                keep(d_kernel, 1, im, far_i)
                tr, ti = wide(waves, 1, re), wide(waves, 1, im)
                keep(d_kernel, 0, re, hr * fr + hi * fi + tr * sr + ti * si + parity * far_i)
                keep(d_kernel, 0, im, hr * fi - hi * fr + tr * si - ti * sr - parity * far_r)
                lr, li = wide(kernels, 0, re), wide(kernels, 0, im)
                keep(d_waves, 1, re, lr * sr + li * si)
                keep(d_waves, 1, im, lr * si - li * sr)
                cr, ci = wide(kernels, 1, re), wide(kernels, 1, im)
                keep(d_waves, 0, re, lr * fr + li * fi + cr * sr + ci * si)
                keep(d_waves, 0, im, lr * fi - li * fr + cr * si - ci * sr)

        pad = 8
        d_taps[0:pad, :] = jnp.zeros((pad, wave_cols), jnp.float32)
        d_taps[pad + tok_count :, :] = jnp.zeros((pad, wave_cols), jnp.float32)
        pool_rows = 16

        def column_step(across):
            cols = pl.ds(across * wave_cols, wave_cols)
            for down in range(half // wave_rows):
                wave_step(down, cols)
            for which in range(2):
                d_taps[pad + which * half : pad + (which + 1) * half, :] = dot_nn(table_tv[...], d_kernel[which])
            for index in range(tok_count // pool_rows):
                at = pad + index * pool_rows
                taps_held[at - pad : at - pad + pool_rows, cols] = (
                    (
                        d_taps[at - 1 : at - 1 + pool_rows, :]
                        + d_taps[at : at + pool_rows, :]
                        + d_taps[at + 1 : at + 1 + pool_rows, :]
                    )
                    / 3.0
                ).astype(jnp.bfloat16)


        def column_piece(across):
            if across == 0:
                loads["table again"].wait()
                loads["table_t again"].wait()
            column_step(across)
            taps[across].start()
            if across == blocks - 1:
                load("w_in signal", w_in.at[:, 0:feat], cot.at[0:feat, :])
                load("w_in gate", w_in.at[:, feat : 2 * feat], d_mix.at[0:feat, :])

        def down_again(t):
            return (waves if t < 2 else kernels).at[t % 2, 0:tile, :]

        def load_again(t):
            rows = pl.ds(t * tile, tile)
            load(("again", t), lambda: w_down.at[rows, :], lambda: down_again(t))

        def unwave_piece(which):
            for at in range(0, half, step_rows):
                d_signal[which * half + at : which * half + at + step_rows, :] = dot_nn(
                    table_tv[at : at + step_rows, :], d_waves[which]
                ).astype(jnp.bfloat16)
            if which == 1:
                for t in range(planes):
                    load_again(t)

        def grad_copy(index):
            rows = rows_of(index)
            return pltpu.make_async_copy(
                running.at[rows, :], input_grad.at[rows, :], load_sems.at[STORES + index]
            )

        def out_copy(index):
            rows = rows_of(index)
            return pltpu.make_async_copy(
                mixed_v.at[rows, :], block_out.at[rows, :], load_sems.at[STORES + row_steps + index]
            )

        def input_piece(index):
            if index == 0:
                loads["tokens again"].wait()
                loads["w_in signal"].wait()
                loads["w_in gate"].wait()
            rows = rows_of(index)
            d_normed = dot_nt(d_signal[rows, :], cot[0:feat, :]) + dot_nt(
                d_gate[rows, :], d_mix[0:feat, :]
            )
            sums_of = [0.0, 0.0]
            for part, _ in blocks_of(step_rows, feat):
                at = under(index, part)
                unit, inverse = norm_of(gate_v[at, :].astype(jnp.float32))
                grad = d_normed[part]
                sums_of = [sums_of[0] + column_sums(grad * unit), sums_of[1] + column_sums(grad)]
                scaled = grad * ln1_gain[...][None, :]
                running[at, :] = running[at, :] + inverse * (
                    scaled
                    - jnp.mean(scaled, axis=-1, keepdims=True)
                    - unit * jnp.mean(scaled * unit, axis=-1, keepdims=True)
                )
            grad_copy(index).start()
            sum_rows(2, index, sums_of[0])
            sum_rows(3, index, sums_of[1])

        def output_piece(index):
            if index == 0:
                for t in range(planes):
                    loads["again", t].wait()
            rows = rows_of(index)
            total = left_v[rows, :]
            for t in range(planes):
                total = total + dot_nn(active[t, rows, :], down_again(t)[...])
            mixed_v[rows, :] = total.astype(jnp.bfloat16)
            out_copy(index).start()

        back_piece(0)
        back_piece(1)
        back_piece(2)
        downs[1].over_second()
        downs[2].over_first()
        downs[3].over_core()
        ups[1].over_second()
        ups[2].over_first()
        ups[3].over_core()
        back_piece(3)
        out_piece()
        column_piece(0)
        downs[2].over_second()
        column_piece(1)
        downs[3].over_first()
        column_piece(2)
        ups[2].over_second()
        ups[3].over_first()
        taps[0].over_core()
        own_down(1)
        taps[1].over_core()
        taps[2].over_core()
        out_chunk.over_core()
        downs[3].over_second()
        gate_piece()
        unwave_piece(0)
        taps[0].over_first()
        unwave_piece(1)
        input_piece(0)
        taps[2].over_first()
        taps[0].over_second()
        taps[1].over_first()
        gate_chunk.over_core()
        ups[3].over_second()
        signal_piece()
        output_piece(0)
        out_chunk.over_first()
        taps[2].over_second()
        signal_chunk.over_core()
        taps[0].over_planes()
        input_piece(1)
        input_piece(2)
        taps[2].over_planes()
        taps[1].over_second()
        input_piece(3)
        sums.start()
        gate_chunk.over_first()
        taps[0].back_y()
        out_chunk.over_second()
        taps[1].over_planes()
        own_down(2)
        sums.over(0)
        signal_chunk.over_first()
        output_piece(1)
        own_down(3)
        gate_chunk.over_second()
        taps[2].back_y()
        own_up(2)
        taps[0].back_core()
        output_piece(2)
        sums.over(1)
        signal_chunk.over_second()
        taps[2].back_core()
        taps[1].back_y()
        own_up(1)
        output_piece(3)
        own_gate()
        taps[1].back_core()
        own_taps(0)
        own_down(0)
        sums.over(2)
        own_up(0)
        own_taps(2)
        own_taps(1)
        own_up(3)
        own_out()
        own_signal()
        for index in range(row_steps):
            grad_copy(index).wait()
            out_copy(index).wait()

    pl.run_scoped(
        backward,
        *[pltpu.VMEM((tok_count, feat), jnp.bfloat16)] * 4,
        pltpu.VMEM((tok_count, half), jnp.bfloat16),
        pltpu.VMEM((half, tok_count), jnp.bfloat16),
        pltpu.VMEM((2, tok_count, tap_cols), jnp.bfloat16),
        pltpu.VMEM((tok_count + 16, tap_cols), jnp.float32),
    )

    sums_out[...] = sums.finish()
    for one in (downs[planes - 2], ups[planes - 1], downs[planes - 1], out_chunk, gate_chunk, signal_chunk):
        one.sent()
    for index in range(blocks):
        taps_copy(index).wait()


def hand_on_kernel(raw_taps, taps_sum, *others):
    count = (len(others) - 5) // 3
    sources, raw_grad, targets = others[:count], others[count], others[count + 1 : 2 * count + 1]
    raw_v, taps_v, grad_v = others[2 * count + 1 : 2 * count + 4]
    rooms, sems = others[2 * count + 4 : -1], others[-1]
    fetches = [pltpu.make_async_copy(taps_sum, taps_v, sems.at[0]), pltpu.make_async_copy(raw_taps, raw_v, sems.at[1])]
    stores = []
    for source, room, target in zip(sources, rooms, targets):
        rows = source.shape[0]
        parts = 4 if rows % 64 == 0 else 1
        for part in range(parts):
            at = pl.ds(part * (rows // parts), rows // parts)
            sem = sems.at[1 + len(fetches)]
            fetches.append(pltpu.make_async_copy(source.at[at, :], room.at[at, :], sem))
            stores.append(pltpu.make_async_copy(room.at[at, :], target.at[at, :], sem))
    for fetch in fetches:
        fetch.start()
    for fetch in fetches[:2]:
        fetch.wait()
    grad_v[...] = jnp.where(jnp.abs(raw_v[...]) > shrink_level, taps_v[...].astype(jnp.float32), 0.0)
    mask = pltpu.make_async_copy(grad_v, raw_grad, sems.at[2])
    mask.start()
    for fetch, store in zip(fetches[2:], stores):
        fetch.wait()
        store.start()
    for store in [mask] + stores:
        store.wait()


def hand_on(raw_taps, taps_sum, *sources):
    whole = pl.BlockSpec(memory_space=pl.ANY)
    return pl.pallas_call(
        hand_on_kernel,
        out_shape=[jax.ShapeDtypeStruct(raw_taps.shape, jnp.float32)]
        + [jax.ShapeDtypeStruct(source.shape, source.dtype) for source in sources],
        in_specs=[whole] * (2 + len(sources)),
        out_specs=[whole] * (1 + len(sources)),
        scratch_shapes=[
            pltpu.VMEM(raw_taps.shape, jnp.float32),
            pltpu.VMEM(taps_sum.shape, taps_sum.dtype),
            pltpu.VMEM(raw_taps.shape, jnp.float32),
        ]
        + [pltpu.VMEM(source.shape, source.dtype) for source in sources]
        + [pltpu.SemaphoreType.DMA((3 + 4 * len(sources),))],
        compiler_params=pltpu.CompilerParams(vmem_limit_bytes=VMEM_BYTES),
    )(raw_taps, taps_sum, *sources)


def linked_block(
    planes,
    tokens,
    lengths,
    raw_taps,
    ln1_gain,
    ln1_shift,
    w_in,
    w_out,
    ln2_gain,
    ln2_shift,
    w_up,
    w_down,
    cotangent,
):
    tok_count, feat = tokens.shape
    half = tok_count // 2
    tile = w_up.shape[1] // planes
    table = jnp.asarray(wave_table(half), jnp.bfloat16)
    table_t = jnp.asarray(wave_table(half).T, jnp.bfloat16)
    shares = 8 * planes
    rows = feat // shares
    block = (16, 128 * PART)
    chunks = 2 * planes + 3
    bf16, f32 = jnp.bfloat16, jnp.float32
    whole = pl.BlockSpec(memory_space=pl.ANY)
    near = pl.BlockSpec(memory_space=pltpu.VMEM)
    results = pl.pallas_call(
        functools.partial(block_kernel, planes),
        out_shape=(
            jax.ShapeDtypeStruct((tok_count, feat), bf16),
            jax.ShapeDtypeStruct((tok_count, feat), f32),
            jax.ShapeDtypeStruct((half, feat), bf16),
            jax.ShapeDtypeStruct((8, feat), f32),
            jax.ShapeDtypeStruct((rows, 2 * feat), f32),
            jax.ShapeDtypeStruct((rows, feat), f32),
            jax.ShapeDtypeStruct((rows, planes * tile), f32),
            jax.ShapeDtypeStruct((tile // 8, feat), f32),
        ),
        in_specs=[pl.BlockSpec(memory_space=pltpu.SMEM)] + [whole] * 9 + [near] * 4,
        out_specs=(whole,) * 3 + (near,) * 5,
        scratch_shapes=[
            pltpu.VMEM((2 * FLIGHTS, shares) + block, bf16),
            pltpu.VMEM((4, 4 * planes) + block, bf16),
            pltpu.VMEM((4, 2 * planes) + block, bf16),
            pltpu.VMEM((4, planes) + block, bf16),
            pltpu.VMEM((planes + 3, planes) + block, bf16),
            pltpu.VMEM((planes, planes) + block, bf16),
            pltpu.VMEM((tok_count, feat), bf16),
            pltpu.VMEM((tok_count // 2, feat), bf16),
            pltpu.VMEM((tok_count // 4, feat), bf16),
            pltpu.VMEM((tok_count // 8, feat), bf16),
            pltpu.VMEM(((planes - 1) * (tok_count // shares), feat), bf16),
            pltpu.VMEM((half, feat), bf16),
            pltpu.VMEM((4, 8, feat), f32),
            pltpu.VMEM((planes + 2, 8, feat), f32),
            pltpu.VMEM((tok_count, feat), bf16),
            pltpu.VMEM((planes, tok_count, tile), bf16),
            pltpu.VMEM((tok_count, feat), f32),
            pltpu.VMEM((feat, tok_count), bf16),
            pltpu.VMEM((feat, tok_count), bf16),
            pltpu.VMEM((feat, feat), bf16),
            pltpu.VMEM((tok_count, feat), bf16),
            pltpu.VMEM((tok_count, feat), bf16),
            pltpu.VMEM((tok_count, feat), f32),
            pltpu.VMEM((2, tok_count, feat), bf16),
            pltpu.VMEM((2, tok_count, feat), bf16),
            pltpu.SemaphoreType.DMA((chunks, planes + 2)),
            pltpu.SemaphoreType.DMA((chunks, planes + 2)),
            pltpu.SemaphoreType.DMA((feat // 256, 2 * planes + 5)),
            pltpu.SemaphoreType.DMA((feat // 256, 2 * planes + 5)),
            pltpu.SemaphoreType.DMA((planes + 2,)),
            pltpu.SemaphoreType.DMA((planes + 2,)),
            pltpu.SemaphoreType.DMA((2, feat // 256)),
            pltpu.SemaphoreType.DMA((2, feat // 256)),
            pltpu.SemaphoreType.DMA((STORES + 2 * tok_count // 256,)),
        ],
        compiler_params=pltpu.CompilerParams(
            collective_id=1, has_side_effects=True, vmem_limit_bytes=VMEM_BYTES
        ),
        cost_estimate=pl.CostEstimate(
            flops=2 * tok_count * feat * (5 * w_up.shape[1] + 9 * feat),
            bytes_accessed=40 * tok_count * feat,
            transcendentals=tok_count * w_up.shape[1],
        ),
    )(
        lengths,
        tokens,
        cotangent,
        raw_taps,
        w_in,
        w_out,
        w_up,
        w_down,
        table,
        table_t,
        ln1_gain,
        ln1_shift,
        ln2_gain,
        ln2_shift,
    )
    block_out, input_grad, taps_sum, sums, w_in_grad, w_out_grad, w_up_grad, w_down_grad = results
    raw_grad, block_out, input_grad, w_in_grad, w_out_grad, w_up_grad, w_down_grad = hand_on(
        raw_taps, taps_sum, block_out, input_grad, w_in_grad, w_out_grad, w_up_grad, w_down_grad
    )
    share = lax.axis_index("wide") * 2 + lax.axis_index("narrow")
    mine = lax.dynamic_slice(sums, (0, share * rows), (8, rows))
    return (
        block_out,
        input_grad,
        raw_grad,
        mine[2],
        mine[3],
        w_in_grad,
        w_out_grad,
        mine[0],
        mine[1],
        w_up_grad,
        w_down_grad,
    )


def solution(mesh):
    spread = P(("wide", "narrow"))
    rows = P(("wide", "narrow"), None)
    placed = (rows, spread, P("narrow", None)) + (P(),) * 8 + (rows,)
    wide, narrow = mesh.shape["wide"], mesh.shape["narrow"]

    def block(tokens, lengths, raw_taps, *others):
        fits = (
            narrow == 2
            and wide == 4 * 4
            and lengths.shape[0] == 1
            and raw_taps.shape[0] * 2 == tokens.shape[0]
            and tokens.shape[1] == 24 * wide * narrow
            and others[-2].shape[0] == 96 * wide * narrow
            and tokens.shape[0] % 512 == 0
        )
        if fits:
            return linked_block(wide // 4, tokens, lengths, raw_taps, *others)
        return local(tokens, lengths, raw_taps, *others)

    return jax.shard_map(
        block,
        mesh=mesh,
        in_specs=placed,
        out_specs=(rows, rows, P("narrow", None), spread, spread, rows, rows, spread, spread, rows, rows),
        check_vma=False,
    )
```

```python
import functools

import jax
import jax.numpy as jnp
import numpy as np
from jax import lax
from jax.experimental import pallas as pl
from jax.experimental.pallas import tpu as pltpu
from jax.sharding import PartitionSpec as P

shrink_level = 0.003
eps_norm = 1e-05


def wave_table(half):
    period = 4 * half
    phase = (np.outer(2 * np.arange(half) + 1, np.arange(half)) % period) * (2 * np.pi / period)
    return np.concatenate([np.cos(phase), -np.sin(phase)], axis=0)


def to_waves(table, block):
    return jnp.einsum("kn,nc->kc", table, block, preferred_element_type=jnp.float32)


def from_waves(table, waves):
    return jnp.einsum(
        "kn,kc->nc", table, waves.astype(jnp.bfloat16), preferred_element_type=jnp.float32
    )


def norm_parts(values):
    centered = values - jnp.mean(values, axis=-1, keepdims=True)
    inverse = lax.rsqrt(jnp.mean(centered * centered, axis=-1, keepdims=True) + eps_norm)
    return (centered * inverse, inverse)


def norm_back(upstream, unit_vals, inverse, gain_vec):
    scaled = upstream * gain_vec
    return inverse * (
        scaled
        - jnp.mean(scaled, axis=-1, keepdims=True)
        - unit_vals * jnp.mean(scaled * unit_vals, axis=-1, keepdims=True)
    )


def split(waves):
    half = waves.shape[0] // 2
    return waves[:half], waves[half:]


def times(left, right):
    lr, li = split(left)
    rr, ri = split(right)
    return jnp.concatenate([lr * rr - li * ri, lr * ri + li * rr], axis=0)


def conj_times(left, right):
    lr, li = split(left)
    rr, ri = split(right)
    return jnp.concatenate([lr * rr + li * ri, lr * ri - li * rr], axis=0)


def turned(waves, sign):
    wr, wi = split(waves)
    index = lax.broadcasted_iota(jnp.int32, (wr.shape[0], 1), 0)
    parity = sign * (1.0 - 2.0 * (index % 2).astype(jnp.float32))
    return jnp.concatenate([-parity * wi, parity * wr], axis=0)


def pool(values):
    padded = jnp.pad(values, ((1, 1), (0, 0)))
    return (padded[:-2] + padded[1:-1] + padded[2:]) / 3.0


def local(
    tokens,
    lengths,
    raw_taps,
    ln1_gain,
    ln1_shift,
    w_in,
    w_out,
    ln2_gain,
    ln2_shift,
    w_up,
    w_down,
    cotangent,
):
    tok_count, feat_width = tokens.shape
    row_count = lengths.shape[0]
    row_len = tok_count // row_count
    half = row_len // 2
    table = jnp.asarray(wave_table(half), jnp.bfloat16)
    scale = 1.0 / half
    long_rows = (lengths > half).astype(jnp.float32)

    squashed = raw_taps - jnp.clip(raw_taps, -shrink_level, shrink_level)
    gathered = lax.all_gather(squashed.astype(jnp.bfloat16), "narrow", axis=0, tiled=True)
    kernel = pool(gathered.astype(jnp.float32)).astype(jnp.bfloat16)
    kernel_low = to_waves(table, kernel[:half])
    kernel_cross = to_waves(table, kernel[half : 2 * half]) + turned(kernel_low, 1.0)

    inputs = tokens.astype(jnp.float32)
    unit_one, inverse_one = norm_parts(inputs)
    normed = (unit_one * ln1_gain + ln1_shift).astype(jnp.bfloat16)
    projected = jnp.dot(normed, w_in, preferred_element_type=jnp.float32)
    signal = projected[:, :feat_width].astype(jnp.bfloat16)
    gate_vals = projected[:, feat_width:]
    signal_waves = []
    mixed = []
    for row in range(row_count):
        first = to_waves(table, signal[row * row_len : row * row_len + half])
        second = to_waves(table, signal[row * row_len + half : (row + 1) * row_len])
        signal_waves.append((first, second))
        mixed.append(from_waves(table, times(first, kernel_low) * scale))
        mixed.append(
            from_waves(
                table,
                (times(second, kernel_low) + long_rows[row] * times(first, kernel_cross)) * scale,
            )
        )
    mixed = jnp.concatenate(mixed, axis=0)
    branch = (mixed * gate_vals).astype(jnp.bfloat16)
    residual = inputs + jnp.dot(branch, w_out, preferred_element_type=jnp.float32)
    unit_two, inverse_two = norm_parts(residual)
    normed2 = (unit_two * ln2_gain + ln2_shift).astype(jnp.bfloat16)
    hidden = jnp.dot(normed2, w_up, preferred_element_type=jnp.float32)
    active = jax.nn.gelu(hidden).astype(jnp.bfloat16)
    block_out = (residual + jnp.dot(active, w_down, preferred_element_type=jnp.float32)).astype(
        jnp.bfloat16
    )
    w_down_grad = jnp.einsum("tf,td->fd", active, cotangent, preferred_element_type=jnp.float32)
    d_active = jnp.einsum("td,fd->tf", cotangent, w_down, preferred_element_type=jnp.float32)
    gelu_pull = jax.vjp(jax.nn.gelu, hidden)[1]
    d_hidden = gelu_pull(d_active)[0].astype(jnp.bfloat16)
    w_up_grad = jnp.einsum("td,tf->df", normed2, d_hidden, preferred_element_type=jnp.float32)
    d_normed2 = jnp.einsum("tf,df->td", d_hidden, w_up, preferred_element_type=jnp.float32)
    ln2_gain_grad = jnp.sum(d_normed2 * unit_two, axis=0)
    ln2_shift_grad = jnp.sum(d_normed2, axis=0)
    d_residual = cotangent.astype(jnp.float32) + norm_back(
        d_normed2, unit_two, inverse_two, ln2_gain
    )
    d_outproj = d_residual.astype(jnp.bfloat16)
    w_out_grad = jnp.einsum("td,te->de", branch, d_outproj, preferred_element_type=jnp.float32)
    d_branch = jnp.einsum("te,de->td", d_outproj, w_out, preferred_element_type=jnp.float32)
    d_mixed = (d_branch * gate_vals).astype(jnp.bfloat16)
    d_gate = d_branch * mixed
    d_signal = []
    low_grad = 0.0
    cross_grad = 0.0
    for row in range(row_count):
        first, second = signal_waves[row]
        d_first = to_waves(table, d_mixed[row * row_len : row * row_len + half]) * scale
        d_second = to_waves(table, d_mixed[row * row_len + half : (row + 1) * row_len]) * scale
        d_cross = d_second * long_rows[row]
        d_signal.append(
            from_waves(table, conj_times(kernel_low, d_first) + conj_times(kernel_cross, d_cross))
        )
        d_signal.append(from_waves(table, conj_times(kernel_low, d_second)))
        low_grad = low_grad + conj_times(first, d_first) + conj_times(second, d_second)
        cross_grad = cross_grad + conj_times(first, d_cross)
    low_grad = low_grad + turned(cross_grad, -1.0)
    d_kernel = jnp.concatenate([from_waves(table, low_grad), from_waves(table, cross_grad)], axis=0)
    d_signal = jnp.concatenate(d_signal, axis=0)
    d_projected = jnp.concatenate([d_signal, d_gate], axis=1).astype(jnp.bfloat16)
    w_in_grad = jnp.einsum("td,te->de", normed, d_projected, preferred_element_type=jnp.float32)
    d_normed = jnp.einsum("te,de->td", d_projected, w_in, preferred_element_type=jnp.float32)
    ln1_gain_grad = jnp.sum(d_normed * unit_one, axis=0)
    ln1_shift_grad = jnp.sum(d_normed, axis=0)
    input_grad = d_residual + norm_back(d_normed, unit_one, inverse_one, ln1_gain)

    shares = lax.psum_scatter(
        pool(d_kernel).astype(jnp.bfloat16), "narrow", scatter_dimension=0, tiled=True
    )
    summed = lax.psum(shares, "wide").astype(jnp.float32)
    raw_grad = summed * (jnp.abs(raw_taps) > shrink_level).astype(jnp.float32)

    def scatter(values):
        return lax.psum_scatter(
            values.astype(jnp.bfloat16), ("wide", "narrow"), scatter_dimension=0, tiled=True
        ).astype(jnp.float32)

    def scatter_wide(values):
        return lax.psum_scatter(values, ("wide", "narrow"), scatter_dimension=0, tiled=True)

    return (
        block_out,
        input_grad,
        raw_grad,
        scatter_wide(ln1_gain_grad),
        scatter_wide(ln1_shift_grad),
        scatter(w_in_grad),
        scatter(w_out_grad),
        scatter_wide(ln2_gain_grad),
        scatter_wide(ln2_shift_grad),
        scatter(w_up_grad),
        scatter(w_down_grad),
    )


MESH = pl.DeviceIdType.MESH
PART = 9
STORES = 30
VMEM_BYTES = 60 * 2**20
FLIGHTS = 3


def dot_nn(left, right):
    return lax.dot_general(left, right, (((1,), (0,)), ((), ())), preferred_element_type=jnp.float32)


def dot_nt(left, right):
    return lax.dot_general(left, right, (((1,), (1,)), ((), ())), preferred_element_type=jnp.float32)


def dot_tn(left, right):
    return lax.dot_general(left, right, (((0,), (0,)), ((), ())), preferred_element_type=jnp.float32)


def gelu_both(hidden):
    inner = 0.7978845608028654
    cubic = inner * 0.044715
    square = hidden * hidden
    bent = jnp.tanh(hidden * (inner + cubic * square))
    share = 0.5 + 0.5 * bent
    slope = share + (0.5 * hidden) * (1.0 - bent * bent) * (inner + (3.0 * cubic) * square)
    return hidden * share, slope


def blocks_of(rows, columns, height=16, width=768):
    return [
        (slice(at, at + height), slice(left, min(left + width, columns)))
        for at in range(0, rows, height)
        for left in range(0, columns, width)
    ]


def column_sums(values):
    rows, width = values.shape
    return jnp.sum(values.reshape(rows // 8, 8, width), axis=0)


class Place:
    def __init__(self, planes):
        wide = lax.axis_index("wide")
        self.narrow = lax.axis_index("narrow")
        self.wide = wide
        self.core = wide % 2
        self.y = (wide // 2) % 2
        self.z = wide // 4
        self.x = self.narrow
        self.planes = planes
        self.sibling = (wide + 1 - 2 * self.core, self.narrow)
        self.next_x = (wide, 1 - self.narrow)
        self.next_y = (wide + 2 - 4 * self.y, self.narrow)
        self.next_z = (wide + 4 - 8 * (self.z % 2), self.narrow)
        self.far_z = (wide + 8 - 16 * (self.z // 2), self.narrow)

    def plane(self, step):
        other = (self.z + step) % self.planes
        return (self.wide + 4 * (other - self.z), self.narrow), other


class Chunk:
    def __init__(self, place, held, inbox, sems, x_first, target=None, split=False):
        self.place = place
        self.views = (held, inbox, sems)
        self.target, self.x_first, self.split = target, x_first, split
        axes = [(place.x, place.next_x), (place.y, place.next_y)]
        axes = axes if x_first else axes[::-1]
        if split:
            axes = [(place.z % 2, place.next_z)] + axes + [(place.z // 2, place.far_z)]
        self.halvings = [(place.core, place.sibling)] + axes
        self.blocks = 8 * place.planes

    @property
    def held(self):
        ref, at = self.views[0]
        return ref.at[at]

    @property
    def inbox(self):
        return [ref if at is None else ref.at[at] for ref, at in self.views[1]]

    @property
    def sems(self):
        return [ref.at[at] for ref, at in self.views[2]]

    def index(self, z, y, core, x):
        planes = self.place.planes
        first, second = (x, y) if self.x_first else (y, x)
        if self.split:
            return (((core * 2 + z % 2) * 2 + first) * 2 + second) * (planes // 2) + z // 2
        return ((core * 2 + first) * 2 + second) * planes + z

    def base(self, stage):
        return sum(mine * (self.blocks >> (at + 1)) for at, (mine, _) in enumerate(self.halvings[:stage]))

    def landing(self, stage):
        if stage < 3:
            return self.inbox[stage]
        count = self.blocks >> (stage + 1)
        return self.inbox[3].at[pl.ds(0 if stage == 3 else 2, count)]

    def copy(self, stage):
        mine, device = self.halvings[stage]
        count = self.blocks >> (stage + 1)
        return pltpu.make_async_remote_copy(
            src_ref=self.held.at[pl.ds(self.base(stage) + (1 - mine) * count, count)],
            dst_ref=self.landing(stage),
            send_sem=self.sems[0].at[stage],
            recv_sem=self.sems[1].at[stage],
            device_id=device,
            device_id_type=MESH,
        )

    def start(self):
        self.copy(0).start()

    def over(self, stage):
        self.copy(stage).wait()
        base, landing = self.base(stage + 1), self.landing(stage)
        for index in range(self.blocks >> (stage + 1)):
            self.held[base + index] += landing[index]
        if stage + 1 == len(self.halvings):
            self.to_planes()
            return
        if stage + 2 == len(self.halvings) and self.split:
            self.inbox[3][self.place.planes - 1] = self.held[self.base(stage + 2)]
        self.copy(stage + 1).start()

    def to_planes(self):
        planes, base = self.place.planes, self.base(3)
        if self.target is None:
            self.inbox[3][planes - 1] = self.held[base + self.place.z]
        else:

            @pl.when(self.place.z == self.target)
            def _():
                for index in range(planes):
                    self.inbox[3][planes - 1, index] = self.held[base + index]

        self.each_plane(lambda copy: copy.start())

    def plane_copy(self, step):
        device, other = self.place.plane(step)
        base = self.base(3)
        if self.target is None:
            source = self.held.at[base + other]
        else:
            source = self.held.at[pl.ds(base, self.place.planes)]
        return pltpu.make_async_remote_copy(
            src_ref=source,
            dst_ref=self.inbox[3].at[step - 1],
            send_sem=self.sems[0].at[2 + step],
            recv_sem=self.sems[1].at[2 + step],
            device_id=device,
            device_id_type=MESH,
        )

    def each_plane(self, act):
        for step in range(1, self.place.planes):
            if self.target is None:
                act(self.plane_copy(step))
            else:

                @pl.when((self.place.z + step) % self.place.planes == self.target)
                def _():
                    act(self.plane_copy(step))

    def sent(self):
        if self.split:
            self.copy(4).wait_send()
        else:
            self.each_plane(lambda copy: copy.wait_send())

    def arrived(self):
        if self.split:
            self.copy(4).wait_recv()
            return
        for step in range(1, self.place.planes):
            self.plane_copy(step).wait_recv()

    def total(self, index):
        far = self.inbox[3]
        if self.split:
            terms = [far[2], far[3]]
        elif self.target is None:
            terms = [far[step] for step in range(self.place.planes)]
        else:
            terms = [far[step, index] for step in range(self.place.planes)]
        return sum(term.astype(jnp.float32) for term in terms)


def store_rows(chunk, values, first_row):
    width = values.shape[1]
    for k in range(values.shape[0] // 24):
        shard = first_row // 24 + k
        z, y, core, x = shard // 8, shard // 4 % 2, shard // 2 % 2, shard % 2
        at = chunk.index(z, y, core, x)
        block = values[24 * k : 24 * k + 24]
        rest = block[16:24]
        chunk.held[at, :, 0:width] = block[0:16].astype(jnp.bfloat16)
        chunk.held[at, :, width : width + width // 2] = jnp.concatenate(
            [rest[:, : width // 2], rest[:, width // 2 :]], axis=0
        ).astype(jnp.bfloat16)


def load_rows(block, width):
    rest = block[:, width:]
    return jnp.concatenate(
        [block[:, :width], jnp.concatenate([rest[0:8], rest[8:16]], axis=1)], axis=0
    )


def tile_runs(sub, width):
    tiles = width // 128
    runs, tile = [], 0
    while tile < tiles:
        line = sub * tiles + tile
        count = min(tiles - tile, PART - line % PART)
        runs.append((tile, line // PART, line % PART, count))
        tile += count
    return runs


def store_shards(chunk, values, first_row):
    width = values.shape[1]
    for k in range(values.shape[0] // 16):
        row = first_row + 16 * k
        shard, sub = row // 96, row % 96 // 16
        base = chunk.index(0, shard // 4, shard // 2 % 2, shard % 2)
        for tile, block, at, count in tile_runs(sub, width):
            chunk.held[base + block, :, 128 * at : 128 * (at + count)] = values[
                16 * k : 16 * k + 16, 128 * tile : 128 * (tile + count)
            ].astype(jnp.bfloat16)


class Taps:
    def __init__(self, place, held, inbox, result, sems, index, rows, cols, x_first):
        self.place, self.held, self.inbox, self.result = place, held, inbox, result
        self.sems, self.index = sems, index
        self.rows = rows
        self.cols = cols
        self.x_first = x_first

    def part(self, x, core, y, plane, count):
        planes = self.place.planes
        return pl.ds((((x * 2 + core) * 2 + y) * planes + plane) * self.rows, count * self.rows)

    def add(self, target, landing):
        self.held[target, self.cols] += landing[...]

    def landing(self, level, first, count):
        return self.inbox[level].at[pl.ds(first * self.rows, count * self.rows), self.cols]

    def copy(self, kind, step=0):
        place, planes = self.place, self.place.planes
        x, core, y, z = place.x, place.core, place.y, place.z
        if kind == "core":
            source, landing = self.part(step, 1 - core, 0, 0, 2 * planes), self.landing(0, step * 2 * planes, 2 * planes)
            stage, device = step, place.sibling
        elif kind == "first" and self.x_first:
            source, landing = self.part(1 - x, core, 0, 0, 2 * planes), self.landing(1, 0, 2 * planes)
            stage, device = 2, place.next_x
        elif kind == "first":
            source, landing = self.part(step, core, 1 - y, 0, planes), self.landing(1, step * planes, planes)
            stage, device = 2 + step, place.next_y
        elif kind == "second":
            first = self.part(x, core, 1 - y, 0, planes) if self.x_first else self.part(1 - x, core, y, 0, planes)
            source, landing = first, self.landing(2, 0, planes)
            stage, device = 4, place.next_y if self.x_first else place.next_x
        elif kind == "plane":
            device, other = place.plane(step)
            source, landing = self.part(x, core, y, other, 1), self.landing(3, step - 1, 1)
            stage = 4 + step
        else:
            if kind == "back plane":
                mine, stage, device = (0, core, y, z, 1), 3 + planes + step, place.plane(step)[0]
            elif kind == "back y":
                mine, stage, device = (0, core, y, 0, planes), 3 + 2 * planes, place.next_y
            else:
                mine, stage, device = (0, core, 0, 0, 2 * planes), 4 + 2 * planes, place.sibling
            landing = self.result.at[self.part(*mine), self.cols]
        return pltpu.make_async_remote_copy(
            src_ref=landing if kind.startswith("back") else self.held.at[source, self.cols],
            dst_ref=landing,
            send_sem=self.sems[0].at[self.index, stage],
            recv_sem=self.sems[1].at[self.index, stage],
            device_id=device,
            device_id_type=MESH,
        )

    def start(self):
        for x in range(2):
            self.copy("core", x).start()

    def over_core(self):
        for x in range(2):
            self.copy("core", x).wait()
            self.add(
                self.part(x, self.place.core, 0, 0, 2 * self.place.planes),
                self.landing(0, x * 2 * self.place.planes, 2 * self.place.planes),
            )
        for step in range(1 if self.x_first else 2):
            self.copy("first", step).start()

    def over_first(self):
        place, planes = self.place, self.place.planes
        if self.x_first:
            self.copy("first").wait()
            self.add(self.part(place.x, place.core, 0, 0, 2 * planes), self.landing(1, 0, 2 * planes))
        else:
            for x in range(2):
                self.copy("first", x).wait()
                self.add(self.part(x, place.core, place.y, 0, planes), self.landing(1, x * planes, planes))
        self.copy("second").start()

    def over_second(self):
        place = self.place
        self.copy("second").wait()
        self.add(self.part(place.x, place.core, place.y, 0, place.planes), self.landing(2, 0, place.planes))
        for step in range(1, place.planes):
            self.copy("plane", step).start()

    def over_planes(self):
        place = self.place
        mine = self.part(place.x, place.core, place.y, place.z, 1)
        total = self.held[mine, self.cols].astype(jnp.float32)
        for step in range(1, place.planes):
            self.copy("plane", step).wait()
            total = total + self.landing(3, step - 1, 1)[...].astype(jnp.float32)
        self.result[self.part(0, place.core, place.y, place.z, 1), self.cols] = total.astype(self.result.dtype)
        for step in range(1, place.planes):
            self.copy("back plane", step).start()

    def back_y(self):
        for step in range(1, self.place.planes):
            self.copy("back plane", step).wait()
        self.copy("back y").start()

    def back_core(self):
        self.copy("back y").wait()
        self.copy("back core").start()

    def finish(self):
        self.copy("back core").wait()


class Sums:
    def __init__(self, place, levels, inbox, sems):
        self.place, self.levels, self.inbox, self.sems = place, levels, inbox, sems

    def copy(self, level, step=0):
        place = self.place
        device = (place.sibling, place.next_x, place.next_y)[level] if level < 3 else place.plane(step)[0]
        landing = level + max(step - 1, 0)
        return pltpu.make_async_remote_copy(
            src_ref=self.levels.at[level],
            dst_ref=self.inbox.at[landing],
            send_sem=self.sems[0].at[landing],
            recv_sem=self.sems[1].at[landing],
            device_id=device,
            device_id_type=MESH,
        )

    def start(self):
        self.copy(0).start()

    def over(self, level):
        self.copy(level).wait()
        self.levels[level + 1] = self.levels[level] + self.inbox[level]
        if level < 2:
            self.copy(level + 1).start()
        else:
            for step in range(1, self.place.planes):
                self.copy(3, step).start()

    def finish(self):
        total = self.levels[3]
        for step in range(1, self.place.planes):
            self.copy(3, step).wait()
            total = total + self.inbox[2 + step]
        return total


def block_kernel(
    planes,
    lengths,
    tokens, cotangent, raw_taps, w_in, w_out, w_up, w_down, table, table_t,
    ln1_gain, ln1_shift, ln2_gain, ln2_shift,
    block_out, input_grad, taps_out, sums_out, w_in_grad, w_out_grad, w_up_grad, w_down_grad,
    held, inbox0, inbox1, inbox2, inbox_u, inbox_n, taps_held, taps0, taps1, taps2, taps3, taps_sum,
    levels, sums_inbox, cot, active, running, branch_v, normed_v, w_out_v,
    gate_v, mixed_v, left_v, waves, kernels,
    send_sems, recv_sems, taps_send, taps_recv, sums_send, sums_recv, share_send, share_recv, load_sems,
):
    tok_count, feat = cot.shape
    half = tok_count // 2
    tile = active.shape[2]
    step_rows = tap_cols = 256
    blocks = feat // tap_cols
    row_steps = tok_count // step_rows
    place = Place(planes)

    loads = {}

    class Load:
        def __init__(self, source, target):
            self.ends, self.at = (source, target), len(loads)

        def copy(self):
            source, target = (end() if callable(end) else end for end in self.ends)
            return pltpu.make_async_copy(source, target, load_sems.at[self.at])

        def wait(self):
            self.copy().wait()

    def load(name, source, target):
        loads[name] = Load(source, target)
        loads[name].copy().start()

    barrier = pltpu.get_barrier_semaphore()
    partners = [place.sibling, place.next_x, place.next_y] + [
        place.plane(step)[0] for step in range(1, planes)
    ]
    for partner in partners:
        pl.semaphore_signal(barrier, inc=1, device_id=partner, device_id_type=MESH)
    long = jnp.where(lengths[0] > half, 1.0, 0.0).astype(jnp.float32)

    def chunk(index, step, kind, ring, target=None, split=False):
        if target is None:
            far = (inbox_u, index // 2 if index < 2 * planes else index - planes)
        else:
            far = (inbox_n, None)
        return Chunk(
            place,
            (held, step % FLIGHTS * 2 + kind),
            ((inbox0, step % 2 * 2 + kind), (inbox1, ring), (inbox2, ring), far),
            ((send_sems, index), (recv_sems, index)),
            kind == 0,
            target,
            split,
        )

    ups = [
        chunk(2 * t, t, 0, 4 + t // 2, split=True) if t % 2 == 1 else chunk(2 * t, t, 0, t // 2 % 2)
        for t in range(planes)
    ]
    downs = [chunk(2 * t + 1, t, 1, 2 + t % 2, t) for t in range(planes)]

    def rows_of(index):
        return pl.ds(index * step_rows, step_rows)

    def under(index, part):
        return pl.ds(index * step_rows + part.start, part.stop - part.start)

    def unrolled(first, last, body, carry):
        for index in range(first, last):
            carry = body(index, carry)
        return carry

    def norm_of(values):
        centered = values - jnp.mean(values, axis=-1, keepdims=True)
        inverse = lax.rsqrt(jnp.mean(centered * centered, axis=-1, keepdims=True) + eps_norm)
        return centered * inverse, inverse

    out_chunk = chunk(2 * planes, planes, 0, 4 + planes // 2, split=True)
    gate_chunk = chunk(2 * planes + 1, planes, 1, 2 + planes % 2)
    signal_chunk = chunk(2 * planes + 2, planes + 1, 0, planes // 2 % 2)
    taps = [
        Taps(
            place, taps_held, (taps0, taps1, taps2, taps3), taps_sum, (taps_send, taps_recv), index,
            tok_count // (8 * planes), pl.ds(index * tap_cols, tap_cols), index % 2 == 0,
        )
        for index in range(feat // tap_cols)
    ]
    sums = Sums(place, levels, sums_inbox, (sums_send, sums_recv))

    def own_rows(target):
        target.arrived()
        return load_rows(target.total(0), feat)

    def own_down(t):
        @pl.when(place.z == t)
        def _():
            downs[t].arrived()
            for index in range(planes):
                block = downs[t].total(index)
                for sub in range(6):
                    for first, line, at, count in tile_runs(sub, feat):
                        if line == index:
                            w_down_grad[16 * sub : 16 * sub + 16, 128 * first : 128 * (first + count)] = block[
                                :, 128 * at : 128 * (at + count)
                            ]

    def weight_rows(target, left_t, right):
        for part in range(2):
            rows = feat // 2
            store_rows(target, dot_nn(left_t[part * rows : (part + 1) * rows, :], right[...]), part * rows)
        target.start()

    def own_up(t):
        w_up_grad[:, t * tile : (t + 1) * tile] = own_rows(ups[t])

    def own_out():
        w_out_grad[...] = own_rows(out_chunk)

    def own_gate():
        w_in_grad[:, feat:] = own_rows(gate_chunk)

    def own_signal():
        w_in_grad[:, 0:feat] = own_rows(signal_chunk)

    def taps_copy(index):
        cols = pl.ds(index * tap_cols, tap_cols)
        return pltpu.make_async_copy(taps_sum.at[:, cols], taps_out.at[:, cols], load_sems.at[STORES - 1 - index])

    def own_taps(index):
        taps[index].finish()
        taps_copy(index).start()

    def share_copy(which, across):
        quarter = half // 4
        block_x = place.x if which == 0 else 1 - place.x
        start = block_x * half + place.core * 2 * quarter
        if which < 2:
            rows = pl.ds(pl.multiple_of(start + place.y * quarter, quarter), quarter)
        else:
            rows = pl.ds(pl.multiple_of(start, quarter), 2 * quarter)
        part = taps_held.at[rows, pl.ds(across * tap_cols, tap_cols)]
        return pltpu.make_async_remote_copy(
            src_ref=part,
            dst_ref=part,
            send_sem=share_send.at[which, across],
            recv_sem=share_recv.at[which, across],
            device_id=(place.next_x, place.next_y, place.sibling)[which],
            device_id_type=MESH,
        )

    def share_on(which, across):
        share_copy(which, across).wait()
        share_copy(which + 1, across).start()

    def forward_back(normed_2, normed_2t, up_tiles, down_tiles):
        def load_tile(t):
            cols = pl.ds(t * tile, tile)
            load(("up", t), lambda: w_up.at[:, cols], lambda: up_tiles.at[t % 2])
            load(("down", t), lambda: w_down.at[cols, :], lambda: down_tiles.at[t % 2])

        def mix(table_v, table_tv):
            kernel = mixed_v
            load("taps", raw_taps, running.at[0:half, :])
            load("tokens", tokens, lambda: active.at[0])
            load("w_in", w_in.at[:, 0:feat], normed_2.at[0:feat, :])
            load("w_in end", w_in.at[:, feat : 2 * feat], normed_2t.at[:, 0:feat])
            load("table", table, table_v)
            load("table_t", table_t, table_tv)
            load("w_out", w_out, w_out_v)
            load_tile(0)
            load("cot", cotangent, cot)

            loads["taps"].wait()

            def squash_step(index, carry):
                rows = pl.ds(pl.multiple_of(index * 128, 128), 128)
                raw = running[rows, :]
                taps_held[pl.ds(pl.multiple_of(place.x * half + index * 128, 128), 128), :] = (
                    raw - jnp.clip(raw, -shrink_level, shrink_level)
                ).astype(jnp.bfloat16)
                return carry

            lax.fori_loop(0, half // 128, squash_step, 0)
            pl.semaphore_wait(barrier, len(partners))
            for across in range(blocks):
                share_copy(0, across).start()
            loads["tokens"].wait()
            loads["w_in"].wait()
            loads["w_in end"].wait()

            def project_step(index, carry):
                rows = rows_of(index)
                for part, _ in blocks_of(step_rows, feat):
                    at = under(index, part)
                    unit, _ = norm_of(active[0, at, :].astype(jnp.float32))
                    mixed_v[at, :] = (unit * ln1_gain[...][None, :] + ln1_shift[...][None, :]).astype(jnp.bfloat16)
                low = mixed_v[rows, :]
                normed_v[:, rows] = low.T
                active[1, rows, :] = dot_nn(low, normed_2[0:feat, :]).astype(jnp.bfloat16)
                gate_v[rows, :] = dot_nn(low, normed_2t[:, 0:feat]).astype(jnp.bfloat16)
                return carry

            unrolled(0, row_steps, project_step, 0)
            share_on(0, 0)
            loads["table"].wait()

            def signal_wave_step(index, carry):
                rows = rows_of(index)
                for which in range(2):
                    waves[which, rows, :] = dot_nn(
                        table_v[rows, :], active[1, which * half : (which + 1) * half, :]
                    ).astype(jnp.bfloat16)
                return carry

            unrolled(0, row_steps // 2, signal_wave_step, 0)
            share_on(0, 1)
            unrolled(row_steps // 2, row_steps, signal_wave_step, 0)
            share_on(1, 0)
            share_on(0, 2)
            pool_rows = 16

            def pool_step(across):
                cols = slice(across * tap_cols, (across + 1) * tap_cols)
                rim = jnp.zeros((16, tap_cols), jnp.float32)
                for index in range(tok_count // pool_rows):
                    at = index * pool_rows
                    first, last = max(at - 16, 0), min(at + pool_rows + 16, tok_count)
                    around = taps_held[first:last, cols].astype(jnp.float32)
                    if at == 0:
                        around = jnp.concatenate([rim, around], axis=0)
                    if last == tok_count:
                        around = jnp.concatenate([around, rim], axis=0)
                    kernel[at : at + pool_rows, cols] = (
                        (around[15 : 15 + pool_rows] + around[16 : 16 + pool_rows] + around[17 : 17 + pool_rows])
                        / 3.0
                    ).astype(jnp.bfloat16)

            def spread_step(down, across):
                real, imag = pl.ds(down * 256, 256), pl.ds(half + down * 256, 256)
                cols = pl.ds(across * 256, 256)
                low_r = dot_nn(table_v[real, :], kernel[0:half, cols])
                low_i = dot_nn(table_v[imag, :], kernel[0:half, cols])
                high_r = dot_nn(table_v[real, :], kernel[half:, cols])
                high_i = dot_nn(table_v[imag, :], kernel[half:, cols])
                odd = lax.broadcasted_iota(jnp.int32, (16, 1), 0) % 2
                parity = (1 - 2 * odd).astype(jnp.float32)
                scale = 1.0 / half
                for part, _ in blocks_of(256, tap_cols):
                    re, im = under(down, part), pl.ds(half + down * 256 + part.start, 16)

                    def keep(ref, which, at, values):
                        ref[which, at, cols] = values.astype(jnp.bfloat16)

                    lr, li = low_r[part], low_i[part]
                    cr, ci = long * (high_r[part] - parity * li), long * (high_i[part] + parity * lr)
                    keep(kernels, 0, re, lr)
                    keep(kernels, 0, im, li)
                    keep(kernels, 1, re, cr)
                    keep(kernels, 1, im, ci)
                    hr, hi, tr, ti = (
                        waves[which, at, cols].astype(jnp.float32) * scale for which in range(2) for at in (re, im)
                    )
                    keep(active, 2, re, lr * hr - li * hi)
                    keep(active, 2, im, lr * hi + li * hr)
                    keep(active, 3, re, lr * tr - li * ti + cr * hr - ci * hi)
                    keep(active, 3, im, lr * ti + li * tr + cr * hi + ci * hr)

            for across in range(blocks):
                share_copy(2, across).wait()
                if across + 1 < blocks:
                    share_on(1, across + 1)
                pool_step(across)
                for down in range(half // 256):
                    spread_step(down, across)
            loads["table_t"].wait()
            loads["w_out"].wait()

            def residual_step(index, carry):
                rows = rows_of(index)
                part_steps = half // step_rows
                which = index // part_steps
                of_part = pl.ds(index % part_steps * step_rows, step_rows)
                mixed = dot_nn(table_tv[of_part, :], active[2 + which])
                for part, columns in blocks_of(step_rows, feat):
                    at = under(index, part)
                    mixed_v[at, columns] = mixed[part, columns].astype(jnp.bfloat16)
                    active[1, at, columns] = (
                        mixed[part, columns] * gate_v[at, columns].astype(jnp.float32)
                    ).astype(jnp.bfloat16)
                branch = active[1, rows, :]
                branch_v[:, rows] = branch.T
                added = dot_nn(branch, w_out_v[...])
                for part, _ in blocks_of(step_rows, feat):
                    at = under(index, part)
                    left = active[0, at, :].astype(jnp.float32) + added[part]
                    left_v[at, :] = left
                    unit, _ = norm_of(left)
                    normed_2[at, :] = (unit * ln2_gain[...][None, :] + ln2_shift[...][None, :]).astype(jnp.bfloat16)
                normed_2t[:, rows] = normed_2[rows, :].T
                return carry

            unrolled(0, row_steps, residual_step, 0)

        pl.run_scoped(
            mix,
            pltpu.VMEM((tok_count, half), jnp.bfloat16),
            pltpu.VMEM((half, tok_count), jnp.bfloat16),
        )

        def feed_forward(d_hidden):
            loads["cot"].wait()

            def forward_piece(t, index):
                if index == 0:
                    loads["up", t].wait()
                    if t == 0:
                        load_tile(1)
                rows = rows_of(index)
                hidden = dot_nn(normed_2[rows, :], up_tiles[t % 2])
                for part, columns in blocks_of(step_rows, tile, 16, 384):
                    at = under(index, part)
                    value, slope = gelu_both(hidden[part, columns])
                    active[t, at, columns] = value.astype(jnp.bfloat16)
                    d_hidden[t % 2, at, columns] = slope.astype(jnp.bfloat16)

            def hidden_piece(t, index):
                if index == 0:
                    loads["down", t].wait()
                rows = rows_of(index)
                d_active = dot_nt(cot[rows, :], down_tiles[t % 2])
                for part, columns in blocks_of(step_rows, tile, 16, 384):
                    at = under(index, part)
                    slope = d_hidden[t % 2, at, columns].astype(jnp.float32)
                    d_hidden[t % 2, at, columns] = (d_active[part, columns] * slope).astype(jnp.bfloat16)
                back = dot_nt(d_hidden[t % 2, rows, :], up_tiles[t % 2])
                if t == 0:
                    running[rows, :] = back
                else:
                    running[rows, :] += back
                if index == row_steps - 1 and t + 2 < planes:
                    load_tile(t + 2)

            def up_piece(t):
                if t >= FLIGHTS:
                    ups[t - FLIGHTS].sent()
                weight_rows(ups[t], normed_2t, d_hidden.at[t % 2])

            def down_piece(t):
                if t >= FLIGHTS:
                    downs[t - FLIGHTS].sent()
                for part in range(2):
                    cols = slice(part * (tile // 2), (part + 1) * (tile // 2))
                    store_shards(downs[t], dot_tn(active[t, :, cols], cot[...]), part * (tile // 2))
                downs[t].start()

            forward_piece(0, 0)
            forward_piece(0, 1)
            forward_piece(0, 2)
            forward_piece(0, 3)
            down_piece(0)
            forward_piece(1, 0)
            hidden_piece(0, 0)
            hidden_piece(0, 1)
            hidden_piece(0, 2)
            downs[0].over(0)
            hidden_piece(0, 3)
            forward_piece(1, 1)
            up_piece(0)
            forward_piece(1, 2)
            forward_piece(1, 3)
            down_piece(1)
            ups[0].over(0)
            hidden_piece(1, 0)
            hidden_piece(1, 1)
            hidden_piece(1, 2)
            hidden_piece(1, 3)
            up_piece(1)
            downs[0].over(1)
            downs[1].over(0)
            forward_piece(2, 0)
            hidden_piece(2, 0)
            ups[1].over(0)
            forward_piece(2, 1)
            forward_piece(2, 2)
            forward_piece(2, 3)
            hidden_piece(2, 1)
            forward_piece(3, 0)
            down_piece(2)
            hidden_piece(2, 2)
            hidden_piece(2, 3)
            ups[0].over(1)
            downs[0].over(2)
            downs[1].over(1)
            downs[2].over(0)
            up_piece(2)
            forward_piece(3, 1)
            hidden_piece(3, 0)
            hidden_piece(3, 1)
            ups[1].over(1)
            ups[2].over(0)
            ups[0].over(2)
            downs[1].over(2)
            forward_piece(3, 2)
            forward_piece(3, 3)
            hidden_piece(3, 2)
            hidden_piece(3, 3)
            up_piece(3)
            down_piece(3)

        pl.run_scoped(feed_forward, pltpu.VMEM((2, tok_count, tile), jnp.bfloat16))

    pl.run_scoped(
        forward_back,
        pltpu.VMEM((tok_count, feat), jnp.bfloat16),
        pltpu.VMEM((feat, tok_count), jnp.bfloat16),
        pltpu.VMEM((2, feat, tile), jnp.bfloat16),
        pltpu.VMEM((2, tile, feat), jnp.bfloat16),
    )

    def backward(d_out, d_gate, d_mix, d_signal, table_v, table_tv, d_kernel, d_taps):
        d_waves = waves
        load("table again", table, table_v)
        load("table_t again", table_t, table_tv)
        totals = {}

        def sum_rows(at, index, values):
            totals[at] = values + (totals[at] if index > 0 else 0.0)
            if index == row_steps - 1:
                levels[0, at : at + 1, :] = jnp.sum(totals[at], axis=0, keepdims=True)

        def back_piece(index):
            if index == 0:
                levels[0] = jnp.zeros(levels.shape[1:], jnp.float32)
            rows = rows_of(index)
            sums_of = [0.0, 0.0]
            for part, _ in blocks_of(step_rows, feat):
                at = under(index, part)
                unit, inverse = norm_of(left_v[at, :])
                grad = running[at, :]
                sums_of = [sums_of[0] + column_sums(grad * unit), sums_of[1] + column_sums(grad)]
                scaled = grad * ln2_gain[...][None, :]
                d_left = cot[at, :].astype(jnp.float32) + inverse * (
                    scaled
                    - jnp.mean(scaled, axis=-1, keepdims=True)
                    - unit * jnp.mean(scaled * unit, axis=-1, keepdims=True)
                )
                running[at, :] = d_left
                d_out[at, :] = d_left.astype(jnp.bfloat16)
            d_branch = dot_nt(d_out[rows, :], w_out_v[...])
            for part, columns in blocks_of(step_rows, feat):
                at = under(index, part)
                values = d_branch[part, columns]
                d_mix[at, columns] = (
                    values * gate_v[at, columns].astype(jnp.float32) * (1.0 / half)
                ).astype(jnp.bfloat16)
                d_gate[at, columns] = (values * mixed_v[at, columns].astype(jnp.float32)).astype(jnp.bfloat16)
            sum_rows(0, index, sums_of[0])
            sum_rows(1, index, sums_of[1])
            if index == row_steps - 1:
                load("tokens again", tokens, gate_v)

        def gate_piece():
            downs[planes - 3].sent()
            weight_rows(gate_chunk, normed_v, d_gate)

        def out_piece():
            ups[planes - 3].sent()
            weight_rows(out_chunk, branch_v, d_out)

        def signal_piece():
            ups[planes - 2].sent()
            weight_rows(signal_chunk, normed_v, d_signal)

        wave_rows, wave_cols = 256, 256

        def wave_step(down, cols):
            real, imag = pl.ds(down * wave_rows, wave_rows), pl.ds(half + down * wave_rows, wave_rows)
            first_r = dot_nn(table_v[real, :], d_mix[0:half, cols])
            first_i = dot_nn(table_v[imag, :], d_mix[0:half, cols])
            second_r = dot_nn(table_v[real, :], d_mix[half:, cols])
            second_i = dot_nn(table_v[imag, :], d_mix[half:, cols])

            odd = lax.broadcasted_iota(jnp.int32, (16, 1), 0) % 2
            parity = (1 - 2 * odd).astype(jnp.float32)
            for part, _ in blocks_of(wave_rows, wave_cols):
                re = pl.ds(down * wave_rows + part.start, 16)
                im = pl.ds(half + down * wave_rows + part.start, 16)

                def wide(ref, which, at):
                    return ref[which, at, cols].astype(jnp.float32)

                def keep(ref, which, at, values):
                    ref[which, at, cols if ref.shape[2] == feat else slice(None)] = values.astype(jnp.bfloat16)

                fr, fi, sr, si = first_r[part], first_i[part], second_r[part], second_i[part]
                hr, hi = wide(waves, 0, re), wide(waves, 0, im)
                far_r, far_i = (hr * sr + hi * si) * long, (hr * si - hi * sr) * long
                keep(d_kernel, 1, re, far_r)
                keep(d_kernel, 1, im, far_i)
                tr, ti = wide(waves, 1, re), wide(waves, 1, im)
                keep(d_kernel, 0, re, hr * fr + hi * fi + tr * sr + ti * si + parity * far_i)
                keep(d_kernel, 0, im, hr * fi - hi * fr + tr * si - ti * sr - parity * far_r)
                lr, li = wide(kernels, 0, re), wide(kernels, 0, im)
                keep(d_waves, 1, re, lr * sr + li * si)
                keep(d_waves, 1, im, lr * si - li * sr)
                cr, ci = wide(kernels, 1, re), wide(kernels, 1, im)
                keep(d_waves, 0, re, lr * fr + li * fi + cr * sr + ci * si)
                keep(d_waves, 0, im, lr * fi - li * fr + cr * si - ci * sr)

        pad = 8
        d_taps[0:pad, :] = jnp.zeros((pad, wave_cols), jnp.float32)
        d_taps[pad + tok_count :, :] = jnp.zeros((pad, wave_cols), jnp.float32)
        pool_rows = 16

        def column_step(across):
            cols = pl.ds(across * wave_cols, wave_cols)
            for down in range(half // wave_rows):
                wave_step(down, cols)
            for which in range(2):
                d_taps[pad + which * half : pad + (which + 1) * half, :] = dot_nn(table_tv[...], d_kernel[which])
            for index in range(tok_count // pool_rows):
                at = pad + index * pool_rows
                taps_held[at - pad : at - pad + pool_rows, cols] = (
                    (
                        d_taps[at - 1 : at - 1 + pool_rows, :]
                        + d_taps[at : at + pool_rows, :]
                        + d_taps[at + 1 : at + 1 + pool_rows, :]
                    )
                    / 3.0
                ).astype(jnp.bfloat16)


        def column_piece(across):
            if across == 0:
                loads["table again"].wait()
                loads["table_t again"].wait()
            column_step(across)
            taps[across].start()
            if across == blocks - 1:
                load("w_in signal", w_in.at[:, 0:feat], cot.at[0:feat, :])
                load("w_in gate", w_in.at[:, feat : 2 * feat], d_mix.at[0:feat, :])

        def down_again(t):
            return (waves if t < 2 else kernels).at[t % 2, 0:tile, :]

        def load_again(t):
            rows = pl.ds(t * tile, tile)
            load(("again", t), lambda: w_down.at[rows, :], lambda: down_again(t))

        def unwave_piece(which):
            for at in range(0, half, step_rows):
                d_signal[which * half + at : which * half + at + step_rows, :] = dot_nn(
                    table_tv[at : at + step_rows, :], d_waves[which]
                ).astype(jnp.bfloat16)
            if which == 1:
                for t in range(planes):
                    load_again(t)

        def grad_copy(index):
            rows = rows_of(index)
            return pltpu.make_async_copy(
                running.at[rows, :], input_grad.at[rows, :], load_sems.at[STORES + index]
            )

        def out_copy(index):
            rows = rows_of(index)
            return pltpu.make_async_copy(
                mixed_v.at[rows, :], block_out.at[rows, :], load_sems.at[STORES + row_steps + index]
            )

        def input_piece(index):
            if index == 0:
                loads["tokens again"].wait()
                loads["w_in signal"].wait()
                loads["w_in gate"].wait()
            rows = rows_of(index)
            d_normed = dot_nt(d_signal[rows, :], cot[0:feat, :]) + dot_nt(
                d_gate[rows, :], d_mix[0:feat, :]
            )
            sums_of = [0.0, 0.0]
            for part, _ in blocks_of(step_rows, feat):
                at = under(index, part)
                unit, inverse = norm_of(gate_v[at, :].astype(jnp.float32))
                grad = d_normed[part]
                sums_of = [sums_of[0] + column_sums(grad * unit), sums_of[1] + column_sums(grad)]
                scaled = grad * ln1_gain[...][None, :]
                running[at, :] = running[at, :] + inverse * (
                    scaled
                    - jnp.mean(scaled, axis=-1, keepdims=True)
                    - unit * jnp.mean(scaled * unit, axis=-1, keepdims=True)
                )
            grad_copy(index).start()
            sum_rows(2, index, sums_of[0])
            sum_rows(3, index, sums_of[1])

        def output_piece(index):
            if index == 0:
                for t in range(planes):
                    loads["again", t].wait()
            rows = rows_of(index)
            total = left_v[rows, :]
            for t in range(planes):
                total = total + dot_nn(active[t, rows, :], down_again(t)[...])
            mixed_v[rows, :] = total.astype(jnp.bfloat16)
            out_copy(index).start()

        back_piece(0)
        ups[3].over(0)
        ups[1].over(2)
        downs[2].over(1)
        back_piece(1)
        back_piece(2)
        downs[3].over(0)
        ups[1].over(3)
        back_piece(3)
        out_piece()
        column_piece(0)
        out_chunk.over(0)
        ups[2].over(1)
        downs[2].over(2)
        taps[0].over_core()
        column_piece(1)
        downs[3].over(1)
        column_piece(2)
        taps[0].over_first()
        own_down(1)
        unwave_piece(0)
        ups[2].over(2)
        taps[2].over_core()
        taps[1].over_core()
        ups[3].over(1)
        gate_piece()
        downs[3].over(2)
        unwave_piece(1)
        input_piece(0)
        taps[2].over_first()
        taps[1].over_first()
        gate_chunk.over(0)
        input_piece(1)
        signal_piece()
        out_chunk.over(1)
        signal_chunk.over(0)
        taps[2].over_second()
        taps[1].over_second()
        input_piece(2)
        input_piece(3)
        ups[3].over(2)
        own_up(1)
        output_piece(0)
        taps[0].over_second()
        out_chunk.over(2)
        ups[3].over(3)
        own_up(2)
        out_chunk.over(3)
        own_up(0)
        gate_chunk.over(1)
        taps[2].over_planes()
        signal_chunk.over(1)
        sums.start()
        taps[1].over_planes()
        own_down(2)
        own_down(0)
        taps[0].over_planes()
        output_piece(1)
        gate_chunk.over(2)
        taps[2].back_y()
        output_piece(2)
        own_down(3)
        taps[1].back_y()
        taps[0].back_y()
        own_up(3)
        sums.over(0)
        taps[2].back_core()
        own_out()
        signal_chunk.over(2)
        output_piece(3)
        sums.over(1)
        taps[0].back_core()
        taps[1].back_core()
        sums.over(2)
        own_taps(2)
        own_gate()
        own_taps(0)
        own_taps(1)
        own_signal()
        for index in range(row_steps):
            grad_copy(index).wait()
            out_copy(index).wait()

    pl.run_scoped(
        backward,
        *[pltpu.VMEM((tok_count, feat), jnp.bfloat16)] * 4,
        pltpu.VMEM((tok_count, half), jnp.bfloat16),
        pltpu.VMEM((half, tok_count), jnp.bfloat16),
        pltpu.VMEM((2, tok_count, tap_cols), jnp.bfloat16),
        pltpu.VMEM((tok_count + 16, tap_cols), jnp.float32),
    )

    sums_out[...] = sums.finish()
    for one in (downs[planes - 2], ups[planes - 1], downs[planes - 1], out_chunk, gate_chunk, signal_chunk):
        one.sent()
    for index in range(blocks):
        taps_copy(index).wait()


def hand_on_kernel(raw_taps, taps_sum, *others):
    count = (len(others) - 5) // 3
    sources, raw_grad, targets = others[:count], others[count], others[count + 1 : 2 * count + 1]
    raw_v, taps_v, grad_v = others[2 * count + 1 : 2 * count + 4]
    rooms, sems = others[2 * count + 4 : -1], others[-1]
    fetches = [pltpu.make_async_copy(taps_sum, taps_v, sems.at[0]), pltpu.make_async_copy(raw_taps, raw_v, sems.at[1])]
    stores = []
    for source, room, target in zip(sources, rooms, targets):
        rows = source.shape[0]
        parts = 4 if rows % 64 == 0 else 1
        for part in range(parts):
            at = pl.ds(part * (rows // parts), rows // parts)
            sem = sems.at[1 + len(fetches)]
            fetches.append(pltpu.make_async_copy(source.at[at, :], room.at[at, :], sem))
            stores.append(pltpu.make_async_copy(room.at[at, :], target.at[at, :], sem))
    for fetch in fetches:
        fetch.start()
    for fetch in fetches[:2]:
        fetch.wait()
    grad_v[...] = jnp.where(jnp.abs(raw_v[...]) > shrink_level, taps_v[...].astype(jnp.float32), 0.0)
    mask = pltpu.make_async_copy(grad_v, raw_grad, sems.at[2])
    mask.start()
    for fetch, store in zip(fetches[2:], stores):
        fetch.wait()
        store.start()
    for store in [mask] + stores:
        store.wait()


def hand_on(raw_taps, taps_sum, *sources):
    whole = pl.BlockSpec(memory_space=pl.ANY)
    return pl.pallas_call(
        hand_on_kernel,
        out_shape=[jax.ShapeDtypeStruct(raw_taps.shape, jnp.float32)]
        + [jax.ShapeDtypeStruct(source.shape, source.dtype) for source in sources],
        in_specs=[whole] * (2 + len(sources)),
        out_specs=[whole] * (1 + len(sources)),
        scratch_shapes=[
            pltpu.VMEM(raw_taps.shape, jnp.float32),
            pltpu.VMEM(taps_sum.shape, taps_sum.dtype),
            pltpu.VMEM(raw_taps.shape, jnp.float32),
        ]
        + [pltpu.VMEM(source.shape, source.dtype) for source in sources]
        + [pltpu.SemaphoreType.DMA((3 + 4 * len(sources),))],
        compiler_params=pltpu.CompilerParams(vmem_limit_bytes=VMEM_BYTES),
    )(raw_taps, taps_sum, *sources)


def linked_block(
    planes,
    tokens,
    lengths,
    raw_taps,
    ln1_gain,
    ln1_shift,
    w_in,
    w_out,
    ln2_gain,
    ln2_shift,
    w_up,
    w_down,
    cotangent,
):
    tok_count, feat = tokens.shape
    half = tok_count // 2
    tile = w_up.shape[1] // planes
    table = jnp.asarray(wave_table(half), jnp.bfloat16)
    table_t = jnp.asarray(wave_table(half).T, jnp.bfloat16)
    shares = 8 * planes
    rows = feat // shares
    block = (16, 128 * PART)
    chunks = 2 * planes + 3
    bf16, f32 = jnp.bfloat16, jnp.float32
    whole = pl.BlockSpec(memory_space=pl.ANY)
    near = pl.BlockSpec(memory_space=pltpu.VMEM)
    results = pl.pallas_call(
        functools.partial(block_kernel, planes),
        out_shape=(
            jax.ShapeDtypeStruct((tok_count, feat), bf16),
            jax.ShapeDtypeStruct((tok_count, feat), f32),
            jax.ShapeDtypeStruct((half, feat), bf16),
            jax.ShapeDtypeStruct((8, feat), f32),
            jax.ShapeDtypeStruct((rows, 2 * feat), f32),
            jax.ShapeDtypeStruct((rows, feat), f32),
            jax.ShapeDtypeStruct((rows, planes * tile), f32),
            jax.ShapeDtypeStruct((tile // 8, feat), f32),
        ),
        in_specs=[pl.BlockSpec(memory_space=pltpu.SMEM)] + [whole] * 9 + [near] * 4,
        out_specs=(whole,) * 3 + (near,) * 5,
        scratch_shapes=[
            pltpu.VMEM((2 * FLIGHTS, shares) + block, bf16),
            pltpu.VMEM((4, 4 * planes) + block, bf16),
            pltpu.VMEM((5 + planes // 2, 2 * planes) + block, bf16),
            pltpu.VMEM((5 + planes // 2, planes) + block, bf16),
            pltpu.VMEM((planes + 3, planes) + block, bf16),
            pltpu.VMEM((planes, planes) + block, bf16),
            pltpu.VMEM((tok_count, feat), bf16),
            pltpu.VMEM((tok_count // 2, feat), bf16),
            pltpu.VMEM((tok_count // 4, feat), bf16),
            pltpu.VMEM((tok_count // 8, feat), bf16),
            pltpu.VMEM(((planes - 1) * (tok_count // shares), feat), bf16),
            pltpu.VMEM((half, feat), bf16),
            pltpu.VMEM((4, 8, feat), f32),
            pltpu.VMEM((planes + 2, 8, feat), f32),
            pltpu.VMEM((tok_count, feat), bf16),
            pltpu.VMEM((planes, tok_count, tile), bf16),
            pltpu.VMEM((tok_count, feat), f32),
            pltpu.VMEM((feat, tok_count), bf16),
            pltpu.VMEM((feat, tok_count), bf16),
            pltpu.VMEM((feat, feat), bf16),
            pltpu.VMEM((tok_count, feat), bf16),
            pltpu.VMEM((tok_count, feat), bf16),
            pltpu.VMEM((tok_count, feat), f32),
            pltpu.VMEM((2, tok_count, feat), bf16),
            pltpu.VMEM((2, tok_count, feat), bf16),
            pltpu.SemaphoreType.DMA((chunks, planes + 2)),
            pltpu.SemaphoreType.DMA((chunks, planes + 2)),
            pltpu.SemaphoreType.DMA((feat // 256, 2 * planes + 5)),
            pltpu.SemaphoreType.DMA((feat // 256, 2 * planes + 5)),
            pltpu.SemaphoreType.DMA((planes + 2,)),
            pltpu.SemaphoreType.DMA((planes + 2,)),
            pltpu.SemaphoreType.DMA((3, feat // 256)),
            pltpu.SemaphoreType.DMA((3, feat // 256)),
            pltpu.SemaphoreType.DMA((STORES + 2 * tok_count // 256,)),
        ],
        compiler_params=pltpu.CompilerParams(
            collective_id=1, has_side_effects=True, vmem_limit_bytes=VMEM_BYTES
        ),
        cost_estimate=pl.CostEstimate(
            flops=2 * tok_count * feat * (5 * w_up.shape[1] + 9 * feat),
            bytes_accessed=40 * tok_count * feat,
            transcendentals=tok_count * w_up.shape[1],
        ),
    )(
        lengths,
        tokens,
        cotangent,
        raw_taps,
        w_in,
        w_out,
        w_up,
        w_down,
        table,
        table_t,
        ln1_gain,
        ln1_shift,
        ln2_gain,
        ln2_shift,
    )
    block_out, input_grad, taps_sum, sums, w_in_grad, w_out_grad, w_up_grad, w_down_grad = results
    raw_grad, block_out, input_grad, w_in_grad, w_out_grad, w_up_grad, w_down_grad = hand_on(
        raw_taps, taps_sum, block_out, input_grad, w_in_grad, w_out_grad, w_up_grad, w_down_grad
    )
    share = lax.axis_index("wide") * 2 + lax.axis_index("narrow")
    mine = lax.dynamic_slice(sums, (0, share * rows), (8, rows))
    return (
        block_out,
        input_grad,
        raw_grad,
        mine[2],
        mine[3],
        w_in_grad,
        w_out_grad,
        mine[0],
        mine[1],
        w_up_grad,
        w_down_grad,
    )


def solution(mesh):
    spread = P(("wide", "narrow"))
    rows = P(("wide", "narrow"), None)
    placed = (rows, spread, P("narrow", None)) + (P(),) * 8 + (rows,)
    wide, narrow = mesh.shape["wide"], mesh.shape["narrow"]

    def block(tokens, lengths, raw_taps, *others):
        fits = (
            narrow == 2
            and wide == 4 * 4
            and lengths.shape[0] == 1
            and raw_taps.shape[0] * 2 == tokens.shape[0]
            and tokens.shape[1] == 24 * wide * narrow
            and others[-2].shape[0] == 96 * wide * narrow
            and tokens.shape[0] % 512 == 0
        )
        if fits:
            return linked_block(wide // 4, tokens, lengths, raw_taps, *others)
        return local(tokens, lengths, raw_taps, *others)

    return jax.shard_map(
        block,
        mesh=mesh,
        in_specs=placed,
        out_specs=(rows, rows, P("narrow", None), spread, spread, rows, rows, spread, spread, rows, rows),
        check_vma=False,
    )
```

```python
import functools

import jax
import jax.numpy as jnp
import numpy as np
from jax import lax
from jax.experimental import pallas as pl
from jax.experimental.pallas import tpu as pltpu
from jax.sharding import PartitionSpec as P

shrink_level = 0.003
eps_norm = 1e-05


def wave_table(half):
    period = 4 * half
    phase = (np.outer(2 * np.arange(half) + 1, np.arange(half)) % period) * (2 * np.pi / period)
    return np.concatenate([np.cos(phase), -np.sin(phase)], axis=0)


def to_waves(table, block):
    return jnp.einsum("kn,nc->kc", table, block, preferred_element_type=jnp.float32)


def from_waves(table, waves):
    return jnp.einsum(
        "kn,kc->nc", table, waves.astype(jnp.bfloat16), preferred_element_type=jnp.float32
    )


def norm_parts(values):
    centered = values - jnp.mean(values, axis=-1, keepdims=True)
    inverse = lax.rsqrt(jnp.mean(centered * centered, axis=-1, keepdims=True) + eps_norm)
    return (centered * inverse, inverse)


def norm_back(upstream, unit_vals, inverse, gain_vec):
    scaled = upstream * gain_vec
    return inverse * (
        scaled
        - jnp.mean(scaled, axis=-1, keepdims=True)
        - unit_vals * jnp.mean(scaled * unit_vals, axis=-1, keepdims=True)
    )


def split(waves):
    half = waves.shape[0] // 2
    return waves[:half], waves[half:]


def times(left, right):
    lr, li = split(left)
    rr, ri = split(right)
    return jnp.concatenate([lr * rr - li * ri, lr * ri + li * rr], axis=0)


def conj_times(left, right):
    lr, li = split(left)
    rr, ri = split(right)
    return jnp.concatenate([lr * rr + li * ri, lr * ri - li * rr], axis=0)


def turned(waves, sign):
    wr, wi = split(waves)
    index = lax.broadcasted_iota(jnp.int32, (wr.shape[0], 1), 0)
    parity = sign * (1.0 - 2.0 * (index % 2).astype(jnp.float32))
    return jnp.concatenate([-parity * wi, parity * wr], axis=0)


def pool(values):
    padded = jnp.pad(values, ((1, 1), (0, 0)))
    return (padded[:-2] + padded[1:-1] + padded[2:]) / 3.0


def local(
    tokens,
    lengths,
    raw_taps,
    ln1_gain,
    ln1_shift,
    w_in,
    w_out,
    ln2_gain,
    ln2_shift,
    w_up,
    w_down,
    cotangent,
):
    tok_count, feat_width = tokens.shape
    row_count = lengths.shape[0]
    row_len = tok_count // row_count
    half = row_len // 2
    table = jnp.asarray(wave_table(half), jnp.bfloat16)
    scale = 1.0 / half
    long_rows = (lengths > half).astype(jnp.float32)

    squashed = raw_taps - jnp.clip(raw_taps, -shrink_level, shrink_level)
    gathered = lax.all_gather(squashed.astype(jnp.bfloat16), "narrow", axis=0, tiled=True)
    kernel = pool(gathered.astype(jnp.float32)).astype(jnp.bfloat16)
    kernel_low = to_waves(table, kernel[:half])
    kernel_cross = to_waves(table, kernel[half : 2 * half]) + turned(kernel_low, 1.0)

    inputs = tokens.astype(jnp.float32)
    unit_one, inverse_one = norm_parts(inputs)
    normed = (unit_one * ln1_gain + ln1_shift).astype(jnp.bfloat16)
    projected = jnp.dot(normed, w_in, preferred_element_type=jnp.float32)
    signal = projected[:, :feat_width].astype(jnp.bfloat16)
    gate_vals = projected[:, feat_width:]
    signal_waves = []
    mixed = []
    for row in range(row_count):
        first = to_waves(table, signal[row * row_len : row * row_len + half])
        second = to_waves(table, signal[row * row_len + half : (row + 1) * row_len])
        signal_waves.append((first, second))
        mixed.append(from_waves(table, times(first, kernel_low) * scale))
        mixed.append(
            from_waves(
                table,
                (times(second, kernel_low) + long_rows[row] * times(first, kernel_cross)) * scale,
            )
        )
    mixed = jnp.concatenate(mixed, axis=0)
    branch = (mixed * gate_vals).astype(jnp.bfloat16)
    residual = inputs + jnp.dot(branch, w_out, preferred_element_type=jnp.float32)
    unit_two, inverse_two = norm_parts(residual)
    normed2 = (unit_two * ln2_gain + ln2_shift).astype(jnp.bfloat16)
    hidden = jnp.dot(normed2, w_up, preferred_element_type=jnp.float32)
    active = jax.nn.gelu(hidden).astype(jnp.bfloat16)
    block_out = (residual + jnp.dot(active, w_down, preferred_element_type=jnp.float32)).astype(
        jnp.bfloat16
    )
    w_down_grad = jnp.einsum("tf,td->fd", active, cotangent, preferred_element_type=jnp.float32)
    d_active = jnp.einsum("td,fd->tf", cotangent, w_down, preferred_element_type=jnp.float32)
    gelu_pull = jax.vjp(jax.nn.gelu, hidden)[1]
    d_hidden = gelu_pull(d_active)[0].astype(jnp.bfloat16)
    w_up_grad = jnp.einsum("td,tf->df", normed2, d_hidden, preferred_element_type=jnp.float32)
    d_normed2 = jnp.einsum("tf,df->td", d_hidden, w_up, preferred_element_type=jnp.float32)
    ln2_gain_grad = jnp.sum(d_normed2 * unit_two, axis=0)
    ln2_shift_grad = jnp.sum(d_normed2, axis=0)
    d_residual = cotangent.astype(jnp.float32) + norm_back(
        d_normed2, unit_two, inverse_two, ln2_gain
    )
    d_outproj = d_residual.astype(jnp.bfloat16)
    w_out_grad = jnp.einsum("td,te->de", branch, d_outproj, preferred_element_type=jnp.float32)
    d_branch = jnp.einsum("te,de->td", d_outproj, w_out, preferred_element_type=jnp.float32)
    d_mixed = (d_branch * gate_vals).astype(jnp.bfloat16)
    d_gate = d_branch * mixed
    d_signal = []
    low_grad = 0.0
    cross_grad = 0.0
    for row in range(row_count):
        first, second = signal_waves[row]
        d_first = to_waves(table, d_mixed[row * row_len : row * row_len + half]) * scale
        d_second = to_waves(table, d_mixed[row * row_len + half : (row + 1) * row_len]) * scale
        d_cross = d_second * long_rows[row]
        d_signal.append(
            from_waves(table, conj_times(kernel_low, d_first) + conj_times(kernel_cross, d_cross))
        )
        d_signal.append(from_waves(table, conj_times(kernel_low, d_second)))
        low_grad = low_grad + conj_times(first, d_first) + conj_times(second, d_second)
        cross_grad = cross_grad + conj_times(first, d_cross)
    low_grad = low_grad + turned(cross_grad, -1.0)
    d_kernel = jnp.concatenate([from_waves(table, low_grad), from_waves(table, cross_grad)], axis=0)
    d_signal = jnp.concatenate(d_signal, axis=0)
    d_projected = jnp.concatenate([d_signal, d_gate], axis=1).astype(jnp.bfloat16)
    w_in_grad = jnp.einsum("td,te->de", normed, d_projected, preferred_element_type=jnp.float32)
    d_normed = jnp.einsum("te,de->td", d_projected, w_in, preferred_element_type=jnp.float32)
    ln1_gain_grad = jnp.sum(d_normed * unit_one, axis=0)
    ln1_shift_grad = jnp.sum(d_normed, axis=0)
    input_grad = d_residual + norm_back(d_normed, unit_one, inverse_one, ln1_gain)

    shares = lax.psum_scatter(
        pool(d_kernel).astype(jnp.bfloat16), "narrow", scatter_dimension=0, tiled=True
    )
    summed = lax.psum(shares, "wide").astype(jnp.float32)
    raw_grad = summed * (jnp.abs(raw_taps) > shrink_level).astype(jnp.float32)

    def scatter(values):
        return lax.psum_scatter(
            values.astype(jnp.bfloat16), ("wide", "narrow"), scatter_dimension=0, tiled=True
        ).astype(jnp.float32)

    def scatter_wide(values):
        return lax.psum_scatter(values, ("wide", "narrow"), scatter_dimension=0, tiled=True)

    return (
        block_out,
        input_grad,
        raw_grad,
        scatter_wide(ln1_gain_grad),
        scatter_wide(ln1_shift_grad),
        scatter(w_in_grad),
        scatter(w_out_grad),
        scatter_wide(ln2_gain_grad),
        scatter_wide(ln2_shift_grad),
        scatter(w_up_grad),
        scatter(w_down_grad),
    )


MESH = pl.DeviceIdType.MESH
PART = 9
STORES = 30
VMEM_BYTES = 60 * 2**20
FLIGHTS = 3


def dot_nn(left, right):
    return lax.dot_general(left, right, (((1,), (0,)), ((), ())), preferred_element_type=jnp.float32)


def dot_nt(left, right):
    return lax.dot_general(left, right, (((1,), (1,)), ((), ())), preferred_element_type=jnp.float32)


def dot_tn(left, right):
    return lax.dot_general(left, right, (((0,), (0,)), ((), ())), preferred_element_type=jnp.float32)


def gelu_both(hidden):
    inner = 0.7978845608028654
    cubic = inner * 0.044715
    square = hidden * hidden
    bent = jnp.tanh(hidden * (inner + cubic * square))
    share = 0.5 + 0.5 * bent
    slope = share + (0.5 * hidden) * (1.0 - bent * bent) * (inner + (3.0 * cubic) * square)
    return hidden * share, slope


def blocks_of(rows, columns, height=16, width=768):
    return [
        (slice(at, at + height), slice(left, min(left + width, columns)))
        for at in range(0, rows, height)
        for left in range(0, columns, width)
    ]


def column_sums(values):
    rows, width = values.shape
    return jnp.sum(values.reshape(rows // 8, 8, width), axis=0)


class Place:
    def __init__(self, planes):
        wide = lax.axis_index("wide")
        self.narrow = lax.axis_index("narrow")
        self.wide = wide
        self.core = wide % 2
        self.y = (wide // 2) % 2
        self.z = wide // 4
        self.x = self.narrow
        self.planes = planes
        self.sibling = (wide + 1 - 2 * self.core, self.narrow)
        self.next_x = (wide, 1 - self.narrow)
        self.next_y = (wide + 2 - 4 * self.y, self.narrow)

    def plane(self, step):
        other = (self.z + step) % self.planes
        return (self.wide + 4 * (other - self.z), self.narrow), other


class Chunk:
    def __init__(self, place, held, inbox, sems, x_first, target=None):
        self.place = place
        self.views = (held, inbox, sems)
        self.target = target
        self.first, self.second = (place.x, place.y) if x_first else (place.y, place.x)
        self.to_first, self.to_second = (
            (place.next_x, place.next_y) if x_first else (place.next_y, place.next_x)
        )
        self.x_first = x_first

    @property
    def held(self):
        ref, at = self.views[0]
        return ref.at[at]

    @property
    def inbox(self):
        return [ref if at is None else ref.at[at] for ref, at in self.views[1]]

    @property
    def sems(self):
        return [ref.at[at] for ref, at in self.views[2]]

    def slot(self, y, core, x):
        first, second = (x, y) if self.x_first else (y, x)
        return ((core * 2 + first) * 2 + second) * self.place.planes

    def copy(self, stage):
        planes, core = self.place.planes, self.place.core
        first, second = self.first, self.second
        start, count, device = (
            (4 * planes * (1 - core), 4 * planes, self.place.sibling),
            (4 * planes * core + 2 * planes * (1 - first), 2 * planes, self.to_first),
            (4 * planes * core + 2 * planes * first + planes * (1 - second), planes, self.to_second),
        )[stage]
        return pltpu.make_async_remote_copy(
            src_ref=self.held.at[pl.ds(start, count)],
            dst_ref=self.inbox[stage],
            send_sem=self.sems[0].at[stage],
            recv_sem=self.sems[1].at[stage],
            device_id=device,
            device_id_type=MESH,
        )

    def add(self, start, landing, count):
        for index in range(count):
            self.held[start + index] += landing[index]

    def start(self):
        self.copy(0).start()

    def over_core(self):
        planes = self.place.planes
        self.copy(0).wait()
        self.add(4 * planes * self.place.core, self.inbox[0], 4 * planes)
        self.copy(1).start()

    def over_first(self):
        planes = self.place.planes
        self.copy(1).wait()
        self.add(4 * planes * self.place.core + 2 * planes * self.first, self.inbox[1], 2 * planes)
        self.copy(2).start()

    def base(self):
        planes, place = self.place.planes, self.place
        return 4 * planes * place.core + 2 * planes * self.first + planes * self.second

    def plane_copy(self, step):
        device, other = self.place.plane(step)
        if self.target is None:
            return pltpu.make_async_remote_copy(
                src_ref=self.held.at[self.base() + other],
                dst_ref=self.inbox[3].at[step - 1],
                send_sem=self.sems[0].at[2 + step],
                recv_sem=self.sems[1].at[2 + step],
                device_id=device,
                device_id_type=MESH,
            )
        return pltpu.make_async_remote_copy(
            src_ref=self.held.at[pl.ds(self.base(), self.place.planes)],
            dst_ref=self.inbox[3].at[step - 1],
            send_sem=self.sems[0].at[2 + step],
            recv_sem=self.sems[1].at[2 + step],
            device_id=device,
            device_id_type=MESH,
        )

    def each_plane(self, act):
        for step in range(1, self.place.planes):
            if self.target is None:
                act(self.plane_copy(step))
            else:

                @pl.when((self.place.z + step) % self.place.planes == self.target)
                def _():
                    act(self.plane_copy(step))

    def over_second(self):
        self.copy(2).wait()
        planes = self.place.planes
        self.add(self.base(), self.inbox[2], planes)
        if self.target is None:
            self.inbox[3][planes - 1] = self.held[self.base() + self.place.z]
        else:

            @pl.when(self.place.z == self.target)
            def _():
                for index in range(planes):
                    self.inbox[3][planes - 1, index] = self.held[self.base() + index]

        self.each_plane(lambda copy: copy.start())

    def sent(self):
        self.each_plane(lambda copy: copy.wait_send())

    def arrived(self):
        for step in range(1, self.place.planes):
            self.plane_copy(step).wait_recv()

    def total(self, index):
        terms = [
            self.inbox[3][step] if self.target is None else self.inbox[3][step, index]
            for step in range(self.place.planes)
        ]
        return sum(term.astype(jnp.float32) for term in terms)


def store_rows(chunk, values, first_row):
    width = values.shape[1]
    for k in range(values.shape[0] // 24):
        shard = first_row // 24 + k
        z, y, core, x = shard // 8, shard // 4 % 2, shard // 2 % 2, shard % 2
        at = chunk.slot(y, core, x) + z
        block = values[24 * k : 24 * k + 24]
        rest = block[16:24]
        chunk.held[at, :, 0:width] = block[0:16].astype(jnp.bfloat16)
        chunk.held[at, :, width : width + width // 2] = jnp.concatenate(
            [rest[:, : width // 2], rest[:, width // 2 :]], axis=0
        ).astype(jnp.bfloat16)


def load_rows(block, width):
    rest = block[:, width:]
    return jnp.concatenate(
        [block[:, :width], jnp.concatenate([rest[0:8], rest[8:16]], axis=1)], axis=0
    )


def tile_runs(sub, width):
    tiles = width // 128
    runs, tile = [], 0
    while tile < tiles:
        line = sub * tiles + tile
        count = min(tiles - tile, PART - line % PART)
        runs.append((tile, line // PART, line % PART, count))
        tile += count
    return runs


def store_shards(chunk, values, first_row):
    width = values.shape[1]
    for k in range(values.shape[0] // 16):
        row = first_row + 16 * k
        shard, sub = row // 96, row % 96 // 16
        base = chunk.slot(shard // 4, shard // 2 % 2, shard % 2)
        for tile, block, at, count in tile_runs(sub, width):
            chunk.held[base + block, :, 128 * at : 128 * (at + count)] = values[
                16 * k : 16 * k + 16, 128 * tile : 128 * (tile + count)
            ].astype(jnp.bfloat16)


class Taps:
    def __init__(self, place, held, inbox, result, sems, index, rows, cols, x_first):
        self.place, self.held, self.inbox, self.result = place, held, inbox, result
        self.sems, self.index = sems, index
        self.rows = rows
        self.cols = cols
        self.x_first = x_first

    def part(self, x, core, y, plane, count):
        planes = self.place.planes
        return pl.ds((((x * 2 + core) * 2 + y) * planes + plane) * self.rows, count * self.rows)

    def add(self, target, landing):
        self.held[target, self.cols] += landing[...]

    def landing(self, level, first, count):
        return self.inbox[level].at[pl.ds(first * self.rows, count * self.rows), self.cols]

    def copy(self, kind, step=0):
        place, planes = self.place, self.place.planes
        x, core, y, z = place.x, place.core, place.y, place.z
        if kind == "core":
            source, landing = self.part(step, 1 - core, 0, 0, 2 * planes), self.landing(0, step * 2 * planes, 2 * planes)
            stage, device = step, place.sibling
        elif kind == "first" and self.x_first:
            source, landing = self.part(1 - x, core, 0, 0, 2 * planes), self.landing(1, 0, 2 * planes)
            stage, device = 2, place.next_x
        elif kind == "first":
            source, landing = self.part(step, core, 1 - y, 0, planes), self.landing(1, step * planes, planes)
            stage, device = 2 + step, place.next_y
        elif kind == "second":
            first = self.part(x, core, 1 - y, 0, planes) if self.x_first else self.part(1 - x, core, y, 0, planes)
            source, landing = first, self.landing(2, 0, planes)
            stage, device = 4, place.next_y if self.x_first else place.next_x
        elif kind == "plane":
            device, other = place.plane(step)
            source, landing = self.part(x, core, y, other, 1), self.landing(3, step - 1, 1)
            stage = 4 + step
        else:
            if kind == "back plane":
                mine, stage, device = (0, core, y, z, 1), 3 + planes + step, place.plane(step)[0]
            elif kind == "back y":
                mine, stage, device = (0, core, y, 0, planes), 3 + 2 * planes, place.next_y
            else:
                mine, stage, device = (0, core, 0, 0, 2 * planes), 4 + 2 * planes, place.sibling
            landing = self.result.at[self.part(*mine), self.cols]
        return pltpu.make_async_remote_copy(
            src_ref=landing if kind.startswith("back") else self.held.at[source, self.cols],
            dst_ref=landing,
            send_sem=self.sems[0].at[self.index, stage],
            recv_sem=self.sems[1].at[self.index, stage],
            device_id=device,
            device_id_type=MESH,
        )

    def start(self):
        for x in range(2):
            self.copy("core", x).start()

    def over_core(self):
        for x in range(2):
            self.copy("core", x).wait()
            self.add(
                self.part(x, self.place.core, 0, 0, 2 * self.place.planes),
                self.landing(0, x * 2 * self.place.planes, 2 * self.place.planes),
            )
        for step in range(1 if self.x_first else 2):
            self.copy("first", step).start()

    def over_first(self):
        place, planes = self.place, self.place.planes
        if self.x_first:
            self.copy("first").wait()
            self.add(self.part(place.x, place.core, 0, 0, 2 * planes), self.landing(1, 0, 2 * planes))
        else:
            for x in range(2):
                self.copy("first", x).wait()
                self.add(self.part(x, place.core, place.y, 0, planes), self.landing(1, x * planes, planes))
        self.copy("second").start()

    def over_second(self):
        place = self.place
        self.copy("second").wait()
        self.add(self.part(place.x, place.core, place.y, 0, place.planes), self.landing(2, 0, place.planes))
        for step in range(1, place.planes):
            self.copy("plane", step).start()

    def over_planes(self):
        place = self.place
        mine = self.part(place.x, place.core, place.y, place.z, 1)
        total = self.held[mine, self.cols].astype(jnp.float32)
        for step in range(1, place.planes):
            self.copy("plane", step).wait()
            total = total + self.landing(3, step - 1, 1)[...].astype(jnp.float32)
        self.result[self.part(0, place.core, place.y, place.z, 1), self.cols] = total.astype(self.result.dtype)
        for step in range(1, place.planes):
            self.copy("back plane", step).start()

    def back_y(self):
        for step in range(1, self.place.planes):
            self.copy("back plane", step).wait()
        self.copy("back y").start()

    def back_core(self):
        self.copy("back y").wait()
        self.copy("back core").start()

    def finish(self):
        self.copy("back core").wait()


class Sums:
    def __init__(self, place, levels, inbox, sems):
        self.place, self.levels, self.inbox, self.sems = place, levels, inbox, sems

    def copy(self, level, step=0):
        place = self.place
        device = (place.sibling, place.next_x, place.next_y)[level] if level < 3 else place.plane(step)[0]
        landing = level + max(step - 1, 0)
        return pltpu.make_async_remote_copy(
            src_ref=self.levels.at[level],
            dst_ref=self.inbox.at[landing],
            send_sem=self.sems[0].at[landing],
            recv_sem=self.sems[1].at[landing],
            device_id=device,
            device_id_type=MESH,
        )

    def start(self):
        self.copy(0).start()

    def over(self, level):
        self.copy(level).wait()
        self.levels[level + 1] = self.levels[level] + self.inbox[level]
        if level < 2:
            self.copy(level + 1).start()
        else:
            for step in range(1, self.place.planes):
                self.copy(3, step).start()

    def finish(self):
        total = self.levels[3]
        for step in range(1, self.place.planes):
            self.copy(3, step).wait()
            total = total + self.inbox[2 + step]
        return total


def block_kernel(
    planes,
    lengths,
    tokens, cotangent, raw_taps, w_in, w_out, w_up, w_down, table, table_t,
    ln1_gain, ln1_shift, ln2_gain, ln2_shift,
    block_out, input_grad, taps_out, sums_out, w_in_grad, w_out_grad, w_up_grad, w_down_grad,
    held, inbox0, inbox1, inbox2, inbox_u, inbox_n, taps_held, taps0, taps1, taps2, taps3, taps_sum,
    levels, sums_inbox, cot, active, running, branch_v, normed_v, w_out_v,
    gate_v, mixed_v, left_v, waves, kernels,
    send_sems, recv_sems, taps_send, taps_recv, sums_send, sums_recv, share_send, share_recv, load_sems,
):
    tok_count, feat = cot.shape
    half = tok_count // 2
    tile = active.shape[2]
    step_rows = tap_cols = 256
    blocks = feat // tap_cols
    row_steps = tok_count // step_rows
    place = Place(planes)

    loads = {}

    class Load:
        def __init__(self, source, target):
            self.ends, self.at = (source, target), len(loads)

        def copy(self):
            source, target = (end() if callable(end) else end for end in self.ends)
            return pltpu.make_async_copy(source, target, load_sems.at[self.at])

        def wait(self):
            self.copy().wait()

    def load(name, source, target):
        loads[name] = Load(source, target)
        loads[name].copy().start()

    barrier = pltpu.get_barrier_semaphore()
    partners = [place.sibling, place.next_x, place.next_y] + [
        place.plane(step)[0] for step in range(1, planes)
    ]
    for partner in partners:
        pl.semaphore_signal(barrier, inc=1, device_id=partner, device_id_type=MESH)
    long = jnp.where(lengths[0] > half, 1.0, 0.0).astype(jnp.float32)

    def chunk(index, step, kind, target=None):
        at = step % FLIGHTS * 2 + kind
        ring = step % 2 * 2 + kind
        if target is None:
            far = (inbox_u, index // 2 if index < 2 * planes else index - planes)
        else:
            far = (inbox_n, None)
        return Chunk(
            place,
            (held, at),
            ((inbox0, ring), (inbox1, ring), (inbox2, ring), far),
            ((send_sems, index), (recv_sems, index)),
            kind == 0,
            target,
        )

    ups = [chunk(2 * t, t, 0) for t in range(planes)]
    downs = [chunk(2 * t + 1, t, 1, t) for t in range(planes)]

    def rows_of(index):
        return pl.ds(index * step_rows, step_rows)

    def under(index, part):
        return pl.ds(index * step_rows + part.start, part.stop - part.start)

    def unrolled(first, last, body, carry):
        for index in range(first, last):
            carry = body(index, carry)
        return carry

    def norm_of(values):
        centered = values - jnp.mean(values, axis=-1, keepdims=True)
        inverse = lax.rsqrt(jnp.mean(centered * centered, axis=-1, keepdims=True) + eps_norm)
        return centered * inverse, inverse

    out_chunk = chunk(2 * planes, planes, 0)
    gate_chunk = chunk(2 * planes + 1, planes, 1)
    signal_chunk = chunk(2 * planes + 2, planes + 1, 0)
    taps = [
        Taps(
            place, taps_held, (taps0, taps1, taps2, taps3), taps_sum, (taps_send, taps_recv), index,
            tok_count // (8 * planes), pl.ds(index * tap_cols, tap_cols), index % 2 == 0,
        )
        for index in range(feat // tap_cols)
    ]
    sums = Sums(place, levels, sums_inbox, (sums_send, sums_recv))

    def own_rows(target):
        target.arrived()
        return load_rows(target.total(0), feat)

    def own_down(t):
        @pl.when(place.z == t)
        def _():
            downs[t].arrived()
            for index in range(planes):
                block = downs[t].total(index)
                for sub in range(6):
                    for first, line, at, count in tile_runs(sub, feat):
                        if line == index:
                            w_down_grad[16 * sub : 16 * sub + 16, 128 * first : 128 * (first + count)] = block[
                                :, 128 * at : 128 * (at + count)
                            ]

    def weight_rows(target, left_t, right):
        for part in range(2):
            rows = feat // 2
            store_rows(target, dot_nn(left_t[part * rows : (part + 1) * rows, :], right[...]), part * rows)
        target.start()

    def own_up(t):
        w_up_grad[:, t * tile : (t + 1) * tile] = own_rows(ups[t])

    def own_out():
        w_out_grad[...] = own_rows(out_chunk)

    def own_gate():
        w_in_grad[:, feat:] = own_rows(gate_chunk)

    def own_signal():
        w_in_grad[:, 0:feat] = own_rows(signal_chunk)

    def taps_copy(index):
        cols = pl.ds(index * tap_cols, tap_cols)
        return pltpu.make_async_copy(taps_sum.at[:, cols], taps_out.at[:, cols], load_sems.at[STORES - 1 - index])

    def own_taps(index):
        taps[index].finish()
        taps_copy(index).start()

    def share_copy(which, across):
        block = half // 2
        block_x = place.x if which == 0 else 1 - place.x
        rows = pl.ds(pl.multiple_of(block_x * half + place.core * block, block), block)
        part = taps_held.at[rows, pl.ds(across * tap_cols, tap_cols)]
        return pltpu.make_async_remote_copy(
            src_ref=part,
            dst_ref=part,
            send_sem=share_send.at[which, across],
            recv_sem=share_recv.at[which, across],
            device_id=place.next_x if which == 0 else place.sibling,
            device_id_type=MESH,
        )

    def share_on(across):
        share_copy(0, across).wait()
        share_copy(1, across).start()

    def forward_back(normed_2, normed_2t, up_tiles, down_tiles):
        def load_tile(t):
            cols = pl.ds(t * tile, tile)
            load(("up", t), lambda: w_up.at[:, cols], lambda: up_tiles.at[t % 2])
            load(("down", t), lambda: w_down.at[cols, :], lambda: down_tiles.at[t % 2])

        def mix(table_v, table_tv):
            kernel = mixed_v
            load("taps", raw_taps, running.at[0:half, :])
            load("tokens", tokens, lambda: active.at[0])
            load("w_in", w_in.at[:, 0:feat], normed_2.at[0:feat, :])
            load("w_in end", w_in.at[:, feat : 2 * feat], normed_2t.at[:, 0:feat])
            load("table", table, table_v)
            load("table_t", table_t, table_tv)
            load("w_out", w_out, w_out_v)
            load_tile(0)
            load("cot", cotangent, cot)

            loads["taps"].wait()

            def squash_step(index, carry):
                rows = pl.ds(pl.multiple_of(index * 128, 128), 128)
                raw = running[rows, :]
                taps_held[pl.ds(pl.multiple_of(place.x * half + index * 128, 128), 128), :] = (
                    raw - jnp.clip(raw, -shrink_level, shrink_level)
                ).astype(jnp.bfloat16)
                return carry

            lax.fori_loop(0, half // 128, squash_step, 0)
            pl.semaphore_wait(barrier, len(partners))
            for across in range(blocks):
                share_copy(0, across).start()
            loads["tokens"].wait()
            loads["w_in"].wait()
            loads["w_in end"].wait()

            def project_step(index, carry):
                rows = rows_of(index)
                for part, _ in blocks_of(step_rows, feat):
                    at = under(index, part)
                    unit, _ = norm_of(active[0, at, :].astype(jnp.float32))
                    mixed_v[at, :] = (unit * ln1_gain[...][None, :] + ln1_shift[...][None, :]).astype(jnp.bfloat16)
                low = mixed_v[rows, :]
                normed_v[:, rows] = low.T
                active[1, rows, :] = dot_nn(low, normed_2[0:feat, :]).astype(jnp.bfloat16)
                gate_v[rows, :] = dot_nn(low, normed_2t[:, 0:feat]).astype(jnp.bfloat16)
                return carry

            unrolled(0, row_steps, project_step, 0)
            share_on(0)
            loads["table"].wait()

            def signal_wave_step(index, carry):
                rows = rows_of(index)
                for which in range(2):
                    waves[which, rows, :] = dot_nn(
                        table_v[rows, :], active[1, which * half : (which + 1) * half, :]
                    ).astype(jnp.bfloat16)
                return carry

            unrolled(0, row_steps, signal_wave_step, 0)
            pool_rows = 16

            def pool_step(across):
                cols = slice(across * tap_cols, (across + 1) * tap_cols)
                rim = jnp.zeros((16, tap_cols), jnp.float32)
                for index in range(tok_count // pool_rows):
                    at = index * pool_rows
                    first, last = max(at - 16, 0), min(at + pool_rows + 16, tok_count)
                    around = taps_held[first:last, cols].astype(jnp.float32)
                    if at == 0:
                        around = jnp.concatenate([rim, around], axis=0)
                    if last == tok_count:
                        around = jnp.concatenate([around, rim], axis=0)
                    kernel[at : at + pool_rows, cols] = (
                        (around[15 : 15 + pool_rows] + around[16 : 16 + pool_rows] + around[17 : 17 + pool_rows])
                        / 3.0
                    ).astype(jnp.bfloat16)

            def spread_step(down, across):
                real, imag = pl.ds(down * 256, 256), pl.ds(half + down * 256, 256)
                cols = pl.ds(across * 256, 256)
                low_r = dot_nn(table_v[real, :], kernel[0:half, cols])
                low_i = dot_nn(table_v[imag, :], kernel[0:half, cols])
                high_r = dot_nn(table_v[real, :], kernel[half:, cols])
                high_i = dot_nn(table_v[imag, :], kernel[half:, cols])
                odd = lax.broadcasted_iota(jnp.int32, (16, 1), 0) % 2
                parity = (1 - 2 * odd).astype(jnp.float32)
                scale = 1.0 / half
                for part, _ in blocks_of(256, tap_cols):
                    re, im = under(down, part), pl.ds(half + down * 256 + part.start, 16)

                    def keep(ref, which, at, values):
                        ref[which, at, cols] = values.astype(jnp.bfloat16)

                    lr, li = low_r[part], low_i[part]
                    cr, ci = long * (high_r[part] - parity * li), long * (high_i[part] + parity * lr)
                    keep(kernels, 0, re, lr)
                    keep(kernels, 0, im, li)
                    keep(kernels, 1, re, cr)
                    keep(kernels, 1, im, ci)
                    hr, hi, tr, ti = (
                        waves[which, at, cols].astype(jnp.float32) * scale for which in range(2) for at in (re, im)
                    )
                    keep(active, 2, re, lr * hr - li * hi)
                    keep(active, 2, im, lr * hi + li * hr)
                    keep(active, 3, re, lr * tr - li * ti + cr * hr - ci * hi)
                    keep(active, 3, im, lr * ti + li * tr + cr * hi + ci * hr)

            share_on(1)
            for across in range(blocks):
                share_copy(1, across).wait()
                pool_step(across)
                for down in range(half // 256):
                    spread_step(down, across)
                if across + 2 < blocks:
                    share_on(across + 2)
            loads["table_t"].wait()
            loads["w_out"].wait()

            def residual_step(index, carry):
                rows = rows_of(index)
                part_steps = half // step_rows
                which = index // part_steps
                of_part = pl.ds(index % part_steps * step_rows, step_rows)
                mixed = dot_nn(table_tv[of_part, :], active[2 + which])
                for part, columns in blocks_of(step_rows, feat):
                    at = under(index, part)
                    mixed_v[at, columns] = mixed[part, columns].astype(jnp.bfloat16)
                    active[1, at, columns] = (
                        mixed[part, columns] * gate_v[at, columns].astype(jnp.float32)
                    ).astype(jnp.bfloat16)
                branch = active[1, rows, :]
                branch_v[:, rows] = branch.T
                added = dot_nn(branch, w_out_v[...])
                for part, _ in blocks_of(step_rows, feat):
                    at = under(index, part)
                    left = active[0, at, :].astype(jnp.float32) + added[part]
                    left_v[at, :] = left
                    unit, _ = norm_of(left)
                    normed_2[at, :] = (unit * ln2_gain[...][None, :] + ln2_shift[...][None, :]).astype(jnp.bfloat16)
                normed_2t[:, rows] = normed_2[rows, :].T
                return carry

            unrolled(0, row_steps, residual_step, 0)

        pl.run_scoped(
            mix,
            pltpu.VMEM((tok_count, half), jnp.bfloat16),
            pltpu.VMEM((half, tok_count), jnp.bfloat16),
        )

        def feed_forward(d_hidden):
            loads["cot"].wait()

            def rows_piece(t, index):
                up_tile, down_tile = up_tiles.at[t % 2], down_tiles.at[t % 2]
                if index == 0:
                    loads["up", t].wait()
                    loads["down", t].wait()
                    if t + 1 < planes:
                        load_tile(t + 1)
                rows = rows_of(index)
                hidden = dot_nn(normed_2[rows, :], up_tile[...])
                d_active = dot_nt(cot[rows, :], down_tile[...])
                for part, columns in blocks_of(step_rows, tile, 16, 384):
                    at = under(index, part)
                    value, slope = gelu_both(hidden[part, columns])
                    active[t, at, columns] = value.astype(jnp.bfloat16)
                    d_hidden[t % 2, at, columns] = (d_active[part, columns] * slope).astype(jnp.bfloat16)
                back = dot_nt(d_hidden[t % 2, rows, :], up_tile[...])
                if t == 0:
                    running[rows, :] = back
                else:
                    running[rows, :] += back

            def up_piece(t):
                if t >= FLIGHTS:
                    ups[t - FLIGHTS].sent()
                weight_rows(ups[t], normed_2t, d_hidden.at[t % 2])

            def down_piece(t):
                if t >= FLIGHTS:
                    downs[t - FLIGHTS].sent()
                for part in range(2):
                    cols = slice(part * (tile // 2), (part + 1) * (tile // 2))
                    store_shards(downs[t], dot_tn(active[t, :, cols], cot[...]), part * (tile // 2))
                downs[t].start()

            rows_piece(0, 0)
            rows_piece(0, 1)
            rows_piece(0, 2)
            rows_piece(0, 3)
            down_piece(0)
            up_piece(0)
            rows_piece(1, 0)
            rows_piece(1, 1)
            downs[0].over_core()
            ups[0].over_core()
            rows_piece(1, 2)
            rows_piece(1, 3)
            down_piece(1)
            up_piece(1)
            rows_piece(2, 0)
            downs[0].over_first()
            downs[1].over_core()
            ups[0].over_first()
            ups[1].over_core()
            rows_piece(2, 1)
            rows_piece(2, 2)
            rows_piece(2, 3)
            down_piece(2)
            up_piece(2)
            rows_piece(3, 0)
            downs[0].over_second()
            downs[1].over_first()
            downs[2].over_core()
            rows_piece(3, 1)
            rows_piece(3, 2)
            ups[0].over_second()
            ups[1].over_first()
            ups[2].over_core()
            rows_piece(3, 3)
            down_piece(3)
            up_piece(3)

        pl.run_scoped(feed_forward, pltpu.VMEM((2, tok_count, tile), jnp.bfloat16))

    pl.run_scoped(
        forward_back,
        pltpu.VMEM((tok_count, feat), jnp.bfloat16),
        pltpu.VMEM((feat, tok_count), jnp.bfloat16),
        pltpu.VMEM((2, feat, tile), jnp.bfloat16),
        pltpu.VMEM((2, tile, feat), jnp.bfloat16),
    )

    def backward(d_out, d_gate, d_mix, d_signal, table_v, table_tv, d_kernel, d_taps):
        d_waves = waves
        load("table again", table, table_v)
        load("table_t again", table_t, table_tv)
        totals = {}

        def sum_rows(at, index, values):
            totals[at] = values + (totals[at] if index > 0 else 0.0)
            if index == row_steps - 1:
                levels[0, at : at + 1, :] = jnp.sum(totals[at], axis=0, keepdims=True)

        def back_piece(index):
            if index == 0:
                levels[0] = jnp.zeros(levels.shape[1:], jnp.float32)
            rows = rows_of(index)
            sums_of = [0.0, 0.0]
            for part, _ in blocks_of(step_rows, feat):
                at = under(index, part)
                unit, inverse = norm_of(left_v[at, :])
                grad = running[at, :]
                sums_of = [sums_of[0] + column_sums(grad * unit), sums_of[1] + column_sums(grad)]
                scaled = grad * ln2_gain[...][None, :]
                d_left = cot[at, :].astype(jnp.float32) + inverse * (
                    scaled
                    - jnp.mean(scaled, axis=-1, keepdims=True)
                    - unit * jnp.mean(scaled * unit, axis=-1, keepdims=True)
                )
                running[at, :] = d_left
                d_out[at, :] = d_left.astype(jnp.bfloat16)
            d_branch = dot_nt(d_out[rows, :], w_out_v[...])
            for part, columns in blocks_of(step_rows, feat):
                at = under(index, part)
                values = d_branch[part, columns]
                d_mix[at, columns] = (
                    values * gate_v[at, columns].astype(jnp.float32) * (1.0 / half)
                ).astype(jnp.bfloat16)
                d_gate[at, columns] = (values * mixed_v[at, columns].astype(jnp.float32)).astype(jnp.bfloat16)
            sum_rows(0, index, sums_of[0])
            sum_rows(1, index, sums_of[1])
            if index == row_steps - 1:
                load("tokens again", tokens, gate_v)

        def gate_piece():
            downs[planes - 3].sent()
            weight_rows(gate_chunk, normed_v, d_gate)

        def out_piece():
            ups[planes - 3].sent()
            weight_rows(out_chunk, branch_v, d_out)

        def signal_piece():
            ups[planes - 2].sent()
            weight_rows(signal_chunk, normed_v, d_signal)

        wave_rows, wave_cols = 256, 256

        def wave_step(down, cols):
            real, imag = pl.ds(down * wave_rows, wave_rows), pl.ds(half + down * wave_rows, wave_rows)
            first_r = dot_nn(table_v[real, :], d_mix[0:half, cols])
            first_i = dot_nn(table_v[imag, :], d_mix[0:half, cols])
            second_r = dot_nn(table_v[real, :], d_mix[half:, cols])
            second_i = dot_nn(table_v[imag, :], d_mix[half:, cols])

            odd = lax.broadcasted_iota(jnp.int32, (16, 1), 0) % 2
            parity = (1 - 2 * odd).astype(jnp.float32)
            for part, _ in blocks_of(wave_rows, wave_cols):
                re = pl.ds(down * wave_rows + part.start, 16)
                im = pl.ds(half + down * wave_rows + part.start, 16)

                def wide(ref, which, at):
                    return ref[which, at, cols].astype(jnp.float32)

                def keep(ref, which, at, values):
                    ref[which, at, cols if ref.shape[2] == feat else slice(None)] = values.astype(jnp.bfloat16)

                fr, fi, sr, si = first_r[part], first_i[part], second_r[part], second_i[part]
                hr, hi = wide(waves, 0, re), wide(waves, 0, im)
                far_r, far_i = (hr * sr + hi * si) * long, (hr * si - hi * sr) * long
                keep(d_kernel, 1, re, far_r)
                keep(d_kernel, 1, im, far_i)
                tr, ti = wide(waves, 1, re), wide(waves, 1, im)
                keep(d_kernel, 0, re, hr * fr + hi * fi + tr * sr + ti * si + parity * far_i)
                keep(d_kernel, 0, im, hr * fi - hi * fr + tr * si - ti * sr - parity * far_r)
                lr, li = wide(kernels, 0, re), wide(kernels, 0, im)
                keep(d_waves, 1, re, lr * sr + li * si)
                keep(d_waves, 1, im, lr * si - li * sr)
                cr, ci = wide(kernels, 1, re), wide(kernels, 1, im)
                keep(d_waves, 0, re, lr * fr + li * fi + cr * sr + ci * si)
                keep(d_waves, 0, im, lr * fi - li * fr + cr * si - ci * sr)

        pad = 8
        d_taps[0:pad, :] = jnp.zeros((pad, wave_cols), jnp.float32)
        d_taps[pad + tok_count :, :] = jnp.zeros((pad, wave_cols), jnp.float32)
        pool_rows = 16

        def column_step(across):
            cols = pl.ds(across * wave_cols, wave_cols)
            for down in range(half // wave_rows):
                wave_step(down, cols)
            for which in range(2):
                d_taps[pad + which * half : pad + (which + 1) * half, :] = dot_nn(table_tv[...], d_kernel[which])
            for index in range(tok_count // pool_rows):
                at = pad + index * pool_rows
                taps_held[at - pad : at - pad + pool_rows, cols] = (
                    (
                        d_taps[at - 1 : at - 1 + pool_rows, :]
                        + d_taps[at : at + pool_rows, :]
                        + d_taps[at + 1 : at + 1 + pool_rows, :]
                    )
                    / 3.0
                ).astype(jnp.bfloat16)


        def column_piece(across):
            if across == 0:
                loads["table again"].wait()
                loads["table_t again"].wait()
            column_step(across)
            taps[across].start()
            if across == blocks - 1:
                load("w_in signal", w_in.at[:, 0:feat], cot.at[0:feat, :])
                load("w_in gate", w_in.at[:, feat : 2 * feat], d_mix.at[0:feat, :])

        def down_again(t):
            return (waves if t < 2 else kernels).at[t % 2, 0:tile, :]

        def load_again(t):
            rows = pl.ds(t * tile, tile)
            load(("again", t), lambda: w_down.at[rows, :], lambda: down_again(t))

        def unwave_piece(which):
            for at in range(0, half, step_rows):
                d_signal[which * half + at : which * half + at + step_rows, :] = dot_nn(
                    table_tv[at : at + step_rows, :], d_waves[which]
                ).astype(jnp.bfloat16)
            if which == 1:
                for t in range(planes):
                    load_again(t)

        def grad_copy(index):
            rows = rows_of(index)
            return pltpu.make_async_copy(
                running.at[rows, :], input_grad.at[rows, :], load_sems.at[STORES + index]
            )

        def out_copy(index):
            rows = rows_of(index)
            return pltpu.make_async_copy(
                mixed_v.at[rows, :], block_out.at[rows, :], load_sems.at[STORES + row_steps + index]
            )

        def input_piece(index):
            if index == 0:
                loads["tokens again"].wait()
                loads["w_in signal"].wait()
                loads["w_in gate"].wait()
            rows = rows_of(index)
            d_normed = dot_nt(d_signal[rows, :], cot[0:feat, :]) + dot_nt(
                d_gate[rows, :], d_mix[0:feat, :]
            )
            sums_of = [0.0, 0.0]
            for part, _ in blocks_of(step_rows, feat):
                at = under(index, part)
                unit, inverse = norm_of(gate_v[at, :].astype(jnp.float32))
                grad = d_normed[part]
                sums_of = [sums_of[0] + column_sums(grad * unit), sums_of[1] + column_sums(grad)]
                scaled = grad * ln1_gain[...][None, :]
                running[at, :] = running[at, :] + inverse * (
                    scaled
                    - jnp.mean(scaled, axis=-1, keepdims=True)
                    - unit * jnp.mean(scaled * unit, axis=-1, keepdims=True)
                )
            grad_copy(index).start()
            sum_rows(2, index, sums_of[0])
            sum_rows(3, index, sums_of[1])

        def output_piece(index):
            if index == 0:
                for t in range(planes):
                    loads["again", t].wait()
            rows = rows_of(index)
            total = left_v[rows, :]
            for t in range(planes):
                total = total + dot_nn(active[t, rows, :], down_again(t)[...])
            mixed_v[rows, :] = total.astype(jnp.bfloat16)
            out_copy(index).start()

        back_piece(0)
        downs[1].over_second()
        downs[2].over_first()
        downs[3].over_core()
        back_piece(1)
        back_piece(2)
        ups[1].over_second()
        ups[2].over_first()
        ups[3].over_core()
        back_piece(3)
        column_piece(0)
        downs[2].over_second()
        out_piece()
        taps[0].over_core()
        column_piece(1)
        ups[2].over_second()
        downs[3].over_first()
        ups[3].over_first()
        column_piece(2)
        taps[1].over_core()
        out_chunk.over_core()
        gate_piece()
        taps[2].over_core()
        taps[0].over_first()
        ups[3].over_second()
        unwave_piece(0)
        gate_chunk.over_core()
        taps[1].over_first()
        taps[0].over_second()
        downs[3].over_second()
        unwave_piece(1)
        signal_piece()
        input_piece(0)
        out_chunk.over_first()
        taps[0].over_planes()
        own_up(3)
        signal_chunk.over_core()
        taps[2].over_first()
        input_piece(1)
        output_piece(0)
        input_piece(2)
        taps[1].over_second()
        taps[2].over_second()
        out_chunk.over_second()
        gate_chunk.over_first()
        taps[0].back_y()
        input_piece(3)
        sums.start()
        taps[1].over_planes()
        own_up(1)
        own_down(2)
        own_up(2)
        own_down(0)
        signal_chunk.over_first()
        taps[0].back_core()
        taps[2].over_planes()
        output_piece(1)
        gate_chunk.over_second()
        own_taps(0)
        taps[1].back_y()
        sums.over(0)
        own_down(1)
        sums.over(1)
        signal_chunk.over_second()
        own_out()
        taps[2].back_y()
        own_up(0)
        output_piece(2)
        taps[1].back_core()
        sums.over(2)
        own_gate()
        taps[2].back_core()
        own_down(3)
        output_piece(3)
        own_taps(1)
        own_taps(2)
        own_signal()
        for index in range(row_steps):
            grad_copy(index).wait()
            out_copy(index).wait()

    pl.run_scoped(
        backward,
        *[pltpu.VMEM((tok_count, feat), jnp.bfloat16)] * 4,
        pltpu.VMEM((tok_count, half), jnp.bfloat16),
        pltpu.VMEM((half, tok_count), jnp.bfloat16),
        pltpu.VMEM((2, tok_count, tap_cols), jnp.bfloat16),
        pltpu.VMEM((tok_count + 16, tap_cols), jnp.float32),
    )

    sums_out[...] = sums.finish()
    for one in (downs[planes - 2], ups[planes - 1], downs[planes - 1], out_chunk, gate_chunk, signal_chunk):
        one.sent()
    for index in range(blocks):
        taps_copy(index).wait()


def hand_on_kernel(raw_taps, taps_sum, *others):
    count = (len(others) - 5) // 3
    sources, raw_grad, targets = others[:count], others[count], others[count + 1 : 2 * count + 1]
    raw_v, taps_v, grad_v = others[2 * count + 1 : 2 * count + 4]
    rooms, sems = others[2 * count + 4 : -1], others[-1]
    fetches = [pltpu.make_async_copy(taps_sum, taps_v, sems.at[0]), pltpu.make_async_copy(raw_taps, raw_v, sems.at[1])]
    stores = []
    for source, room, target in zip(sources, rooms, targets):
        rows = source.shape[0]
        parts = 4 if rows % 64 == 0 else 1
        for part in range(parts):
            at = pl.ds(part * (rows // parts), rows // parts)
            sem = sems.at[1 + len(fetches)]
            fetches.append(pltpu.make_async_copy(source.at[at, :], room.at[at, :], sem))
            stores.append(pltpu.make_async_copy(room.at[at, :], target.at[at, :], sem))
    for fetch in fetches:
        fetch.start()
    for fetch in fetches[:2]:
        fetch.wait()
    grad_v[...] = jnp.where(jnp.abs(raw_v[...]) > shrink_level, taps_v[...].astype(jnp.float32), 0.0)
    mask = pltpu.make_async_copy(grad_v, raw_grad, sems.at[2])
    mask.start()
    for fetch, store in zip(fetches[2:], stores):
        fetch.wait()
        store.start()
    for store in [mask] + stores:
        store.wait()


def hand_on(raw_taps, taps_sum, *sources):
    whole = pl.BlockSpec(memory_space=pl.ANY)
    return pl.pallas_call(
        hand_on_kernel,
        out_shape=[jax.ShapeDtypeStruct(raw_taps.shape, jnp.float32)]
        + [jax.ShapeDtypeStruct(source.shape, source.dtype) for source in sources],
        in_specs=[whole] * (2 + len(sources)),
        out_specs=[whole] * (1 + len(sources)),
        scratch_shapes=[
            pltpu.VMEM(raw_taps.shape, jnp.float32),
            pltpu.VMEM(taps_sum.shape, taps_sum.dtype),
            pltpu.VMEM(raw_taps.shape, jnp.float32),
        ]
        + [pltpu.VMEM(source.shape, source.dtype) for source in sources]
        + [pltpu.SemaphoreType.DMA((3 + 4 * len(sources),))],
        compiler_params=pltpu.CompilerParams(vmem_limit_bytes=VMEM_BYTES),
    )(raw_taps, taps_sum, *sources)


def linked_block(
    planes,
    tokens,
    lengths,
    raw_taps,
    ln1_gain,
    ln1_shift,
    w_in,
    w_out,
    ln2_gain,
    ln2_shift,
    w_up,
    w_down,
    cotangent,
):
    tok_count, feat = tokens.shape
    half = tok_count // 2
    tile = w_up.shape[1] // planes
    table = jnp.asarray(wave_table(half), jnp.bfloat16)
    table_t = jnp.asarray(wave_table(half).T, jnp.bfloat16)
    shares = 8 * planes
    rows = feat // shares
    block = (16, 128 * PART)
    chunks = 2 * planes + 3
    bf16, f32 = jnp.bfloat16, jnp.float32
    whole = pl.BlockSpec(memory_space=pl.ANY)
    near = pl.BlockSpec(memory_space=pltpu.VMEM)
    results = pl.pallas_call(
        functools.partial(block_kernel, planes),
        out_shape=(
            jax.ShapeDtypeStruct((tok_count, feat), bf16),
            jax.ShapeDtypeStruct((tok_count, feat), f32),
            jax.ShapeDtypeStruct((half, feat), bf16),
            jax.ShapeDtypeStruct((8, feat), f32),
            jax.ShapeDtypeStruct((rows, 2 * feat), f32),
            jax.ShapeDtypeStruct((rows, feat), f32),
            jax.ShapeDtypeStruct((rows, planes * tile), f32),
            jax.ShapeDtypeStruct((tile // 8, feat), f32),
        ),
        in_specs=[pl.BlockSpec(memory_space=pltpu.SMEM)] + [whole] * 9 + [near] * 4,
        out_specs=(whole,) * 3 + (near,) * 5,
        scratch_shapes=[
            pltpu.VMEM((2 * FLIGHTS, shares) + block, bf16),
            pltpu.VMEM((4, 4 * planes) + block, bf16),
            pltpu.VMEM((4, 2 * planes) + block, bf16),
            pltpu.VMEM((4, planes) + block, bf16),
            pltpu.VMEM((planes + 3, planes) + block, bf16),
            pltpu.VMEM((planes, planes) + block, bf16),
            pltpu.VMEM((tok_count, feat), bf16),
            pltpu.VMEM((tok_count // 2, feat), bf16),
            pltpu.VMEM((tok_count // 4, feat), bf16),
            pltpu.VMEM((tok_count // 8, feat), bf16),
            pltpu.VMEM(((planes - 1) * (tok_count // shares), feat), bf16),
            pltpu.VMEM((half, feat), bf16),
            pltpu.VMEM((4, 8, feat), f32),
            pltpu.VMEM((planes + 2, 8, feat), f32),
            pltpu.VMEM((tok_count, feat), bf16),
            pltpu.VMEM((planes, tok_count, tile), bf16),
            pltpu.VMEM((tok_count, feat), f32),
            pltpu.VMEM((feat, tok_count), bf16),
            pltpu.VMEM((feat, tok_count), bf16),
            pltpu.VMEM((feat, feat), bf16),
            pltpu.VMEM((tok_count, feat), bf16),
            pltpu.VMEM((tok_count, feat), bf16),
            pltpu.VMEM((tok_count, feat), f32),
            pltpu.VMEM((2, tok_count, feat), bf16),
            pltpu.VMEM((2, tok_count, feat), bf16),
            pltpu.SemaphoreType.DMA((chunks, planes + 2)),
            pltpu.SemaphoreType.DMA((chunks, planes + 2)),
            pltpu.SemaphoreType.DMA((feat // 256, 2 * planes + 5)),
            pltpu.SemaphoreType.DMA((feat // 256, 2 * planes + 5)),
            pltpu.SemaphoreType.DMA((planes + 2,)),
            pltpu.SemaphoreType.DMA((planes + 2,)),
            pltpu.SemaphoreType.DMA((2, feat // 256)),
            pltpu.SemaphoreType.DMA((2, feat // 256)),
            pltpu.SemaphoreType.DMA((STORES + 2 * tok_count // 256,)),
        ],
        compiler_params=pltpu.CompilerParams(
            collective_id=1, has_side_effects=True, vmem_limit_bytes=VMEM_BYTES
        ),
        cost_estimate=pl.CostEstimate(
            flops=2 * tok_count * feat * (5 * w_up.shape[1] + 9 * feat),
            bytes_accessed=40 * tok_count * feat,
            transcendentals=tok_count * w_up.shape[1],
        ),
    )(
        lengths,
        tokens,
        cotangent,
        raw_taps,
        w_in,
        w_out,
        w_up,
        w_down,
        table,
        table_t,
        ln1_gain,
        ln1_shift,
        ln2_gain,
        ln2_shift,
    )
    block_out, input_grad, taps_sum, sums, w_in_grad, w_out_grad, w_up_grad, w_down_grad = results
    raw_grad, block_out, input_grad, w_in_grad, w_out_grad, w_up_grad, w_down_grad = hand_on(
        raw_taps, taps_sum, block_out, input_grad, w_in_grad, w_out_grad, w_up_grad, w_down_grad
    )
    share = lax.axis_index("wide") * 2 + lax.axis_index("narrow")
    mine = lax.dynamic_slice(sums, (0, share * rows), (8, rows))
    return (
        block_out,
        input_grad,
        raw_grad,
        mine[2],
        mine[3],
        w_in_grad,
        w_out_grad,
        mine[0],
        mine[1],
        w_up_grad,
        w_down_grad,
    )


def solution(mesh):
    spread = P(("wide", "narrow"))
    rows = P(("wide", "narrow"), None)
    placed = (rows, spread, P("narrow", None)) + (P(),) * 8 + (rows,)
    wide, narrow = mesh.shape["wide"], mesh.shape["narrow"]

    def block(tokens, lengths, raw_taps, *others):
        fits = (
            narrow == 2
            and wide == 4 * 4
            and lengths.shape[0] == 1
            and raw_taps.shape[0] * 2 == tokens.shape[0]
            and tokens.shape[1] == 24 * wide * narrow
            and others[-2].shape[0] == 96 * wide * narrow
            and tokens.shape[0] % 512 == 0
        )
        if fits:
            return linked_block(wide // 4, tokens, lengths, raw_taps, *others)
        return local(tokens, lengths, raw_taps, *others)

    return jax.shard_map(
        block,
        mesh=mesh,
        in_specs=placed,
        out_specs=(rows, rows, P("narrow", None), spread, spread, rows, rows, spread, spread, rows, rows),
        check_vma=False,
    )
```

```python
import functools

import jax
import jax.numpy as jnp
import numpy as np
from jax import lax
from jax.experimental import pallas as pl
from jax.experimental.pallas import tpu as pltpu
from jax.sharding import PartitionSpec as P

shrink_level = 0.003
eps_norm = 1e-05


def wave_table(half):
    period = 4 * half
    phase = (np.outer(2 * np.arange(half) + 1, np.arange(half)) % period) * (2 * np.pi / period)
    return np.concatenate([np.cos(phase), -np.sin(phase)], axis=0)


def to_waves(table, block):
    return jnp.einsum("kn,nc->kc", table, block, preferred_element_type=jnp.float32)


def from_waves(table, waves):
    return jnp.einsum(
        "kn,kc->nc", table, waves.astype(jnp.bfloat16), preferred_element_type=jnp.float32
    )


def norm_parts(values):
    centered = values - jnp.mean(values, axis=-1, keepdims=True)
    inverse = lax.rsqrt(jnp.mean(centered * centered, axis=-1, keepdims=True) + eps_norm)
    return (centered * inverse, inverse)


def norm_back(upstream, unit_vals, inverse, gain_vec):
    scaled = upstream * gain_vec
    return inverse * (
        scaled
        - jnp.mean(scaled, axis=-1, keepdims=True)
        - unit_vals * jnp.mean(scaled * unit_vals, axis=-1, keepdims=True)
    )


def split(waves):
    half = waves.shape[0] // 2
    return waves[:half], waves[half:]


def times(left, right):
    lr, li = split(left)
    rr, ri = split(right)
    return jnp.concatenate([lr * rr - li * ri, lr * ri + li * rr], axis=0)


def conj_times(left, right):
    lr, li = split(left)
    rr, ri = split(right)
    return jnp.concatenate([lr * rr + li * ri, lr * ri - li * rr], axis=0)


def turned(waves, sign):
    wr, wi = split(waves)
    index = lax.broadcasted_iota(jnp.int32, (wr.shape[0], 1), 0)
    parity = sign * (1.0 - 2.0 * (index % 2).astype(jnp.float32))
    return jnp.concatenate([-parity * wi, parity * wr], axis=0)


def pool(values):
    padded = jnp.pad(values, ((1, 1), (0, 0)))
    return (padded[:-2] + padded[1:-1] + padded[2:]) / 3.0


def local(
    tokens,
    lengths,
    raw_taps,
    ln1_gain,
    ln1_shift,
    w_in,
    w_out,
    ln2_gain,
    ln2_shift,
    w_up,
    w_down,
    cotangent,
):
    tok_count, feat_width = tokens.shape
    row_count = lengths.shape[0]
    row_len = tok_count // row_count
    half = row_len // 2
    table = jnp.asarray(wave_table(half), jnp.bfloat16)
    scale = 1.0 / half
    long_rows = (lengths > half).astype(jnp.float32)

    squashed = raw_taps - jnp.clip(raw_taps, -shrink_level, shrink_level)
    gathered = lax.all_gather(squashed.astype(jnp.bfloat16), "narrow", axis=0, tiled=True)
    kernel = pool(gathered.astype(jnp.float32)).astype(jnp.bfloat16)
    kernel_low = to_waves(table, kernel[:half])
    kernel_cross = to_waves(table, kernel[half : 2 * half]) + turned(kernel_low, 1.0)

    inputs = tokens.astype(jnp.float32)
    unit_one, inverse_one = norm_parts(inputs)
    normed = (unit_one * ln1_gain + ln1_shift).astype(jnp.bfloat16)
    projected = jnp.dot(normed, w_in, preferred_element_type=jnp.float32)
    signal = projected[:, :feat_width].astype(jnp.bfloat16)
    gate_vals = projected[:, feat_width:]
    signal_waves = []
    mixed = []
    for row in range(row_count):
        first = to_waves(table, signal[row * row_len : row * row_len + half])
        second = to_waves(table, signal[row * row_len + half : (row + 1) * row_len])
        signal_waves.append((first, second))
        mixed.append(from_waves(table, times(first, kernel_low) * scale))
        mixed.append(
            from_waves(
                table,
                (times(second, kernel_low) + long_rows[row] * times(first, kernel_cross)) * scale,
            )
        )
    mixed = jnp.concatenate(mixed, axis=0)
    branch = (mixed * gate_vals).astype(jnp.bfloat16)
    residual = inputs + jnp.dot(branch, w_out, preferred_element_type=jnp.float32)
    unit_two, inverse_two = norm_parts(residual)
    normed2 = (unit_two * ln2_gain + ln2_shift).astype(jnp.bfloat16)
    hidden = jnp.dot(normed2, w_up, preferred_element_type=jnp.float32)
    active = jax.nn.gelu(hidden).astype(jnp.bfloat16)
    block_out = (residual + jnp.dot(active, w_down, preferred_element_type=jnp.float32)).astype(
        jnp.bfloat16
    )
    w_down_grad = jnp.einsum("tf,td->fd", active, cotangent, preferred_element_type=jnp.float32)
    d_active = jnp.einsum("td,fd->tf", cotangent, w_down, preferred_element_type=jnp.float32)
    gelu_pull = jax.vjp(jax.nn.gelu, hidden)[1]
    d_hidden = gelu_pull(d_active)[0].astype(jnp.bfloat16)
    w_up_grad = jnp.einsum("td,tf->df", normed2, d_hidden, preferred_element_type=jnp.float32)
    d_normed2 = jnp.einsum("tf,df->td", d_hidden, w_up, preferred_element_type=jnp.float32)
    ln2_gain_grad = jnp.sum(d_normed2 * unit_two, axis=0)
    ln2_shift_grad = jnp.sum(d_normed2, axis=0)
    d_residual = cotangent.astype(jnp.float32) + norm_back(
        d_normed2, unit_two, inverse_two, ln2_gain
    )
    d_outproj = d_residual.astype(jnp.bfloat16)
    w_out_grad = jnp.einsum("td,te->de", branch, d_outproj, preferred_element_type=jnp.float32)
    d_branch = jnp.einsum("te,de->td", d_outproj, w_out, preferred_element_type=jnp.float32)
    d_mixed = (d_branch * gate_vals).astype(jnp.bfloat16)
    d_gate = d_branch * mixed
    d_signal = []
    low_grad = 0.0
    cross_grad = 0.0
    for row in range(row_count):
        first, second = signal_waves[row]
        d_first = to_waves(table, d_mixed[row * row_len : row * row_len + half]) * scale
        d_second = to_waves(table, d_mixed[row * row_len + half : (row + 1) * row_len]) * scale
        d_cross = d_second * long_rows[row]
        d_signal.append(
            from_waves(table, conj_times(kernel_low, d_first) + conj_times(kernel_cross, d_cross))
        )
        d_signal.append(from_waves(table, conj_times(kernel_low, d_second)))
        low_grad = low_grad + conj_times(first, d_first) + conj_times(second, d_second)
        cross_grad = cross_grad + conj_times(first, d_cross)
    low_grad = low_grad + turned(cross_grad, -1.0)
    d_kernel = jnp.concatenate([from_waves(table, low_grad), from_waves(table, cross_grad)], axis=0)
    d_signal = jnp.concatenate(d_signal, axis=0)
    d_projected = jnp.concatenate([d_signal, d_gate], axis=1).astype(jnp.bfloat16)
    w_in_grad = jnp.einsum("td,te->de", normed, d_projected, preferred_element_type=jnp.float32)
    d_normed = jnp.einsum("te,de->td", d_projected, w_in, preferred_element_type=jnp.float32)
    ln1_gain_grad = jnp.sum(d_normed * unit_one, axis=0)
    ln1_shift_grad = jnp.sum(d_normed, axis=0)
    input_grad = d_residual + norm_back(d_normed, unit_one, inverse_one, ln1_gain)

    shares = lax.psum_scatter(
        pool(d_kernel).astype(jnp.bfloat16), "narrow", scatter_dimension=0, tiled=True
    )
    summed = lax.psum(shares, "wide").astype(jnp.float32)
    raw_grad = summed * (jnp.abs(raw_taps) > shrink_level).astype(jnp.float32)

    def scatter(values):
        return lax.psum_scatter(
            values.astype(jnp.bfloat16), ("wide", "narrow"), scatter_dimension=0, tiled=True
        ).astype(jnp.float32)

    def scatter_wide(values):
        return lax.psum_scatter(values, ("wide", "narrow"), scatter_dimension=0, tiled=True)

    return (
        block_out,
        input_grad,
        raw_grad,
        scatter_wide(ln1_gain_grad),
        scatter_wide(ln1_shift_grad),
        scatter(w_in_grad),
        scatter(w_out_grad),
        scatter_wide(ln2_gain_grad),
        scatter_wide(ln2_shift_grad),
        scatter(w_up_grad),
        scatter(w_down_grad),
    )


MESH = pl.DeviceIdType.MESH
PART = 9
STORES = 30
VMEM_BYTES = 61 * 2**20
FLIGHTS = 3


def dot_nn(left, right):
    return lax.dot_general(left, right, (((1,), (0,)), ((), ())), preferred_element_type=jnp.float32)


def dot_nt(left, right):
    return lax.dot_general(left, right, (((1,), (1,)), ((), ())), preferred_element_type=jnp.float32)


def dot_tn(left, right):
    return lax.dot_general(left, right, (((0,), (0,)), ((), ())), preferred_element_type=jnp.float32)


def gelu_both(hidden):
    inner = 0.7978845608028654
    cubic = inner * 0.044715
    square = hidden * hidden
    bent = jnp.tanh(hidden * (inner + cubic * square))
    share = 0.5 + 0.5 * bent
    slope = share + (0.5 * hidden) * (1.0 - bent * bent) * (inner + (3.0 * cubic) * square)
    return hidden * share, slope


def blocks_of(rows, columns, height=16, width=768):
    return [
        (slice(at, at + height), slice(left, min(left + width, columns)))
        for at in range(0, rows, height)
        for left in range(0, columns, width)
    ]


def column_sums(values):
    rows, width = values.shape
    return jnp.sum(values.reshape(rows // 8, 8, width), axis=0)


class Place:
    def __init__(self, planes):
        wide = lax.axis_index("wide")
        self.narrow = lax.axis_index("narrow")
        self.wide = wide
        self.core = wide % 2
        self.y = (wide // 2) % 2
        self.z = wide // 4
        self.x = self.narrow
        self.planes = planes
        self.sibling = (wide + 1 - 2 * self.core, self.narrow)
        self.next_x = (wide, 1 - self.narrow)
        self.next_y = (wide + 2 - 4 * self.y, self.narrow)

    def plane(self, step):
        other = (self.z + step) % self.planes
        return (self.wide + 4 * (other - self.z), self.narrow), other


class Chunk:
    def __init__(self, place, held, inbox, sems, x_first, target=None):
        self.place = place
        self.views = (held, inbox, sems)
        self.target = target
        self.first, self.second = (place.x, place.y) if x_first else (place.y, place.x)
        self.to_first, self.to_second = (
            (place.next_x, place.next_y) if x_first else (place.next_y, place.next_x)
        )
        self.x_first = x_first

    @property
    def held(self):
        ref, at = self.views[0]
        return ref.at[at]

    @property
    def inbox(self):
        return [ref if at is None else ref.at[at] for ref, at in self.views[1]]

    @property
    def sems(self):
        return [ref.at[at] for ref, at in self.views[2]]

    def slot(self, y, core, x):
        first, second = (x, y) if self.x_first else (y, x)
        return ((core * 2 + first) * 2 + second) * self.place.planes

    def copy(self, stage):
        planes, core = self.place.planes, self.place.core
        first, second = self.first, self.second
        start, count, device = (
            (4 * planes * (1 - core), 4 * planes, self.place.sibling),
            (4 * planes * core + 2 * planes * (1 - first), 2 * planes, self.to_first),
            (4 * planes * core + 2 * planes * first + planes * (1 - second), planes, self.to_second),
        )[stage]
        return pltpu.make_async_remote_copy(
            src_ref=self.held.at[pl.ds(start, count)],
            dst_ref=self.inbox[stage],
            send_sem=self.sems[0].at[stage],
            recv_sem=self.sems[1].at[stage],
            device_id=device,
            device_id_type=MESH,
        )

    def add(self, start, landing, count):
        for index in range(count):
            self.held[start + index] += landing[index]

    def start(self):
        self.copy(0).start()

    def over_core(self):
        planes = self.place.planes
        self.copy(0).wait()
        self.add(4 * planes * self.place.core, self.inbox[0], 4 * planes)
        self.copy(1).start()

    def over_first(self):
        planes = self.place.planes
        self.copy(1).wait()
        self.add(4 * planes * self.place.core + 2 * planes * self.first, self.inbox[1], 2 * planes)
        self.copy(2).start()

    def base(self):
        planes, place = self.place.planes, self.place
        return 4 * planes * place.core + 2 * planes * self.first + planes * self.second

    def plane_copy(self, step):
        device, other = self.place.plane(step)
        if self.target is None:
            return pltpu.make_async_remote_copy(
                src_ref=self.held.at[self.base() + other],
                dst_ref=self.inbox[3].at[step - 1],
                send_sem=self.sems[0].at[2 + step],
                recv_sem=self.sems[1].at[2 + step],
                device_id=device,
                device_id_type=MESH,
            )
        return pltpu.make_async_remote_copy(
            src_ref=self.held.at[pl.ds(self.base(), self.place.planes)],
            dst_ref=self.inbox[3].at[step - 1],
            send_sem=self.sems[0].at[2 + step],
            recv_sem=self.sems[1].at[2 + step],
            device_id=device,
            device_id_type=MESH,
        )

    def each_plane(self, act):
        for step in range(1, self.place.planes):
            if self.target is None:
                act(self.plane_copy(step))
            else:

                @pl.when((self.place.z + step) % self.place.planes == self.target)
                def _():
                    act(self.plane_copy(step))

    def over_second(self):
        self.copy(2).wait()
        planes = self.place.planes
        self.add(self.base(), self.inbox[2], planes)
        if self.target is None:
            self.inbox[3][planes - 1] = self.held[self.base() + self.place.z]
        else:

            @pl.when(self.place.z == self.target)
            def _():
                for index in range(planes):
                    self.inbox[3][planes - 1, index] = self.held[self.base() + index]

        self.each_plane(lambda copy: copy.start())

    def sent(self):
        self.each_plane(lambda copy: copy.wait_send())

    def arrived(self):
        for step in range(1, self.place.planes):
            self.plane_copy(step).wait_recv()

    def total(self, index):
        terms = [
            self.inbox[3][step] if self.target is None else self.inbox[3][step, index]
            for step in range(self.place.planes)
        ]
        return sum(term.astype(jnp.float32) for term in terms)


def store_rows(chunk, values, first_row):
    width = values.shape[1]
    for k in range(values.shape[0] // 24):
        shard = first_row // 24 + k
        z, y, core, x = shard // 8, shard // 4 % 2, shard // 2 % 2, shard % 2
        at = chunk.slot(y, core, x) + z
        block = values[24 * k : 24 * k + 24]
        rest = block[16:24]
        chunk.held[at, :, 0:width] = block[0:16].astype(jnp.bfloat16)
        chunk.held[at, :, width : width + width // 2] = jnp.concatenate(
            [rest[:, : width // 2], rest[:, width // 2 :]], axis=0
        ).astype(jnp.bfloat16)


def load_rows(block, width):
    rest = block[:, width:]
    return jnp.concatenate(
        [block[:, :width], jnp.concatenate([rest[0:8], rest[8:16]], axis=1)], axis=0
    )


def tile_runs(sub, width):
    tiles = width // 128
    runs, tile = [], 0
    while tile < tiles:
        line = sub * tiles + tile
        count = min(tiles - tile, PART - line % PART)
        runs.append((tile, line // PART, line % PART, count))
        tile += count
    return runs


def store_shards(chunk, values, first_row):
    width = values.shape[1]
    for k in range(values.shape[0] // 16):
        row = first_row + 16 * k
        shard, sub = row // 96, row % 96 // 16
        base = chunk.slot(shard // 4, shard // 2 % 2, shard % 2)
        for tile, block, at, count in tile_runs(sub, width):
            chunk.held[base + block, :, 128 * at : 128 * (at + count)] = values[
                16 * k : 16 * k + 16, 128 * tile : 128 * (tile + count)
            ].astype(jnp.bfloat16)


class Taps:
    def __init__(self, place, held, inbox, result, sems, index, rows, cols, x_first):
        self.place, self.held, self.inbox, self.result = place, held, inbox, result
        self.sems, self.index = sems, index
        self.rows = rows
        self.cols = cols
        self.x_first = x_first

    def part(self, x, core, y, plane, count):
        planes = self.place.planes
        return pl.ds((((x * 2 + core) * 2 + y) * planes + plane) * self.rows, count * self.rows)

    def add(self, target, landing):
        self.held[target, self.cols] += landing[...]

    def landing(self, level, first, count):
        return self.inbox[level].at[pl.ds(first * self.rows, count * self.rows), self.cols]

    def copy(self, kind, step=0):
        place, planes = self.place, self.place.planes
        x, core, y, z = place.x, place.core, place.y, place.z
        if kind == "core":
            source, landing = self.part(step, 1 - core, 0, 0, 2 * planes), self.landing(0, step * 2 * planes, 2 * planes)
            stage, device = step, place.sibling
        elif kind == "first" and self.x_first:
            source, landing = self.part(1 - x, core, 0, 0, 2 * planes), self.landing(1, 0, 2 * planes)
            stage, device = 2, place.next_x
        elif kind == "first":
            source, landing = self.part(step, core, 1 - y, 0, planes), self.landing(1, step * planes, planes)
            stage, device = 2 + step, place.next_y
        elif kind == "second":
            first = self.part(x, core, 1 - y, 0, planes) if self.x_first else self.part(1 - x, core, y, 0, planes)
            source, landing = first, self.landing(2, 0, planes)
            stage, device = 4, place.next_y if self.x_first else place.next_x
        elif kind == "plane":
            device, other = place.plane(step)
            source, landing = self.part(x, core, y, other, 1), self.landing(3, step - 1, 1)
            stage = 4 + step
        else:
            if kind == "back plane":
                mine, stage, device = (0, core, y, z, 1), 3 + planes + step, place.plane(step)[0]
            elif kind == "back y":
                mine, stage, device = (0, core, y, 0, planes), 3 + 2 * planes, place.next_y
            else:
                mine, stage, device = (0, core, 0, 0, 2 * planes), 4 + 2 * planes, place.sibling
            landing = self.result.at[self.part(*mine), self.cols]
        return pltpu.make_async_remote_copy(
            src_ref=landing if kind.startswith("back") else self.held.at[source, self.cols],
            dst_ref=landing,
            send_sem=self.sems[0].at[self.index, stage],
            recv_sem=self.sems[1].at[self.index, stage],
            device_id=device,
            device_id_type=MESH,
        )

    def start(self):
        for x in range(2):
            self.copy("core", x).start()

    def over_core(self):
        for x in range(2):
            self.copy("core", x).wait()
            self.add(
                self.part(x, self.place.core, 0, 0, 2 * self.place.planes),
                self.landing(0, x * 2 * self.place.planes, 2 * self.place.planes),
            )
        for step in range(1 if self.x_first else 2):
            self.copy("first", step).start()

    def over_first(self):
        place, planes = self.place, self.place.planes
        if self.x_first:
            self.copy("first").wait()
            self.add(self.part(place.x, place.core, 0, 0, 2 * planes), self.landing(1, 0, 2 * planes))
        else:
            for x in range(2):
                self.copy("first", x).wait()
                self.add(self.part(x, place.core, place.y, 0, planes), self.landing(1, x * planes, planes))
        self.copy("second").start()

    def over_second(self):
        place = self.place
        self.copy("second").wait()
        self.add(self.part(place.x, place.core, place.y, 0, place.planes), self.landing(2, 0, place.planes))
        for step in range(1, place.planes):
            self.copy("plane", step).start()

    def over_planes(self):
        place = self.place
        mine = self.part(place.x, place.core, place.y, place.z, 1)
        total = self.held[mine, self.cols].astype(jnp.float32)
        for step in range(1, place.planes):
            self.copy("plane", step).wait()
            total = total + self.landing(3, step - 1, 1)[...].astype(jnp.float32)
        self.result[self.part(0, place.core, place.y, place.z, 1), self.cols] = total.astype(self.result.dtype)
        for step in range(1, place.planes):
            self.copy("back plane", step).start()

    def back_y(self):
        for step in range(1, self.place.planes):
            self.copy("back plane", step).wait()
        self.copy("back y").start()

    def back_core(self):
        self.copy("back y").wait()
        self.copy("back core").start()

    def finish(self):
        self.copy("back core").wait()


class Sums:
    def __init__(self, place, levels, inbox, sems):
        self.place, self.levels, self.inbox, self.sems = place, levels, inbox, sems

    def copy(self, level, step=0):
        place = self.place
        device = (place.sibling, place.next_x, place.next_y)[level] if level < 3 else place.plane(step)[0]
        landing = level + max(step - 1, 0)
        return pltpu.make_async_remote_copy(
            src_ref=self.levels.at[level],
            dst_ref=self.inbox.at[landing],
            send_sem=self.sems[0].at[landing],
            recv_sem=self.sems[1].at[landing],
            device_id=device,
            device_id_type=MESH,
        )

    def start(self):
        self.copy(0).start()

    def over(self, level):
        self.copy(level).wait()
        self.levels[level + 1] = self.levels[level] + self.inbox[level]
        if level < 2:
            self.copy(level + 1).start()
        else:
            for step in range(1, self.place.planes):
                self.copy(3, step).start()

    def finish(self):
        total = self.levels[3]
        for step in range(1, self.place.planes):
            self.copy(3, step).wait()
            total = total + self.inbox[2 + step]
        return total


def block_kernel(
    planes,
    lengths,
    tokens, cotangent, raw_taps, w_in, w_out, w_up, w_down, table, table_t,
    ln1_gain, ln1_shift, ln2_gain, ln2_shift,
    block_out, input_grad, taps_out, sums_out, w_in_grad, w_out_grad, w_up_grad, w_down_grad,
    held, inbox0, inbox1, inbox2, inbox_u, inbox_n, taps_held, taps0, taps1, taps2, taps3, taps_sum,
    levels, sums_inbox, cot, active, running, branch_v, normed_v, w_out_v,
    gate_v, mixed_v, left_v, waves, kernels,
    send_sems, recv_sems, taps_send, taps_recv, sums_send, sums_recv, share_send, share_recv, load_sems,
):
    tok_count, feat = cot.shape
    half = tok_count // 2
    tile = active.shape[2]
    step_rows = tap_cols = 256
    blocks = feat // tap_cols
    row_steps = tok_count // step_rows
    place = Place(planes)

    loads = {}

    class Load:
        def __init__(self, source, target):
            self.ends, self.at = (source, target), len(loads)

        def copy(self):
            source, target = (end() if callable(end) else end for end in self.ends)
            return pltpu.make_async_copy(source, target, load_sems.at[self.at])

        def wait(self):
            self.copy().wait()

    def load(name, source, target):
        loads[name] = Load(source, target)
        loads[name].copy().start()

    barrier = pltpu.get_barrier_semaphore()
    partners = [place.sibling, place.next_x, place.next_y] + [
        place.plane(step)[0] for step in range(1, planes)
    ]
    for partner in partners:
        pl.semaphore_signal(barrier, inc=1, device_id=partner, device_id_type=MESH)
    long = jnp.where(lengths[0] > half, 1.0, 0.0).astype(jnp.float32)

    def chunk(index, step, kind, target=None):
        at = step % FLIGHTS * 2 + kind
        ring = step % 2 * 2 + kind
        if target is None:
            far = (inbox_u, index // 2 if index < 2 * planes else index - planes)
        else:
            far = (inbox_n, None)
        return Chunk(
            place,
            (held, at),
            ((inbox0, ring), (inbox1, index), (inbox2, index), far),
            ((send_sems, index), (recv_sems, index)),
            kind == 0,
            target,
        )

    ups = [chunk(2 * t, t, 0) for t in range(planes)]
    downs = [chunk(2 * t + 1, t, 1, t) for t in range(planes)]

    def rows_of(index):
        return pl.ds(index * step_rows, step_rows)

    def under(index, part):
        return pl.ds(index * step_rows + part.start, part.stop - part.start)

    def unrolled(first, last, body, carry):
        for index in range(first, last):
            carry = body(index, carry)
        return carry

    def norm_of(values):
        centered = values - jnp.mean(values, axis=-1, keepdims=True)
        inverse = lax.rsqrt(jnp.mean(centered * centered, axis=-1, keepdims=True) + eps_norm)
        return centered * inverse, inverse

    out_chunk = chunk(2 * planes, planes, 0)
    gate_chunk = chunk(2 * planes + 1, planes, 1)
    signal_chunk = chunk(2 * planes + 2, planes + 1, 0)
    taps = [
        Taps(
            place, taps_held, (taps0, taps1, taps2, taps3), taps_sum, (taps_send, taps_recv), index,
            tok_count // (8 * planes), pl.ds(index * tap_cols, tap_cols), index % 2 == 0,
        )
        for index in range(feat // tap_cols)
    ]
    sums = Sums(place, levels, sums_inbox, (sums_send, sums_recv))

    def own_rows(target):
        target.arrived()
        return load_rows(target.total(0), feat)

    def own_down(t):
        @pl.when(place.z == t)
        def _():
            downs[t].arrived()
            for index in range(planes):
                block = downs[t].total(index)
                for sub in range(6):
                    for first, line, at, count in tile_runs(sub, feat):
                        if line == index:
                            w_down_grad[16 * sub : 16 * sub + 16, 128 * first : 128 * (first + count)] = block[
                                :, 128 * at : 128 * (at + count)
                            ]

    def weight_rows(target, left_t, right):
        for part in range(2):
            rows = feat // 2
            store_rows(target, dot_nn(left_t[part * rows : (part + 1) * rows, :], right[...]), part * rows)
        target.start()

    def own_up(t):
        w_up_grad[:, t * tile : (t + 1) * tile] = own_rows(ups[t])

    def own_out():
        w_out_grad[...] = own_rows(out_chunk)

    def own_gate():
        w_in_grad[:, feat:] = own_rows(gate_chunk)

    def own_signal():
        w_in_grad[:, 0:feat] = own_rows(signal_chunk)

    def taps_copy(index):
        cols = pl.ds(index * tap_cols, tap_cols)
        return pltpu.make_async_copy(taps_sum.at[:, cols], taps_out.at[:, cols], load_sems.at[STORES - 1 - index])

    def own_taps(index):
        taps[index].finish()
        taps_copy(index).start()

    def share_copy(which, across):
        block = half // 2
        block_x = place.x if which == 0 else 1 - place.x
        rows = pl.ds(pl.multiple_of(block_x * half + place.core * block, block), block)
        part = taps_held.at[rows, pl.ds(across * tap_cols, tap_cols)]
        return pltpu.make_async_remote_copy(
            src_ref=part,
            dst_ref=part,
            send_sem=share_send.at[which, across],
            recv_sem=share_recv.at[which, across],
            device_id=place.next_x if which == 0 else place.sibling,
            device_id_type=MESH,
        )

    def share_on(across):
        share_copy(0, across).wait()
        share_copy(1, across).start()

    def forward_back(normed_2, normed_2t, up_tiles, down_tiles):
        def load_tile(t):
            cols = pl.ds(t * tile, tile)
            load(("up", t), lambda: w_up.at[:, cols], lambda: up_tiles.at[t % 2])
            load(("down", t), lambda: w_down.at[cols, :], lambda: down_tiles.at[t % 2])

        def mix(table_tv):
            table_v = cot.at[:, 0:half]
            kernel = mixed_v
            load("taps", raw_taps, running.at[0:half, :])
            load("tokens", tokens, lambda: active.at[0])
            load("w_in", w_in.at[:, 0:feat], normed_2.at[0:feat, :])
            load("w_in end", w_in.at[:, feat : 2 * feat], normed_2t.at[:, 0:feat])
            load("table", table, lambda: cot.at[:, 0:half])
            load("table_t", table_t, table_tv)
            load("w_out", w_out, w_out_v)
            load_tile(0)

            loads["taps"].wait()

            def squash_step(index, carry):
                rows = pl.ds(pl.multiple_of(index * 128, 128), 128)
                raw = running[rows, :]
                taps_held[pl.ds(pl.multiple_of(place.x * half + index * 128, 128), 128), :] = (
                    raw - jnp.clip(raw, -shrink_level, shrink_level)
                ).astype(jnp.bfloat16)
                return carry

            lax.fori_loop(0, half // 128, squash_step, 0)
            pl.semaphore_wait(barrier, len(partners))
            for across in range(blocks):
                share_copy(0, across).start()
            loads["tokens"].wait()
            loads["w_in"].wait()
            loads["w_in end"].wait()

            def project_step(index, carry):
                rows = rows_of(index)
                for part, _ in blocks_of(step_rows, feat):
                    at = under(index, part)
                    unit, _ = norm_of(active[0, at, :].astype(jnp.float32))
                    mixed_v[at, :] = (unit * ln1_gain[...][None, :] + ln1_shift[...][None, :]).astype(jnp.bfloat16)
                low = mixed_v[rows, :]
                normed_v[:, rows] = low.T
                active[1, rows, :] = dot_nn(low, normed_2[0:feat, :]).astype(jnp.bfloat16)
                gate_v[rows, :] = dot_nn(low, normed_2t[:, 0:feat]).astype(jnp.bfloat16)
                return carry

            unrolled(0, row_steps, project_step, 0)
            share_on(0)
            loads["table"].wait()

            def signal_wave_step(index, carry):
                rows = rows_of(index)
                for which in range(2):
                    waves[which, rows, :] = dot_nn(
                        table_v[rows, :], active[1, which * half : (which + 1) * half, :]
                    ).astype(jnp.bfloat16)
                return carry

            unrolled(0, row_steps, signal_wave_step, 0)
            pool_rows = 16

            def pool_step(across):
                cols = slice(across * tap_cols, (across + 1) * tap_cols)
                rim = jnp.zeros((16, tap_cols), jnp.float32)
                for index in range(tok_count // pool_rows):
                    at = index * pool_rows
                    first, last = max(at - 16, 0), min(at + pool_rows + 16, tok_count)
                    around = taps_held[first:last, cols].astype(jnp.float32)
                    if at == 0:
                        around = jnp.concatenate([rim, around], axis=0)
                    if last == tok_count:
                        around = jnp.concatenate([around, rim], axis=0)
                    kernel[at : at + pool_rows, cols] = (
                        (around[15 : 15 + pool_rows] + around[16 : 16 + pool_rows] + around[17 : 17 + pool_rows])
                        / 3.0
                    ).astype(jnp.bfloat16)

            def spread_step(down, across):
                real, imag = pl.ds(down * 256, 256), pl.ds(half + down * 256, 256)
                cols = pl.ds(across * 256, 256)
                low_r = dot_nn(table_v[real, :], kernel[0:half, cols])
                low_i = dot_nn(table_v[imag, :], kernel[0:half, cols])
                high_r = dot_nn(table_v[real, :], kernel[half:, cols])
                high_i = dot_nn(table_v[imag, :], kernel[half:, cols])
                odd = lax.broadcasted_iota(jnp.int32, (16, 1), 0) % 2
                parity = (1 - 2 * odd).astype(jnp.float32)
                scale = 1.0 / half
                for part, _ in blocks_of(256, tap_cols):
                    re, im = under(down, part), pl.ds(half + down * 256 + part.start, 16)

                    def keep(ref, which, at, values):
                        ref[which, at, cols] = values.astype(jnp.bfloat16)

                    lr, li = low_r[part], low_i[part]
                    cr, ci = long * (high_r[part] - parity * li), long * (high_i[part] + parity * lr)
                    keep(kernels, 0, re, lr)
                    keep(kernels, 0, im, li)
                    keep(kernels, 1, re, cr)
                    keep(kernels, 1, im, ci)
                    hr, hi, tr, ti = (
                        waves[which, at, cols].astype(jnp.float32) * scale for which in range(2) for at in (re, im)
                    )
                    keep(active, 2, re, lr * hr - li * hi)
                    keep(active, 2, im, lr * hi + li * hr)
                    keep(active, 3, re, lr * tr - li * ti + cr * hr - ci * hi)
                    keep(active, 3, im, lr * ti + li * tr + cr * hi + ci * hr)

            share_on(1)
            for across in range(blocks):
                share_copy(1, across).wait()
                pool_step(across)
                for down in range(half // 256):
                    spread_step(down, across)
                if across + 2 < blocks:
                    share_on(across + 2)
            load("cot", cotangent, cot)
            loads["table_t"].wait()
            loads["w_out"].wait()

            def residual_step(index, carry):
                rows = rows_of(index)
                part_steps = half // step_rows
                which = index // part_steps
                of_part = pl.ds(index % part_steps * step_rows, step_rows)
                mixed = dot_nn(table_tv[of_part, :], active[2 + which])
                for part, columns in blocks_of(step_rows, feat):
                    at = under(index, part)
                    mixed_v[at, columns] = mixed[part, columns].astype(jnp.bfloat16)
                    active[1, at, columns] = (
                        mixed[part, columns] * gate_v[at, columns].astype(jnp.float32)
                    ).astype(jnp.bfloat16)
                branch = active[1, rows, :]
                branch_v[:, rows] = branch.T
                added = dot_nn(branch, w_out_v[...])
                for part, _ in blocks_of(step_rows, feat):
                    at = under(index, part)
                    left = active[0, at, :].astype(jnp.float32) + added[part]
                    left_v[at, :] = left
                    unit, _ = norm_of(left)
                    normed_2[at, :] = (unit * ln2_gain[...][None, :] + ln2_shift[...][None, :]).astype(jnp.bfloat16)
                normed_2t[:, rows] = normed_2[rows, :].T
                return carry

            unrolled(0, row_steps, residual_step, 0)

        pl.run_scoped(
            mix,
            pltpu.VMEM((half, tok_count), jnp.bfloat16),
        )

        def feed_forward(d_hidden):
            loads["cot"].wait()

            def rows_piece(t, index):
                up_tile, down_tile = up_tiles.at[t % 2], down_tiles.at[t % 2]
                if index == 0:
                    loads["up", t].wait()
                    loads["down", t].wait()
                    if t + 1 < planes:
                        load_tile(t + 1)
                rows = rows_of(index)
                hidden = dot_nn(normed_2[rows, :], up_tile[...])
                d_active = dot_nt(cot[rows, :], down_tile[...])
                for part, columns in blocks_of(step_rows, tile, 16, 384):
                    at = under(index, part)
                    value, slope = gelu_both(hidden[part, columns])
                    active[t, at, columns] = value.astype(jnp.bfloat16)
                    d_hidden[at, columns] = (d_active[part, columns] * slope).astype(jnp.bfloat16)
                back = dot_nt(d_hidden[rows, :], up_tile[...])
                if t == 0:
                    running[rows, :] = back
                else:
                    running[rows, :] += back

            def up_piece(t):
                if t >= FLIGHTS:
                    ups[t - FLIGHTS].sent()
                weight_rows(ups[t], normed_2t, d_hidden)

            def down_piece(t):
                if t >= FLIGHTS:
                    downs[t - FLIGHTS].sent()
                for part in range(2):
                    cols = slice(part * (tile // 2), (part + 1) * (tile // 2))
                    store_shards(downs[t], dot_tn(active[t, :, cols], cot[...]), part * (tile // 2))
                downs[t].start()

            rows_piece(0, 0)
            rows_piece(0, 1)
            rows_piece(0, 2)
            rows_piece(0, 3)
            up_piece(0)
            rows_piece(1, 0)
            down_piece(0)
            rows_piece(1, 1)
            rows_piece(1, 2)
            ups[0].over_core()
            rows_piece(1, 3)
            up_piece(1)
            downs[0].over_core()
            down_piece(1)
            rows_piece(2, 0)
            rows_piece(2, 1)
            ups[1].over_core()
            rows_piece(2, 2)
            ups[0].over_first()
            rows_piece(2, 3)
            up_piece(2)
            downs[1].over_core()
            downs[0].over_first()
            down_piece(2)
            rows_piece(3, 0)
            rows_piece(3, 1)
            ups[2].over_core()
            ups[1].over_first()
            ups[0].over_second()
            rows_piece(3, 2)
            rows_piece(3, 3)
            up_piece(3)
            downs[2].over_core()
            downs[1].over_first()
            downs[0].over_second()
            down_piece(3)

        pl.run_scoped(feed_forward, pltpu.VMEM((tok_count, tile), jnp.bfloat16))

    pl.run_scoped(
        forward_back,
        pltpu.VMEM((tok_count, feat), jnp.bfloat16),
        pltpu.VMEM((feat, tok_count), jnp.bfloat16),
        pltpu.VMEM((2, feat, tile), jnp.bfloat16),
        pltpu.VMEM((2, tile, feat), jnp.bfloat16),
    )

    def backward(d_out, d_gate, d_mix, d_signal, table_v, table_tv, d_taps):
        d_waves = waves
        load("table again", table, table_v)
        load("table_t again", table_t, table_tv)
        totals = {}

        def sum_rows(at, index, values):
            totals[at] = values + (totals[at] if index > 0 else 0.0)
            if index == row_steps - 1:
                levels[0, at : at + 1, :] = jnp.sum(totals[at], axis=0, keepdims=True)

        def back_piece(index):
            if index == 0:
                levels[0] = jnp.zeros(levels.shape[1:], jnp.float32)
            rows = rows_of(index)
            sums_of = [0.0, 0.0]
            for part, _ in blocks_of(step_rows, feat):
                at = under(index, part)
                unit, inverse = norm_of(left_v[at, :])
                grad = running[at, :]
                sums_of = [sums_of[0] + column_sums(grad * unit), sums_of[1] + column_sums(grad)]
                scaled = grad * ln2_gain[...][None, :]
                d_left = cot[at, :].astype(jnp.float32) + inverse * (
                    scaled
                    - jnp.mean(scaled, axis=-1, keepdims=True)
                    - unit * jnp.mean(scaled * unit, axis=-1, keepdims=True)
                )
                running[at, :] = d_left
                d_out[at, :] = d_left.astype(jnp.bfloat16)
            d_branch = dot_nt(d_out[rows, :], w_out_v[...])
            for part, columns in blocks_of(step_rows, feat):
                at = under(index, part)
                values = d_branch[part, columns]
                d_mix[at, columns] = (
                    values * gate_v[at, columns].astype(jnp.float32) * (1.0 / half)
                ).astype(jnp.bfloat16)
                d_gate[at, columns] = (values * mixed_v[at, columns].astype(jnp.float32)).astype(jnp.bfloat16)
            sum_rows(0, index, sums_of[0])
            sum_rows(1, index, sums_of[1])
            if index == row_steps - 1:
                load("tokens again", tokens, gate_v)

        def gate_piece():
            downs[planes - 3].sent()
            weight_rows(gate_chunk, normed_v, d_gate)

        def out_piece():
            ups[planes - 3].sent()
            weight_rows(out_chunk, branch_v, d_out)

        def signal_piece():
            ups[planes - 2].sent()
            weight_rows(signal_chunk, normed_v, d_signal)

        wave_rows, wave_cols = 256, 256

        def wave_step(down, cols):
            real, imag = pl.ds(down * wave_rows, wave_rows), pl.ds(half + down * wave_rows, wave_rows)
            first_r = dot_nn(table_v[real, :], d_mix[0:half, cols])
            first_i = dot_nn(table_v[imag, :], d_mix[0:half, cols])
            second_r = dot_nn(table_v[real, :], d_mix[half:, cols])
            second_i = dot_nn(table_v[imag, :], d_mix[half:, cols])

            odd = lax.broadcasted_iota(jnp.int32, (16, 1), 0) % 2
            parity = (1 - 2 * odd).astype(jnp.float32)
            for part, _ in blocks_of(wave_rows, wave_cols):
                re = pl.ds(down * wave_rows + part.start, 16)
                im = pl.ds(half + down * wave_rows + part.start, 16)

                def wide(ref, which, at):
                    return ref[which, at, cols].astype(jnp.float32)

                def keep(ref, which, at, values):
                    ref[which, at, cols] = values.astype(jnp.bfloat16)

                def keep_taps(which, at, values):
                    d_signal[at, which * wave_cols : (which + 1) * wave_cols] = values.astype(jnp.bfloat16)

                fr, fi, sr, si = first_r[part], first_i[part], second_r[part], second_i[part]
                hr, hi = wide(waves, 0, re), wide(waves, 0, im)
                far_r, far_i = (hr * sr + hi * si) * long, (hr * si - hi * sr) * long
                keep_taps(1, re, far_r)
                keep_taps(1, im, far_i)
                tr, ti = wide(waves, 1, re), wide(waves, 1, im)
                keep_taps(0, re, hr * fr + hi * fi + tr * sr + ti * si + parity * far_i)
                keep_taps(0, im, hr * fi - hi * fr + tr * si - ti * sr - parity * far_r)
                lr, li = wide(kernels, 0, re), wide(kernels, 0, im)
                keep(d_waves, 1, re, lr * sr + li * si)
                keep(d_waves, 1, im, lr * si - li * sr)
                cr, ci = wide(kernels, 1, re), wide(kernels, 1, im)
                keep(d_waves, 0, re, lr * fr + li * fi + cr * sr + ci * si)
                keep(d_waves, 0, im, lr * fi - li * fr + cr * si - ci * sr)

        pad = 8
        d_taps[0:pad, :] = jnp.zeros((pad, wave_cols), jnp.float32)
        d_taps[pad + tok_count :, :] = jnp.zeros((pad, wave_cols), jnp.float32)
        pool_rows = 16

        def column_step(across):
            cols = pl.ds(across * wave_cols, wave_cols)
            for down in range(half // wave_rows):
                wave_step(down, cols)
            for which in range(2):
                d_taps[pad + which * half : pad + (which + 1) * half, :] = dot_nn(
                    table_tv[...], d_signal[:, which * wave_cols : (which + 1) * wave_cols]
                )
            for index in range(tok_count // pool_rows):
                at = pad + index * pool_rows
                taps_held[at - pad : at - pad + pool_rows, cols] = (
                    (
                        d_taps[at - 1 : at - 1 + pool_rows, :]
                        + d_taps[at : at + pool_rows, :]
                        + d_taps[at + 1 : at + 1 + pool_rows, :]
                    )
                    / 3.0
                ).astype(jnp.bfloat16)


        def column_piece(across):
            if across == 0:
                loads["table again"].wait()
                loads["table_t again"].wait()
            column_step(across)
            taps[across].start()
            if across == blocks - 1:
                load("w_in signal", w_in.at[:, 0:feat], cot.at[0:feat, :])
                load("w_in gate", w_in.at[:, feat : 2 * feat], d_mix.at[0:feat, :])

        def down_again(t):
            return (waves if t < 2 else kernels).at[t % 2, 0:tile, :]

        def load_again(t):
            rows = pl.ds(t * tile, tile)
            load(("again", t), lambda: w_down.at[rows, :], lambda: down_again(t))

        def unwave_piece(which):
            for at in range(0, half, step_rows):
                d_signal[which * half + at : which * half + at + step_rows, :] = dot_nn(
                    table_tv[at : at + step_rows, :], d_waves[which]
                ).astype(jnp.bfloat16)
            if which == 1:
                for t in range(planes):
                    load_again(t)

        def grad_copy(index):
            rows = rows_of(index)
            return pltpu.make_async_copy(
                running.at[rows, :], input_grad.at[rows, :], load_sems.at[STORES + index]
            )

        def out_copy(index):
            rows = rows_of(index)
            return pltpu.make_async_copy(
                mixed_v.at[rows, :], block_out.at[rows, :], load_sems.at[STORES + row_steps + index]
            )

        def input_piece(index):
            if index == 0:
                loads["tokens again"].wait()
                loads["w_in signal"].wait()
                loads["w_in gate"].wait()
            rows = rows_of(index)
            d_normed = dot_nt(d_signal[rows, :], cot[0:feat, :]) + dot_nt(
                d_gate[rows, :], d_mix[0:feat, :]
            )
            sums_of = [0.0, 0.0]
            for part, _ in blocks_of(step_rows, feat):
                at = under(index, part)
                unit, inverse = norm_of(gate_v[at, :].astype(jnp.float32))
                grad = d_normed[part]
                sums_of = [sums_of[0] + column_sums(grad * unit), sums_of[1] + column_sums(grad)]
                scaled = grad * ln1_gain[...][None, :]
                running[at, :] = running[at, :] + inverse * (
                    scaled
                    - jnp.mean(scaled, axis=-1, keepdims=True)
                    - unit * jnp.mean(scaled * unit, axis=-1, keepdims=True)
                )
            grad_copy(index).start()
            sum_rows(2, index, sums_of[0])
            sum_rows(3, index, sums_of[1])

        def output_piece(index):
            if index == 0:
                for t in range(planes):
                    loads["again", t].wait()
            rows = rows_of(index)
            total = left_v[rows, :]
            for t in range(planes):
                total = total + dot_nn(active[t, rows, :], down_again(t)[...])
            mixed_v[rows, :] = total.astype(jnp.bfloat16)
            out_copy(index).start()

        back_piece(0)
        back_piece(1)
        ups[3].over_core()
        ups[2].over_first()
        back_piece(2)
        ups[1].over_second()
        back_piece(3)
        column_piece(0)
        downs[2].over_first()
        column_piece(1)
        downs[3].over_core()
        taps[0].over_core()
        ups[2].over_second()
        own_up(0)
        column_piece(2)
        taps[1].over_core()
        downs[2].over_second()
        unwave_piece(0)
        taps[2].over_core()
        out_piece()
        taps[0].over_first()
        downs[1].over_second()
        downs[3].over_first()
        ups[3].over_first()
        unwave_piece(1)
        gate_piece()
        taps[0].over_second()
        taps[2].over_first()
        out_chunk.over_core()
        downs[3].over_second()
        signal_piece()
        gate_chunk.over_core()
        taps[0].over_planes()
        taps[2].over_second()
        taps[1].over_first()
        own_down(1)
        input_piece(0)
        ups[3].over_second()
        signal_chunk.over_core()
        output_piece(0)
        input_piece(1)
        out_chunk.over_first()
        input_piece(2)
        output_piece(1)
        input_piece(3)
        taps[1].over_second()
        gate_chunk.over_first()
        sums.start()
        taps[2].over_planes()
        taps[0].back_y()
        out_chunk.over_second()
        own_down(3)
        signal_chunk.over_first()
        taps[1].over_planes()
        output_piece(2)
        taps[2].back_y()
        own_down(2)
        own_down(0)
        own_up(3)
        gate_chunk.over_second()
        sums.over(0)
        output_piece(3)
        taps[1].back_y()
        signal_chunk.over_second()
        sums.over(1)
        taps[2].back_core()
        taps[0].back_core()
        taps[1].back_core()
        own_gate()
        sums.over(2)
        own_up(2)
        own_out()
        own_taps(2)
        own_taps(0)
        own_up(1)
        own_taps(1)
        own_signal()
        for index in range(row_steps):
            grad_copy(index).wait()
            out_copy(index).wait()

    pl.run_scoped(
        backward,
        *[pltpu.VMEM((tok_count, feat), jnp.bfloat16)] * 4,
        pltpu.VMEM((tok_count, half), jnp.bfloat16),
        pltpu.VMEM((half, tok_count), jnp.bfloat16),
        pltpu.VMEM((tok_count + 16, tap_cols), jnp.float32),
    )

    sums_out[...] = sums.finish()
    for one in (downs[planes - 2], ups[planes - 1], downs[planes - 1], out_chunk, gate_chunk, signal_chunk):
        one.sent()
    for index in range(blocks):
        taps_copy(index).wait()


def hand_on_kernel(raw_taps, taps_sum, *others):
    count = (len(others) - 5) // 3
    sources, raw_grad, targets = others[:count], others[count], others[count + 1 : 2 * count + 1]
    raw_v, taps_v, grad_v = others[2 * count + 1 : 2 * count + 4]
    rooms, sems = others[2 * count + 4 : -1], others[-1]
    fetches = [pltpu.make_async_copy(taps_sum, taps_v, sems.at[0]), pltpu.make_async_copy(raw_taps, raw_v, sems.at[1])]
    stores = []
    for source, room, target in zip(sources, rooms, targets):
        rows = source.shape[0]
        parts = 4 if rows % 64 == 0 else 1
        for part in range(parts):
            at = pl.ds(part * (rows // parts), rows // parts)
            sem = sems.at[1 + len(fetches)]
            fetches.append(pltpu.make_async_copy(source.at[at, :], room.at[at, :], sem))
            stores.append(pltpu.make_async_copy(room.at[at, :], target.at[at, :], sem))
    for fetch in fetches:
        fetch.start()
    for fetch in fetches[:2]:
        fetch.wait()
    grad_v[...] = jnp.where(jnp.abs(raw_v[...]) > shrink_level, taps_v[...].astype(jnp.float32), 0.0)
    mask = pltpu.make_async_copy(grad_v, raw_grad, sems.at[2])
    mask.start()
    for fetch, store in zip(fetches[2:], stores):
        fetch.wait()
        store.start()
    for store in [mask] + stores:
        store.wait()


def hand_on(raw_taps, taps_sum, *sources):
    whole = pl.BlockSpec(memory_space=pl.ANY)
    return pl.pallas_call(
        hand_on_kernel,
        out_shape=[jax.ShapeDtypeStruct(raw_taps.shape, jnp.float32)]
        + [jax.ShapeDtypeStruct(source.shape, source.dtype) for source in sources],
        in_specs=[whole] * (2 + len(sources)),
        out_specs=[whole] * (1 + len(sources)),
        scratch_shapes=[
            pltpu.VMEM(raw_taps.shape, jnp.float32),
            pltpu.VMEM(taps_sum.shape, taps_sum.dtype),
            pltpu.VMEM(raw_taps.shape, jnp.float32),
        ]
        + [pltpu.VMEM(source.shape, source.dtype) for source in sources]
        + [pltpu.SemaphoreType.DMA((3 + 4 * len(sources),))],
        compiler_params=pltpu.CompilerParams(vmem_limit_bytes=VMEM_BYTES),
    )(raw_taps, taps_sum, *sources)


def linked_block(
    planes,
    tokens,
    lengths,
    raw_taps,
    ln1_gain,
    ln1_shift,
    w_in,
    w_out,
    ln2_gain,
    ln2_shift,
    w_up,
    w_down,
    cotangent,
):
    tok_count, feat = tokens.shape
    half = tok_count // 2
    tile = w_up.shape[1] // planes
    table = jnp.asarray(wave_table(half), jnp.bfloat16)
    table_t = jnp.asarray(wave_table(half).T, jnp.bfloat16)
    shares = 8 * planes
    rows = feat // shares
    block = (16, 128 * PART)
    chunks = 2 * planes + 3
    bf16, f32 = jnp.bfloat16, jnp.float32
    whole = pl.BlockSpec(memory_space=pl.ANY)
    near = pl.BlockSpec(memory_space=pltpu.VMEM)
    results = pl.pallas_call(
        functools.partial(block_kernel, planes),
        out_shape=(
            jax.ShapeDtypeStruct((tok_count, feat), bf16),
            jax.ShapeDtypeStruct((tok_count, feat), f32),
            jax.ShapeDtypeStruct((half, feat), bf16),
            jax.ShapeDtypeStruct((8, feat), f32),
            jax.ShapeDtypeStruct((rows, 2 * feat), f32),
            jax.ShapeDtypeStruct((rows, feat), f32),
            jax.ShapeDtypeStruct((rows, planes * tile), f32),
            jax.ShapeDtypeStruct((tile // 8, feat), f32),
        ),
        in_specs=[pl.BlockSpec(memory_space=pltpu.SMEM)] + [whole] * 9 + [near] * 4,
        out_specs=(whole,) * 3 + (near,) * 5,
        scratch_shapes=[
            pltpu.VMEM((2 * FLIGHTS, shares) + block, bf16),
            pltpu.VMEM((4, 4 * planes) + block, bf16),
            pltpu.VMEM((chunks, 2 * planes) + block, bf16),
            pltpu.VMEM((chunks, planes) + block, bf16),
            pltpu.VMEM((planes + 3, planes) + block, bf16),
            pltpu.VMEM((planes, planes) + block, bf16),
            pltpu.VMEM((tok_count, feat), bf16),
            pltpu.VMEM((tok_count // 2, feat), bf16),
            pltpu.VMEM((tok_count // 4, feat), bf16),
            pltpu.VMEM((tok_count // 8, feat), bf16),
            pltpu.VMEM(((planes - 1) * (tok_count // shares), feat), bf16),
            pltpu.VMEM((half, feat), bf16),
            pltpu.VMEM((4, 8, feat), f32),
            pltpu.VMEM((planes + 2, 8, feat), f32),
            pltpu.VMEM((tok_count, feat), bf16),
            pltpu.VMEM((planes, tok_count, tile), bf16),
            pltpu.VMEM((tok_count, feat), f32),
            pltpu.VMEM((feat, tok_count), bf16),
            pltpu.VMEM((feat, tok_count), bf16),
            pltpu.VMEM((feat, feat), bf16),
            pltpu.VMEM((tok_count, feat), bf16),
            pltpu.VMEM((tok_count, feat), bf16),
            pltpu.VMEM((tok_count, feat), f32),
            pltpu.VMEM((2, tok_count, feat), bf16),
            pltpu.VMEM((2, tok_count, feat), bf16),
            pltpu.SemaphoreType.DMA((chunks, planes + 2)),
            pltpu.SemaphoreType.DMA((chunks, planes + 2)),
            pltpu.SemaphoreType.DMA((feat // 256, 2 * planes + 5)),
            pltpu.SemaphoreType.DMA((feat // 256, 2 * planes + 5)),
            pltpu.SemaphoreType.DMA((planes + 2,)),
            pltpu.SemaphoreType.DMA((planes + 2,)),
            pltpu.SemaphoreType.DMA((2, feat // 256)),
            pltpu.SemaphoreType.DMA((2, feat // 256)),
            pltpu.SemaphoreType.DMA((STORES + 2 * tok_count // 256,)),
        ],
        compiler_params=pltpu.CompilerParams(
            collective_id=1, has_side_effects=True, vmem_limit_bytes=VMEM_BYTES
        ),
        cost_estimate=pl.CostEstimate(
            flops=2 * tok_count * feat * (5 * w_up.shape[1] + 9 * feat),
            bytes_accessed=40 * tok_count * feat,
            transcendentals=tok_count * w_up.shape[1],
        ),
    )(
        lengths,
        tokens,
        cotangent,
        raw_taps,
        w_in,
        w_out,
        w_up,
        w_down,
        table,
        table_t,
        ln1_gain,
        ln1_shift,
        ln2_gain,
        ln2_shift,
    )
    block_out, input_grad, taps_sum, sums, w_in_grad, w_out_grad, w_up_grad, w_down_grad = results
    raw_grad, block_out, input_grad, w_in_grad, w_out_grad, w_up_grad, w_down_grad = hand_on(
        raw_taps, taps_sum, block_out, input_grad, w_in_grad, w_out_grad, w_up_grad, w_down_grad
    )
    share = lax.axis_index("wide") * 2 + lax.axis_index("narrow")
    mine = lax.dynamic_slice(sums, (0, share * rows), (8, rows))
    return (
        block_out,
        input_grad,
        raw_grad,
        mine[2],
        mine[3],
        w_in_grad,
        w_out_grad,
        mine[0],
        mine[1],
        w_up_grad,
        w_down_grad,
    )


def solution(mesh):
    spread = P(("wide", "narrow"))
    rows = P(("wide", "narrow"), None)
    placed = (rows, spread, P("narrow", None)) + (P(),) * 8 + (rows,)
    wide, narrow = mesh.shape["wide"], mesh.shape["narrow"]

    def block(tokens, lengths, raw_taps, *others):
        fits = (
            narrow == 2
            and wide == 4 * 4
            and lengths.shape[0] == 1
            and raw_taps.shape[0] * 2 == tokens.shape[0]
            and tokens.shape[1] == 24 * wide * narrow
            and others[-2].shape[0] == 96 * wide * narrow
            and tokens.shape[0] % 512 == 0
        )
        if fits:
            return linked_block(wide // 4, tokens, lengths, raw_taps, *others)
        return local(tokens, lengths, raw_taps, *others)

    return jax.shard_map(
        block,
        mesh=mesh,
        in_specs=placed,
        out_specs=(rows, rows, P("narrow", None), spread, spread, rows, rows, spread, spread, rows, rows),
        check_vma=False,
    )
```

```python
import functools

import jax
import jax.numpy as jnp
import numpy as np
from jax import lax
from jax.experimental import pallas as pl
from jax.experimental.pallas import tpu as pltpu
from jax.sharding import PartitionSpec as P

shrink_level = 0.003
eps_norm = 1e-05


def wave_table(half):
    period = 4 * half
    phase = (np.outer(2 * np.arange(half) + 1, np.arange(half)) % period) * (2 * np.pi / period)
    return np.concatenate([np.cos(phase), -np.sin(phase)], axis=0)


def to_waves(table, block):
    return jnp.einsum("kn,nc->kc", table, block, preferred_element_type=jnp.float32)


def from_waves(table, waves):
    return jnp.einsum(
        "kn,kc->nc", table, waves.astype(jnp.bfloat16), preferred_element_type=jnp.float32
    )


def norm_parts(values):
    centered = values - jnp.mean(values, axis=-1, keepdims=True)
    inverse = lax.rsqrt(jnp.mean(centered * centered, axis=-1, keepdims=True) + eps_norm)
    return (centered * inverse, inverse)


def norm_back(upstream, unit_vals, inverse, gain_vec):
    scaled = upstream * gain_vec
    return inverse * (
        scaled
        - jnp.mean(scaled, axis=-1, keepdims=True)
        - unit_vals * jnp.mean(scaled * unit_vals, axis=-1, keepdims=True)
    )


def split(waves):
    half = waves.shape[0] // 2
    return waves[:half], waves[half:]


def times(left, right):
    lr, li = split(left)
    rr, ri = split(right)
    return jnp.concatenate([lr * rr - li * ri, lr * ri + li * rr], axis=0)


def conj_times(left, right):
    lr, li = split(left)
    rr, ri = split(right)
    return jnp.concatenate([lr * rr + li * ri, lr * ri - li * rr], axis=0)


def turned(waves, sign):
    wr, wi = split(waves)
    index = lax.broadcasted_iota(jnp.int32, (wr.shape[0], 1), 0)
    parity = sign * (1.0 - 2.0 * (index % 2).astype(jnp.float32))
    return jnp.concatenate([-parity * wi, parity * wr], axis=0)


def pool(values):
    padded = jnp.pad(values, ((1, 1), (0, 0)))
    return (padded[:-2] + padded[1:-1] + padded[2:]) / 3.0


def local(
    tokens,
    lengths,
    raw_taps,
    ln1_gain,
    ln1_shift,
    w_in,
    w_out,
    ln2_gain,
    ln2_shift,
    w_up,
    w_down,
    cotangent,
):
    tok_count, feat_width = tokens.shape
    row_count = lengths.shape[0]
    row_len = tok_count // row_count
    half = row_len // 2
    table = jnp.asarray(wave_table(half), jnp.bfloat16)
    scale = 1.0 / half
    long_rows = (lengths > half).astype(jnp.float32)

    squashed = raw_taps - jnp.clip(raw_taps, -shrink_level, shrink_level)
    gathered = lax.all_gather(squashed.astype(jnp.bfloat16), "narrow", axis=0, tiled=True)
    kernel = pool(gathered.astype(jnp.float32)).astype(jnp.bfloat16)
    kernel_low = to_waves(table, kernel[:half])
    kernel_cross = to_waves(table, kernel[half : 2 * half]) + turned(kernel_low, 1.0)

    inputs = tokens.astype(jnp.float32)
    unit_one, inverse_one = norm_parts(inputs)
    normed = (unit_one * ln1_gain + ln1_shift).astype(jnp.bfloat16)
    projected = jnp.dot(normed, w_in, preferred_element_type=jnp.float32)
    signal = projected[:, :feat_width].astype(jnp.bfloat16)
    gate_vals = projected[:, feat_width:]
    signal_waves = []
    mixed = []
    for row in range(row_count):
        first = to_waves(table, signal[row * row_len : row * row_len + half])
        second = to_waves(table, signal[row * row_len + half : (row + 1) * row_len])
        signal_waves.append((first, second))
        mixed.append(from_waves(table, times(first, kernel_low) * scale))
        mixed.append(
            from_waves(
                table,
                (times(second, kernel_low) + long_rows[row] * times(first, kernel_cross)) * scale,
            )
        )
    mixed = jnp.concatenate(mixed, axis=0)
    branch = (mixed * gate_vals).astype(jnp.bfloat16)
    residual = inputs + jnp.dot(branch, w_out, preferred_element_type=jnp.float32)
    unit_two, inverse_two = norm_parts(residual)
    normed2 = (unit_two * ln2_gain + ln2_shift).astype(jnp.bfloat16)
    hidden = jnp.dot(normed2, w_up, preferred_element_type=jnp.float32)
    active = jax.nn.gelu(hidden).astype(jnp.bfloat16)
    block_out = (residual + jnp.dot(active, w_down, preferred_element_type=jnp.float32)).astype(
        jnp.bfloat16
    )
    w_down_grad = jnp.einsum("tf,td->fd", active, cotangent, preferred_element_type=jnp.float32)
    d_active = jnp.einsum("td,fd->tf", cotangent, w_down, preferred_element_type=jnp.float32)
    gelu_pull = jax.vjp(jax.nn.gelu, hidden)[1]
    d_hidden = gelu_pull(d_active)[0].astype(jnp.bfloat16)
    w_up_grad = jnp.einsum("td,tf->df", normed2, d_hidden, preferred_element_type=jnp.float32)
    d_normed2 = jnp.einsum("tf,df->td", d_hidden, w_up, preferred_element_type=jnp.float32)
    ln2_gain_grad = jnp.sum(d_normed2 * unit_two, axis=0)
    ln2_shift_grad = jnp.sum(d_normed2, axis=0)
    d_residual = cotangent.astype(jnp.float32) + norm_back(
        d_normed2, unit_two, inverse_two, ln2_gain
    )
    d_outproj = d_residual.astype(jnp.bfloat16)
    w_out_grad = jnp.einsum("td,te->de", branch, d_outproj, preferred_element_type=jnp.float32)
    d_branch = jnp.einsum("te,de->td", d_outproj, w_out, preferred_element_type=jnp.float32)
    d_mixed = (d_branch * gate_vals).astype(jnp.bfloat16)
    d_gate = d_branch * mixed
    d_signal = []
    low_grad = 0.0
    cross_grad = 0.0
    for row in range(row_count):
        first, second = signal_waves[row]
        d_first = to_waves(table, d_mixed[row * row_len : row * row_len + half]) * scale
        d_second = to_waves(table, d_mixed[row * row_len + half : (row + 1) * row_len]) * scale
        d_cross = d_second * long_rows[row]
        d_signal.append(
            from_waves(table, conj_times(kernel_low, d_first) + conj_times(kernel_cross, d_cross))
        )
        d_signal.append(from_waves(table, conj_times(kernel_low, d_second)))
        low_grad = low_grad + conj_times(first, d_first) + conj_times(second, d_second)
        cross_grad = cross_grad + conj_times(first, d_cross)
    low_grad = low_grad + turned(cross_grad, -1.0)
    d_kernel = jnp.concatenate([from_waves(table, low_grad), from_waves(table, cross_grad)], axis=0)
    d_signal = jnp.concatenate(d_signal, axis=0)
    d_projected = jnp.concatenate([d_signal, d_gate], axis=1).astype(jnp.bfloat16)
    w_in_grad = jnp.einsum("td,te->de", normed, d_projected, preferred_element_type=jnp.float32)
    d_normed = jnp.einsum("te,de->td", d_projected, w_in, preferred_element_type=jnp.float32)
    ln1_gain_grad = jnp.sum(d_normed * unit_one, axis=0)
    ln1_shift_grad = jnp.sum(d_normed, axis=0)
    input_grad = d_residual + norm_back(d_normed, unit_one, inverse_one, ln1_gain)

    shares = lax.psum_scatter(
        pool(d_kernel).astype(jnp.bfloat16), "narrow", scatter_dimension=0, tiled=True
    )
    summed = lax.psum(shares, "wide").astype(jnp.float32)
    raw_grad = summed * (jnp.abs(raw_taps) > shrink_level).astype(jnp.float32)

    def scatter(values):
        return lax.psum_scatter(
            values.astype(jnp.bfloat16), ("wide", "narrow"), scatter_dimension=0, tiled=True
        ).astype(jnp.float32)

    def scatter_wide(values):
        return lax.psum_scatter(values, ("wide", "narrow"), scatter_dimension=0, tiled=True)

    return (
        block_out,
        input_grad,
        raw_grad,
        scatter_wide(ln1_gain_grad),
        scatter_wide(ln1_shift_grad),
        scatter(w_in_grad),
        scatter(w_out_grad),
        scatter_wide(ln2_gain_grad),
        scatter_wide(ln2_shift_grad),
        scatter(w_up_grad),
        scatter(w_down_grad),
    )


MESH = pl.DeviceIdType.MESH
PART = 9
STORES = 30
VMEM_BYTES = 60 * 2**20
PEERS = [(dx, dy, dcore) for dx in range(2) for dy in range(2) for dcore in range(2)][1:]
FLIGHTS = 3


def dot_nn(left, right):
    return lax.dot_general(left, right, (((1,), (0,)), ((), ())), preferred_element_type=jnp.float32)


def dot_nt(left, right):
    return lax.dot_general(left, right, (((1,), (1,)), ((), ())), preferred_element_type=jnp.float32)


def dot_tn(left, right):
    return lax.dot_general(left, right, (((0,), (0,)), ((), ())), preferred_element_type=jnp.float32)


def gelu_both(hidden):
    inner = 0.7978845608028654
    cubic = inner * 0.044715
    square = hidden * hidden
    bent = jnp.tanh(hidden * (inner + cubic * square))
    share = 0.5 + 0.5 * bent
    slope = share + (0.5 * hidden) * (1.0 - bent * bent) * (inner + (3.0 * cubic) * square)
    return hidden * share, slope


def blocks_of(rows, columns, height=16, width=768):
    return [
        (slice(at, at + height), slice(left, min(left + width, columns)))
        for at in range(0, rows, height)
        for left in range(0, columns, width)
    ]


def column_sums(values):
    rows, width = values.shape
    return jnp.sum(values.reshape(rows // 8, 8, width), axis=0)


class Place:
    def __init__(self, planes):
        wide = lax.axis_index("wide")
        self.narrow = lax.axis_index("narrow")
        self.wide = wide
        self.core = wide % 2
        self.y = (wide // 2) % 2
        self.z = wide // 4
        self.x = self.narrow
        self.planes = planes
        self.sibling = (wide + 1 - 2 * self.core, self.narrow)
        self.next_x = (wide, 1 - self.narrow)
        self.next_y = (wide + 2 - 4 * self.y, self.narrow)

    def peer(self, dx, dy, dcore):
        wide = self.wide + dy * (2 - 4 * self.y) + dcore * (1 - 2 * self.core)
        return wide, self.narrow + dx * (1 - 2 * self.narrow)

    def plane(self, step):
        other = (self.z + step) % self.planes
        return (self.wide + 4 * (other - self.z), self.narrow), other


class Chunk:
    def __init__(self, place, held, inbox, sems, x_first, target=None):
        self.place = place
        self.views = (held, inbox, sems)
        self.target = target
        self.first, self.second = (place.x, place.y) if x_first else (place.y, place.x)
        self.to_first, self.to_second = (
            (place.next_x, place.next_y) if x_first else (place.next_y, place.next_x)
        )
        self.x_first = x_first

    @property
    def held(self):
        ref, at = self.views[0]
        return ref.at[at]

    @property
    def inbox(self):
        return [ref if at is None else ref.at[at] for ref, at in self.views[1]]

    @property
    def sems(self):
        return [ref.at[at] for ref, at in self.views[2]]

    def slot(self, y, core, x):
        first, second = (x, y) if self.x_first else (y, x)
        return ((core * 2 + first) * 2 + second) * self.place.planes

    def copy(self, stage):
        planes, core = self.place.planes, self.place.core
        first, second = self.first, self.second
        start, count, device = (
            (4 * planes * (1 - core), 4 * planes, self.place.sibling),
            (4 * planes * core + 2 * planes * (1 - first), 2 * planes, self.to_first),
            (4 * planes * core + 2 * planes * first + planes * (1 - second), planes, self.to_second),
        )[stage]
        return pltpu.make_async_remote_copy(
            src_ref=self.held.at[pl.ds(start, count)],
            dst_ref=self.inbox[stage],
            send_sem=self.sems[0].at[stage],
            recv_sem=self.sems[1].at[stage],
            device_id=device,
            device_id_type=MESH,
        )

    def add(self, start, landing, count):
        for index in range(count):
            self.held[start + index] += landing[index]

    def start(self):
        self.copy(0).start()

    def over_core(self):
        planes = self.place.planes
        self.copy(0).wait()
        self.add(4 * planes * self.place.core, self.inbox[0], 4 * planes)
        self.copy(1).start()

    def over_first(self):
        planes = self.place.planes
        self.copy(1).wait()
        self.add(4 * planes * self.place.core + 2 * planes * self.first, self.inbox[1], 2 * planes)
        self.copy(2).start()

    def base(self):
        planes, place = self.place.planes, self.place
        return 4 * planes * place.core + 2 * planes * self.first + planes * self.second

    def plane_copy(self, step):
        device, other = self.place.plane(step)
        if self.target is None:
            return pltpu.make_async_remote_copy(
                src_ref=self.held.at[self.base() + other],
                dst_ref=self.inbox[3].at[step - 1],
                send_sem=self.sems[0].at[2 + step],
                recv_sem=self.sems[1].at[2 + step],
                device_id=device,
                device_id_type=MESH,
            )
        return pltpu.make_async_remote_copy(
            src_ref=self.held.at[pl.ds(self.base(), self.place.planes)],
            dst_ref=self.inbox[3].at[step - 1],
            send_sem=self.sems[0].at[2 + step],
            recv_sem=self.sems[1].at[2 + step],
            device_id=device,
            device_id_type=MESH,
        )

    def each_plane(self, act):
        for step in range(1, self.place.planes):
            if self.target is None:
                act(self.plane_copy(step))
            else:

                @pl.when((self.place.z + step) % self.place.planes == self.target)
                def _():
                    act(self.plane_copy(step))

    def over_second(self):
        self.copy(2).wait()
        planes = self.place.planes
        self.add(self.base(), self.inbox[2], planes)
        if self.target is None:
            self.inbox[3][planes - 1] = self.held[self.base() + self.place.z]
        else:

            @pl.when(self.place.z == self.target)
            def _():
                for index in range(planes):
                    self.inbox[3][planes - 1, index] = self.held[self.base() + index]

        self.each_plane(lambda copy: copy.start())

    def sent(self):
        self.each_plane(lambda copy: copy.wait_send())

    def arrived(self):
        for step in range(1, self.place.planes):
            self.plane_copy(step).wait_recv()

    def total(self, index):
        terms = [
            self.inbox[3][step] if self.target is None else self.inbox[3][step, index]
            for step in range(self.place.planes)
        ]
        return sum(term.astype(jnp.float32) for term in terms)


def store_rows(chunk, values, first_row):
    width = values.shape[1]
    for k in range(values.shape[0] // 24):
        shard = first_row // 24 + k
        z, y, core, x = shard // 8, shard // 4 % 2, shard // 2 % 2, shard % 2
        at = chunk.slot(y, core, x) + z
        block = values[24 * k : 24 * k + 24]
        rest = block[16:24]
        chunk.held[at, :, 0:width] = block[0:16].astype(jnp.bfloat16)
        chunk.held[at, :, width : width + width // 2] = jnp.concatenate(
            [rest[:, : width // 2], rest[:, width // 2 :]], axis=0
        ).astype(jnp.bfloat16)


def load_rows(block, width):
    rest = block[:, width:]
    return jnp.concatenate(
        [block[:, :width], jnp.concatenate([rest[0:8], rest[8:16]], axis=1)], axis=0
    )


def tile_runs(sub, width):
    tiles = width // 128
    runs, tile = [], 0
    while tile < tiles:
        line = sub * tiles + tile
        count = min(tiles - tile, PART - line % PART)
        runs.append((tile, line // PART, line % PART, count))
        tile += count
    return runs


def store_shards(chunk, values, first_row):
    width = values.shape[1]
    for k in range(values.shape[0] // 16):
        row = first_row + 16 * k
        shard, sub = row // 96, row % 96 // 16
        base = chunk.slot(shard // 4, shard // 2 % 2, shard % 2)
        for tile, block, at, count in tile_runs(sub, width):
            chunk.held[base + block, :, 128 * at : 128 * (at + count)] = values[
                16 * k : 16 * k + 16, 128 * tile : 128 * (tile + count)
            ].astype(jnp.bfloat16)


class Taps:
    def __init__(self, place, held, inbox, result, sems, index, rows, cols, x_first):
        self.place, self.held, self.inbox, self.result = place, held, inbox, result
        self.sems, self.index = sems, index
        self.rows = rows
        self.cols = cols
        self.x_first = x_first

    def part(self, x, core, y, plane, count):
        planes = self.place.planes
        return pl.ds((((x * 2 + core) * 2 + y) * planes + plane) * self.rows, count * self.rows)

    def add(self, target, landing):
        self.held[target, self.cols] += landing[...]

    def landing(self, level, first, count):
        return self.inbox[level].at[pl.ds(first * self.rows, count * self.rows), self.cols]

    def copy(self, kind, step=0):
        place, planes = self.place, self.place.planes
        x, core, y, z = place.x, place.core, place.y, place.z
        if kind == "core":
            source, landing = self.part(step, 1 - core, 0, 0, 2 * planes), self.landing(0, step * 2 * planes, 2 * planes)
            stage, device = step, place.sibling
        elif kind == "first" and self.x_first:
            source, landing = self.part(1 - x, core, 0, 0, 2 * planes), self.landing(1, 0, 2 * planes)
            stage, device = 2, place.next_x
        elif kind == "first":
            source, landing = self.part(step, core, 1 - y, 0, planes), self.landing(1, step * planes, planes)
            stage, device = 2 + step, place.next_y
        elif kind == "second":
            first = self.part(x, core, 1 - y, 0, planes) if self.x_first else self.part(1 - x, core, y, 0, planes)
            source, landing = first, self.landing(2, 0, planes)
            stage, device = 4, place.next_y if self.x_first else place.next_x
        elif kind == "plane":
            device, other = place.plane(step)
            source, landing = self.part(x, core, y, other, 1), self.landing(3, step - 1, 1)
            stage = 4 + step
        else:
            if kind == "back plane":
                mine, stage, device = (0, core, y, z, 1), 3 + planes + step, place.plane(step)[0]
            else:
                device = (place.next_y, place.sibling, place.peer(0, 1, 1))[step]
                mine, stage = (0, core, y, 0, planes), 3 + 2 * planes + step
            landing = self.result.at[self.part(*mine), self.cols]
        return pltpu.make_async_remote_copy(
            src_ref=landing if kind.startswith("back") else self.held.at[source, self.cols],
            dst_ref=landing,
            send_sem=self.sems[0].at[self.index, stage],
            recv_sem=self.sems[1].at[self.index, stage],
            device_id=device,
            device_id_type=MESH,
        )

    def start(self):
        for x in range(2):
            self.copy("core", x).start()

    def over_core(self):
        for x in range(2):
            self.copy("core", x).wait()
            self.add(
                self.part(x, self.place.core, 0, 0, 2 * self.place.planes),
                self.landing(0, x * 2 * self.place.planes, 2 * self.place.planes),
            )
        for step in range(1 if self.x_first else 2):
            self.copy("first", step).start()

    def over_first(self):
        place, planes = self.place, self.place.planes
        if self.x_first:
            self.copy("first").wait()
            self.add(self.part(place.x, place.core, 0, 0, 2 * planes), self.landing(1, 0, 2 * planes))
        else:
            for x in range(2):
                self.copy("first", x).wait()
                self.add(self.part(x, place.core, place.y, 0, planes), self.landing(1, x * planes, planes))
        self.copy("second").start()

    def over_second(self):
        place = self.place
        self.copy("second").wait()
        self.add(self.part(place.x, place.core, place.y, 0, place.planes), self.landing(2, 0, place.planes))
        for step in range(1, place.planes):
            self.copy("plane", step).start()

    def over_planes(self):
        place = self.place
        mine = self.part(place.x, place.core, place.y, place.z, 1)
        total = self.held[mine, self.cols].astype(jnp.float32)
        for step in range(1, place.planes):
            self.copy("plane", step).wait()
            total = total + self.landing(3, step - 1, 1)[...].astype(jnp.float32)
        self.result[self.part(0, place.core, place.y, place.z, 1), self.cols] = total.astype(self.result.dtype)
        for step in range(1, place.planes):
            self.copy("back plane", step).start()

    def back_y(self):
        for step in range(1, self.place.planes):
            self.copy("back plane", step).wait()
        for step in range(3):
            self.copy("back", step).start()

    def finish(self):
        for step in range(3):
            self.copy("back", step).wait()


class Sums:
    def __init__(self, place, levels, inbox, sems):
        self.place, self.levels, self.inbox, self.sems = place, levels, inbox, sems

    def copy(self, level, landing):
        place = self.place
        device = place.peer(*PEERS[landing]) if level == 0 else place.plane(landing - len(PEERS) + 1)[0]
        return pltpu.make_async_remote_copy(
            src_ref=self.levels.at[level],
            dst_ref=self.inbox.at[landing],
            send_sem=self.sems[0].at[landing],
            recv_sem=self.sems[1].at[landing],
            device_id=device,
            device_id_type=MESH,
        )

    def landings(self, level):
        first = len(PEERS) * level
        return range(first, first + (len(PEERS) if level == 0 else self.place.planes - 1))

    def start(self):
        for landing in self.landings(0):
            self.copy(0, landing).start()

    def gather(self, level):
        total = self.levels[level]
        for landing in self.landings(level):
            self.copy(level, landing).wait()
            total = total + self.inbox[landing]
        return total

    def over(self, level):
        self.levels[level + 1] = self.gather(level)
        for landing in self.landings(level + 1):
            self.copy(level + 1, landing).start()

    def finish(self):
        return self.gather(1)


def block_kernel(
    planes,
    lengths,
    tokens, cotangent, raw_taps, w_in, w_out, w_up, w_down, table, table_t,
    ln1_gain, ln1_shift, ln2_gain, ln2_shift,
    block_out, input_grad, taps_out, sums_out, w_in_grad, w_out_grad, w_up_grad, w_down_grad,
    held, inbox0, inbox1, inbox2, inbox_u, inbox_n, taps_held, taps0, taps1, taps2, taps3, taps_sum,
    levels, sums_inbox, cot, active, running, branch_v, normed_v, w_out_v,
    gate_v, mixed_v, left_v, waves, kernels,
    send_sems, recv_sems, taps_send, taps_recv, sums_send, sums_recv, share_send, share_recv, load_sems,
):
    tok_count, feat = cot.shape
    half = tok_count // 2
    tile = active.shape[2]
    step_rows = tap_cols = 256
    blocks = feat // tap_cols
    row_steps = tok_count // step_rows
    place = Place(planes)

    loads = {}

    class Load:
        def __init__(self, source, target):
            self.ends, self.at = (source, target), len(loads)

        def copy(self):
            source, target = (end() if callable(end) else end for end in self.ends)
            return pltpu.make_async_copy(source, target, load_sems.at[self.at])

        def wait(self):
            self.copy().wait()

    def load(name, source, target):
        loads[name] = Load(source, target)
        loads[name].copy().start()

    barrier = pltpu.get_barrier_semaphore()
    partners = [place.peer(*marks) for marks in PEERS] + [place.plane(step)[0] for step in range(1, planes)]
    for partner in partners:
        pl.semaphore_signal(barrier, inc=1, device_id=partner, device_id_type=MESH)
    long = jnp.where(lengths[0] > half, 1.0, 0.0).astype(jnp.float32)

    def chunk(index, step, kind, target=None):
        at = step % FLIGHTS * 2 + kind
        ring = step % 2 * 2 + kind
        if target is None:
            far = (inbox_u, index // 2 if index < 2 * planes else index - planes)
        else:
            far = (inbox_n, None)
        return Chunk(
            place,
            (held, at),
            ((inbox0, ring), (inbox1, ring), (inbox2, ring), far),
            ((send_sems, index), (recv_sems, index)),
            kind == 0,
            target,
        )

    ups = [chunk(2 * t, t, 0) for t in range(planes)]
    downs = [chunk(2 * t + 1, t, 1, t) for t in range(planes)]

    def rows_of(index):
        return pl.ds(index * step_rows, step_rows)

    def under(index, part):
        return pl.ds(index * step_rows + part.start, part.stop - part.start)

    def unrolled(first, last, body, carry):
        for index in range(first, last):
            carry = body(index, carry)
        return carry

    def norm_of(values):
        centered = values - jnp.mean(values, axis=-1, keepdims=True)
        inverse = lax.rsqrt(jnp.mean(centered * centered, axis=-1, keepdims=True) + eps_norm)
        return centered * inverse, inverse

    out_chunk = chunk(2 * planes, planes, 0)
    gate_chunk = chunk(2 * planes + 1, planes, 1)
    signal_chunk = chunk(2 * planes + 2, planes + 1, 0)
    taps = [
        Taps(
            place, taps_held, (taps0, taps1, taps2, taps3), taps_sum, (taps_send, taps_recv), index,
            tok_count // (8 * planes), pl.ds(index * tap_cols, tap_cols), index % 2 == 0,
        )
        for index in range(feat // tap_cols)
    ]
    sums = Sums(place, levels, sums_inbox, (sums_send, sums_recv))

    def own_rows(target):
        target.arrived()
        return load_rows(target.total(0), feat)

    def own_down(t):
        @pl.when(place.z == t)
        def _():
            downs[t].arrived()
            for index in range(planes):
                block = downs[t].total(index)
                for sub in range(6):
                    for first, line, at, count in tile_runs(sub, feat):
                        if line == index:
                            w_down_grad[16 * sub : 16 * sub + 16, 128 * first : 128 * (first + count)] = block[
                                :, 128 * at : 128 * (at + count)
                            ]

    def weight_rows(target, left_t, right):
        for part in range(2):
            rows = feat // 2
            store_rows(target, dot_nn(left_t[part * rows : (part + 1) * rows, :], right[...]), part * rows)
        target.start()

    def own_up(t):
        w_up_grad[:, t * tile : (t + 1) * tile] = own_rows(ups[t])

    def own_out():
        w_out_grad[...] = own_rows(out_chunk)

    def own_gate():
        w_in_grad[:, feat:] = own_rows(gate_chunk)

    def own_signal():
        w_in_grad[:, 0:feat] = own_rows(signal_chunk)

    def taps_copy(index):
        cols = pl.ds(index * tap_cols, tap_cols)
        return pltpu.make_async_copy(taps_sum.at[:, cols], taps_out.at[:, cols], load_sems.at[STORES - 1 - index])

    def own_taps(index):
        taps[index].finish()
        taps_copy(index).start()

    def share_copy(which, across):
        block = half // 2
        block_x = place.x if which == 0 else 1 - place.x
        rows = pl.ds(pl.multiple_of(block_x * half + place.core * block, block), block)
        part = taps_held.at[rows, pl.ds(across * tap_cols, tap_cols)]
        return pltpu.make_async_remote_copy(
            src_ref=part,
            dst_ref=part,
            send_sem=share_send.at[which, across],
            recv_sem=share_recv.at[which, across],
            device_id=place.next_x if which == 0 else place.sibling,
            device_id_type=MESH,
        )

    def share_on(across):
        share_copy(0, across).wait()
        share_copy(1, across).start()

    def forward_back(normed_2, normed_2t, up_tiles, down_tiles):
        def load_tile(t):
            cols = pl.ds(t * tile, tile)
            load(("up", t), lambda: w_up.at[:, cols], lambda: up_tiles.at[t % 2])
            load(("down", t), lambda: w_down.at[cols, :], lambda: down_tiles.at[t % 2])

        def mix(table_v, table_tv):
            kernel = mixed_v
            load("taps", raw_taps, running.at[0:half, :])
            load("tokens", tokens, lambda: active.at[0])
            load("w_in", w_in.at[:, 0:feat], normed_2.at[0:feat, :])
            load("w_in end", w_in.at[:, feat : 2 * feat], normed_2t.at[:, 0:feat])
            load("table", table, table_v)
            load("table_t", table_t, table_tv)
            load("w_out", w_out, w_out_v)
            load_tile(0)
            load("cot", cotangent, cot)

            loads["taps"].wait()

            def squash_step(index, carry):
                rows = pl.ds(pl.multiple_of(index * 128, 128), 128)
                raw = running[rows, :]
                taps_held[pl.ds(pl.multiple_of(place.x * half + index * 128, 128), 128), :] = (
                    raw - jnp.clip(raw, -shrink_level, shrink_level)
                ).astype(jnp.bfloat16)
                return carry

            lax.fori_loop(0, half // 128, squash_step, 0)
            pl.semaphore_wait(barrier, len(partners))
            for across in range(blocks):
                share_copy(0, across).start()
            loads["tokens"].wait()
            loads["w_in"].wait()
            loads["w_in end"].wait()

            def project_step(index, carry):
                rows = rows_of(index)
                for part, _ in blocks_of(step_rows, feat):
                    at = under(index, part)
                    unit, _ = norm_of(active[0, at, :].astype(jnp.float32))
                    mixed_v[at, :] = (unit * ln1_gain[...][None, :] + ln1_shift[...][None, :]).astype(jnp.bfloat16)
                low = mixed_v[rows, :]
                normed_v[:, rows] = low.T
                active[1, rows, :] = dot_nn(low, normed_2[0:feat, :]).astype(jnp.bfloat16)
                gate_v[rows, :] = dot_nn(low, normed_2t[:, 0:feat]).astype(jnp.bfloat16)
                return carry

            unrolled(0, row_steps, project_step, 0)
            share_on(0)
            loads["table"].wait()

            def signal_wave_step(index, carry):
                rows = rows_of(index)
                for which in range(2):
                    waves[which, rows, :] = dot_nn(
                        table_v[rows, :], active[1, which * half : (which + 1) * half, :]
                    ).astype(jnp.bfloat16)
                return carry

            unrolled(0, row_steps, signal_wave_step, 0)
            pool_rows = 16

            def pool_step(across):
                cols = slice(across * tap_cols, (across + 1) * tap_cols)
                rim = jnp.zeros((16, tap_cols), jnp.float32)
                for index in range(tok_count // pool_rows):
                    at = index * pool_rows
                    first, last = max(at - 16, 0), min(at + pool_rows + 16, tok_count)
                    around = taps_held[first:last, cols].astype(jnp.float32)
                    if at == 0:
                        around = jnp.concatenate([rim, around], axis=0)
                    if last == tok_count:
                        around = jnp.concatenate([around, rim], axis=0)
                    kernel[at : at + pool_rows, cols] = (
                        (around[15 : 15 + pool_rows] + around[16 : 16 + pool_rows] + around[17 : 17 + pool_rows])
                        / 3.0
                    ).astype(jnp.bfloat16)

            def spread_step(down, across):
                real, imag = pl.ds(down * 256, 256), pl.ds(half + down * 256, 256)
                cols = pl.ds(across * 256, 256)
                low_r = dot_nn(table_v[real, :], kernel[0:half, cols])
                low_i = dot_nn(table_v[imag, :], kernel[0:half, cols])
                high_r = dot_nn(table_v[real, :], kernel[half:, cols])
                high_i = dot_nn(table_v[imag, :], kernel[half:, cols])
                odd = lax.broadcasted_iota(jnp.int32, (16, 1), 0) % 2
                parity = (1 - 2 * odd).astype(jnp.float32)
                scale = 1.0 / half
                for part, _ in blocks_of(256, tap_cols):
                    re, im = under(down, part), pl.ds(half + down * 256 + part.start, 16)

                    def keep(ref, which, at, values):
                        ref[which, at, cols] = values.astype(jnp.bfloat16)

                    lr, li = low_r[part], low_i[part]
                    cr, ci = long * (high_r[part] - parity * li), long * (high_i[part] + parity * lr)
                    keep(kernels, 0, re, lr)
                    keep(kernels, 0, im, li)
                    keep(kernels, 1, re, cr)
                    keep(kernels, 1, im, ci)
                    hr, hi, tr, ti = (
                        waves[which, at, cols].astype(jnp.float32) * scale for which in range(2) for at in (re, im)
                    )
                    keep(active, 2, re, lr * hr - li * hi)
                    keep(active, 2, im, lr * hi + li * hr)
                    keep(active, 3, re, lr * tr - li * ti + cr * hr - ci * hi)
                    keep(active, 3, im, lr * ti + li * tr + cr * hi + ci * hr)

            share_on(1)
            for across in range(blocks):
                share_copy(1, across).wait()
                pool_step(across)
                for down in range(half // 256):
                    spread_step(down, across)
                if across + 2 < blocks:
                    share_on(across + 2)
            loads["table_t"].wait()
            loads["w_out"].wait()

            def residual_step(index, carry):
                rows = rows_of(index)
                part_steps = half // step_rows
                which = index // part_steps
                of_part = pl.ds(index % part_steps * step_rows, step_rows)
                mixed = dot_nn(table_tv[of_part, :], active[2 + which])
                for part, columns in blocks_of(step_rows, feat):
                    at = under(index, part)
                    mixed_v[at, columns] = mixed[part, columns].astype(jnp.bfloat16)
                    active[1, at, columns] = (
                        mixed[part, columns] * gate_v[at, columns].astype(jnp.float32)
                    ).astype(jnp.bfloat16)
                branch = active[1, rows, :]
                branch_v[:, rows] = branch.T
                added = dot_nn(branch, w_out_v[...])
                for part, _ in blocks_of(step_rows, feat):
                    at = under(index, part)
                    left = active[0, at, :].astype(jnp.float32) + added[part]
                    left_v[at, :] = left
                    unit, _ = norm_of(left)
                    normed_2[at, :] = (unit * ln2_gain[...][None, :] + ln2_shift[...][None, :]).astype(jnp.bfloat16)
                normed_2t[:, rows] = normed_2[rows, :].T
                return carry

            unrolled(0, row_steps, residual_step, 0)

        pl.run_scoped(
            mix,
            pltpu.VMEM((tok_count, half), jnp.bfloat16),
            pltpu.VMEM((half, tok_count), jnp.bfloat16),
        )

        def feed_forward(d_hidden):
            loads["cot"].wait()

            def rows_piece(t, index):
                up_tile, down_tile = up_tiles.at[t % 2], down_tiles.at[t % 2]
                if index == 0:
                    loads["up", t].wait()
                    loads["down", t].wait()
                    if t + 1 < planes:
                        load_tile(t + 1)
                rows = rows_of(index)
                hidden = dot_nn(normed_2[rows, :], up_tile[...])
                d_active = dot_nt(cot[rows, :], down_tile[...])
                for part, columns in blocks_of(step_rows, tile, 16, 384):
                    at = under(index, part)
                    value, slope = gelu_both(hidden[part, columns])
                    active[t, at, columns] = value.astype(jnp.bfloat16)
                    d_hidden[t % 2, at, columns] = (d_active[part, columns] * slope).astype(jnp.bfloat16)
                back = dot_nt(d_hidden[t % 2, rows, :], up_tile[...])
                if t == 0:
                    running[rows, :] = back
                else:
                    running[rows, :] += back

            def up_piece(t):
                if t >= FLIGHTS:
                    ups[t - FLIGHTS].sent()
                weight_rows(ups[t], normed_2t, d_hidden.at[t % 2])

            def down_piece(t):
                if t >= FLIGHTS:
                    downs[t - FLIGHTS].sent()
                for part in range(2):
                    cols = slice(part * (tile // 2), (part + 1) * (tile // 2))
                    store_shards(downs[t], dot_tn(active[t, :, cols], cot[...]), part * (tile // 2))
                downs[t].start()

            rows_piece(0, 0)
            rows_piece(0, 1)
            rows_piece(0, 2)
            rows_piece(0, 3)
            down_piece(0)
            up_piece(0)
            rows_piece(1, 0)
            rows_piece(1, 1)
            downs[0].over_core()
            ups[0].over_core()
            rows_piece(1, 2)
            rows_piece(1, 3)
            down_piece(1)
            up_piece(1)
            rows_piece(2, 0)
            downs[0].over_first()
            downs[1].over_core()
            ups[0].over_first()
            ups[1].over_core()
            rows_piece(2, 1)
            rows_piece(2, 2)
            rows_piece(2, 3)
            down_piece(2)
            up_piece(2)
            rows_piece(3, 0)
            downs[0].over_second()
            downs[1].over_first()
            downs[2].over_core()
            rows_piece(3, 1)
            rows_piece(3, 2)
            ups[0].over_second()
            ups[1].over_first()
            ups[2].over_core()
            rows_piece(3, 3)
            down_piece(3)
            up_piece(3)

        pl.run_scoped(feed_forward, pltpu.VMEM((2, tok_count, tile), jnp.bfloat16))

    pl.run_scoped(
        forward_back,
        pltpu.VMEM((tok_count, feat), jnp.bfloat16),
        pltpu.VMEM((feat, tok_count), jnp.bfloat16),
        pltpu.VMEM((2, feat, tile), jnp.bfloat16),
        pltpu.VMEM((2, tile, feat), jnp.bfloat16),
    )

    def backward(d_out, d_gate, d_mix, d_signal, table_v, table_tv, d_kernel, d_taps):
        d_waves = waves
        load("table again", table, table_v)
        load("table_t again", table_t, table_tv)
        totals = {}

        def sum_rows(at, index, values):
            totals[at] = values + (totals[at] if index > 0 else 0.0)
            if index == row_steps - 1:
                levels[0, at : at + 1, :] = jnp.sum(totals[at], axis=0, keepdims=True)

        def back_piece(index):
            if index == 0:
                levels[0] = jnp.zeros(levels.shape[1:], jnp.float32)
            rows = rows_of(index)
            sums_of = [0.0, 0.0]
            for part, _ in blocks_of(step_rows, feat):
                at = under(index, part)
                unit, inverse = norm_of(left_v[at, :])
                grad = running[at, :]
                sums_of = [sums_of[0] + column_sums(grad * unit), sums_of[1] + column_sums(grad)]
                scaled = grad * ln2_gain[...][None, :]
                d_left = cot[at, :].astype(jnp.float32) + inverse * (
                    scaled
                    - jnp.mean(scaled, axis=-1, keepdims=True)
                    - unit * jnp.mean(scaled * unit, axis=-1, keepdims=True)
                )
                running[at, :] = d_left
                d_out[at, :] = d_left.astype(jnp.bfloat16)
            d_branch = dot_nt(d_out[rows, :], w_out_v[...])
            for part, columns in blocks_of(step_rows, feat):
                at = under(index, part)
                values = d_branch[part, columns]
                d_mix[at, columns] = (
                    values * gate_v[at, columns].astype(jnp.float32) * (1.0 / half)
                ).astype(jnp.bfloat16)
                d_gate[at, columns] = (values * mixed_v[at, columns].astype(jnp.float32)).astype(jnp.bfloat16)
            sum_rows(0, index, sums_of[0])
            sum_rows(1, index, sums_of[1])
            if index == row_steps - 1:
                load("tokens again", tokens, gate_v)

        def gate_piece():
            downs[planes - 3].sent()
            weight_rows(gate_chunk, normed_v, d_gate)

        def out_piece():
            ups[planes - 3].sent()
            weight_rows(out_chunk, branch_v, d_out)

        def signal_piece():
            ups[planes - 2].sent()
            weight_rows(signal_chunk, normed_v, d_signal)

        wave_rows, wave_cols = 256, 256

        def wave_step(down, cols):
            real, imag = pl.ds(down * wave_rows, wave_rows), pl.ds(half + down * wave_rows, wave_rows)
            first_r = dot_nn(table_v[real, :], d_mix[0:half, cols])
            first_i = dot_nn(table_v[imag, :], d_mix[0:half, cols])
            second_r = dot_nn(table_v[real, :], d_mix[half:, cols])
            second_i = dot_nn(table_v[imag, :], d_mix[half:, cols])

            odd = lax.broadcasted_iota(jnp.int32, (16, 1), 0) % 2
            parity = (1 - 2 * odd).astype(jnp.float32)
            for part, _ in blocks_of(wave_rows, wave_cols):
                re = pl.ds(down * wave_rows + part.start, 16)
                im = pl.ds(half + down * wave_rows + part.start, 16)

                def wide(ref, which, at):
                    return ref[which, at, cols].astype(jnp.float32)

                def keep(ref, which, at, values):
                    ref[which, at, cols if ref.shape[2] == feat else slice(None)] = values.astype(jnp.bfloat16)

                fr, fi, sr, si = first_r[part], first_i[part], second_r[part], second_i[part]
                hr, hi = wide(waves, 0, re), wide(waves, 0, im)
                far_r, far_i = (hr * sr + hi * si) * long, (hr * si - hi * sr) * long
                keep(d_kernel, 1, re, far_r)
                keep(d_kernel, 1, im, far_i)
                tr, ti = wide(waves, 1, re), wide(waves, 1, im)
                keep(d_kernel, 0, re, hr * fr + hi * fi + tr * sr + ti * si + parity * far_i)
                keep(d_kernel, 0, im, hr * fi - hi * fr + tr * si - ti * sr - parity * far_r)
                lr, li = wide(kernels, 0, re), wide(kernels, 0, im)
                keep(d_waves, 1, re, lr * sr + li * si)
                keep(d_waves, 1, im, lr * si - li * sr)
                cr, ci = wide(kernels, 1, re), wide(kernels, 1, im)
                keep(d_waves, 0, re, lr * fr + li * fi + cr * sr + ci * si)
                keep(d_waves, 0, im, lr * fi - li * fr + cr * si - ci * sr)

        pad = 8
        d_taps[0:pad, :] = jnp.zeros((pad, wave_cols), jnp.float32)
        d_taps[pad + tok_count :, :] = jnp.zeros((pad, wave_cols), jnp.float32)
        pool_rows = 16

        def column_step(across):
            cols = pl.ds(across * wave_cols, wave_cols)
            for down in range(half // wave_rows):
                wave_step(down, cols)
            for which in range(2):
                d_taps[pad + which * half : pad + (which + 1) * half, :] = dot_nn(table_tv[...], d_kernel[which])
            for index in range(tok_count // pool_rows):
                at = pad + index * pool_rows
                taps_held[at - pad : at - pad + pool_rows, cols] = (
                    (
                        d_taps[at - 1 : at - 1 + pool_rows, :]
                        + d_taps[at : at + pool_rows, :]
                        + d_taps[at + 1 : at + 1 + pool_rows, :]
                    )
                    / 3.0
                ).astype(jnp.bfloat16)


        def column_piece(across):
            if across == 0:
                loads["table again"].wait()
                loads["table_t again"].wait()
            column_step(across)
            taps[across].start()
            if across == blocks - 1:
                load("w_in signal", w_in.at[:, 0:feat], cot.at[0:feat, :])
                load("w_in gate", w_in.at[:, feat : 2 * feat], d_mix.at[0:feat, :])

        def down_again(t):
            return (waves if t < 2 else kernels).at[t % 2, 0:tile, :]

        def load_again(t):
            rows = pl.ds(t * tile, tile)
            load(("again", t), lambda: w_down.at[rows, :], lambda: down_again(t))

        def unwave_piece(which):
            for at in range(0, half, step_rows):
                d_signal[which * half + at : which * half + at + step_rows, :] = dot_nn(
                    table_tv[at : at + step_rows, :], d_waves[which]
                ).astype(jnp.bfloat16)
            if which == 1:
                for t in range(planes):
                    load_again(t)

        def grad_copy(index):
            rows = rows_of(index)
            return pltpu.make_async_copy(
                running.at[rows, :], input_grad.at[rows, :], load_sems.at[STORES + index]
            )

        def out_copy(index):
            rows = rows_of(index)
            return pltpu.make_async_copy(
                mixed_v.at[rows, :], block_out.at[rows, :], load_sems.at[STORES + row_steps + index]
            )

        def input_piece(index):
            if index == 0:
                loads["tokens again"].wait()
                loads["w_in signal"].wait()
                loads["w_in gate"].wait()
            rows = rows_of(index)
            d_normed = dot_nt(d_signal[rows, :], cot[0:feat, :]) + dot_nt(
                d_gate[rows, :], d_mix[0:feat, :]
            )
            sums_of = [0.0, 0.0]
            for part, _ in blocks_of(step_rows, feat):
                at = under(index, part)
                unit, inverse = norm_of(gate_v[at, :].astype(jnp.float32))
                grad = d_normed[part]
                sums_of = [sums_of[0] + column_sums(grad * unit), sums_of[1] + column_sums(grad)]
                scaled = grad * ln1_gain[...][None, :]
                running[at, :] = running[at, :] + inverse * (
                    scaled
                    - jnp.mean(scaled, axis=-1, keepdims=True)
                    - unit * jnp.mean(scaled * unit, axis=-1, keepdims=True)
                )
            grad_copy(index).start()
            sum_rows(2, index, sums_of[0])
            sum_rows(3, index, sums_of[1])

        def output_piece(index):
            if index == 0:
                for t in range(planes):
                    loads["again", t].wait()
            rows = rows_of(index)
            total = left_v[rows, :]
            for t in range(planes):
                total = total + dot_nn(active[t, rows, :], down_again(t)[...])
            mixed_v[rows, :] = total.astype(jnp.bfloat16)
            out_copy(index).start()

        back_piece(0)
        downs[1].over_second()
        downs[2].over_first()
        downs[3].over_core()
        back_piece(1)
        back_piece(2)
        ups[1].over_second()
        ups[2].over_first()
        ups[3].over_core()
        back_piece(3)
        column_piece(0)
        downs[2].over_second()
        out_piece()
        taps[0].over_core()
        column_piece(1)
        ups[2].over_second()
        downs[3].over_first()
        ups[3].over_first()
        column_piece(2)
        taps[1].over_core()
        out_chunk.over_core()
        gate_piece()
        taps[2].over_core()
        taps[0].over_first()
        ups[3].over_second()
        unwave_piece(0)
        gate_chunk.over_core()
        taps[1].over_first()
        taps[0].over_second()
        downs[3].over_second()
        unwave_piece(1)
        signal_piece()
        input_piece(0)
        out_chunk.over_first()
        taps[0].over_planes()
        own_up(3)
        signal_chunk.over_core()
        taps[2].over_first()
        input_piece(1)
        output_piece(0)
        input_piece(2)
        taps[1].over_second()
        taps[2].over_second()
        out_chunk.over_second()
        gate_chunk.over_first()
        taps[0].back_y()
        input_piece(3)
        sums.start()
        taps[1].over_planes()
        own_up(1)
        own_down(2)
        own_up(2)
        own_down(0)
        signal_chunk.over_first()
        taps[2].over_planes()
        output_piece(1)
        gate_chunk.over_second()
        own_taps(0)
        taps[1].back_y()
        own_down(1)
        sums.over(0)
        signal_chunk.over_second()
        own_out()
        taps[2].back_y()
        own_up(0)
        output_piece(2)
        own_gate()
        own_down(3)
        output_piece(3)
        own_taps(1)
        own_taps(2)
        own_signal()
        for index in range(row_steps):
            grad_copy(index).wait()
            out_copy(index).wait()

    pl.run_scoped(
        backward,
        *[pltpu.VMEM((tok_count, feat), jnp.bfloat16)] * 4,
        pltpu.VMEM((tok_count, half), jnp.bfloat16),
        pltpu.VMEM((half, tok_count), jnp.bfloat16),
        pltpu.VMEM((2, tok_count, tap_cols), jnp.bfloat16),
        pltpu.VMEM((tok_count + 16, tap_cols), jnp.float32),
    )

    sums_out[...] = sums.finish()
    for one in (downs[planes - 2], ups[planes - 1], downs[planes - 1], out_chunk, gate_chunk, signal_chunk):
        one.sent()
    for index in range(blocks):
        taps_copy(index).wait()


def hand_on_kernel(raw_taps, taps_sum, *others):
    count = (len(others) - 5) // 3
    sources, raw_grad, targets = others[:count], others[count], others[count + 1 : 2 * count + 1]
    raw_v, taps_v, grad_v = others[2 * count + 1 : 2 * count + 4]
    rooms, sems = others[2 * count + 4 : -1], others[-1]
    fetches = [pltpu.make_async_copy(taps_sum, taps_v, sems.at[0]), pltpu.make_async_copy(raw_taps, raw_v, sems.at[1])]
    stores = []
    for source, room, target in zip(sources, rooms, targets):
        rows = source.shape[0]
        parts = 4 if rows % 64 == 0 else 1
        for part in range(parts):
            at = pl.ds(part * (rows // parts), rows // parts)
            sem = sems.at[1 + len(fetches)]
            fetches.append(pltpu.make_async_copy(source.at[at, :], room.at[at, :], sem))
            stores.append(pltpu.make_async_copy(room.at[at, :], target.at[at, :], sem))
    for fetch in fetches:
        fetch.start()
    for fetch in fetches[:2]:
        fetch.wait()
    grad_v[...] = jnp.where(jnp.abs(raw_v[...]) > shrink_level, taps_v[...].astype(jnp.float32), 0.0)
    mask = pltpu.make_async_copy(grad_v, raw_grad, sems.at[2])
    mask.start()
    for fetch, store in zip(fetches[2:], stores):
        fetch.wait()
        store.start()
    for store in [mask] + stores:
        store.wait()


def hand_on(raw_taps, taps_sum, *sources):
    whole = pl.BlockSpec(memory_space=pl.ANY)
    return pl.pallas_call(
        hand_on_kernel,
        out_shape=[jax.ShapeDtypeStruct(raw_taps.shape, jnp.float32)]
        + [jax.ShapeDtypeStruct(source.shape, source.dtype) for source in sources],
        in_specs=[whole] * (2 + len(sources)),
        out_specs=[whole] * (1 + len(sources)),
        scratch_shapes=[
            pltpu.VMEM(raw_taps.shape, jnp.float32),
            pltpu.VMEM(taps_sum.shape, taps_sum.dtype),
            pltpu.VMEM(raw_taps.shape, jnp.float32),
        ]
        + [pltpu.VMEM(source.shape, source.dtype) for source in sources]
        + [pltpu.SemaphoreType.DMA((3 + 4 * len(sources),))],
        compiler_params=pltpu.CompilerParams(vmem_limit_bytes=VMEM_BYTES),
    )(raw_taps, taps_sum, *sources)


def linked_block(
    planes,
    tokens,
    lengths,
    raw_taps,
    ln1_gain,
    ln1_shift,
    w_in,
    w_out,
    ln2_gain,
    ln2_shift,
    w_up,
    w_down,
    cotangent,
):
    tok_count, feat = tokens.shape
    half = tok_count // 2
    tile = w_up.shape[1] // planes
    table = jnp.asarray(wave_table(half), jnp.bfloat16)
    table_t = jnp.asarray(wave_table(half).T, jnp.bfloat16)
    shares = 8 * planes
    rows = feat // shares
    block = (16, 128 * PART)
    chunks = 2 * planes + 3
    bf16, f32 = jnp.bfloat16, jnp.float32
    whole = pl.BlockSpec(memory_space=pl.ANY)
    near = pl.BlockSpec(memory_space=pltpu.VMEM)
    results = pl.pallas_call(
        functools.partial(block_kernel, planes),
        out_shape=(
            jax.ShapeDtypeStruct((tok_count, feat), bf16),
            jax.ShapeDtypeStruct((tok_count, feat), f32),
            jax.ShapeDtypeStruct((half, feat), bf16),
            jax.ShapeDtypeStruct((8, feat), f32),
            jax.ShapeDtypeStruct((rows, 2 * feat), f32),
            jax.ShapeDtypeStruct((rows, feat), f32),
            jax.ShapeDtypeStruct((rows, planes * tile), f32),
            jax.ShapeDtypeStruct((tile // 8, feat), f32),
        ),
        in_specs=[pl.BlockSpec(memory_space=pltpu.SMEM)] + [whole] * 9 + [near] * 4,
        out_specs=(whole,) * 3 + (near,) * 5,
        scratch_shapes=[
            pltpu.VMEM((2 * FLIGHTS, shares) + block, bf16),
            pltpu.VMEM((4, 4 * planes) + block, bf16),
            pltpu.VMEM((4, 2 * planes) + block, bf16),
            pltpu.VMEM((4, planes) + block, bf16),
            pltpu.VMEM((planes + 3, planes) + block, bf16),
            pltpu.VMEM((planes, planes) + block, bf16),
            pltpu.VMEM((tok_count, feat), bf16),
            pltpu.VMEM((tok_count // 2, feat), bf16),
            pltpu.VMEM((tok_count // 4, feat), bf16),
            pltpu.VMEM((tok_count // 8, feat), bf16),
            pltpu.VMEM(((planes - 1) * (tok_count // shares), feat), bf16),
            pltpu.VMEM((half, feat), bf16),
            pltpu.VMEM((2, 8, feat), f32),
            pltpu.VMEM((planes + 6, 8, feat), f32),
            pltpu.VMEM((tok_count, feat), bf16),
            pltpu.VMEM((planes, tok_count, tile), bf16),
            pltpu.VMEM((tok_count, feat), f32),
            pltpu.VMEM((feat, tok_count), bf16),
            pltpu.VMEM((feat, tok_count), bf16),
            pltpu.VMEM((feat, feat), bf16),
            pltpu.VMEM((tok_count, feat), bf16),
            pltpu.VMEM((tok_count, feat), bf16),
            pltpu.VMEM((tok_count, feat), f32),
            pltpu.VMEM((2, tok_count, feat), bf16),
            pltpu.VMEM((2, tok_count, feat), bf16),
            pltpu.SemaphoreType.DMA((chunks, planes + 2)),
            pltpu.SemaphoreType.DMA((chunks, planes + 2)),
            pltpu.SemaphoreType.DMA((feat // 256, 2 * planes + 6)),
            pltpu.SemaphoreType.DMA((feat // 256, 2 * planes + 6)),
            pltpu.SemaphoreType.DMA((planes + 6,)),
            pltpu.SemaphoreType.DMA((planes + 6,)),
            pltpu.SemaphoreType.DMA((2, feat // 256)),
            pltpu.SemaphoreType.DMA((2, feat // 256)),
            pltpu.SemaphoreType.DMA((STORES + 2 * tok_count // 256,)),
        ],
        compiler_params=pltpu.CompilerParams(
            collective_id=1, has_side_effects=True, vmem_limit_bytes=VMEM_BYTES
        ),
        cost_estimate=pl.CostEstimate(
            flops=2 * tok_count * feat * (5 * w_up.shape[1] + 9 * feat),
            bytes_accessed=40 * tok_count * feat,
            transcendentals=tok_count * w_up.shape[1],
        ),
    )(
        lengths,
        tokens,
        cotangent,
        raw_taps,
        w_in,
        w_out,
        w_up,
        w_down,
        table,
        table_t,
        ln1_gain,
        ln1_shift,
        ln2_gain,
        ln2_shift,
    )
    block_out, input_grad, taps_sum, sums, w_in_grad, w_out_grad, w_up_grad, w_down_grad = results
    raw_grad, block_out, input_grad, w_in_grad, w_out_grad, w_up_grad, w_down_grad = hand_on(
        raw_taps, taps_sum, block_out, input_grad, w_in_grad, w_out_grad, w_up_grad, w_down_grad
    )
    share = lax.axis_index("wide") * 2 + lax.axis_index("narrow")
    mine = lax.dynamic_slice(sums, (0, share * rows), (8, rows))
    return (
        block_out,
        input_grad,
        raw_grad,
        mine[2],
        mine[3],
        w_in_grad,
        w_out_grad,
        mine[0],
        mine[1],
        w_up_grad,
        w_down_grad,
    )


def solution(mesh):
    spread = P(("wide", "narrow"))
    rows = P(("wide", "narrow"), None)
    placed = (rows, spread, P("narrow", None)) + (P(),) * 8 + (rows,)
    wide, narrow = mesh.shape["wide"], mesh.shape["narrow"]

    def block(tokens, lengths, raw_taps, *others):
        fits = (
            narrow == 2
            and wide == 4 * 4
            and lengths.shape[0] == 1
            and raw_taps.shape[0] * 2 == tokens.shape[0]
            and tokens.shape[1] == 24 * wide * narrow
            and others[-2].shape[0] == 96 * wide * narrow
            and tokens.shape[0] % 512 == 0
        )
        if fits:
            return linked_block(wide // 4, tokens, lengths, raw_taps, *others)
        return local(tokens, lengths, raw_taps, *others)

    return jax.shard_map(
        block,
        mesh=mesh,
        in_specs=placed,
        out_specs=(rows, rows, P("narrow", None), spread, spread, rows, rows, spread, spread, rows, rows),
        check_vma=False,
    )
```
